32 devices in a mesh: section: 2 (over x), dp: 8 (over z, y), rep: 2 (over core).
Axes of the slice: x: 2, y: 2, z: 4, core: 2. Of those that a mesh axis runs over, the one named last changes fastest.
Arguments:
- encoder_input: bfloat16 [32, 1024, 512], P(('dp', 'rep')), may hold values from -6 to 6
- action_targets: float32 [32, 100, 14], P(('dp', 'rep')), may hold values from -6 to 6
- arm_counts: int32 [32], P(('dp', 'rep')), may hold values from 1 to 2
- encoder_project: bfloat16 [512, 1536], replicated, may hold values from -0.25 to 0.25
- encoder_combine: bfloat16 [512, 512], replicated, may hold values from -6 to 6
- encoder_expand: bfloat16 [512, 3200], replicated, may hold values from -0.25 to 0.25
- encoder_reduce: bfloat16 [3200, 512], replicated, may hold values from -0.21875 to 0.21875
- encoder_gains: float32 [2, 512], replicated, may hold values from 0.1 to 1.9
- encoder_shifts: float32 [2, 512], replicated, may hold values from -3 to 3
- query_embed: bfloat16 [100, 512], replicated, may hold values from -6 to 6
- decoder_project: bfloat16 [512, 1536], replicated, may hold values from -0.25 to 0.25
- decoder_combine: bfloat16 [512, 512], replicated, may hold values from -1.5 to 1.5
- cross_query: bfloat16 [512, 512], replicated, may hold values from -0.25 to 0.25
- cross_memory: bfloat16 [512, 1024], replicated, may hold values from -0.25 to 0.25
- cross_combine: bfloat16 [512, 512], replicated, may hold values from -6 to 6
- decoder_expand: bfloat16 [512, 3200], replicated, may hold values from -0.25 to 0.25
- decoder_reduce: bfloat16 [3200, 512], replicated, may hold values from -0.21875 to 0.21875
- decoder_gains: float32 [3, 512], replicated, may hold values from 0.1 to 1.9
- decoder_shifts: float32 [3, 512], replicated, may hold values from -3 to 3
- action_head: bfloat16 [512, 14], replicated, may hold values from -0.5 to 0.5
Outputs:
- memory: bfloat16 [32, 1024, 512], P(('dp', 'rep'))
- slab_gradient: bfloat16 [2, 32, 1024, 512], P('section', ('dp', 'rep'))
- grad_encoder_project: float32 [512, 1536], P(('section', 'dp'))
- grad_encoder_combine: float32 [512, 512], P(('section', 'dp'))
- grad_encoder_expand: float32 [512, 3200], P(('section', 'dp'))
- grad_encoder_reduce: float32 [3200, 512], P(('section', 'dp'))
- grad_encoder_gains: float32 [2, 512], P(None, ('section', 'dp'))
- grad_encoder_shifts: float32 [2, 512], P(None, ('section', 'dp'))
- grad_query_embed: float32 [100, 512], P(None, ('section', 'dp'))
- grad_decoder_project: float32 [512, 1536], P(('section', 'dp'))
- grad_decoder_combine: float32 [512, 512], P(('section', 'dp'))
- grad_cross_query: float32 [512, 512], P(('section', 'dp'))
- grad_cross_memory: float32 [512, 1024], P(('section', 'dp'))
- grad_cross_combine: float32 [512, 512], P(('section', 'dp'))
- grad_decoder_expand: float32 [512, 3200], P(('section', 'dp'))
- grad_decoder_reduce: float32 [3200, 512], P(('section', 'dp'))
- grad_decoder_gains: float32 [3, 512], P(None, ('section', 'dp'))
- grad_decoder_shifts: float32 [3, 512], P(None, ('section', 'dp'))
- grad_action_head: float32 [512, 14], P(('section', 'dp'))
The draws below stay inside these ranges and needn't reach their ends.
All inputs are finite; a program needn't handle non-finite values.
Results may differ from the reference program's by a relative error of at most 0.012.
Values may be sent and summed in bfloat16 or wider, within the bound.
A program may use at most 320 MiB of HBM per device.

```python
import jax
import jax.numpy as jnp
from jax import lax

D = 512
HEADS = 8
HEAD_DIM = 64
FF = 3200
JOINTS = 14
QUERIES = 100
MEM_LEN = 1024
EPISODES = 32


def touch_ends(result, rng, low, high):
    dims = result.shape
    place = [jax.random.randint(jax.random.fold_in(rng, axis), (), 0, dims[axis]) for axis in range(len(dims))]
    result = result.at[tuple(place)].set(low)
    longest = dims.index(max(dims))
    place[longest] = (place[longest] + 1) % dims[longest]
    return result.at[tuple(place)].set(high)


def steps_of(rng, extent, shards, smallest, high):
    gain, own = 1.0, jax.random.fold_in(rng, 6)
    for dim, parts in shards:
        steps = jnp.exp(jax.random.uniform(jax.random.fold_in(own, dim), (parts,), jnp.float32, smallest / len(shards), high / len(shards)))
        gain = gain * jnp.repeat(steps, extent[dim] // parts).reshape([-1 if axis == dim else 1 for axis in range(len(extent))])
    return gain


def noise(rng, shape, scale, reach, cuts=(), held_as=jnp.bfloat16):
    level = steps_of(rng, shape, cuts, -0.22, 0.18) if cuts else 1.0
    values = jax.random.normal(rng, shape, jnp.float32) * scale * level
    return jnp.minimum(jnp.maximum(values, -reach), reach).astype(held_as)


def setup_inputs(seed: int = 0) -> dict:
    key_of = jax.random.split(jax.random.key(seed), 21)
    return {
        "encoder_input": noise(key_of[0], (EPISODES, MEM_LEN, D), 1.0, 6.0, ((0, 16),)),
        "action_targets": noise(key_of[1], (EPISODES, QUERIES, JOINTS), 1.0, 6.0, ((0, 16),), jnp.float32),
        "arm_counts": touch_ends(jax.random.randint(key_of[2], (EPISODES,), 1, 3), jax.random.fold_in(key_of[2], 1), 1, 2).astype(jnp.int32),
        "encoder_project": noise(key_of[3], (D, 3 * D), D ** -0.5, 0.25),
        "encoder_combine": noise(key_of[4], (D, D), (max(1, D // MEM_LEN)) ** -0.5, 6.0),
        "encoder_expand": noise(key_of[5], (D, FF), D ** -0.5, 0.25),
        "encoder_reduce": noise(key_of[6], (FF, D), (FF // 4) ** -0.5, 0.21875),
        "encoder_gains": jnp.clip(1.0 + 0.18 * jax.random.normal(key_of[7], (2, D), jnp.float32), 0.1, 1.9),
        "encoder_shifts": noise(key_of[8], (2, D), 0.3, 3.0, (), jnp.float32),
        "query_embed": noise(key_of[9], (QUERIES, D), 1.0, 6.0),
        "decoder_project": noise(key_of[10], (D, 3 * D), D ** -0.5, 0.25),
        "decoder_combine": noise(key_of[11], (D, D), (max(1, 3 * D // QUERIES)) ** -0.5, 1.5),
        "cross_query": noise(key_of[12], (D, D), D ** -0.5, 0.25),
        "cross_memory": noise(key_of[13], (D, 2 * D), D ** -0.5, 0.25),
        "cross_combine": noise(key_of[14], (D, D), (max(1, D // MEM_LEN)) ** -0.5, 6.0),
        "decoder_expand": noise(key_of[15], (D, FF), D ** -0.5, 0.25),
        "decoder_reduce": noise(key_of[16], (FF, D), (FF // 4) ** -0.5, 0.21875),
        "decoder_gains": jnp.clip(1.0 + 0.18 * jax.random.normal(key_of[17], (3, D), jnp.float32), 0.1, 1.9),
        "decoder_shifts": noise(key_of[18], (3, D), 0.3, 3.0, (), jnp.float32),
        "action_head": noise(key_of[19], (D, JOINTS), (D // 4) ** -0.5, 0.5),
    }


EPSILON = 1e-05
PRECISE = lax.Precision.HIGHEST

@jax.custom_vjp
def low(v):
    return lax.optimization_barrier(v.astype(jnp.bfloat16)).astype(jnp.float32)

@jax.custom_vjp
def low_back(v):
    return v

def low_keep(v):
    return (low(v), None)

def low_pass(kept, grad):
    return (grad,)

def back_keep(v):
    return (v, None)

def back_low(kept, grad):
    return (low(grad),)
low.defvjp(low_keep, low_pass)
low_back.defvjp(back_keep, back_low)

def product(left_side, right_side):
    return jnp.dot(left_side, right_side, precision=PRECISE, preferred_element_type=jnp.float32)

def layer_norm(residual, gain_row, shift_row):
    centre = lax.optimization_barrier(jnp.mean(residual, axis=-1, keepdims=True))
    centred = residual - centre
    spread = lax.optimization_barrier(jnp.mean(centred * centred, axis=-1, keepdims=True))
    return centred * lax.rsqrt(spread + EPSILON) * gain_row + shift_row

def attention(queries, key_rows, value_rows):
    row_count = queries.shape[0]
    column_count = key_rows.shape[0]
    query_heads = queries.reshape(row_count, HEADS, HEAD_DIM)
    key_heads = key_rows.reshape(column_count, HEADS, HEAD_DIM)
    value_heads = value_rows.reshape(column_count, HEADS, HEAD_DIM)
    scores = jnp.einsum('qhd,khd->hqk', query_heads, key_heads, precision=PRECISE) * HEAD_DIM ** (-0.5)
    scores = low_back(scores)
    weights = low(jax.nn.softmax(scores, axis=-1))
    mixed_heads = jnp.einsum('hqk,khd->qhd', weights, value_heads, precision=PRECISE)
    return low(low_back(mixed_heads.reshape(row_count, HEADS * HEAD_DIM)))

def feed_forward(normed, inner_w, outer_w):
    hidden = low_back(product(low(normed), inner_w))
    return low_back(product(low(jax.nn.gelu(hidden, approximate=True)), outer_w))

def encoder(inputs, project_w, combine_w, expand_w, reduce_w, gain_rows, shift_rows):
    model_width = inputs.shape[1]
    packed = low(low_back(product(inputs, project_w)))
    mixed_heads = attention(packed[:, :model_width], packed[:, model_width:2 * model_width], packed[:, 2 * model_width:])
    first_norm = layer_norm(inputs + low_back(product(mixed_heads, combine_w)), gain_rows[0], shift_rows[0])
    return layer_norm(first_norm + feed_forward(first_norm, expand_w, reduce_w), gain_rows[1], shift_rows[1])

def episode_loss(predicted, target, arm_count):
    misfit = predicted - target
    joint_index = jnp.arange(JOINTS)
    active = (joint_index < JOINTS // 2 * arm_count).astype(jnp.float32)
    return 2.0 / arm_count.astype(jnp.float32) * jnp.sum(active * (jnp.sqrt(misfit * misfit + 1.0) - 1.0))

def decoder(memory_rows, starts, project_w, combine_w, query_w, memory_w, cross_w, expand_w, reduce_w, gain_rows, shift_rows, head_w, target, arm_count):
    model_width = starts.shape[1]
    packed = low(low_back(product(starts, project_w)))
    self_mixed = attention(packed[:, :model_width], packed[:, model_width:2 * model_width], packed[:, 2 * model_width:])
    first_norm = layer_norm(starts + low_back(product(self_mixed, combine_w)), gain_rows[0], shift_rows[0])
    cross_queries = low(low_back(product(low(first_norm), query_w)))
    memory_pair = low(low_back(product(memory_rows, memory_w)))
    cross_mixed = attention(cross_queries, memory_pair[:, :model_width], memory_pair[:, model_width:])
    second_norm = layer_norm(first_norm + low_back(product(cross_mixed, cross_w)), gain_rows[1], shift_rows[1])
    third_norm = layer_norm(second_norm + feed_forward(second_norm, expand_w, reduce_w), gain_rows[2], shift_rows[2])
    predicted = low_back(product(low(third_norm), head_w))
    return episode_loss(predicted, target, arm_count)

def reference(encoder_input, action_targets, arm_counts, encoder_project, encoder_combine, encoder_expand, encoder_reduce, encoder_gains, encoder_shifts, query_embed, decoder_project, decoder_combine, cross_query, cross_memory, cross_combine, decoder_expand, decoder_reduce, decoder_gains, decoder_shifts, action_head):

    def widen(array):
        return array.astype(jnp.float32)
    encoder_weights = tuple((widen(item) for item in (encoder_project, encoder_combine, encoder_expand, encoder_reduce, encoder_gains, encoder_shifts)))
    decoder_weights = tuple((widen(item) for item in (query_embed, decoder_project, decoder_combine, cross_query, cross_memory, cross_combine, decoder_expand, decoder_reduce, decoder_gains, decoder_shifts, action_head)))

    def episode(totals, pieces):
        inputs, target, arm_count = pieces
        layer_out, encoder_back = jax.vjp(lambda source, *params: encoder(source, *params), widen(inputs), *encoder_weights)
        memory_rows = low(layer_out)
        loss_value, decoder_back = jax.vjp(lambda stored, *params: decoder(stored, *params, target, arm_count), memory_rows, *decoder_weights)
        decoder_grads = decoder_back(jnp.ones((), jnp.float32))
        memory_grad = low(decoder_grads[0])
        encoder_grads = encoder_back(memory_grad)
        fresh = tuple(encoder_grads[1:]) + tuple(decoder_grads[1:])
        totals = tuple((old + new for old, new in zip(totals, fresh)))
        return (totals, (memory_rows.astype(jnp.bfloat16), encoder_grads[0].astype(jnp.bfloat16), memory_grad.astype(jnp.bfloat16)))
    start_totals = tuple((jnp.zeros(item.shape, jnp.float32) for item in encoder_weights + decoder_weights))
    totals, outputs = lax.scan(episode, start_totals, (encoder_input, action_targets, arm_counts))
    memory_all, input_grads, memory_grads = outputs
    return (memory_all, jnp.stack((input_grads, memory_grads)), totals[0], totals[1], totals[2], totals[3], totals[4], totals[5], totals[6], totals[7], totals[8], totals[9], totals[10], totals[11], totals[12], totals[13], totals[14], totals[15], totals[16])
```

```python
import functools

import jax
import jax.numpy as jnp
from jax import lax
from jax.experimental import pallas as pl
from jax.experimental.pallas import tpu as pltpu
from jax.sharding import PartitionSpec as P

HEADS = 8
EPSILON = 1e-05
LANES = 128
PAD_ROWS = 128
F32 = jnp.float32
BF16 = jnp.bfloat16
NN = (((1,), (0,)), ((), ()))
NT = (((1,), (1,)), ((), ()))
TN = (((0,), (0,)), ((), ()))
VMEM_BYTES = 56 * 1024 * 1024
ROOT_2_PI = 0.7978845608028654
CUBE = 0.044715


def dot(left, right, dims):
    return lax.dot_general(left, right, dims, preferred_element_type=F32)


def call(kernel, flops, moved, **options):
    return pl.pallas_call(
        kernel,
        compiler_params=pltpu.CompilerParams(vmem_limit_bytes=VMEM_BYTES),
        cost_estimate=pl.CostEstimate(flops=flops, bytes_accessed=moved, transcendentals=0),
        **options,
    )


def shape_of(dims, dtype):
    return jax.ShapeDtypeStruct(dims, dtype)


def whole(array):
    rank = len(array.shape)
    return pl.BlockSpec(array.shape, lambda *_: (0,) * rank, pipeline_mode=pl.Buffered(1))


def normed(residual):
    centre = jnp.mean(residual, axis=-1, keepdims=True)
    centred = residual - centre
    spread = jnp.mean(centred * centred, axis=-1, keepdims=True)
    scale = lax.rsqrt(spread + EPSILON)
    return centred * scale, scale


def normed_back(grad, gain, rows, scale):
    weighted = grad * gain
    return scale * (
        weighted
        - jnp.mean(weighted, axis=-1, keepdims=True)
        - rows * jnp.mean(weighted * rows, axis=-1, keepdims=True)
    )


def gelu_and_slope(value):
    square = value * value
    bend = jnp.tanh(value * (ROOT_2_PI + (ROOT_2_PI * CUBE) * square))
    half = 0.5 + 0.5 * bend
    slope = half + value * (0.5 - 0.5 * bend * bend) * (
        ROOT_2_PI + (3.0 * ROOT_2_PI * CUBE) * square
    )
    return value * half, slope


def column_sum(value):
    return jnp.sum(value, axis=0, keepdims=True)


def attend_kernel(q_ref, k_ref, v_ref, mixed_ref, log_ref):
    count = q_ref.shape[0]
    lane = lax.broadcasted_iota(jnp.int32, (1, LANES), 1)
    keys = k_ref[...]
    values = v_ref[...].T
    queries = q_ref[...] * jnp.asarray(0.125, BF16)
    for head in range(2):
        own = (lane < 64) if head == 0 else (lane >= 64)
        head_keys = jnp.where(own, keys, jnp.zeros_like(keys))
        extended = jnp.concatenate(
            [values[64 * head : 64 * head + 64], jnp.ones((16, count), BF16)], axis=0
        )
        scores = dot(head_keys, queries, NT)
        largest = jnp.max(scores, axis=0, keepdims=True)
        raised = jnp.exp(scores - largest).astype(BF16)
        mixed = dot(extended, raised, NN)
        total = mixed[64:65]
        mixed_ref[pl.ds(64 * head, 64), :] = (mixed[:64] * (1.0 / total)).astype(BF16)
        log_ref[0, pl.ds(head, 1), :] = largest + jnp.log(total)


def attend(packed):
    rows, width = packed.shape[0], packed.shape[1] // 3
    pairs = width // LANES
    column = lambda first: pl.BlockSpec((rows, LANES), lambda j: (0, first + j))
    return call(
        attend_kernel,
        4 * rows * rows * width * 4,
        rows * width * 8,
        grid=(pairs,),
        in_specs=[column(0), column(pairs), column(2 * pairs)],
        out_specs=[
            pl.BlockSpec((LANES, rows), lambda j: (j, 0)),
            pl.BlockSpec((1, 2, rows), lambda j: (j, 0, 0)),
        ],
        out_shape=[shape_of((width, rows), BF16), shape_of((pairs, 2, rows), F32)],
    )(packed, packed, packed)


def attend_back_kernel(block, q_ref, k_ref, v_ref, do_ref, mixed_ref, log_ref, dq_ref, dk_ref, dv_ref):
    count = q_ref.shape[0]
    lane = lax.broadcasted_iota(jnp.int32, (1, LANES), 1)
    keys = k_ref[...]
    values = v_ref[...]
    queries = q_ref[...] * jnp.asarray(0.125, BF16)
    scaled_keys = keys * jnp.asarray(0.125, BF16)
    grads = do_ref[...]
    queries_t = queries.T
    grads_t = grads.T
    logs = log_ref[0].T
    shared = mixed_ref[...].astype(F32) * grads_t.astype(F32)
    inner = jnp.concatenate([column_sum(shared[:64]), column_sum(shared[64:])], axis=0).T
    dq_parts = [[], []]
    dk_parts = []
    dv_parts = []
    for head in range(2):
        own = (lane < 64) if head == 0 else (lane >= 64)
        head_queries = jnp.where(own, queries, jnp.zeros_like(queries))
        head_grads = jnp.where(own, grads, jnp.zeros_like(grads))
        dk = None
        dv = None
        for start in range(0, count, block):
            part = slice(start, start + block)
            scores = dot(head_queries[part], keys, NT)
            probs = jnp.exp(scores - logs[part, head : head + 1])
            grad_probs = dot(head_grads[part], values, NT)
            grad_scores = (probs * (grad_probs - inner[part, head : head + 1])).astype(BF16)
            new_v = dot(grads_t[64 * head : 64 * head + 64, part], probs.astype(BF16), NN)
            new_k = dot(queries_t[64 * head : 64 * head + 64, part], grad_scores, NN)
            dv = new_v if dv is None else dv + new_v
            dk = new_k if dk is None else dk + new_k
            dq_parts[head].append(dot(grad_scores, scaled_keys, NN))
        dk_parts.append(dk)
        dv_parts.append(dv)
    dk_ref[...] = jnp.concatenate(dk_parts, axis=0).T.astype(BF16)
    dv_ref[...] = jnp.concatenate(dv_parts, axis=0).T.astype(BF16)
    for index in range(count // block):
        dq_ref[pl.ds(index * block, block), :] = jnp.where(
            lane < 64, dq_parts[0][index], dq_parts[1][index]
        ).astype(BF16)


def attend_back(packed, grad_mixed, mixed, logs):
    rows, width = packed.shape[0], packed.shape[1] // 3
    pairs = width // LANES
    column = lambda first: pl.BlockSpec((rows, LANES), lambda j: (0, first + j))
    return call(
        functools.partial(attend_back_kernel, 256),
        10 * rows * rows * width * 3,
        rows * width * 16,
        grid=(pairs,),
        in_specs=[
            column(0),
            column(pairs),
            column(2 * pairs),
            column(0),
            pl.BlockSpec((LANES, rows), lambda j: (j, 0)),
            pl.BlockSpec((1, 2, rows), lambda j: (j, 0, 0)),
        ],
        out_specs=[column(0)] * 3,
        out_shape=[shape_of((rows, width), BF16)] * 3,
    )(packed, packed, packed, grad_mixed, mixed, logs)


def encode_rows_kernel(
    x_ref, mixed_ref, combine_ref, expand_ref, reduce_ref, gain_ref, shift_ref, memory_w_ref,
    first_ref, low_ref, active_ref, slope_ref, second_ref, memory_ref, pair_ref,
):
    residual = x_ref[...].astype(F32) + dot(mixed_ref[...], combine_ref[...], TN)
    first_ref[...] = residual
    rows, _ = normed(residual)
    first = rows * gain_ref[0:1, :] + shift_ref[0:1, :]
    low = first.astype(BF16)
    low_ref[...] = low
    total = first
    hidden_size = expand_ref.shape[1]
    step = hidden_size // 5
    for start in range(0, hidden_size, step):
        part = pl.ds(start, step)
        active, slope = gelu_and_slope(dot(low, expand_ref[:, part], NN))
        active = active.astype(BF16)
        active_ref[:, part] = active
        slope_ref[:, part] = slope.astype(BF16)
        total = total + dot(active, reduce_ref[part, :], NN)
    second_ref[...] = total
    rows, _ = normed(total)
    memory = (rows * gain_ref[1:2, :] + shift_ref[1:2, :]).astype(BF16)
    memory_ref[...] = memory
    pair_ref[...] = dot(memory, memory_w_ref[...], NN).astype(BF16)


def encode_rows(x, mixed, combine_w, expand_w, reduce_w, gains, shifts, memory_w):
    rows, width = x.shape
    hidden = expand_w.shape[1]
    block = 256
    line = lambda size: pl.BlockSpec((block, size), lambda i: (i, 0))
    sizes = [(width, F32), (width, BF16), (hidden, BF16), (hidden, BF16), (width, F32), (width, BF16), (2 * width, BF16)]
    return call(
        encode_rows_kernel,
        2 * rows * width * (2 * hidden + 3 * width),
        rows * (hidden * 4 + width * 18) + 8 * width * hidden,
        grid=(rows // block,),
        in_specs=[line(width), pl.BlockSpec((width, block), lambda i: (0, i))]
        + [whole(item) for item in (combine_w, expand_w, reduce_w, gains, shifts, memory_w)],
        out_specs=[line(size) for size, _ in sizes],
        out_shape=[shape_of((rows, size), kind) for size, kind in sizes],
    )(x, mixed, combine_w, expand_w, reduce_w, gains, shifts, memory_w)


def encode_back_kernel(
    pair_ref, first_ref, second_ref, slope_ref, combine_ref, expand_ref, reduce_ref, gain_ref, memory_w_ref,
    grad_memory_ref, branch_ref, hidden_ref, resid_ref, low_ref, mixed_ref, sums_ref,
):
    grad_memory = dot(pair_ref[...], memory_w_ref[...], NT).astype(BF16)
    grad_memory_ref[...] = grad_memory
    grad_last = grad_memory.astype(F32)
    rows, scale = normed(second_ref[...])
    gain_last = column_sum(grad_last * rows)
    shift_last = column_sum(grad_last)
    grad_second = normed_back(grad_last, gain_ref[1:2, :], rows, scale)
    branch = grad_second.astype(BF16)
    branch_ref[...] = branch
    total = grad_second
    hidden_size = expand_ref.shape[1]
    step = hidden_size // 5
    for start in range(0, hidden_size, step):
        part = pl.ds(start, step)
        grad_active = dot(branch, reduce_ref[part, :], NT)
        grad_hidden = (grad_active * slope_ref[:, part].astype(F32)).astype(BF16)
        hidden_ref[:, part] = grad_hidden
        total = total + dot(grad_hidden, expand_ref[:, part], NT)
    rows, scale = normed(first_ref[...])
    gain_first = column_sum(total * rows)
    shift_first = column_sum(total)
    grad_first = normed_back(total, gain_ref[0:1, :], rows, scale)
    resid_ref[...] = grad_first
    low = grad_first.astype(BF16)
    low_ref[...] = low
    mixed_ref[...] = dot(low, combine_ref[...], NT).astype(BF16)
    fresh = jnp.concatenate(
        [gain_first, gain_last, shift_first, shift_last, jnp.zeros((4, gain_first.shape[1]), F32)], axis=0
    )

    @pl.when(pl.program_id(0) == 0)
    def _():
        sums_ref[...] = fresh

    @pl.when(pl.program_id(0) > 0)
    def _():
        sums_ref[...] += fresh


def encode_back(grad_pair, first, second, slope, combine_w, expand_w, reduce_w, gains, memory_w):
    rows, width = first.shape
    hidden = expand_w.shape[1]
    block = 256
    line = lambda size: pl.BlockSpec((block, size), lambda i: (i, 0))
    sizes = [(width, BF16), (width, BF16), (hidden, BF16), (width, F32), (width, BF16), (width, BF16)]
    return call(
        encode_back_kernel,
        2 * rows * width * (2 * hidden + 3 * width),
        rows * (hidden * 4 + width * 18) + 8 * width * hidden,
        grid=(rows // block,),
        in_specs=[line(2 * width), line(width), line(width), line(hidden)]
        + [whole(item) for item in (combine_w, expand_w, reduce_w, gains, memory_w)],
        out_specs=[line(size) for size, _ in sizes] + [pl.BlockSpec((8, width), lambda i: (0, 0))],
        out_shape=[shape_of((rows, size), kind) for size, kind in sizes] + [shape_of((8, width), F32)],
    )(grad_pair, first, second, slope, combine_w, expand_w, reduce_w, gains, memory_w)


def by_rows_kernel(half, left_ref, right_ref, out_ref):
    result = dot(left_ref[...], right_ref[...], TN).astype(BF16)
    for start in range(0, result.shape[0], 2 * half):
        for core in range(2):
            out_ref[core, pl.ds(start // 2, half), :] = result[
                start + core * half : start + core * half + half
            ]


def gradient_by_rows(left, right, step):
    count, rows = left.shape
    columns = right.shape[1]
    return call(
        functools.partial(by_rows_kernel, 16),
        2 * count * rows * columns,
        2 * (count * (rows + columns) + rows * columns),
        grid=(columns // step,),
        in_specs=[whole(left), pl.BlockSpec((count, step), lambda i: (0, i))],
        out_specs=pl.BlockSpec((2, rows // 2, step), lambda i: (0, 0, i)),
        out_shape=shape_of((2, rows // 2, columns), BF16),
    )(left, right)


def by_columns_kernel(left_ref, right_ref, out_ref):
    result = dot(left_ref[...], right_ref[...], TN).astype(BF16)
    half = result.shape[1] // 2
    out_ref[0] = result[:, :half]
    out_ref[1] = result[:, half:]


def gradient_by_columns(left, right, step):
    count, rows = left.shape
    columns = right.shape[1]
    return call(
        by_columns_kernel,
        2 * count * rows * columns,
        2 * (count * (rows + columns) + rows * columns),
        grid=(rows // step,),
        in_specs=[pl.BlockSpec((count, step), lambda i: (0, i)), whole(right)],
        out_specs=pl.BlockSpec((2, step, columns // 2), lambda i: (0, i, 0)),
        out_shape=shape_of((2, rows, columns // 2), BF16),
    )(left, right)


def stacked(rows):
    lane = lax.broadcasted_iota(jnp.int32, (1, rows.shape[1]), 1)
    return jnp.concatenate(
        [jnp.where((lane >= 64 * h) & (lane < 64 * h + 64), rows, jnp.zeros_like(rows)) for h in range(4)],
        axis=0,
    )


def unstacked(rows):
    lane = lax.broadcasted_iota(jnp.int32, (1, rows.shape[1]), 1)
    count = rows.shape[0] // 4
    result = rows[:count]
    for h in range(1, 4):
        result = jnp.where(lane >= 64 * h, rows[h * count : h * count + count], result)
    return result


def few_attend(queries, keys, values, valid):
    mixed = []
    kept = []
    for half in range(2):
        part = slice(256 * half, 256 * half + 256)
        scores = dot(stacked(queries[:, part] * jnp.asarray(0.125, BF16)), keys[:, part], NT)
        if valid < scores.shape[1]:
            column = lax.broadcasted_iota(jnp.int32, (1, scores.shape[1]), 1)
            scores = jnp.where(column < valid, scores, -1e30)
        raised = jnp.exp(scores - jnp.max(scores, axis=1, keepdims=True))
        probs = raised * (1.0 / jnp.sum(raised, axis=1, keepdims=True))
        mixed.append(unstacked(dot(probs.astype(BF16), values[:, part], NN)))
        kept.append(probs)
    return jnp.concatenate(mixed, axis=1).astype(BF16), kept


def few_attend_back(queries, keys, values, kept, grads):
    dq, dk, dv = [], [], []
    for half in range(2):
        part = slice(256 * half, 256 * half + 256)
        probs = kept[half]
        own_queries = stacked(queries[:, part] * jnp.asarray(0.125, BF16))
        own_grads = stacked(grads[:, part])
        grad_probs = dot(own_grads, values[:, part], NT)
        product = probs * grad_probs
        grad_scores = (product - probs * jnp.sum(product, axis=1, keepdims=True)).astype(BF16)
        dv.append(dot(probs.astype(BF16), own_grads, TN))
        dk.append(dot(grad_scores, own_queries, TN))
        dq.append(unstacked(dot(grad_scores, keys[:, part], NN)) * 0.125)
    return jnp.concatenate(dq, axis=1), jnp.concatenate(dk, axis=1), jnp.concatenate(dv, axis=1)


def self_block(starts, project_w, combine_w, gain, shift, valid):
    width = starts.shape[1]
    packed = dot(starts, project_w, NN).astype(BF16)
    queries, keys, values = (packed[:, i * width : (i + 1) * width] for i in range(3))
    mixed, kept = few_attend(queries, keys, values, valid)
    residual = starts.astype(F32) + dot(mixed, combine_w, NN)
    rows, scale = normed(residual)
    return queries, keys, values, mixed, kept, rows, scale, rows * gain + shift


def decode_kernel(
    valid, joints,
    starts_ref, project_ref, combine_ref, query_ref, cross_ref, expand_ref, reduce_ref, gain_ref, shift_ref,
    head_ref, pair_ref, target_ref, arm_ref,
    grad_pair_ref, second_low_ref, hidden_ref, active_ref, branch_ref, cross_grad_ref, small_ref, query_grad_ref,
    head_grad_ref, sums_ref,
):
    width = starts_ref.shape[1]
    first = self_block(
        starts_ref[...], project_ref[...], combine_ref[...], gain_ref[0:1, :], shift_ref[0:1, :], valid
    )[-1]
    queries = dot(first.astype(BF16), query_ref[...], NN).astype(BF16)
    keys = pair_ref[:, :width]
    values = pair_ref[:, width:]
    mixed, kept = few_attend(queries, keys, values, keys.shape[0])
    second_rows, second_scale = normed(first + dot(mixed, cross_ref[...], NN))
    second = second_rows * gain_ref[1:2, :] + shift_ref[1:2, :]
    second_low = second.astype(BF16)
    second_low_ref[...] = second_low
    hidden_size = expand_ref.shape[1]
    step = hidden_size // 5
    total = second
    slopes = []
    for start in range(0, hidden_size, step):
        part = pl.ds(start, step)
        active, slope = gelu_and_slope(dot(second_low, expand_ref[:, part], NN))
        slopes.append(slope)
        active = active.astype(BF16)
        active_ref[:, part] = active
        total = total + dot(active, reduce_ref[part, :], NN)
    third_rows, third_scale = normed(total)
    third_low = (third_rows * gain_ref[2:3, :] + shift_ref[2:3, :]).astype(BF16)
    misfit = dot(third_low, head_ref[...], NN) - target_ref[...]
    arms = arm_ref[0]
    row = lax.broadcasted_iota(jnp.int32, misfit.shape, 0)
    joint = lax.broadcasted_iota(jnp.int32, misfit.shape, 1)
    factor = 2.0 / jnp.full((1, 1), arms, jnp.int32).astype(F32)
    used = (row < valid) & (joint < joints // 2 * arms)
    grad_pred = jnp.where(used, factor * misfit * lax.rsqrt(misfit * misfit + 1.0), 0.0).astype(BF16)
    head_grad_ref[...] = dot(third_low, grad_pred, TN)
    grad_third = dot(grad_pred, head_ref[...], NT)
    gain_third = column_sum(grad_third * third_rows)
    shift_third = column_sum(grad_third)
    total = normed_back(grad_third, gain_ref[2:3, :], third_rows, third_scale)
    branch = total.astype(BF16)
    branch_ref[...] = branch
    for index, start in enumerate(range(0, hidden_size, step)):
        part = pl.ds(start, step)
        grad_hidden = (dot(branch, reduce_ref[part, :], NT) * slopes[index]).astype(BF16)
        hidden_ref[:, part] = grad_hidden
        total = total + dot(grad_hidden, expand_ref[:, part], NT)
    gain_second = column_sum(total * second_rows)
    shift_second = column_sum(total)
    grad_second = normed_back(total, gain_ref[1:2, :], second_rows, second_scale)
    small_ref[...] = grad_second
    branch = grad_second.astype(BF16)
    cross_grad_ref[...] = dot(mixed, branch, TN).astype(BF16)
    grad_mixed = dot(branch, cross_ref[...], NT).astype(BF16)
    dq, dk, dv = few_attend_back(queries, keys, values, kept, grad_mixed)
    query_grad_ref[...] = dq.astype(BF16).astype(F32)
    grad_pair_ref[:, :width] = dk.astype(BF16)
    grad_pair_ref[:, width:] = dv.astype(BF16)
    sums_ref[...] = jnp.concatenate(
        [gain_second, gain_third, shift_second, shift_third, jnp.zeros((4, width), F32)], axis=0
    )


def decode(valid, joints, starts, weights, pair, target, arm):
    project_w, combine_w, query_w, cross_w, expand_w, reduce_w, gains, shifts, head_w = weights
    count, width = starts.shape
    hidden = expand_w.shape[1]
    shapes = [
        (pair.shape, BF16),
        ((count, width), BF16),
        ((count, hidden), BF16),
        ((count, hidden), BF16),
        ((count, width), BF16),
        ((width, width), BF16),
        ((count, width), F32),
        ((count, width), F32),
        (head_w.shape, F32),
        ((8, width), F32),
    ]
    arrays = (starts, project_w, combine_w, query_w, cross_w, expand_w, reduce_w, gains, shifts, head_w, pair, target)
    return call(
        functools.partial(decode_kernel, valid, joints),
        8 * count * width * hidden * 4,
        16 * 1024 * 1024,
        in_specs=[pl.BlockSpec(memory_space=pltpu.VMEM)] * len(arrays) + [pl.BlockSpec(memory_space=pltpu.SMEM)],
        out_specs=[pl.BlockSpec(memory_space=pltpu.VMEM)] * len(shapes),
        out_shape=[shape_of(dims, kind) for dims, kind in shapes],
    )(*arrays, arm)


def decode_start_back_kernel(
    valid,
    starts_ref, project_ref, combine_ref, query_ref, gain_ref, shift_ref, resid_ref, query_grad_ref,
    start_grad_ref, project_grad_ref, combine_grad_ref, query_w_grad_ref, sums_ref,
):
    starts = starts_ref[...]
    project_w = project_ref[...]
    queries, keys, values, mixed, kept, rows, scale, first = self_block(
        starts, project_w, combine_ref[...], gain_ref[0:1, :], shift_ref[0:1, :], valid
    )
    low = query_grad_ref[...].astype(BF16)
    query_w_grad_ref[...] = dot(first.astype(BF16), low, TN)
    grad_first = resid_ref[...] + dot(low, query_ref[...], NT)
    gain_sum = column_sum(grad_first * rows)
    shift_sum = column_sum(grad_first)
    grad_resid = normed_back(grad_first, gain_ref[0:1, :], rows, scale)
    branch = grad_resid.astype(BF16)
    combine_grad_ref[...] = dot(mixed, branch, TN)
    grad_mixed = dot(branch, combine_ref[...], NT).astype(BF16)
    dq, dk, dv = few_attend_back(queries, keys, values, kept, grad_mixed)
    grad_packed = jnp.concatenate([dq, dk, dv], axis=1).astype(BF16)
    project_grad_ref[...] = dot(starts, grad_packed, TN)
    start_grad_ref[...] = grad_resid + dot(grad_packed, project_w, NT)
    sums_ref[...] = jnp.concatenate([gain_sum, shift_sum, jnp.zeros((6, gain_sum.shape[1]), F32)], axis=0)


def decode_start_back(valid, starts, project_w, combine_w, query_w, gains, shifts, resid, query_grad):
    count, width = starts.shape
    arrays = (starts, project_w, combine_w, query_w, gains, shifts, resid, query_grad)
    shapes = [(count, width), (width, 3 * width), (width, width), (width, width), (8, width)]
    return call(
        functools.partial(decode_start_back_kernel, valid),
        2 * count * width * width * 20,
        8 * 1024 * 1024,
        in_specs=[pl.BlockSpec(memory_space=pltpu.VMEM)] * len(arrays),
        out_specs=[pl.BlockSpec(memory_space=pltpu.VMEM)] * len(shapes),
        out_shape=[shape_of(dims, F32) for dims in shapes],
    )(*arrays)


def episode(x, target, arm, weights):
    (
        encoder_project, encoder_combine, encoder_expand, encoder_reduce, encoder_gains, encoder_shifts,
        starts, decoder_project, decoder_combine, cross_query, cross_memory, cross_combine,
        decoder_expand, decoder_reduce, decoder_gains, decoder_shifts, head,
    ) = weights
    valid, joints = starts.shape[0], head.shape[1]
    packed = dot(x, encoder_project, NN).astype(BF16)
    mixed, logs = attend(packed)
    first, first_low, active, slope, second, memory, pair = encode_rows(
        x, mixed, encoder_combine, encoder_expand, encoder_reduce, encoder_gains, encoder_shifts, cross_memory
    )
    padded = jnp.pad(starts, ((0, PAD_ROWS - valid), (0, 0)))
    wide_head = jnp.pad(head, ((0, 0), (0, LANES - joints)))
    wide_target = jnp.pad(target, ((0, PAD_ROWS - valid), (0, LANES - joints)))
    (
        grad_pair, second_low, grad_hidden_d, active_d, branch_d, cross_grad, resid_d, query_grad, head_grad, sums_d,
    ) = decode(
        valid, joints, padded,
        (
            decoder_project, decoder_combine, cross_query, cross_combine, decoder_expand, decoder_reduce,
            decoder_gains, decoder_shifts, wide_head,
        ),
        pair, wide_target, arm,
    )
    expand_d = gradient_by_rows(second_low, grad_hidden_d, 640)
    reduce_d = gradient_by_columns(active_d, branch_d, 640)
    grad_memory, branch, grad_hidden, resid, low, grad_mixed, sums_e = encode_back(
        grad_pair, first, second, slope, encoder_combine, encoder_expand, encoder_reduce, encoder_gains, cross_memory
    )
    memory_w_grad = gradient_by_rows(memory, grad_pair, 512)
    reduce_e = gradient_by_columns(active, branch, 640)
    expand_e = gradient_by_rows(first_low, grad_hidden, 640)
    combine_e = gradient_by_rows(mixed.T, low, 512)
    dq, dk, dv = attend_back(packed, grad_mixed, mixed, logs)
    grad_packed = jnp.concatenate([dq, dk, dv], axis=1)
    project_e = gradient_by_rows(x, grad_packed, 512)
    grad_x = (resid + dot(grad_packed, encoder_project, NT)).astype(BF16)
    cross_rows = cross_grad.reshape(-1, 2, 16, cross_grad.shape[1]).transpose(1, 0, 2, 3).reshape(2, -1, cross_grad.shape[1])
    return memory, grad_x, grad_memory, {
        "encoder_project": project_e,
        "encoder_combine": combine_e,
        "encoder_expand": expand_e,
        "encoder_reduce": reduce_e,
        "decoder_expand": expand_d,
        "decoder_reduce": reduce_d,
        "cross_memory": memory_w_grad,
        "cross_combine": cross_rows,
        "sums_e": sums_e,
        "sums_d": sums_d,
        "resid_d": resid_d,
        "query_d": query_grad,
        "head": head_grad[:, :joints],
    }


def swap(value, axis, bit):
    pairs = [(i, i ^ (1 << bit)) for i in range(lax.axis_size(axis))]
    return lax.ppermute(value, axis, pairs)


class Shards:
    def __init__(self):
        self.bits = [("section", b) for b in reversed(range(lax.axis_size("section").bit_length() - 1))]
        self.bits += [("dp", b) for b in reversed(range(lax.axis_size("dp").bit_length() - 1))]
        self.mine = [(lax.axis_index(axis) >> bit) & 1 for axis, bit in self.bits]

    def take(self, term, fixed):
        starts, sizes = [], []
        for dim, size in enumerate(term.shape):
            if dim in fixed and size == 2:
                starts.append(fixed[dim])
                sizes.append(1)
            else:
                starts.append(0)
                sizes.append(size)
        return lax.dynamic_slice(term, starts, sizes).astype(F32)

    def total(self, terms, fixed):
        value = self.take(terms[0], fixed)
        for term in terms[1:]:
            value = value + self.take(term, fixed)
        return value

    def reduce(self, halves, order):
        core = lax.axis_index("rep")
        rows = halves.shape[1] >> len(self.bits)
        lead = (2,) * len(self.bits)
        shape = lead + (rows, halves.shape[2])
        pick = lambda index: lax.dynamic_index_in_dim(halves, index, 0, keepdims=False).reshape(shape)
        terms = [pick(core), swap(pick(1 - core), "rep", 0)]
        fixed = {}
        for dim in order:
            axis, bit = self.bits[dim]
            sent = self.total(terms, {**fixed, dim: 1 - self.mine[dim]}).astype(BF16)
            terms.append(swap(sent, axis, bit))
            fixed[dim] = self.mine[dim]
        return self.total(terms, fixed).astype(BF16).reshape(rows, halves.shape[2])


def both_cores(own, axis):
    other = swap(own, "rep", 0)
    first = lax.axis_index("rep") == 0
    return jnp.concatenate(
        [jnp.where(first, own, other), jnp.where(first, other, own)], axis=axis
    ).astype(F32)


def everywhere(value, kind):
    for axis in ("rep", "section", "dp"):
        for bit in range(lax.axis_size(axis).bit_length() - 1):
            low = value.astype(kind)
            value = low.astype(F32) + swap(low, axis, bit).astype(F32)
    return value


def from_halves_rows(halves):
    rows, columns = 2 * halves.shape[1], halves.shape[2]
    return halves.reshape(2, -1, 16, columns).transpose(1, 0, 2, 3).reshape(rows, columns)


def from_halves_columns(halves):
    return jnp.concatenate([halves[0], halves[1]], axis=1)


def plain_scatter(full):
    part = lax.psum_scatter(full.astype(F32), ("section", "dp"), scatter_dimension=0, tiled=True)
    return lax.psum(part, "rep")


ROW_GROUPS = {
    "decoder_expand": (0, 3, 2, 1),
    "cross": (3, 2, 1, 0),
    "encoder_expand": (2, 3, 1, 0),
    "encoder_attend": (3, 2, 0, 1),
}
COLUMN_GROUPS = {"decoder_reduce": (3, 0, 2, 1), "encoder_reduce": (3, 2, 1, 0)}


def per_device(x, targets, arms, *weights):
    section = lax.axis_index("section")
    sections = lax.axis_size("section")
    lanes = lax.axis_size("dp")
    count = x.shape[0] // sections
    starts, head = weights[6], weights[16]
    valid, joints = starts.shape[0], head.shape[1]
    width = starts.shape[1]
    memories, grads_x, grads_m, sums = [], [], [], None
    for index in range(count):
        place = section * count + index
        pick = lambda array: lax.dynamic_index_in_dim(array, place, 0, keepdims=False)
        memory, grad_x, grad_memory, fresh = episode(
            pick(x), pick(targets), lax.dynamic_slice(arms, (place,), (1,)), weights
        )
        memories.append(memory)
        grads_x.append(grad_x)
        grads_m.append(grad_memory)
        sums = fresh if sums is None else {
            name: (sums[name].astype(F32) + fresh[name].astype(F32)).astype(fresh[name].dtype) for name in fresh
        }
    first = section == 0
    memory = jnp.stack(memories)
    other = swap(memory, "section", 0)
    memory_out = jnp.concatenate([jnp.where(first, memory, other), jnp.where(first, other, memory)])
    grad_m = jnp.stack(grads_m)
    grad_x = jnp.stack(grads_x)
    from_first = lax.ppermute(grad_m, "section", [(0, 1)])
    from_second = lax.ppermute(grad_x, "section", [(1, 0)])
    slab = jnp.concatenate([jnp.where(first, grad_x, from_first), jnp.where(first, from_second, grad_m)])[None]

    place = section * lanes + lax.axis_index("dp")
    own = width // (sections * lanes)
    columns_of = lambda array: lax.dynamic_slice_in_dim(array, place * own, own, 1)
    rows_of = lambda array: lax.dynamic_slice_in_dim(array, place * own, own, 0)

    small_low = everywhere(jnp.concatenate([sums["resid_d"][:104], sums["query_d"][:104]]), BF16)
    rest = PAD_ROWS - 104
    resid_d = jnp.pad(small_low[:104], ((0, rest), (0, 0)))
    query_d = jnp.pad(small_low[104:], ((0, rest), (0, 0)))
    small = everywhere(
        jnp.concatenate([sums["sums_d"][:4], sums["sums_e"][:4], sums["head"].T]), F32
    )
    head_sum = small[8:].T
    start_grad, project_d, combine_d, query_w, sums_s = decode_start_back(
        valid, jnp.pad(starts, ((0, PAD_ROWS - valid), (0, 0))), weights[7], weights[8], weights[9],
        weights[14], weights[15], resid_d, query_d,
    )
    gains_d = jnp.concatenate([sums_s[0:1], small[0:2]])
    shifts_d = jnp.concatenate([sums_s[1:2], small[2:4]])

    groups = {
        "decoder_expand": sums["decoder_expand"],
        "cross": jnp.concatenate([sums["cross_memory"], sums["cross_combine"]], axis=2),
        "encoder_expand": sums["encoder_expand"],
        "encoder_attend": jnp.concatenate([sums["encoder_project"], sums["encoder_combine"]], axis=2),
        "decoder_reduce": sums["decoder_reduce"],
        "encoder_reduce": sums["encoder_reduce"],
    }
    done = {}
    if own == 32:
        shards = Shards()
        for name, order in ROW_GROUPS.items():
            done[name] = both_cores(shards.reduce(groups[name], order), 0)
        for name, order in COLUMN_GROUPS.items():
            done[name] = both_cores(shards.reduce(groups[name], order), 1)
    else:
        for name in ROW_GROUPS:
            done[name] = plain_scatter(from_halves_rows(groups[name]))
        for name in COLUMN_GROUPS:
            done[name] = plain_scatter(from_halves_columns(groups[name]))
    return (
        memory_out,
        slab,
        done["encoder_attend"][:, : 3 * width],
        done["encoder_attend"][:, 3 * width :],
        done["encoder_expand"],
        done["encoder_reduce"],
        columns_of(small[4:6]),
        columns_of(small[6:8]),
        columns_of(start_grad[:valid]),
        rows_of(project_d),
        rows_of(combine_d),
        rows_of(query_w),
        done["cross"][:, : 2 * width],
        done["cross"][:, 2 * width :],
        done["decoder_expand"],
        done["decoder_reduce"],
        columns_of(gains_d),
        columns_of(shifts_d),
        rows_of(head_sum),
    )


def solution(mesh):
    spread = ("section", "dp")
    rows = P(spread, None)
    columns = P(None, spread)
    return jax.shard_map(
        per_device,
        mesh=mesh,
        in_specs=(P(("dp", "rep"), None, None), P(("dp", "rep"), None, None), P(("dp", "rep"))) + (P(),) * 17,
        out_specs=(
            P(("dp", "rep"), None, None),
            P("section", ("dp", "rep"), None, None),
            rows, rows, rows, rows, columns, columns, columns,
            rows, rows, rows, rows, rows, rows, rows, columns, columns, rows,
        ),
        check_vma=False,
    )
```

```python
import functools

import jax
import jax.numpy as jnp
from jax import lax
from jax.experimental import pallas as pl
from jax.experimental.pallas import tpu as pltpu
from jax.sharding import PartitionSpec as P

HEADS = 8
EPSILON = 1e-05
LANES = 128
PAD_ROWS = 128
F32 = jnp.float32
BF16 = jnp.bfloat16
NN = (((1,), (0,)), ((), ()))
NT = (((1,), (1,)), ((), ()))
TN = (((0,), (0,)), ((), ()))
VMEM_BYTES = 56 * 1024 * 1024
ROOT_2_PI = 0.7978845608028654
CUBE = 0.044715


def dot(left, right, dims):
    return lax.dot_general(left, right, dims, preferred_element_type=F32)


def call(kernel, flops, moved, **options):
    return pl.pallas_call(
        kernel,
        compiler_params=pltpu.CompilerParams(vmem_limit_bytes=VMEM_BYTES),
        cost_estimate=pl.CostEstimate(flops=flops, bytes_accessed=moved, transcendentals=0),
        **options,
    )


def shape_of(dims, dtype):
    return jax.ShapeDtypeStruct(dims, dtype)


def whole(array):
    rank = len(array.shape)
    return pl.BlockSpec(array.shape, lambda *_: (0,) * rank, pipeline_mode=pl.Buffered(1))


def normed(residual):
    centre = jnp.mean(residual, axis=-1, keepdims=True)
    centred = residual - centre
    spread = jnp.mean(centred * centred, axis=-1, keepdims=True)
    scale = lax.rsqrt(spread + EPSILON)
    return centred * scale, scale


def normed_back(grad, gain, rows, scale):
    weighted = grad * gain
    return scale * (
        weighted
        - jnp.mean(weighted, axis=-1, keepdims=True)
        - rows * jnp.mean(weighted * rows, axis=-1, keepdims=True)
    )


def gelu_and_slope(value):
    square = value * value
    bend = jnp.tanh(value * (ROOT_2_PI + (ROOT_2_PI * CUBE) * square))
    half = 0.5 + 0.5 * bend
    slope = half + value * (0.5 - 0.5 * bend * bend) * (
        ROOT_2_PI + (3.0 * ROOT_2_PI * CUBE) * square
    )
    return value * half, slope


def column_sum(value):
    return jnp.sum(value, axis=0, keepdims=True)


def attend_kernel(q_ref, k_ref, v_ref, mixed_ref, log_ref):
    count = q_ref.shape[0]
    lane = lax.broadcasted_iota(jnp.int32, (1, LANES), 1)
    keys = k_ref[...]
    values = v_ref[...].T
    queries = q_ref[...] * jnp.asarray(0.125, BF16)
    for head in range(2):
        own = (lane < 64) if head == 0 else (lane >= 64)
        head_keys = jnp.where(own, keys, jnp.zeros_like(keys))
        extended = jnp.concatenate(
            [values[64 * head : 64 * head + 64], jnp.ones((16, count), BF16)], axis=0
        )
        scores = dot(head_keys, queries, NT)
        largest = jnp.max(scores, axis=0, keepdims=True)
        raised = jnp.exp(scores - largest).astype(BF16)
        mixed = dot(extended, raised, NN)
        total = mixed[64:65]
        mixed_ref[pl.ds(64 * head, 64), :] = (mixed[:64] * (1.0 / total)).astype(BF16)
        log_ref[0, pl.ds(head, 1), :] = largest + jnp.log(total)


def attend(packed):
    rows, width = packed.shape[0], packed.shape[1] // 3
    pairs = width // LANES
    column = lambda first: pl.BlockSpec((rows, LANES), lambda j: (0, first + j))
    return call(
        attend_kernel,
        4 * rows * rows * width * 4,
        rows * width * 8,
        grid=(pairs,),
        in_specs=[column(0), column(pairs), column(2 * pairs)],
        out_specs=[
            pl.BlockSpec((LANES, rows), lambda j: (j, 0)),
            pl.BlockSpec((1, 2, rows), lambda j: (j, 0, 0)),
        ],
        out_shape=[shape_of((width, rows), BF16), shape_of((pairs, 2, rows), F32)],
    )(packed, packed, packed)


def attend_back_kernel(block, q_ref, k_ref, v_ref, do_ref, mixed_ref, log_ref, dq_ref, dk_ref, dv_ref):
    count = q_ref.shape[0]
    lane = lax.broadcasted_iota(jnp.int32, (1, LANES), 1)
    keys = k_ref[...]
    values = v_ref[...]
    queries = q_ref[...] * jnp.asarray(0.125, BF16)
    scaled_keys = keys * jnp.asarray(0.125, BF16)
    grads = do_ref[...]
    queries_t = queries.T
    grads_t = grads.T
    logs = log_ref[0].T
    shared = mixed_ref[...].astype(F32) * grads_t.astype(F32)
    inner = jnp.concatenate([column_sum(shared[:64]), column_sum(shared[64:])], axis=0).T
    dq_parts = [[], []]
    dk_parts = []
    dv_parts = []
    for head in range(2):
        own = (lane < 64) if head == 0 else (lane >= 64)
        head_queries = jnp.where(own, queries, jnp.zeros_like(queries))
        head_grads = jnp.where(own, grads, jnp.zeros_like(grads))
        dk = None
        dv = None
        for start in range(0, count, block):
            part = slice(start, start + block)
            scores = dot(head_queries[part], keys, NT)
            probs = jnp.exp(scores - logs[part, head : head + 1])
            grad_probs = dot(head_grads[part], values, NT)
            grad_scores = (probs * (grad_probs - inner[part, head : head + 1])).astype(BF16)
            new_v = dot(grads_t[64 * head : 64 * head + 64, part], probs.astype(BF16), NN)
            new_k = dot(queries_t[64 * head : 64 * head + 64, part], grad_scores, NN)
            dv = new_v if dv is None else dv + new_v
            dk = new_k if dk is None else dk + new_k
            dq_parts[head].append(dot(grad_scores, scaled_keys, NN))
        dk_parts.append(dk)
        dv_parts.append(dv)
    dk_ref[...] = jnp.concatenate(dk_parts, axis=0).T.astype(BF16)
    dv_ref[...] = jnp.concatenate(dv_parts, axis=0).T.astype(BF16)
    for index in range(count // block):
        dq_ref[pl.ds(index * block, block), :] = jnp.where(
            lane < 64, dq_parts[0][index], dq_parts[1][index]
        ).astype(BF16)


def attend_back(packed, grad_mixed, mixed, logs):
    rows, width = packed.shape[0], packed.shape[1] // 3
    pairs = width // LANES
    column = lambda first: pl.BlockSpec((rows, LANES), lambda j: (0, first + j))
    return call(
        functools.partial(attend_back_kernel, 256),
        10 * rows * rows * width * 3,
        rows * width * 16,
        grid=(pairs,),
        in_specs=[
            column(0),
            column(pairs),
            column(2 * pairs),
            column(0),
            pl.BlockSpec((LANES, rows), lambda j: (j, 0)),
            pl.BlockSpec((1, 2, rows), lambda j: (j, 0, 0)),
        ],
        out_specs=[column(0)] * 3,
        out_shape=[shape_of((rows, width), BF16)] * 3,
    )(packed, packed, packed, grad_mixed, mixed, logs)


def encode_rows_kernel(
    x_ref, mixed_ref, combine_ref, expand_ref, reduce_ref, gain_ref, shift_ref, memory_w_ref,
    first_ref, low_ref, active_ref, slope_ref, second_ref, memory_ref, pair_ref,
):
    residual = x_ref[...].astype(F32) + dot(mixed_ref[...], combine_ref[...], TN)
    first_ref[...] = residual
    rows, _ = normed(residual)
    first = rows * gain_ref[0:1, :] + shift_ref[0:1, :]
    low = first.astype(BF16)
    low_ref[...] = low
    total = first
    hidden_size = expand_ref.shape[1]
    step = hidden_size // 5
    for start in range(0, hidden_size, step):
        part = pl.ds(start, step)
        active, slope = gelu_and_slope(dot(low, expand_ref[:, part], NN))
        active = active.astype(BF16)
        active_ref[:, part] = active
        slope_ref[:, part] = slope.astype(BF16)
        total = total + dot(active, reduce_ref[part, :], NN)
    second_ref[...] = total
    rows, _ = normed(total)
    memory = (rows * gain_ref[1:2, :] + shift_ref[1:2, :]).astype(BF16)
    memory_ref[...] = memory
    pair_ref[...] = dot(memory, memory_w_ref[...], NN).astype(BF16)


def encode_rows(x, mixed, combine_w, expand_w, reduce_w, gains, shifts, memory_w):
    rows, width = x.shape
    hidden = expand_w.shape[1]
    block = 256
    line = lambda size: pl.BlockSpec((block, size), lambda i: (i, 0))
    sizes = [(width, F32), (width, BF16), (hidden, BF16), (hidden, BF16), (width, F32), (width, BF16), (2 * width, BF16)]
    return call(
        encode_rows_kernel,
        2 * rows * width * (2 * hidden + 3 * width),
        rows * (hidden * 4 + width * 18) + 8 * width * hidden,
        grid=(rows // block,),
        in_specs=[line(width), pl.BlockSpec((width, block), lambda i: (0, i))]
        + [whole(item) for item in (combine_w, expand_w, reduce_w, gains, shifts, memory_w)],
        out_specs=[line(size) for size, _ in sizes],
        out_shape=[shape_of((rows, size), kind) for size, kind in sizes],
    )(x, mixed, combine_w, expand_w, reduce_w, gains, shifts, memory_w)


def encode_back_kernel(
    pair_ref, first_ref, second_ref, slope_ref, combine_ref, expand_ref, reduce_ref, gain_ref, memory_w_ref,
    grad_memory_ref, branch_ref, hidden_ref, resid_ref, low_ref, mixed_ref, sums_ref,
):
    grad_memory = dot(pair_ref[...], memory_w_ref[...], NT).astype(BF16)
    grad_memory_ref[...] = grad_memory
    grad_last = grad_memory.astype(F32)
    rows, scale = normed(second_ref[...])
    gain_last = column_sum(grad_last * rows)
    shift_last = column_sum(grad_last)
    grad_second = normed_back(grad_last, gain_ref[1:2, :], rows, scale)
    branch = grad_second.astype(BF16)
    branch_ref[...] = branch
    total = grad_second
    hidden_size = expand_ref.shape[1]
    step = hidden_size // 5
    for start in range(0, hidden_size, step):
        part = pl.ds(start, step)
        grad_active = dot(branch, reduce_ref[part, :], NT)
        grad_hidden = (grad_active * slope_ref[:, part].astype(F32)).astype(BF16)
        hidden_ref[:, part] = grad_hidden
        total = total + dot(grad_hidden, expand_ref[:, part], NT)
    rows, scale = normed(first_ref[...])
    gain_first = column_sum(total * rows)
    shift_first = column_sum(total)
    grad_first = normed_back(total, gain_ref[0:1, :], rows, scale)
    resid_ref[...] = grad_first
    low = grad_first.astype(BF16)
    low_ref[...] = low
    mixed_ref[...] = dot(low, combine_ref[...], NT).astype(BF16)
    fresh = jnp.concatenate(
        [gain_first, gain_last, shift_first, shift_last, jnp.zeros((4, gain_first.shape[1]), F32)], axis=0
    )

    @pl.when(pl.program_id(0) == 0)
    def _():
        sums_ref[...] = fresh

    @pl.when(pl.program_id(0) > 0)
    def _():
        sums_ref[...] += fresh


def encode_back(grad_pair, first, second, slope, combine_w, expand_w, reduce_w, gains, memory_w):
    rows, width = first.shape
    hidden = expand_w.shape[1]
    block = 256
    line = lambda size: pl.BlockSpec((block, size), lambda i: (i, 0))
    sizes = [(width, BF16), (width, BF16), (hidden, BF16), (width, F32), (width, BF16), (width, BF16)]
    return call(
        encode_back_kernel,
        2 * rows * width * (2 * hidden + 3 * width),
        rows * (hidden * 4 + width * 18) + 8 * width * hidden,
        grid=(rows // block,),
        in_specs=[line(2 * width), line(width), line(width), line(hidden)]
        + [whole(item) for item in (combine_w, expand_w, reduce_w, gains, memory_w)],
        out_specs=[line(size) for size, _ in sizes] + [pl.BlockSpec((8, width), lambda i: (0, 0))],
        out_shape=[shape_of((rows, size), kind) for size, kind in sizes] + [shape_of((8, width), F32)],
    )(grad_pair, first, second, slope, combine_w, expand_w, reduce_w, gains, memory_w)


def by_rows_kernel(half, left_ref, right_ref, out_ref):
    result = dot(left_ref[...], right_ref[...], TN).astype(BF16)
    for start in range(0, result.shape[0], 2 * half):
        for core in range(2):
            out_ref[core, pl.ds(start // 2, half), :] = result[
                start + core * half : start + core * half + half
            ]


def gradient_by_rows(left, right, step):
    count, rows = left.shape
    columns = right.shape[1]
    return call(
        functools.partial(by_rows_kernel, 16),
        2 * count * rows * columns,
        2 * (count * (rows + columns) + rows * columns),
        grid=(columns // step,),
        in_specs=[whole(left), pl.BlockSpec((count, step), lambda i: (0, i))],
        out_specs=pl.BlockSpec((2, rows // 2, step), lambda i: (0, 0, i)),
        out_shape=shape_of((2, rows // 2, columns), BF16),
    )(left, right)


def by_columns_kernel(left_ref, right_ref, out_ref):
    result = dot(left_ref[...], right_ref[...], TN).astype(BF16)
    half = result.shape[1] // 2
    out_ref[0] = result[:, :half]
    out_ref[1] = result[:, half:]


def gradient_by_columns(left, right, step):
    count, rows = left.shape
    columns = right.shape[1]
    return call(
        by_columns_kernel,
        2 * count * rows * columns,
        2 * (count * (rows + columns) + rows * columns),
        grid=(rows // step,),
        in_specs=[pl.BlockSpec((count, step), lambda i: (0, i)), whole(right)],
        out_specs=pl.BlockSpec((2, step, columns // 2), lambda i: (0, i, 0)),
        out_shape=shape_of((2, rows, columns // 2), BF16),
    )(left, right)


def stacked(rows):
    lane = lax.broadcasted_iota(jnp.int32, (1, rows.shape[1]), 1)
    return jnp.concatenate(
        [jnp.where((lane >= 64 * h) & (lane < 64 * h + 64), rows, jnp.zeros_like(rows)) for h in range(4)],
        axis=0,
    )


def unstacked(rows):
    lane = lax.broadcasted_iota(jnp.int32, (1, rows.shape[1]), 1)
    count = rows.shape[0] // 4
    result = rows[:count]
    for h in range(1, 4):
        result = jnp.where(lane >= 64 * h, rows[h * count : h * count + count], result)
    return result


def few_attend(queries, keys, values, valid):
    mixed = []
    kept = []
    for half in range(2):
        part = slice(256 * half, 256 * half + 256)
        scores = dot(stacked(queries[:, part] * jnp.asarray(0.125, BF16)), keys[:, part], NT)
        if valid < scores.shape[1]:
            column = lax.broadcasted_iota(jnp.int32, (1, scores.shape[1]), 1)
            scores = jnp.where(column < valid, scores, -1e30)
        raised = jnp.exp(scores - jnp.max(scores, axis=1, keepdims=True))
        probs = raised * (1.0 / jnp.sum(raised, axis=1, keepdims=True))
        mixed.append(unstacked(dot(probs.astype(BF16), values[:, part], NN)))
        kept.append(probs)
    return jnp.concatenate(mixed, axis=1).astype(BF16), kept


def few_attend_back(queries, keys, values, kept, grads):
    dq, dk, dv = [], [], []
    for half in range(2):
        part = slice(256 * half, 256 * half + 256)
        probs = kept[half]
        own_queries = stacked(queries[:, part] * jnp.asarray(0.125, BF16))
        own_grads = stacked(grads[:, part])
        grad_probs = dot(own_grads, values[:, part], NT)
        product = probs * grad_probs
        grad_scores = (product - probs * jnp.sum(product, axis=1, keepdims=True)).astype(BF16)
        dv.append(dot(probs.astype(BF16), own_grads, TN))
        dk.append(dot(grad_scores, own_queries, TN))
        dq.append(unstacked(dot(grad_scores, keys[:, part], NN)) * 0.125)
    return jnp.concatenate(dq, axis=1), jnp.concatenate(dk, axis=1), jnp.concatenate(dv, axis=1)


def self_block(starts, project_w, combine_w, gain, shift, valid):
    width = starts.shape[1]
    packed = dot(starts, project_w, NN).astype(BF16)
    queries, keys, values = (packed[:, i * width : (i + 1) * width] for i in range(3))
    mixed, kept = few_attend(queries, keys, values, valid)
    residual = starts.astype(F32) + dot(mixed, combine_w, NN)
    rows, scale = normed(residual)
    return queries, keys, values, mixed, kept, rows, scale, rows * gain + shift


def decode_kernel(
    valid, joints,
    starts_ref, project_ref, combine_ref, query_ref, cross_ref, expand_ref, reduce_ref, gain_ref, shift_ref,
    head_ref, pair_ref, target_ref, arm_ref,
    grad_pair_ref, second_low_ref, hidden_ref, active_ref, branch_ref, cross_grad_ref, small_ref, query_grad_ref,
    head_grad_ref, sums_ref,
):
    width = starts_ref.shape[1]
    first = self_block(
        starts_ref[...], project_ref[...], combine_ref[...], gain_ref[0:1, :], shift_ref[0:1, :], valid
    )[-1]
    queries = dot(first.astype(BF16), query_ref[...], NN).astype(BF16)
    keys = pair_ref[:, :width]
    values = pair_ref[:, width:]
    mixed, kept = few_attend(queries, keys, values, keys.shape[0])
    second_rows, second_scale = normed(first + dot(mixed, cross_ref[...], NN))
    second = second_rows * gain_ref[1:2, :] + shift_ref[1:2, :]
    second_low = second.astype(BF16)
    second_low_ref[...] = second_low
    hidden_size = expand_ref.shape[1]
    step = hidden_size // 5
    total = second
    slopes = []
    for start in range(0, hidden_size, step):
        part = pl.ds(start, step)
        active, slope = gelu_and_slope(dot(second_low, expand_ref[:, part], NN))
        slopes.append(slope)
        active = active.astype(BF16)
        active_ref[:, part] = active
        total = total + dot(active, reduce_ref[part, :], NN)
    third_rows, third_scale = normed(total)
    third_low = (third_rows * gain_ref[2:3, :] + shift_ref[2:3, :]).astype(BF16)
    misfit = dot(third_low, head_ref[...], NN) - target_ref[...]
    arms = arm_ref[0]
    row = lax.broadcasted_iota(jnp.int32, misfit.shape, 0)
    joint = lax.broadcasted_iota(jnp.int32, misfit.shape, 1)
    factor = 2.0 / jnp.full((1, 1), arms, jnp.int32).astype(F32)
    used = (row < valid) & (joint < joints // 2 * arms)
    grad_pred = jnp.where(used, factor * misfit * lax.rsqrt(misfit * misfit + 1.0), 0.0).astype(BF16)
    head_grad_ref[...] = dot(third_low, grad_pred, TN)
    grad_third = dot(grad_pred, head_ref[...], NT)
    gain_third = column_sum(grad_third * third_rows)
    shift_third = column_sum(grad_third)
    total = normed_back(grad_third, gain_ref[2:3, :], third_rows, third_scale)
    branch = total.astype(BF16)
    branch_ref[...] = branch
    for index, start in enumerate(range(0, hidden_size, step)):
        part = pl.ds(start, step)
        grad_hidden = (dot(branch, reduce_ref[part, :], NT) * slopes[index]).astype(BF16)
        hidden_ref[:, part] = grad_hidden
        total = total + dot(grad_hidden, expand_ref[:, part], NT)
    gain_second = column_sum(total * second_rows)
    shift_second = column_sum(total)
    grad_second = normed_back(total, gain_ref[1:2, :], second_rows, second_scale)
    small_ref[...] = grad_second
    branch = grad_second.astype(BF16)
    cross_grad_ref[...] = dot(mixed, branch, TN).astype(BF16)
    grad_mixed = dot(branch, cross_ref[...], NT).astype(BF16)
    dq, dk, dv = few_attend_back(queries, keys, values, kept, grad_mixed)
    query_grad_ref[...] = dq.astype(BF16).astype(F32)
    grad_pair_ref[:, :width] = dk.astype(BF16)
    grad_pair_ref[:, width:] = dv.astype(BF16)
    sums_ref[...] = jnp.concatenate(
        [gain_second, gain_third, shift_second, shift_third, jnp.zeros((4, width), F32)], axis=0
    )


def decode(valid, joints, starts, weights, pair, target, arm):
    project_w, combine_w, query_w, cross_w, expand_w, reduce_w, gains, shifts, head_w = weights
    count, width = starts.shape
    hidden = expand_w.shape[1]
    shapes = [
        (pair.shape, BF16),
        ((count, width), BF16),
        ((count, hidden), BF16),
        ((count, hidden), BF16),
        ((count, width), BF16),
        ((width, width), BF16),
        ((count, width), F32),
        ((count, width), F32),
        (head_w.shape, F32),
        ((8, width), F32),
    ]
    arrays = (starts, project_w, combine_w, query_w, cross_w, expand_w, reduce_w, gains, shifts, head_w, pair, target)
    return call(
        functools.partial(decode_kernel, valid, joints),
        8 * count * width * hidden * 4,
        16 * 1024 * 1024,
        in_specs=[pl.BlockSpec(memory_space=pltpu.VMEM)] * len(arrays) + [pl.BlockSpec(memory_space=pltpu.SMEM)],
        out_specs=[pl.BlockSpec(memory_space=pltpu.VMEM)] * len(shapes),
        out_shape=[shape_of(dims, kind) for dims, kind in shapes],
    )(*arrays, arm)


def decode_start_back_kernel(
    valid,
    starts_ref, project_ref, combine_ref, query_ref, gain_ref, shift_ref, resid_ref, query_grad_ref,
    start_grad_ref, project_grad_ref, combine_grad_ref, query_w_grad_ref, sums_ref,
):
    starts = starts_ref[...]
    project_w = project_ref[...]
    queries, keys, values, mixed, kept, rows, scale, first = self_block(
        starts, project_w, combine_ref[...], gain_ref[0:1, :], shift_ref[0:1, :], valid
    )
    low = query_grad_ref[...].astype(BF16)
    query_w_grad_ref[...] = dot(first.astype(BF16), low, TN)
    grad_first = resid_ref[...] + dot(low, query_ref[...], NT)
    gain_sum = column_sum(grad_first * rows)
    shift_sum = column_sum(grad_first)
    grad_resid = normed_back(grad_first, gain_ref[0:1, :], rows, scale)
    branch = grad_resid.astype(BF16)
    combine_grad_ref[...] = dot(mixed, branch, TN)
    grad_mixed = dot(branch, combine_ref[...], NT).astype(BF16)
    dq, dk, dv = few_attend_back(queries, keys, values, kept, grad_mixed)
    grad_packed = jnp.concatenate([dq, dk, dv], axis=1).astype(BF16)
    project_grad_ref[...] = dot(starts, grad_packed, TN)
    start_grad_ref[...] = grad_resid + dot(grad_packed, project_w, NT)
    sums_ref[...] = jnp.concatenate([gain_sum, shift_sum, jnp.zeros((6, gain_sum.shape[1]), F32)], axis=0)


def decode_start_back(valid, starts, project_w, combine_w, query_w, gains, shifts, resid, query_grad):
    count, width = starts.shape
    arrays = (starts, project_w, combine_w, query_w, gains, shifts, resid, query_grad)
    shapes = [(count, width), (width, 3 * width), (width, width), (width, width), (8, width)]
    return call(
        functools.partial(decode_start_back_kernel, valid),
        2 * count * width * width * 20,
        8 * 1024 * 1024,
        in_specs=[pl.BlockSpec(memory_space=pltpu.VMEM)] * len(arrays),
        out_specs=[pl.BlockSpec(memory_space=pltpu.VMEM)] * len(shapes),
        out_shape=[shape_of(dims, F32) for dims in shapes],
    )(*arrays)


def episode(x, target, arm, weights):
    (
        encoder_project, encoder_combine, encoder_expand, encoder_reduce, encoder_gains, encoder_shifts,
        starts, decoder_project, decoder_combine, cross_query, cross_memory, cross_combine,
        decoder_expand, decoder_reduce, decoder_gains, decoder_shifts, head,
    ) = weights
    valid, joints = starts.shape[0], head.shape[1]
    packed = dot(x, encoder_project, NN).astype(BF16)
    mixed, logs = attend(packed)
    first, first_low, active, slope, second, memory, pair = encode_rows(
        x, mixed, encoder_combine, encoder_expand, encoder_reduce, encoder_gains, encoder_shifts, cross_memory
    )
    padded = jnp.pad(starts, ((0, PAD_ROWS - valid), (0, 0)))
    wide_head = jnp.pad(head, ((0, 0), (0, LANES - joints)))
    wide_target = jnp.pad(target, ((0, PAD_ROWS - valid), (0, LANES - joints)))
    (
        grad_pair, second_low, grad_hidden_d, active_d, branch_d, cross_grad, resid_d, query_grad, head_grad, sums_d,
    ) = decode(
        valid, joints, padded,
        (
            decoder_project, decoder_combine, cross_query, cross_combine, decoder_expand, decoder_reduce,
            decoder_gains, decoder_shifts, wide_head,
        ),
        pair, wide_target, arm,
    )
    expand_d = gradient_by_rows(second_low, grad_hidden_d, 640)
    reduce_d = gradient_by_columns(active_d, branch_d, 640)
    grad_memory, branch, grad_hidden, resid, low, grad_mixed, sums_e = encode_back(
        grad_pair, first, second, slope, encoder_combine, encoder_expand, encoder_reduce, encoder_gains, cross_memory
    )
    memory_w_grad = gradient_by_rows(memory, grad_pair, 512)
    reduce_e = gradient_by_columns(active, branch, 640)
    expand_e = gradient_by_rows(first_low, grad_hidden, 640)
    combine_e = gradient_by_rows(mixed.T, low, 512)
    dq, dk, dv = attend_back(packed, grad_mixed, mixed, logs)
    grad_packed = jnp.concatenate([dq, dk, dv], axis=1)
    project_e = gradient_by_rows(x, grad_packed, 512)
    grad_x = (resid + dot(grad_packed, encoder_project, NT)).astype(BF16)
    cross_rows = cross_grad.reshape(-1, 2, 16, cross_grad.shape[1]).transpose(1, 0, 2, 3).reshape(2, -1, cross_grad.shape[1])
    return memory, grad_x, grad_memory, {
        "encoder_project": project_e,
        "encoder_combine": combine_e,
        "encoder_expand": expand_e,
        "encoder_reduce": reduce_e,
        "decoder_expand": expand_d,
        "decoder_reduce": reduce_d,
        "cross_memory": memory_w_grad,
        "cross_combine": cross_rows,
        "sums_e": sums_e,
        "sums_d": sums_d,
        "resid_d": resid_d,
        "query_d": query_grad,
        "head": head_grad[:, :joints],
    }


BITS = (("section", 0), ("dp", 2), ("dp", 1), ("dp", 0))
SECTION, FAR, NEAR, SIDE = range(4)
GROUPS = {
    "decoder_expand": (SECTION, SIDE, NEAR, FAR),
    "decoder_reduce": (SIDE, SECTION, NEAR, FAR),
    "cross": (NEAR, FAR, SIDE, SECTION),
    "encoder_reduce": (SIDE, NEAR, FAR, SECTION),
    "encoder_expand": (SECTION, SIDE, NEAR, FAR),
    "encoder_attend": (SIDE, SECTION, NEAR, FAR),
}
COLUMN_GROUPS = ("decoder_reduce", "encoder_reduce")
NAMES = tuple(GROUPS)
STAGES = 5
SMALL_ROWS = 208
TINY_ROWS = 24


class Links:
    def __init__(self):
        core = lax.axis_index("rep")
        section = lax.axis_index("section")
        lane = lax.axis_index("dp")
        self.core = core
        self.section = section
        self.mine = [section, lane // 4, (lane // 2) % 2, lane % 2]
        self.partner = [{"section": 1 - section}]
        for dim, step in ((1, 4), (2, 2), (3, 1)):
            self.partner.append({"dp": lane + step - 2 * step * self.mine[dim]})
        self.other_core = {"rep": 1 - core}

    def greet(self):
        barrier = pltpu.get_barrier_semaphore()
        for device in [self.other_core] + self.partner:
            pl.semaphore_signal(barrier, inc=1, device_id=device, device_id_type=pl.DeviceIdType.MESH)
        pl.semaphore_wait(barrier, 5)

    def copy(self, source, target, sems, device):
        return pltpu.make_async_remote_copy(
            src_ref=source,
            dst_ref=target,
            send_sem=sems[0],
            recv_sem=sems[1],
            device_id=device,
            device_id_type=pl.DeviceIdType.MESH,
        )


class Halving:
    def __init__(self, links, order, keep, sent, arrived, stages, send_sems, recv_sems, index, out):
        self.links, self.order, self.keep, self.out = links, order, keep, out
        self.sent, self.arrived, self.stages = sent, arrived, stages
        self.sems = lambda step: (send_sems.at[index, step], recv_sems.at[index, step])
        self.base = 0
        self.half = 16
        self.step = 0
        self.copies = []

    def place(self, shard):
        bits = [(shard >> (3 - dim)) & 1 for dim in range(4)]
        return sum(bits[dim] << (3 - k) for k, dim in enumerate(self.order))

    def start(self):
        step = self.step
        if step == 0:
            copy = self.links.copy(self.sent, self.arrived, self.sems(0), self.links.other_core)
        elif step < STAGES:
            dim = self.order[step - 1]
            mine = self.links.mine[dim]
            self.half //= 2
            copy = self.links.copy(
                self.keep.at[pl.ds(self.base + (1 - mine) * self.half, self.half)],
                self.stages[step - 1],
                self.sems(step),
                self.links.partner[dim],
            )
            self.base = self.base + mine * self.half
        else:
            self.out[pl.ds(self.links.core, 1)] = self.keep[pl.ds(self.base, 1)]
            copy = self.links.copy(
                self.out.at[self.links.core], self.out.at[self.links.core], self.sems(step), self.links.other_core
            )
        copy.start()
        self.copies.append(copy)

    def finish(self):
        self.copies[-1].wait_recv()
        step = self.step
        if step < STAGES:
            source = self.arrived if step == 0 else self.stages[step - 1]
            base, keep = self.base, self.keep

            def add(i, carry):
                keep[base + i] = (keep[base + i].astype(F32) + source[i].astype(F32)).astype(BF16)
                return carry

            lax.fori_loop(0, self.half, add, 0)
        self.step += 1

    def advance(self):
        self.finish()
        if self.step <= STAGES:
            self.start()

    def close(self):
        for copy in self.copies:
            copy.wait_send()


class Butterfly:
    def __init__(self, links, levels, arrived, send_sems, recv_sems, index):
        self.links, self.levels, self.arrived = links, levels, arrived
        self.sems = lambda step: (send_sems.at[index, step], recv_sems.at[index, step])
        self.step = 0
        self.copies = []

    def start(self):
        device = ([self.links.other_core] + self.links.partner)[self.step]
        copy = self.links.copy(
            self.levels.at[self.step], self.arrived.at[self.step], self.sems(self.step), device
        )
        copy.start()
        self.copies.append(copy)

    def advance(self):
        self.copies[-1].wait_recv()
        total = self.levels[self.step].astype(F32) + self.arrived[self.step].astype(F32)
        self.levels[self.step + 1] = total.astype(self.levels.dtype)
        self.step += 1
        if self.step < 5:
            self.start()

    def close(self):
        for copy in self.copies:
            copy.wait_send()


def exchange_kernel(*refs):
    inputs = dict(zip(NAMES, refs[:6]))
    memory_ref, grad_memory_ref, grad_x_ref, small_ref, tiny_ref = refs[6:11]
    outs = dict(zip(NAMES, refs[11:17]))
    memory_out, slab_out, small_out, tiny_out = refs[17:21]
    scratch = refs[21:]
    buffers = {name: scratch[7 * i : 7 * i + 7] for i, name in enumerate(NAMES)}
    small_levels, small_arrived, tiny_levels, tiny_arrived, send_sems, recv_sems, local_sems = scratch[42:]
    links = Links()
    links.greet()
    memory_copy = links.copy(memory_ref, memory_out, (send_sems.at[8, 0], recv_sems.at[8, 0]), links.partner[SECTION])
    memory_copy.start()
    slab_sems = (send_sems.at[8, 1], recv_sems.at[8, 1])
    back_copy = links.copy(grad_memory_ref, slab_out, slab_sems, links.partner[SECTION])
    front_copy = links.copy(grad_x_ref, slab_out, slab_sems, links.partner[SECTION])

    @pl.when(links.section == 0)
    def _():
        back_copy.start()

    @pl.when(links.section == 1)
    def _():
        front_copy.start()

    sums = []
    for index, name in enumerate(NAMES):
        keep, sent, arrived, *stages = buffers[name]
        work = Halving(links, GROUPS[name], keep, sent, arrived, stages, send_sems, recv_sems, index, outs[name])
        sums.append(work)
        for shard in range(16):
            place = work.place(shard)
            pltpu.make_async_copy(
                inputs[name].at[links.core, shard], keep.at[place], local_sems.at[index, 0]
            ).start()
            pltpu.make_async_copy(
                inputs[name].at[1 - links.core, shard], sent.at[place], local_sems.at[index, 1]
            ).start()
    small_levels[0] = small_ref[...]
    tiny_levels[0] = tiny_ref[...]
    butterflies = [
        Butterfly(links, small_levels, small_arrived, send_sems, recv_sems, 6),
        Butterfly(links, tiny_levels, tiny_arrived, send_sems, recv_sems, 7),
    ]
    for work in butterflies:
        work.start()
    for index, (name, work) in enumerate(zip(NAMES, sums)):
        keep, sent = buffers[name][:2]
        pltpu.make_async_copy(inputs[name].at[0], keep, local_sems.at[index, 0]).wait()
        pltpu.make_async_copy(inputs[name].at[0], sent, local_sems.at[index, 1]).wait()
        work.start()
    for step in range(STAGES + 1):
        for work in sums:
            work.advance()
        if step < 5:
            for work in butterflies:
                work.advance()
    small_out[...] = small_levels[5]
    tiny_out[...] = tiny_levels[5]
    memory_copy.wait_recv()
    back_copy.wait_recv()
    for work in sums + butterflies:
        work.close()
    memory_copy.wait_send()
    back_copy.wait_send()


def exchange(groups, memory, grad_memory, grad_x, small, tiny):
    arrays = [groups[name].reshape(2, 16, -1, groups[name].shape[2]) for name in NAMES]
    blocks = [array.shape[2:] for array in arrays]
    scratch = []
    for block in blocks:
        for count in (16, 16, 16, 8, 4, 2, 1):
            scratch.append(pltpu.VMEM((count,) + block, BF16))
    scratch += [
        pltpu.VMEM((6,) + small.shape, BF16),
        pltpu.VMEM((5,) + small.shape, BF16),
        pltpu.VMEM((6,) + tiny.shape, F32),
        pltpu.VMEM((5,) + tiny.shape, F32),
        pltpu.SemaphoreType.DMA((9, STAGES + 1)),
        pltpu.SemaphoreType.DMA((9, STAGES + 1)),
        pltpu.SemaphoreType.DMA((6, 2)),
    ]
    in_any = pl.BlockSpec(memory_space=pl.ANY)
    in_vmem = pl.BlockSpec(memory_space=pltpu.VMEM)
    results = pl.pallas_call(
        exchange_kernel,
        in_specs=[in_any] * 9 + [in_vmem] * 2,
        out_specs=[in_vmem] * 6 + [in_any] * 2 + [in_vmem] * 2,
        out_shape=[shape_of((2,) + block, BF16) for block in blocks]
        + [shape_of(memory.shape, BF16), shape_of(memory.shape, BF16), shape_of(small.shape, BF16), shape_of(tiny.shape, F32)],
        scratch_shapes=scratch,
        compiler_params=pltpu.CompilerParams(
            collective_id=0, has_side_effects=True, vmem_limit_bytes=VMEM_BYTES
        ),
        cost_estimate=pl.CostEstimate(flops=10**8, bytes_accessed=10**8, transcendentals=0),
    )(*arrays, memory, grad_memory, grad_x, small, tiny)
    return dict(zip(NAMES, results[:6])), *results[6:]


def swap(value, axis, bit):
    pairs = [(i, i ^ (1 << bit)) for i in range(lax.axis_size(axis))]
    return lax.ppermute(value, axis, pairs)


def from_halves_rows(halves):
    rows, columns = 2 * halves.shape[1], halves.shape[2]
    return halves.reshape(2, -1, 16, columns).transpose(1, 0, 2, 3).reshape(rows, columns)


def from_halves_columns(halves):
    return jnp.concatenate([halves[0], halves[1]], axis=1)


def plain_scatter(full):
    part = lax.psum_scatter(full.astype(F32), ("section", "dp"), scatter_dimension=0, tiled=True)
    return lax.psum(part, "rep")


def per_device(x, targets, arms, *weights):
    section = lax.axis_index("section")
    sections = lax.axis_size("section")
    lanes = lax.axis_size("dp")
    count = x.shape[0] // sections
    starts, head = weights[6], weights[16]
    valid, joints = starts.shape[0], head.shape[1]
    width = starts.shape[1]
    memories, grads_x, grads_m, sums = [], [], [], None
    for index in range(count):
        place = section * count + index
        pick = lambda array: lax.dynamic_index_in_dim(array, place, 0, keepdims=False)
        memory, grad_x, grad_memory, fresh = episode(
            pick(x), pick(targets), lax.dynamic_slice(arms, (place,), (1,)), weights
        )
        memories.append(memory)
        grads_x.append(grad_x)
        grads_m.append(grad_memory)
        sums = fresh if sums is None else {
            name: (sums[name].astype(F32) + fresh[name].astype(F32)).astype(fresh[name].dtype) for name in fresh
        }
    groups = {
        "decoder_expand": sums["decoder_expand"],
        "decoder_reduce": sums["decoder_reduce"],
        "cross": jnp.concatenate([sums["cross_memory"], sums["cross_combine"]], axis=2),
        "encoder_reduce": sums["encoder_reduce"],
        "encoder_expand": sums["encoder_expand"],
        "encoder_attend": jnp.concatenate([sums["encoder_project"], sums["encoder_combine"]], axis=2),
    }
    small = jnp.concatenate([sums["resid_d"][: SMALL_ROWS // 2], sums["query_d"][: SMALL_ROWS // 2]]).astype(BF16)
    tiny = jnp.concatenate([sums["sums_d"][:4], sums["sums_e"][:4], sums["head"].T])
    tiny = jnp.pad(tiny, ((0, TINY_ROWS - tiny.shape[0]), (0, 0)))
    place = section * lanes + lax.axis_index("dp")
    own = width // (sections * lanes)
    first = section == 0
    memory = jnp.concatenate([item[None] for item in memories])
    grad_memory = jnp.concatenate([item[None] for item in grads_m])
    grad_x = jnp.concatenate([item[None] for item in grads_x])
    done = {}
    if (sections, lanes, lax.axis_size("rep"), count) == (2, 8, 2, 1):
        halves, other, other_slab, small, tiny = exchange(groups, memory, grad_memory, grad_x, small, tiny)
        for name in NAMES:
            done[name] = jnp.concatenate(
                [halves[name][0], halves[name][1]], axis=1 if name in COLUMN_GROUPS else 0
            ).astype(F32)
    else:
        other = swap(memory, "section", 0)
        other_slab = swap(jnp.where(first, grad_memory, grad_x), "section", 0)
        small = lax.psum(small, ("section", "dp", "rep"))
        tiny = lax.psum(tiny, ("section", "dp", "rep"))
        for name in NAMES:
            full = from_halves_columns(groups[name]) if name in COLUMN_GROUPS else from_halves_rows(groups[name])
            done[name] = plain_scatter(full)
    memory_out = jnp.concatenate([jnp.where(first, memory, other), jnp.where(first, other, memory)])
    slab = jnp.concatenate(
        [jnp.where(first, grad_x, other_slab), jnp.where(first, other_slab, grad_memory)]
    )[None]

    columns_of = lambda array: lax.dynamic_slice_in_dim(array, place * own, own, 1)
    rows_of = lambda array: lax.dynamic_slice_in_dim(array, place * own, own, 0)
    rest = PAD_ROWS - SMALL_ROWS // 2
    resid_d = jnp.pad(small[: SMALL_ROWS // 2].astype(F32), ((0, rest), (0, 0)))
    query_d = jnp.pad(small[SMALL_ROWS // 2 :].astype(F32), ((0, rest), (0, 0)))
    head_sum = tiny[8 : 8 + joints].T
    start_grad, project_d, combine_d, query_w, sums_s = decode_start_back(
        valid, jnp.pad(starts, ((0, PAD_ROWS - valid), (0, 0))), weights[7], weights[8], weights[9],
        weights[14], weights[15], resid_d, query_d,
    )
    gains_d = jnp.concatenate([sums_s[0:1], tiny[0:2]])
    shifts_d = jnp.concatenate([sums_s[1:2], tiny[2:4]])
    return (
        memory_out,
        slab,
        done["encoder_attend"][:, : 3 * width],
        done["encoder_attend"][:, 3 * width :],
        done["encoder_expand"],
        done["encoder_reduce"],
        columns_of(tiny[4:6]),
        columns_of(tiny[6:8]),
        columns_of(start_grad[:valid]),
        rows_of(project_d),
        rows_of(combine_d),
        rows_of(query_w),
        done["cross"][:, : 2 * width],
        done["cross"][:, 2 * width :],
        done["decoder_expand"],
        done["decoder_reduce"],
        columns_of(gains_d),
        columns_of(shifts_d),
        rows_of(head_sum),
    )


def solution(mesh):
    spread = ("section", "dp")
    rows = P(spread, None)
    columns = P(None, spread)
    return jax.shard_map(
        per_device,
        mesh=mesh,
        in_specs=(P(("dp", "rep"), None, None), P(("dp", "rep"), None, None), P(("dp", "rep"))) + (P(),) * 17,
        out_specs=(
            P(("dp", "rep"), None, None),
            P("section", ("dp", "rep"), None, None),
            rows, rows, rows, rows, columns, columns, columns,
            rows, rows, rows, rows, rows, rows, rows, columns, columns, rows,
        ),
        check_vma=False,
    )
```

```python
import functools

import jax
import jax.numpy as jnp
from jax import lax
from jax.experimental import pallas as pl
from jax.experimental.pallas import tpu as pltpu
from jax.sharding import PartitionSpec as P

HEADS = 8
EPSILON = 1e-05
LANES = 128
PAD_ROWS = 112
F32 = jnp.float32
BF16 = jnp.bfloat16
NN = (((1,), (0,)), ((), ()))
NT = (((1,), (1,)), ((), ()))
TN = (((0,), (0,)), ((), ()))
VMEM_BYTES = 56 * 1024 * 1024
LINKED_VMEM_BYTES = 63 * 1024 * 1024
ROOT_2_PI = 0.7978845608028654
CUBE = 0.044715


def dot(left, right, dims):
    return lax.dot_general(left, right, dims, preferred_element_type=F32)


def call(kernel, flops, moved, **options):
    return pl.pallas_call(
        kernel,
        compiler_params=pltpu.CompilerParams(vmem_limit_bytes=VMEM_BYTES),
        cost_estimate=pl.CostEstimate(flops=flops, bytes_accessed=moved, transcendentals=0),
        **options,
    )


def shape_of(dims, dtype):
    return jax.ShapeDtypeStruct(dims, dtype)


def whole(array):
    rank = len(array.shape)
    return pl.BlockSpec(array.shape, lambda *_: (0,) * rank, pipeline_mode=pl.Buffered(1))


def normed(residual):
    centre = jnp.mean(residual, axis=-1, keepdims=True)
    centred = residual - centre
    spread = jnp.mean(centred * centred, axis=-1, keepdims=True)
    scale = lax.rsqrt(spread + EPSILON)
    return centred * scale, scale


def normed_back(grad, gain, rows, scale):
    weighted = grad * gain
    return scale * (
        weighted
        - jnp.mean(weighted, axis=-1, keepdims=True)
        - rows * jnp.mean(weighted * rows, axis=-1, keepdims=True)
    )


def gelu_and_slope(value):
    square = value * value
    bend = jnp.tanh(value * (ROOT_2_PI + (ROOT_2_PI * CUBE) * square))
    half = 0.5 + 0.5 * bend
    slope = half + value * (0.5 - 0.5 * bend * bend) * (
        ROOT_2_PI + (3.0 * ROOT_2_PI * CUBE) * square
    )
    return value * half, slope


def column_sum(value):
    return jnp.sum(value, axis=0, keepdims=True)


def attend_kernel(q_ref, k_ref, v_ref, mixed_ref, log_ref):
    count = q_ref.shape[0]
    lane = lax.broadcasted_iota(jnp.int32, (1, LANES), 1)
    keys = k_ref[...]
    values = v_ref[...].T
    queries = q_ref[...] * jnp.asarray(0.125, BF16)
    for head in range(2):
        own = (lane < 64) if head == 0 else (lane >= 64)
        head_keys = jnp.where(own, keys, jnp.zeros_like(keys))
        extended = jnp.concatenate(
            [values[64 * head : 64 * head + 64], jnp.ones((16, count), BF16)], axis=0
        )
        scores = dot(head_keys, queries, NT)
        largest = jnp.max(scores, axis=0, keepdims=True)
        raised = jnp.exp(scores - largest).astype(BF16)
        mixed = dot(extended, raised, NN)
        total = mixed[64:65]
        mixed_ref[pl.ds(64 * head, 64), :] = (mixed[:64] * (1.0 / total)).astype(BF16)
        log_ref[0, pl.ds(head, 1), :] = largest + jnp.log(total)


def attend(packed):
    rows, width = packed.shape[0], packed.shape[1] // 3
    pairs = width // LANES
    column = lambda first: pl.BlockSpec((rows, LANES), lambda j: (0, first + j))
    return call(
        attend_kernel,
        4 * rows * rows * width * 4,
        rows * width * 8,
        grid=(pairs,),
        in_specs=[column(0), column(pairs), column(2 * pairs)],
        out_specs=[
            pl.BlockSpec((LANES, rows), lambda j: (j, 0)),
            pl.BlockSpec((1, 2, rows), lambda j: (j, 0, 0)),
        ],
        out_shape=[shape_of((width, rows), BF16), shape_of((pairs, 2, rows), F32)],
    )(packed, packed, packed)


def attend_back_kernel(block, q_ref, k_ref, v_ref, do_ref, mixed_ref, log_ref, dq_ref, dk_ref, dv_ref):
    count = q_ref.shape[0]
    lane = lax.broadcasted_iota(jnp.int32, (1, LANES), 1)
    keys = k_ref[...]
    values = v_ref[...]
    queries = q_ref[...] * jnp.asarray(0.125, BF16)
    scaled_keys = keys * jnp.asarray(0.125, BF16)
    grads = do_ref[...]
    queries_t = queries.T
    grads_t = grads.T
    logs = log_ref[0].T
    shared = mixed_ref[...].astype(F32) * grads_t.astype(F32)
    inner = jnp.concatenate([column_sum(shared[:64]), column_sum(shared[64:])], axis=0).T
    dq_parts = [[], []]
    dk_parts = []
    dv_parts = []
    for head in range(2):
        own = (lane < 64) if head == 0 else (lane >= 64)
        head_queries = jnp.where(own, queries, jnp.zeros_like(queries))
        head_grads = jnp.where(own, grads, jnp.zeros_like(grads))
        dk = None
        dv = None
        for start in range(0, count, block):
            part = slice(start, start + block)
            scores = dot(head_queries[part], keys, NT)
            probs = jnp.exp(scores - logs[part, head : head + 1])
            grad_probs = dot(head_grads[part], values, NT)
            grad_scores = (probs * (grad_probs - inner[part, head : head + 1])).astype(BF16)
            new_v = dot(grads_t[64 * head : 64 * head + 64, part], probs.astype(BF16), NN)
            new_k = dot(queries_t[64 * head : 64 * head + 64, part], grad_scores, NN)
            dv = new_v if dv is None else dv + new_v
            dk = new_k if dk is None else dk + new_k
            dq_parts[head].append(dot(grad_scores, scaled_keys, NN))
        dk_parts.append(dk)
        dv_parts.append(dv)
    dk_ref[...] = jnp.concatenate(dk_parts, axis=0).T.astype(BF16)
    dv_ref[...] = jnp.concatenate(dv_parts, axis=0).T.astype(BF16)
    for index in range(count // block):
        dq_ref[pl.ds(index * block, block), :] = jnp.where(
            lane < 64, dq_parts[0][index], dq_parts[1][index]
        ).astype(BF16)


def attend_back(packed, grad_mixed, mixed, logs):
    rows, width = packed.shape[0], packed.shape[1] // 3
    pairs = width // LANES
    column = lambda first: pl.BlockSpec((rows, LANES), lambda j: (0, first + j))
    return call(
        functools.partial(attend_back_kernel, 256),
        10 * rows * rows * width * 3,
        rows * width * 16,
        grid=(pairs,),
        in_specs=[
            column(0),
            column(pairs),
            column(2 * pairs),
            column(0),
            pl.BlockSpec((LANES, rows), lambda j: (j, 0)),
            pl.BlockSpec((1, 2, rows), lambda j: (j, 0, 0)),
        ],
        out_specs=[column(0)] * 3,
        out_shape=[shape_of((rows, width), BF16)] * 3,
    )(packed, packed, packed, grad_mixed, mixed, logs)


def encode_rows_kernel(
    x_ref, mixed_ref, combine_ref, expand_ref, reduce_ref, gain_ref, shift_ref, memory_w_ref,
    first_ref, low_ref, active_ref, slope_ref, second_ref, memory_ref, pair_ref,
):
    residual = x_ref[...].astype(F32) + dot(mixed_ref[...], combine_ref[...], TN)
    first_ref[...] = residual
    rows, _ = normed(residual)
    first = rows * gain_ref[0:1, :] + shift_ref[0:1, :]
    low = first.astype(BF16)
    low_ref[...] = low
    total = first
    hidden_size = expand_ref.shape[1]
    step = hidden_size // 5
    for start in range(0, hidden_size, step):
        part = pl.ds(start, step)
        active, slope = gelu_and_slope(dot(low, expand_ref[:, part], NN))
        active = active.astype(BF16)
        active_ref[:, part] = active
        slope_ref[:, part] = slope.astype(BF16)
        total = total + dot(active, reduce_ref[part, :], NN)
    second_ref[...] = total
    rows, _ = normed(total)
    memory = (rows * gain_ref[1:2, :] + shift_ref[1:2, :]).astype(BF16)
    memory_ref[...] = memory
    pair_ref[...] = dot(memory, memory_w_ref[...], NN).astype(BF16)


def encode_rows(x, mixed, combine_w, expand_w, reduce_w, gains, shifts, memory_w):
    rows, width = x.shape
    hidden = expand_w.shape[1]
    block = 256
    line = lambda size: pl.BlockSpec((block, size), lambda i: (i, 0))
    sizes = [(width, F32), (width, BF16), (hidden, BF16), (hidden, BF16), (width, F32), (width, BF16), (2 * width, BF16)]
    return call(
        encode_rows_kernel,
        2 * rows * width * (2 * hidden + 3 * width),
        rows * (hidden * 4 + width * 18) + 8 * width * hidden,
        grid=(rows // block,),
        in_specs=[line(width), pl.BlockSpec((width, block), lambda i: (0, i))]
        + [whole(item) for item in (combine_w, expand_w, reduce_w, gains, shifts, memory_w)],
        out_specs=[line(size) for size, _ in sizes],
        out_shape=[shape_of((rows, size), kind) for size, kind in sizes],
    )(x, mixed, combine_w, expand_w, reduce_w, gains, shifts, memory_w)


def encode_back_kernel(
    pair_ref, first_ref, second_ref, slope_ref, combine_ref, expand_ref, reduce_ref, gain_ref, memory_w_ref,
    grad_memory_ref, branch_ref, hidden_ref, resid_ref, low_ref, mixed_ref, sums_ref,
):
    grad_memory = dot(pair_ref[...], memory_w_ref[...], NT).astype(BF16)
    grad_memory_ref[...] = grad_memory
    grad_last = grad_memory.astype(F32)
    rows, scale = normed(second_ref[...])
    gain_last = column_sum(grad_last * rows)
    shift_last = column_sum(grad_last)
    grad_second = normed_back(grad_last, gain_ref[1:2, :], rows, scale)
    branch = grad_second.astype(BF16)
    branch_ref[...] = branch
    total = grad_second
    hidden_size = expand_ref.shape[1]
    step = hidden_size // 5
    for start in range(0, hidden_size, step):
        part = pl.ds(start, step)
        grad_active = dot(branch, reduce_ref[part, :], NT)
        grad_hidden = (grad_active * slope_ref[:, part].astype(F32)).astype(BF16)
        hidden_ref[:, part] = grad_hidden
        total = total + dot(grad_hidden, expand_ref[:, part], NT)
    rows, scale = normed(first_ref[...])
    gain_first = column_sum(total * rows)
    shift_first = column_sum(total)
    grad_first = normed_back(total, gain_ref[0:1, :], rows, scale)
    resid_ref[...] = grad_first
    low = grad_first.astype(BF16)
    low_ref[...] = low
    mixed_ref[...] = dot(low, combine_ref[...], NT).astype(BF16)
    fresh = jnp.concatenate(
        [gain_first, gain_last, shift_first, shift_last, jnp.zeros((4, gain_first.shape[1]), F32)], axis=0
    )

    @pl.when(pl.program_id(0) == 0)
    def _():
        sums_ref[...] = fresh

    @pl.when(pl.program_id(0) > 0)
    def _():
        sums_ref[...] += fresh


def encode_back(grad_pair, first, second, slope, combine_w, expand_w, reduce_w, gains, memory_w):
    rows, width = first.shape
    hidden = expand_w.shape[1]
    block = 256
    line = lambda size: pl.BlockSpec((block, size), lambda i: (i, 0))
    sizes = [(width, BF16), (width, BF16), (hidden, BF16), (width, F32), (width, BF16), (width, BF16)]
    return call(
        encode_back_kernel,
        2 * rows * width * (2 * hidden + 3 * width),
        rows * (hidden * 4 + width * 18) + 8 * width * hidden,
        grid=(rows // block,),
        in_specs=[line(2 * width), line(width), line(width), line(hidden)]
        + [whole(item) for item in (combine_w, expand_w, reduce_w, gains, memory_w)],
        out_specs=[line(size) for size, _ in sizes] + [pl.BlockSpec((8, width), lambda i: (0, 0))],
        out_shape=[shape_of((rows, size), kind) for size, kind in sizes] + [shape_of((8, width), F32)],
    )(grad_pair, first, second, slope, combine_w, expand_w, reduce_w, gains, memory_w)


def stacked(rows):
    lane = lax.broadcasted_iota(jnp.int32, (1, rows.shape[1]), 1)
    return jnp.concatenate(
        [jnp.where((lane >= 64 * h) & (lane < 64 * h + 64), rows, jnp.zeros_like(rows)) for h in range(4)],
        axis=0,
    )


def unstacked(rows):
    lane = lax.broadcasted_iota(jnp.int32, (1, rows.shape[1]), 1)
    count = rows.shape[0] // 4
    result = rows[:count]
    for h in range(1, 4):
        result = jnp.where(lane >= 64 * h, rows[h * count : h * count + count], result)
    return result


def few_attend(queries, keys, values, valid):
    mixed = []
    kept = []
    for half in range(2):
        part = slice(256 * half, 256 * half + 256)
        scores = dot(stacked(queries[:, part] * jnp.asarray(0.125, BF16)), keys[:, part], NT)
        if valid < scores.shape[1]:
            column = lax.broadcasted_iota(jnp.int32, (1, scores.shape[1]), 1)
            scores = jnp.where(column < valid, scores, -1e30)
        raised = jnp.exp(scores - jnp.max(scores, axis=1, keepdims=True))
        probs = raised * (1.0 / jnp.sum(raised, axis=1, keepdims=True))
        mixed.append(unstacked(dot(probs.astype(BF16), values[:, part], NN)))
        kept.append(probs)
    return jnp.concatenate(mixed, axis=1).astype(BF16), kept


def few_attend_back(queries, keys, values, kept, grads):
    dq, dk, dv = [], [], []
    for half in range(2):
        part = slice(256 * half, 256 * half + 256)
        probs = kept[half]
        own_queries = stacked(queries[:, part] * jnp.asarray(0.125, BF16))
        own_grads = stacked(grads[:, part])
        grad_probs = dot(own_grads, values[:, part], NT)
        product = probs * grad_probs
        grad_scores = (product - probs * jnp.sum(product, axis=1, keepdims=True)).astype(BF16)
        dv.append(dot(probs.astype(BF16), own_grads, TN))
        dk.append(dot(grad_scores, own_queries, TN))
        dq.append(unstacked(dot(grad_scores, keys[:, part], NN)) * 0.125)
    return jnp.concatenate(dq, axis=1), jnp.concatenate(dk, axis=1), jnp.concatenate(dv, axis=1)


def self_block(starts, project_w, combine_w, gain, shift, valid):
    width = starts.shape[1]
    packed = dot(starts, project_w, NN).astype(BF16)
    queries, keys, values = (packed[:, i * width : (i + 1) * width] for i in range(3))
    mixed, kept = few_attend(queries, keys, values, valid)
    residual = starts.astype(F32) + dot(mixed, combine_w, NN)
    rows, scale = normed(residual)
    return queries, keys, values, mixed, kept, rows, scale, rows * gain + shift


def dealt(rows):
    width = rows.shape[1]
    source = lax.broadcasted_iota(jnp.int32, (width, width), 0)
    target = lax.broadcasted_iota(jnp.int32, (width, width), 1)
    half = width // 2
    wanted = (target % half) // 16 * 32 + target // half * 16 + target % 16
    return dot(rows, jnp.where(source == wanted, 1.0, 0.0).astype(BF16), NN).astype(BF16)


def undealt(columns):
    count, width = columns.shape
    return columns.reshape(count, 2, width // 32, 16).transpose(0, 2, 1, 3).reshape(count, width)


def decode_kernel(
    valid, joints,
    starts_ref, project_ref, combine_ref, query_ref, cross_ref, expand_ref, reduce_ref, gain_ref, shift_ref,
    head_ref, pair_ref, target_ref, arm_ref,
    grad_pair_ref, second_low_ref, hidden_ref, active_ref, branch_ref, cross_grad_ref, small_ref, query_grad_ref,
    head_grad_ref, sums_ref,
):
    width = starts_ref.shape[1]
    first = self_block(
        starts_ref[...], project_ref[...], combine_ref[...], gain_ref[0:1, :], shift_ref[0:1, :], valid
    )[-1]
    queries = dot(first.astype(BF16), query_ref[...], NN).astype(BF16)
    keys = pair_ref[:, :width]
    values = pair_ref[:, width:]
    mixed, kept = few_attend(queries, keys, values, keys.shape[0])
    second_rows, second_scale = normed(first + dot(mixed, cross_ref[...], NN))
    second = second_rows * gain_ref[1:2, :] + shift_ref[1:2, :]
    second_low = second.astype(BF16)
    second_low_ref[...] = dealt(second_low)
    hidden_size = expand_ref.shape[1]
    step = hidden_size // 5
    total = second
    slopes = []
    for start in range(0, hidden_size, step):
        part = pl.ds(start, step)
        active, slope = gelu_and_slope(dot(second_low, expand_ref[:, part], NN))
        slopes.append(slope)
        active = active.astype(BF16)
        active_ref[:, part] = active
        total = total + dot(active, reduce_ref[part, :], NN)
    third_rows, third_scale = normed(total)
    third_low = (third_rows * gain_ref[2:3, :] + shift_ref[2:3, :]).astype(BF16)
    misfit = dot(third_low, head_ref[...], NN) - target_ref[...]
    arms = arm_ref[0]
    row = lax.broadcasted_iota(jnp.int32, misfit.shape, 0)
    joint = lax.broadcasted_iota(jnp.int32, misfit.shape, 1)
    factor = 2.0 / jnp.full((1, 1), arms, jnp.int32).astype(F32)
    used = (row < valid) & (joint < joints // 2 * arms)
    grad_pred = jnp.where(used, factor * misfit * lax.rsqrt(misfit * misfit + 1.0), 0.0).astype(BF16)
    head_grad_ref[...] = dot(third_low, grad_pred, TN)
    grad_third = dot(grad_pred, head_ref[...], NT)
    gain_third = column_sum(grad_third * third_rows)
    shift_third = column_sum(grad_third)
    total = normed_back(grad_third, gain_ref[2:3, :], third_rows, third_scale)
    branch = total.astype(BF16)
    branch_ref[...] = branch
    for index, start in enumerate(range(0, hidden_size, step)):
        part = pl.ds(start, step)
        grad_hidden = (dot(branch, reduce_ref[part, :], NT) * slopes[index]).astype(BF16)
        hidden_ref[:, part] = grad_hidden
        total = total + dot(grad_hidden, expand_ref[:, part], NT)
    gain_second = column_sum(total * second_rows)
    shift_second = column_sum(total)
    grad_second = normed_back(total, gain_ref[1:2, :], second_rows, second_scale)
    small_ref[...] = grad_second
    branch = grad_second.astype(BF16)
    cross_grad_ref[...] = dot(mixed, branch, TN).astype(BF16)
    grad_mixed = dot(branch, cross_ref[...], NT).astype(BF16)
    dq, dk, dv = few_attend_back(queries, keys, values, kept, grad_mixed)
    query_grad_ref[...] = dq.astype(BF16).astype(F32)
    grad_pair_ref[:, :width] = dk.astype(BF16)
    grad_pair_ref[:, width:] = dv.astype(BF16)
    sums_ref[...] = jnp.concatenate(
        [gain_second, gain_third, shift_second, shift_third, jnp.zeros((4, width), F32)], axis=0
    )


def decode(valid, joints, starts, weights, pair, target, arm):
    project_w, combine_w, query_w, cross_w, expand_w, reduce_w, gains, shifts, head_w = weights
    count, width = starts.shape
    hidden = expand_w.shape[1]
    shapes = [
        (pair.shape, BF16),
        ((count, width), BF16),
        ((count, hidden), BF16),
        ((count, hidden), BF16),
        ((count, width), BF16),
        ((width, width), BF16),
        ((count, width), F32),
        ((count, width), F32),
        (head_w.shape, F32),
        ((8, width), F32),
    ]
    arrays = (starts, project_w, combine_w, query_w, cross_w, expand_w, reduce_w, gains, shifts, head_w, pair, target)
    return call(
        functools.partial(decode_kernel, valid, joints),
        8 * count * width * hidden * 4,
        16 * 1024 * 1024,
        in_specs=[pl.BlockSpec(memory_space=pltpu.VMEM)] * len(arrays) + [pl.BlockSpec(memory_space=pltpu.SMEM)],
        out_specs=[pl.BlockSpec(memory_space=pltpu.VMEM)] * len(shapes),
        out_shape=[shape_of(dims, kind) for dims, kind in shapes],
    )(*arrays, arm)


def decode_start_back_kernel(
    valid,
    starts_ref, project_ref, combine_ref, query_ref, gain_ref, shift_ref, resid_ref, query_grad_ref,
    start_grad_ref, project_grad_ref, combine_grad_ref, query_w_grad_ref, sums_ref,
):
    starts = starts_ref[...]
    project_w = project_ref[...]
    queries, keys, values, mixed, kept, rows, scale, first = self_block(
        starts, project_w, combine_ref[...], gain_ref[0:1, :], shift_ref[0:1, :], valid
    )
    low = query_grad_ref[...].astype(BF16)
    query_w_grad_ref[...] = dot(first.astype(BF16), low, TN)
    grad_first = resid_ref[...] + dot(low, query_ref[...], NT)
    gain_sum = column_sum(grad_first * rows)
    shift_sum = column_sum(grad_first)
    grad_resid = normed_back(grad_first, gain_ref[0:1, :], rows, scale)
    branch = grad_resid.astype(BF16)
    combine_grad_ref[...] = dot(mixed, branch, TN)
    grad_mixed = dot(branch, combine_ref[...], NT).astype(BF16)
    dq, dk, dv = few_attend_back(queries, keys, values, kept, grad_mixed)
    grad_packed = jnp.concatenate([dq, dk, dv], axis=1).astype(BF16)
    project_grad_ref[...] = dot(starts, grad_packed, TN)
    start_grad_ref[...] = grad_resid + dot(grad_packed, project_w, NT)
    sums_ref[...] = jnp.concatenate([gain_sum, shift_sum, jnp.zeros((6, gain_sum.shape[1]), F32)], axis=0)


def decode_start_back(valid, starts, project_w, combine_w, query_w, gains, shifts, resid, query_grad):
    count, width = starts.shape
    arrays = (starts, project_w, combine_w, query_w, gains, shifts, resid, query_grad)
    shapes = [(count, width), (width, 3 * width), (width, width), (width, width), (8, width)]
    return call(
        functools.partial(decode_start_back_kernel, valid),
        2 * count * width * width * 20,
        8 * 1024 * 1024,
        in_specs=[pl.BlockSpec(memory_space=pltpu.VMEM)] * len(arrays),
        out_specs=[pl.BlockSpec(memory_space=pltpu.VMEM)] * len(shapes),
        out_shape=[shape_of(dims, F32) for dims in shapes],
    )(*arrays)


def forward(x, target, arm, weights):
    (
        encoder_project, encoder_combine, encoder_expand, encoder_reduce, encoder_gains, encoder_shifts,
        starts, decoder_project, decoder_combine, cross_query, cross_memory, cross_combine,
        decoder_expand, decoder_reduce, decoder_gains, decoder_shifts, head,
    ) = weights
    valid, joints = starts.shape[0], head.shape[1]
    packed = dot(x, encoder_project, NN).astype(BF16)
    mixed, logs = attend(packed)
    first, first_low, active, slope, second, memory, pair = encode_rows(
        x, mixed, encoder_combine, encoder_expand, encoder_reduce, encoder_gains, encoder_shifts, cross_memory
    )
    padded = jnp.pad(starts, ((0, PAD_ROWS - valid), (0, 0)))
    wide_head = jnp.pad(head, ((0, 0), (0, LANES - joints)))
    wide_target = jnp.pad(target, ((0, PAD_ROWS - valid), (0, LANES - joints)))
    (
        grad_pair, second_low, grad_hidden_d, active_d, branch_d, cross_grad, resid_d, query_grad, head_grad, sums_d,
    ) = decode(
        valid, joints, padded,
        (
            decoder_project, decoder_combine, cross_query, cross_combine, decoder_expand, decoder_reduce,
            decoder_gains, decoder_shifts, wide_head,
        ),
        pair, wide_target, arm,
    )
    return {
        "x": x, "packed": packed, "mixed": mixed, "logs": logs, "first": first, "low": first_low, "active": active,
        "slope": slope, "second": second, "memory": memory, "grad_pair": grad_pair, "low_d": second_low,
        "hidden_d": grad_hidden_d, "active_d": active_d, "branch_d": branch_d, "cross": cross_grad,
        "resid_d": resid_d, "query_d": query_grad, "head": head_grad[:, :joints], "sums_d": sums_d,
    }


def backward_alone(saved, weights):
    (encoder_project, encoder_combine, encoder_expand, encoder_reduce, encoder_gains) = weights[:5]
    cross_memory = weights[10]
    grad_memory, branch, grad_hidden, resid, low, grad_mixed, sums_e = encode_back(
        saved["grad_pair"], saved["first"], saved["second"], saved["slope"],
        encoder_combine, encoder_expand, encoder_reduce, encoder_gains, cross_memory,
    )
    dq, dk, dv = attend_back(saved["packed"], grad_mixed, saved["mixed"], saved["logs"])
    grad_packed = jnp.concatenate([dq, dk, dv], axis=1)
    grad_x = (resid + dot(grad_packed, encoder_project, NT)).astype(BF16)
    plain = lambda left, right: dot(left, right, TN)
    return grad_x, grad_memory, {
        "decoder_expand": plain(undealt(saved["low_d"]), saved["hidden_d"]),
        "decoder_reduce": plain(saved["active_d"], saved["branch_d"]),
        "encoder_reduce": plain(saved["active"], branch),
        "encoder_expand": plain(saved["low"], grad_hidden),
        "middle": jnp.concatenate(
            [plain(saved["memory"], saved["grad_pair"]), saved["cross"].astype(F32), dot(saved["mixed"], low, NN)], axis=1
        ),
        "last": plain(saved["x"], grad_packed),
        "sums_e": sums_e[:4], "sums_d": saved["sums_d"][:4], "head": saved["head"].T,
        "resid_d": saved["resid_d"], "query_d": saved["query_d"],
    }


BITS = (("section", 0), ("dp", 2), ("dp", 1), ("dp", 0))
SECTION, FAR, NEAR, SIDE = range(4)
GROUPS = {
    "decoder_expand": (NEAR, FAR, SIDE, SECTION),
    "decoder_reduce": (SIDE, SECTION, NEAR, FAR),
    "encoder_reduce": (SIDE, NEAR, FAR, SECTION),
    "encoder_expand": (SIDE, NEAR, FAR, SECTION),
    "middle": (SECTION, SIDE, NEAR, FAR),
    "last": (NEAR, FAR, SIDE, SECTION),
}
COLUMN_GROUPS = ("decoder_reduce", "encoder_reduce")
NAMES = tuple(GROUPS)
STAGES = 5
SMALL_ROWS = 208
TINY_ROWS = 24


class Links:
    def __init__(self):
        core = lax.axis_index("rep")
        section = lax.axis_index("section")
        lane = lax.axis_index("dp")
        self.core = core
        self.section = section
        self.mine = [section, lane // 4, (lane // 2) % 2, lane % 2]
        self.partner = [{"section": 1 - section}]
        for dim, step in ((1, 4), (2, 2), (3, 1)):
            self.partner.append({"dp": lane + step - 2 * step * self.mine[dim]})
        self.other_core = {"rep": 1 - core}

    def greet(self):
        barrier = pltpu.get_barrier_semaphore()
        for device in [self.other_core] + self.partner:
            pl.semaphore_signal(barrier, inc=1, device_id=device, device_id_type=pl.DeviceIdType.MESH)
        pl.semaphore_wait(barrier, 5)

    def copy(self, source, target, sems, device):
        return pltpu.make_async_remote_copy(
            src_ref=source,
            dst_ref=target,
            send_sem=sems[0],
            recv_sem=sems[1],
            device_id=device,
            device_id_type=pl.DeviceIdType.MESH,
        )


class Halving:
    def __init__(self, links, order, keep, sent, arrived, stages, send_sems, recv_sems, index, out, credits=None):
        self.links, self.order, self.keep, self.out = links, order, keep, out
        self.credits = credits
        self.sent, self.arrived, self.stages = sent, arrived, stages
        self.sems = lambda step: (send_sems.at[index, step], recv_sems.at[index, step])
        self.offsets = []
        base = 0
        for step, dim in enumerate(order):
            half = 8 >> step
            mine = links.mine[dim]
            self.offsets.append((base + (1 - mine) * half, base + mine * half, half))
            base = base + mine * half
        self.base = base
        self.first = 1 if sent is None else 0
        self.step = self.first

    def place(self, shard):
        bits = [(shard >> (3 - dim)) & 1 for dim in range(4)]
        return sum(bits[dim] << (3 - k) for k, dim in enumerate(self.order))

    def copy_of(self, step):
        links = self.links
        if step == 0:
            return links.copy(self.sent, self.arrived, self.sems(0), links.other_core)
        if step < STAGES:
            away, _, half = self.offsets[step - 1]
            return links.copy(
                self.keep.at[pl.ds(away, half)], self.stages[step - 1], self.sems(step),
                links.partner[self.order[step - 1]],
            )
        return links.copy(self.out.at[links.core], self.out.at[links.core], self.sems(step), links.other_core)

    def start(self):
        step = self.step
        if self.credits is not None and step < STAGES:
            device = 0 if step == 0 else 1 + self.order[step - 1]
            pl.semaphore_wait(self.credits.at[device], 1)
        if step == STAGES:
            self.out[pl.ds(self.links.core, 1)] = self.keep[pl.ds(self.base, 1)]
        self.copy_of(step).start()

    def finish(self):
        step = self.step
        self.copy_of(step).wait_recv()
        if step < STAGES:
            source = self.arrived if step == 0 else self.stages[step - 1]
            keep = self.keep
            base, half = (0, 16) if step == 0 else self.offsets[step - 1][1:]

            def add(i, carry):
                keep[base + i] = (keep[base + i].astype(F32) + source[i].astype(F32)).astype(BF16)
                return carry

            lax.fori_loop(0, half, add, 0)
        self.step += 1

    def advance(self):
        self.finish()
        if self.step <= STAGES:
            self.start()

    def close(self):
        for step in range(self.first, STAGES + 1):
            self.copy_of(step).wait_send()


class Butterfly:
    def __init__(self, links, levels, arrived, send_sems, recv_sems, index):
        self.links, self.levels, self.arrived = links, levels, arrived
        self.sems = lambda step: (send_sems.at[index, step], recv_sems.at[index, step])
        self.step = 0

    def copy_of(self, step):
        device = ([self.links.other_core] + self.links.partner)[step]
        return self.links.copy(self.levels.at[step], self.arrived.at[step], self.sems(step), device)

    def start(self):
        self.copy_of(self.step).start()

    def advance(self):
        self.copy_of(self.step).wait_recv()
        total = self.levels[self.step].astype(F32) + self.arrived[self.step].astype(F32)
        self.levels[self.step + 1] = total.astype(self.levels.dtype)
        self.step += 1
        if self.step < 5:
            self.start()

    def close(self):
        for step in range(5):
            self.copy_of(step).wait_send()


IN_NAMES = (
    "low_d", "hidden_d", "active_d", "branch_d", "grad_pair", "cross_memory", "second", "memory", "active",
    "reduce", "slope", "expand", "first", "low", "mixed", "combine", "cross", "packed", "logs", "x", "project",
)
SMALL_NAMES = ("gains", "small", "tiny")
ATTEND_BLOCK = 256


def backward_kernel(*refs):
    refs = list(refs)

    def draw(count):
        taken = refs[:count]
        del refs[:count]
        return taken

    source = dict(zip(IN_NAMES, draw(len(IN_NAMES))))
    gain_ref, small_ref, tiny_ref = draw(3)
    outs = dict(zip(NAMES, draw(6)))
    memory_out, slab_out, grad_memory_out, grad_x_out, small_out, tiny_out = draw(6)
    acts = dict(zip(IN_NAMES[:4], draw(4)))
    buffers = {
        "decoder_expand": [None, None] + draw(4),
        "decoder_reduce": [None, None] + draw(4),
        "encoder_reduce": draw(6),
        "middle": draw(6),
        "last": draw(6),
    }
    keeps = dict(zip(("decoder_expand", "decoder_reduce", "encoder_reduce", "middle", "last"), draw(5)))
    hidden, slope, grad_mixed, resid, mixed, branch, small_levels, small_arrived, tiny_levels, tiny_arrived = draw(10)
    send_sems, recv_sems, load_sems, store_sems, credits = draw(5)
    buffers["encoder_expand"] = [
        slope.at[pl.ds(16, 16)], slope.at[pl.ds(32, 16)], slope.at[pl.ds(48, 8)], slope.at[pl.ds(56, 4)],
        slope.at[pl.ds(60, 2)], slope.at[pl.ds(62, 1)],
    ]
    keeps["encoder_expand"] = slope.at[pl.ds(0, 16)]

    links = Links()
    core = links.core
    count, width = resid.shape
    hidden_size = hidden.shape[1]
    step = hidden_size // 5
    block = 256
    own_columns = pl.ds(pl.multiple_of(core * 256, 256), 256)
    other_columns = pl.ds(pl.multiple_of((1 - core) * 256, 256), 256)
    work = {}
    for index, name in enumerate(NAMES):
        sent, arrived, *stages = buffers[name]
        work[name] = Halving(
            links, GROUPS[name], keeps[name], sent, arrived, stages, send_sems, recv_sems, index, outs[name],
            credits if name == "encoder_expand" else None,
        )

    def load(name, target):
        copy = pltpu.make_async_copy(source[name], target, load_sems.at[IN_NAMES.index(name)])
        copy.start()
        return copy

    def deal(name, rows, first_column):
        item = work[name]
        columns = pl.ds(first_column, rows.shape[1])
        low = rows.astype(BF16)
        for shard in range(16):
            here = low[32 * shard : 32 * shard + 16]
            there = low[32 * shard + 16 : 32 * shard + 32]
            place = item.place(shard)
            item.keep[place, :, columns] = jnp.where(core == 0, here, there)
            item.sent[place, :, columns] = jnp.where(core == 0, there, here)

    def deal_columns(name, target, rows):
        size = rows.shape[0] // 16
        for shard in range(16):
            target[work[name].place(shard)] = rows[size * shard : size * shard + size].astype(BF16)

    own_acts = {name: load(name, acts[name].at[pl.ds(0, PAD_ROWS)]) for name in IN_NAMES[:4]}
    links.greet()
    memory_copy = links.copy(source["memory"], memory_out, (send_sems.at[8, 0], recv_sems.at[8, 0]), links.partner[SECTION])
    memory_copy.start()
    slab_sems = (send_sems.at[8, 1], recv_sems.at[8, 1])
    back_copy = links.copy(grad_memory_out, slab_out, slab_sems, links.partner[SECTION])
    front_copy = links.copy(grad_x_out, slab_out, slab_sems, links.partner[SECTION])

    butterfly = Butterfly(links, small_levels, small_arrived, send_sems, recv_sems, 6)
    tiny_butterfly = Butterfly(links, tiny_levels, tiny_arrived, send_sems, recv_sems, 7)

    def rows_phase(grad_pair, memory_w, residual, memory, reduce_w, expand_w, low, combine_w, cross):
        loads = {
            name: load(name, target)
            for name, target in (
                ("grad_pair", grad_pair), ("cross_memory", memory_w), ("second", residual), ("memory", memory),
                ("active", hidden), ("reduce", reduce_w), ("slope", slope), ("expand", expand_w),
                ("low", low), ("mixed", mixed), ("combine", combine_w), ("cross", cross),
            )
        }
        act_copies = []
        for index, name in enumerate(IN_NAMES[:4]):
            own_acts[name].wait()
            act_copies.append(
                links.copy(
                    acts[name].at[pl.ds(0, PAD_ROWS)], acts[name].at[pl.ds(PAD_ROWS, PAD_ROWS)],
                    (send_sems.at[9, index], recv_sems.at[9, index]), links.other_core,
                )
            )
            act_copies[-1].start()
        small_levels[0] = small_ref[...]
        butterfly.start()

        loads["grad_pair"].wait()
        loads["cross_memory"].wait()
        loads["second"].wait()
        sums = None
        for start in range(0, count, block):
            part = pl.ds(start, block)
            low_grad = dot(grad_pair[part, :], memory_w[...], NT).astype(BF16)
            grad_mixed[part, :] = low_grad
            grad = low_grad.astype(F32)
            rows, scale = normed(residual[part, :])
            fresh = [column_sum(grad * rows), column_sum(grad)]
            sums = fresh if sums is None else [old + new for old, new in zip(sums, fresh)]
            total = normed_back(grad, gain_ref[1:2, :], rows, scale)
            resid[part, :] = total
            branch[part, :] = total.astype(BF16)
        memory_store = pltpu.make_async_copy(grad_mixed, grad_memory_out, store_sems.at[0])
        memory_store.start()
        loads["first"] = load("first", residual)
        last_sums = sums

        for copy in act_copies:
            copy.wait_recv()
        item = work["decoder_reduce"]
        deal_columns(
            "decoder_reduce", item.keep, dot(acts["active_d"][...], acts["branch_d"][:, own_columns], TN)
        )
        item.start()
        item = work["decoder_expand"]
        for start in range(0, hidden_size, step):
            columns = pl.ds(start, step)
            rows = dot(acts["low_d"][:, own_columns], acts["hidden_d"][:, columns], TN).astype(BF16)
            for shard in range(16):
                item.keep[item.place(shard), :, columns] = rows[16 * shard : 16 * shard + 16]
        item.start()
        memory_store.wait()

        @pl.when(links.section == 0)
        def _():
            back_copy.start()

        loads["active"].wait()
        item = work["encoder_reduce"]
        deal_columns("encoder_reduce", item.sent, dot(hidden[...], branch[:, other_columns], TN))
        item.start()
        deal_columns("encoder_reduce", item.keep, dot(hidden[...], branch[:, own_columns], TN))
        butterfly.advance()
        loads["memory"].wait()
        deal("middle", dot(memory[...], grad_pair[...], TN), 0)
        loads["reduce"].wait()
        loads["slope"].wait()
        for start in range(0, hidden_size, step):
            columns = pl.ds(start, step)
            grad_active = dot(branch[...], reduce_w[columns, :], NT)
            inner = slope[:, :, columns].reshape(count, step).astype(F32)
            hidden[:, columns] = (grad_active * inner).astype(BF16)
        for index, device in enumerate([links.other_core] + links.partner):
            pl.semaphore_signal(
                credits.at[index], inc=1, device_id=device, device_id_type=pl.DeviceIdType.MESH
            )
        work["encoder_reduce"].advance()
        loads["expand"].wait()
        resid[...] += dot(hidden[...], expand_w[...], NT)
        butterfly.advance()

        loads["first"].wait()
        loads["combine"].wait()
        sums = None
        for start in range(0, count, block):
            part = pl.ds(start, block)
            grad = resid[part, :]
            rows, scale = normed(residual[part, :])
            fresh = [column_sum(grad * rows), column_sum(grad)]
            sums = fresh if sums is None else [old + new for old, new in zip(sums, fresh)]
            total = normed_back(grad, gain_ref[0:1, :], rows, scale)
            resid[part, :] = total
            low_grad = total.astype(BF16)
            branch[part, :] = low_grad
            grad_mixed[part, :] = dot(low_grad, combine_w[...], NT).astype(BF16)
        tiny_levels[0] = tiny_ref[...]
        tiny_levels[0, 4:8, :] = jnp.concatenate([sums[0], last_sums[0], sums[1], last_sums[1]], axis=0)
        tiny_butterfly.start()
        loads["low"].wait()
        for start in range(0, hidden_size, step):
            deal("encoder_expand", dot(low[...], hidden[:, pl.ds(start, step)], TN), start)
        work["encoder_expand"].start()
        loads["mixed"].wait()
        loads["cross"].wait()
        deal("middle", cross[...].astype(F32), 2 * width)
        deal("middle", dot(mixed[...], branch[...], NN), 3 * width)
        work["middle"].start()

    pl.run_scoped(
        rows_phase,
        pltpu.VMEM((count, 2 * width), BF16),
        pltpu.VMEM((width, 2 * width), BF16),
        pltpu.VMEM((count, width), F32),
        pltpu.VMEM((count, width), BF16),
        pltpu.VMEM((hidden_size, width), BF16),
        pltpu.VMEM((width, hidden_size), BF16),
        pltpu.VMEM((count, width), BF16),
        pltpu.VMEM((width, width), BF16),
        pltpu.VMEM((width, width), BF16),
    )

    def attend_phase(packed, logs, x, project_w, grad_packed, grad_x):
        loads = {
            name: load(name, target)
            for name, target in (("packed", packed), ("logs", logs), ("x", x), ("project", project_w))
        }
        work["encoder_expand"].advance()
        work["middle"].advance()
        tiny_butterfly.advance()
        loads["packed"].wait()
        loads["logs"].wait()
        schedule = {
            0: ["decoder_reduce", "butterfly", "tiny"],
            1: ["decoder_expand", "encoder_reduce", "butterfly", "tiny"],
            2: ["decoder_reduce", "middle", "butterfly", "tiny"],
            3: ["decoder_expand", "encoder_expand", "encoder_reduce", "tiny"],
        }
        for pair in range(width // LANES):
            columns = pl.ds(pair * LANES, LANES)
            attend_back_pair(
                packed[:, columns],
                packed[:, pl.ds(width + pair * LANES, LANES)],
                packed[:, pl.ds(2 * width + pair * LANES, LANES)],
                grad_mixed[:, columns],
                mixed[columns, :],
                logs[pair],
                grad_packed, columns,
            )
            for name in schedule[pair]:
                {"butterfly": butterfly, "tiny": tiny_butterfly, **work}[name].advance()
        loads["x"].wait()
        loads["project"].wait()
        grad_x_half = count // 2
        stores = []
        for index in range(2):
            part = pl.ds(index * grad_x_half, grad_x_half)
            total = resid[part, :]
            for third in range(3):
                total = total + dot(
                    grad_packed[third, part, :], project_w[:, third * width : (third + 1) * width], NT
                )
            grad_x[part, :] = total.astype(BF16)
        store = pltpu.make_async_copy(grad_x, grad_x_out, store_sems.at[1])
        store.start()
        for third in range(3):
            deal("last", dot(x[...], grad_packed[third], TN), third * width)
        work["last"].start()
        store.wait()

        @pl.when(links.section == 1)
        def _():
            front_copy.start()

    pl.run_scoped(
        attend_phase,
        pltpu.VMEM((count, 3 * width), BF16),
        pltpu.VMEM(source["logs"].shape, F32),
        pltpu.VMEM((count, width), BF16),
        pltpu.VMEM((width, 3 * width), BF16),
        pltpu.VMEM((3, count, width), BF16),
        pltpu.VMEM((count, width), BF16),
    )

    turns = ["last"] + list(NAMES[:5])
    for _ in range(STAGES + 1):
        for name in turns:
            if work[name].step <= STAGES:
                work[name].advance()
        for item in (butterfly, tiny_butterfly):
            if item.step < 5:
                item.advance()
    small_out[...] = small_levels[5]
    tiny_out[...] = tiny_levels[5]
    memory_copy.wait_recv()
    back_copy.wait_recv()
    for index, name in enumerate(IN_NAMES[:4]):
        links.copy(
            acts[name].at[pl.ds(0, PAD_ROWS)], acts[name].at[pl.ds(PAD_ROWS, PAD_ROWS)],
            (send_sems.at[9, index], recv_sems.at[9, index]), links.other_core,
        ).wait_send()
    for item in list(work.values()) + [butterfly, tiny_butterfly]:
        item.close()
    memory_copy.wait_send()
    back_copy.wait_send()


def attend_back_pair(queries, keys, values, grads, mixed, logs, out, columns):
    count = queries.shape[0]
    lane = lax.broadcasted_iota(jnp.int32, (1, LANES), 1)
    queries = queries * jnp.asarray(0.125, BF16)
    scaled_keys = keys * jnp.asarray(0.125, BF16)
    queries_t = queries.T
    grads_t = grads.T
    logs = logs.T
    shared = mixed.astype(F32) * grads_t.astype(F32)
    inner = jnp.concatenate([column_sum(shared[:64]), column_sum(shared[64:])], axis=0).T
    dq_parts = [[], []]
    dk_parts = []
    dv_parts = []
    for head in range(2):
        own = (lane < 64) if head == 0 else (lane >= 64)
        head_queries = jnp.where(own, queries, jnp.zeros_like(queries))
        head_grads = jnp.where(own, grads, jnp.zeros_like(grads))
        dk = None
        dv = None
        for start in range(0, count, ATTEND_BLOCK):
            part = slice(start, start + ATTEND_BLOCK)
            scores = dot(head_queries[part], keys, NT)
            probs = jnp.exp(scores - logs[part, head : head + 1])
            grad_probs = dot(head_grads[part], values, NT)
            grad_scores = (probs * (grad_probs - inner[part, head : head + 1])).astype(BF16)
            new_v = dot(grads_t[64 * head : 64 * head + 64, part], probs.astype(BF16), NN)
            new_k = dot(queries_t[64 * head : 64 * head + 64, part], grad_scores, NN)
            dv = new_v if dv is None else dv + new_v
            dk = new_k if dk is None else dk + new_k
            dq_parts[head].append(dot(grad_scores, scaled_keys, NN))
        dk_parts.append(dk)
        dv_parts.append(dv)
    out[1, :, columns] = jnp.concatenate(dk_parts, axis=0).T.astype(BF16)
    out[2, :, columns] = jnp.concatenate(dv_parts, axis=0).T.astype(BF16)
    for index in range(count // ATTEND_BLOCK):
        out[0, pl.ds(index * ATTEND_BLOCK, ATTEND_BLOCK), columns] = jnp.where(
            lane < 64, dq_parts[0][index], dq_parts[1][index]
        ).astype(BF16)


def backward_linked(saved, weights, small, tiny):
    count, width = saved["x"].shape
    hidden_size = saved["active"].shape[1]
    arrays = dict(saved)
    arrays.update(
        cross_memory=weights[10], reduce=weights[3], expand=weights[2], combine=weights[1], project=weights[0],
        slope=saved["slope"].reshape(count // 16, 16, hidden_size),
    )
    inputs = [arrays[name] for name in IN_NAMES]
    row_block = lambda columns: (16, columns)
    blocks = {
        "decoder_expand": (16, hidden_size), "decoder_reduce": (hidden_size // 16, width // 2),
        "encoder_reduce": (hidden_size // 16, width // 2), "encoder_expand": (16, hidden_size),
        "middle": (16, 4 * width), "last": (16, 3 * width),
    }
    vmem = lambda counts, name: [pltpu.VMEM((n,) + blocks[name], BF16) for n in counts]
    scratch = [pltpu.VMEM((2 * PAD_ROWS, arrays[name].shape[1]), BF16) for name in IN_NAMES[:4]]
    scratch += vmem((8, 4, 2, 1), "decoder_expand") + vmem((8, 4, 2, 1), "decoder_reduce")
    for name in ("encoder_reduce", "middle", "last"):
        scratch += vmem((16, 16, 8, 4, 2, 1), name)
    for name in ("decoder_expand", "decoder_reduce", "encoder_reduce", "middle", "last"):
        scratch += vmem((16,), name)
    scratch += [
        pltpu.VMEM((count, hidden_size), BF16),
        pltpu.VMEM((count // 16, 16, hidden_size), BF16),
        pltpu.VMEM((count, width), BF16),
        pltpu.VMEM((count, width), F32),
        pltpu.VMEM((width, count), BF16),
        pltpu.VMEM((count, width), BF16),
        pltpu.VMEM((6,) + small.shape, BF16),
        pltpu.VMEM((5,) + small.shape, BF16),
        pltpu.VMEM((6,) + tiny.shape, F32),
        pltpu.VMEM((5,) + tiny.shape, F32),
        pltpu.SemaphoreType.DMA((10, STAGES + 1)),
        pltpu.SemaphoreType.DMA((10, STAGES + 1)),
        pltpu.SemaphoreType.DMA((len(IN_NAMES),)),
        pltpu.SemaphoreType.DMA((2,)),
        pltpu.SemaphoreType.REGULAR((STAGES,)),
    ]
    in_any = pl.BlockSpec(memory_space=pl.ANY)
    in_vmem = pl.BlockSpec(memory_space=pltpu.VMEM)
    shape = shape_of((count, width), BF16)
    results = pl.pallas_call(
        backward_kernel,
        in_specs=[in_any] * len(IN_NAMES) + [in_vmem] * 3,
        out_specs=[in_vmem] * 6 + [in_any] * 4 + [in_vmem] * 2,
        out_shape=[shape_of((2,) + blocks[name], BF16) for name in NAMES]
        + [shape] * 4 + [shape_of(small.shape, BF16), shape_of(tiny.shape, F32)],
        scratch_shapes=scratch,
        compiler_params=pltpu.CompilerParams(
            collective_id=0, has_side_effects=True, vmem_limit_bytes=LINKED_VMEM_BYTES
        ),
        cost_estimate=pl.CostEstimate(flops=10**8, bytes_accessed=10**8, transcendentals=0),
    )(*inputs, weights[4], small, tiny)
    return dict(zip(NAMES, results[:6])), *results[6:]


def swap(value, axis, bit):
    pairs = [(i, i ^ (1 << bit)) for i in range(lax.axis_size(axis))]
    return lax.ppermute(value, axis, pairs)


def plain_scatter(full):
    part = lax.psum_scatter(full.astype(F32), ("section", "dp"), scatter_dimension=0, tiled=True)
    return lax.psum(part, "rep")


def pack_small(saved):
    rows = SMALL_ROWS // 2
    small = jnp.concatenate([saved["resid_d"][:rows], saved["query_d"][:rows]])
    tiny = jnp.concatenate([saved["sums_d"][:4], jnp.zeros_like(saved["sums_d"][:4]), saved["head"].T])
    return small, jnp.pad(tiny, ((0, TINY_ROWS - tiny.shape[0]), (0, 0)))


def per_device(x, targets, arms, *weights):
    section = lax.axis_index("section")
    sections = lax.axis_size("section")
    lanes = lax.axis_size("dp")
    count = x.shape[0] // sections
    starts, head = weights[6], weights[16]
    valid, joints = starts.shape[0], head.shape[1]
    width = starts.shape[1]
    first = section == 0
    place = section * lanes + lax.axis_index("dp")
    own = width // (sections * lanes)
    saved = []
    for index in range(count):
        spot = section * count + index
        pick = lambda array: lax.dynamic_index_in_dim(array, spot, 0, keepdims=False)
        saved.append(forward(pick(x), pick(targets), lax.dynamic_slice(arms, (spot,), (1,)), weights))
    memory = jnp.concatenate([item["memory"][None] for item in saved])
    done = {}
    if (sections, lanes, lax.axis_size("rep"), count) == (2, 8, 2, 1):
        small, tiny = pack_small(saved[0])
        halves, other, other_slab, grad_memory, grad_x, small, tiny = backward_linked(
            saved[0], weights, small.astype(BF16), tiny
        )
        other, other_slab, grad_memory, grad_x = (item[None] for item in (other, other_slab, grad_memory, grad_x))
        for name in NAMES:
            done[name] = jnp.concatenate(
                [halves[name][0], halves[name][1]], axis=1 if name in COLUMN_GROUPS else 0
            ).astype(F32)
    else:
        results = [backward_alone(item, weights) for item in saved]
        grad_x = jnp.concatenate([item[0][None] for item in results])
        grad_memory = jnp.concatenate([item[1][None] for item in results])
        total = lambda name: functools.reduce(jnp.add, [item[2][name] for item in results])
        other = swap(memory, "section", 0)
        other_slab = swap(jnp.where(first, grad_memory, grad_x), "section", 0)
        small, tiny = pack_small({name: total(name) for name in ("resid_d", "query_d", "sums_d")} | {"head": total("head").T})
        tiny = tiny.at[4:8].set(total("sums_e"))
        small = lax.psum(small, ("section", "dp", "rep"))
        tiny = lax.psum(tiny, ("section", "dp", "rep"))
        for name in NAMES:
            done[name] = plain_scatter(total(name))
    memory_out = jnp.concatenate([jnp.where(first, memory, other), jnp.where(first, other, memory)])
    slab = jnp.concatenate(
        [jnp.where(first, grad_x, other_slab), jnp.where(first, other_slab, grad_memory)]
    )[None]

    columns_of = lambda array: lax.dynamic_slice_in_dim(array, place * own, own, 1)
    rows_of = lambda array: lax.dynamic_slice_in_dim(array, place * own, own, 0)
    rest = PAD_ROWS - SMALL_ROWS // 2
    resid_d = jnp.pad(small[: SMALL_ROWS // 2].astype(F32), ((0, rest), (0, 0)))
    query_d = jnp.pad(small[SMALL_ROWS // 2 :].astype(F32), ((0, rest), (0, 0)))
    start_grad, project_d, combine_d, query_w, sums_s = decode_start_back(
        valid, jnp.pad(starts, ((0, PAD_ROWS - valid), (0, 0))), weights[7], weights[8], weights[9],
        weights[14], weights[15], resid_d, query_d,
    )
    gains_d = jnp.concatenate([sums_s[0:1], tiny[0:2]])
    shifts_d = jnp.concatenate([sums_s[1:2], tiny[2:4]])
    return (
        memory_out,
        slab,
        done["last"],
        done["middle"][:, 3 * width :],
        done["encoder_expand"],
        done["encoder_reduce"],
        columns_of(tiny[4:6]),
        columns_of(tiny[6:8]),
        columns_of(start_grad[:valid]),
        rows_of(project_d),
        rows_of(combine_d),
        rows_of(query_w),
        done["middle"][:, : 2 * width],
        done["middle"][:, 2 * width : 3 * width],
        done["decoder_expand"],
        done["decoder_reduce"],
        columns_of(gains_d),
        columns_of(shifts_d),
        rows_of(tiny[8 : 8 + joints].T),
    )


def solution(mesh):
    spread = ("section", "dp")
    rows = P(spread, None)
    columns = P(None, spread)
    return jax.shard_map(
        per_device,
        mesh=mesh,
        in_specs=(P(("dp", "rep"), None, None), P(("dp", "rep"), None, None), P(("dp", "rep"))) + (P(),) * 17,
        out_specs=(
            P(("dp", "rep"), None, None),
            P("section", ("dp", "rep"), None, None),
            rows, rows, rows, rows, columns, columns, columns,
            rows, rows, rows, rows, rows, rows, rows, columns, columns, rows,
        ),
        check_vma=False,
    )
```

```python
import functools

import jax
import jax.numpy as jnp
from jax import lax
from jax.experimental import pallas as pl
from jax.experimental.pallas import tpu as pltpu
from jax.sharding import PartitionSpec as P

HEADS = 8
EPSILON = 1e-05
LANES = 128
PAD_ROWS = 112
F32 = jnp.float32
BF16 = jnp.bfloat16
NN = (((1,), (0,)), ((), ()))
NT = (((1,), (1,)), ((), ()))
TN = (((0,), (0,)), ((), ()))
VMEM_BYTES = 56 * 1024 * 1024
LINKED_VMEM_BYTES = 638 * 1024 * 1024 // 10
ROOT_2_PI = 0.7978845608028654
CUBE = 0.044715


def dot(left, right, dims):
    return lax.dot_general(left, right, dims, preferred_element_type=F32)


def call(kernel, flops, moved, **options):
    return pl.pallas_call(
        kernel,
        compiler_params=pltpu.CompilerParams(vmem_limit_bytes=VMEM_BYTES),
        cost_estimate=pl.CostEstimate(flops=flops, bytes_accessed=moved, transcendentals=0),
        **options,
    )


def shape_of(dims, dtype):
    return jax.ShapeDtypeStruct(dims, dtype)


def whole(array):
    rank = len(array.shape)
    return pl.BlockSpec(array.shape, lambda *_: (0,) * rank, pipeline_mode=pl.Buffered(1))


def normed(residual):
    centre = jnp.mean(residual, axis=-1, keepdims=True)
    centred = residual - centre
    spread = jnp.mean(centred * centred, axis=-1, keepdims=True)
    scale = lax.rsqrt(spread + EPSILON)
    return centred * scale, scale


def normed_back(grad, gain, rows, scale):
    weighted = grad * gain
    return scale * (
        weighted
        - jnp.mean(weighted, axis=-1, keepdims=True)
        - rows * jnp.mean(weighted * rows, axis=-1, keepdims=True)
    )


def gelu_and_slope(value):
    square = value * value
    bend = jnp.tanh(value * (ROOT_2_PI + (ROOT_2_PI * CUBE) * square))
    half = 0.5 + 0.5 * bend
    slope = half + value * (0.5 - 0.5 * bend * bend) * (
        ROOT_2_PI + (3.0 * ROOT_2_PI * CUBE) * square
    )
    return value * half, slope


def column_sum(value):
    return jnp.sum(value, axis=0, keepdims=True)


def attend_kernel(q_ref, k_ref, v_ref, mixed_ref, log_ref):
    count = q_ref.shape[0]
    lane = lax.broadcasted_iota(jnp.int32, (1, LANES), 1)
    keys = k_ref[...]
    values = v_ref[...].T
    queries = q_ref[...] * jnp.asarray(0.125, BF16)
    for head in range(2):
        own = (lane < 64) if head == 0 else (lane >= 64)
        head_keys = jnp.where(own, keys, jnp.zeros_like(keys))
        extended = jnp.concatenate(
            [values[64 * head : 64 * head + 64], jnp.ones((16, count), BF16)], axis=0
        )
        scores = dot(head_keys, queries, NT)
        largest = jnp.max(scores, axis=0, keepdims=True)
        raised = jnp.exp(scores - largest).astype(BF16)
        mixed = dot(extended, raised, NN)
        total = mixed[64:65]
        mixed_ref[pl.ds(64 * head, 64), :] = (mixed[:64] * (1.0 / total)).astype(BF16)
        log_ref[0, pl.ds(head, 1), :] = largest + jnp.log(total)


def attend(packed):
    rows, width = packed.shape[0], packed.shape[1] // 3
    pairs = width // LANES
    column = lambda first: pl.BlockSpec((rows, LANES), lambda j: (0, first + j))
    return call(
        attend_kernel,
        4 * rows * rows * width * 4,
        rows * width * 8,
        grid=(pairs,),
        in_specs=[column(0), column(pairs), column(2 * pairs)],
        out_specs=[
            pl.BlockSpec((LANES, rows), lambda j: (j, 0)),
            pl.BlockSpec((1, 2, rows), lambda j: (j, 0, 0)),
        ],
        out_shape=[shape_of((width, rows), BF16), shape_of((pairs, 2, rows), F32)],
    )(packed, packed, packed)


def attend_back_kernel(block, q_ref, k_ref, v_ref, do_ref, mixed_ref, log_ref, dq_ref, dk_ref, dv_ref):
    count = q_ref.shape[0]
    lane = lax.broadcasted_iota(jnp.int32, (1, LANES), 1)
    keys = k_ref[...]
    values = v_ref[...]
    queries = q_ref[...] * jnp.asarray(0.125, BF16)
    scaled_keys = keys * jnp.asarray(0.125, BF16)
    grads = do_ref[...]
    queries_t = queries.T
    grads_t = grads.T
    logs = log_ref[0].T
    shared = mixed_ref[...].astype(F32) * grads_t.astype(F32)
    inner = jnp.concatenate([column_sum(shared[:64]), column_sum(shared[64:])], axis=0).T
    dq_parts = [[], []]
    dk_parts = []
    dv_parts = []
    for head in range(2):
        own = (lane < 64) if head == 0 else (lane >= 64)
        head_queries = jnp.where(own, queries, jnp.zeros_like(queries))
        head_grads = jnp.where(own, grads, jnp.zeros_like(grads))
        dk = None
        dv = None
        for start in range(0, count, block):
            part = slice(start, start + block)
            scores = dot(head_queries[part], keys, NT)
            probs = jnp.exp(scores - logs[part, head : head + 1])
            grad_probs = dot(head_grads[part], values, NT)
            grad_scores = (probs * (grad_probs - inner[part, head : head + 1])).astype(BF16)
            new_v = dot(grads_t[64 * head : 64 * head + 64, part], probs.astype(BF16), NN)
            new_k = dot(queries_t[64 * head : 64 * head + 64, part], grad_scores, NN)
            dv = new_v if dv is None else dv + new_v
            dk = new_k if dk is None else dk + new_k
            dq_parts[head].append(dot(grad_scores, scaled_keys, NN))
        dk_parts.append(dk)
        dv_parts.append(dv)
    dk_ref[...] = jnp.concatenate(dk_parts, axis=0).T.astype(BF16)
    dv_ref[...] = jnp.concatenate(dv_parts, axis=0).T.astype(BF16)
    for index in range(count // block):
        dq_ref[pl.ds(index * block, block), :] = jnp.where(
            lane < 64, dq_parts[0][index], dq_parts[1][index]
        ).astype(BF16)


def attend_back(packed, grad_mixed, mixed, logs):
    rows, width = packed.shape[0], packed.shape[1] // 3
    pairs = width // LANES
    column = lambda first: pl.BlockSpec((rows, LANES), lambda j: (0, first + j))
    return call(
        functools.partial(attend_back_kernel, 256),
        10 * rows * rows * width * 3,
        rows * width * 16,
        grid=(pairs,),
        in_specs=[
            column(0),
            column(pairs),
            column(2 * pairs),
            column(0),
            pl.BlockSpec((LANES, rows), lambda j: (j, 0)),
            pl.BlockSpec((1, 2, rows), lambda j: (j, 0, 0)),
        ],
        out_specs=[column(0)] * 3,
        out_shape=[shape_of((rows, width), BF16)] * 3,
    )(packed, packed, packed, grad_mixed, mixed, logs)


def encode_rows_kernel(
    x_ref, mixed_ref, combine_ref, expand_ref, reduce_ref, gain_ref, shift_ref, memory_w_ref,
    first_ref, low_ref, active_ref, slope_ref, second_ref, memory_ref, pair_ref,
):
    residual = x_ref[...].astype(F32) + dot(mixed_ref[...], combine_ref[...], TN)
    first_ref[...] = residual
    rows, _ = normed(residual)
    first = rows * gain_ref[0:1, :] + shift_ref[0:1, :]
    low = first.astype(BF16)
    low_ref[...] = low
    total = first
    hidden_size = expand_ref.shape[1]
    step = hidden_size // 5
    for start in range(0, hidden_size, step):
        part = pl.ds(start, step)
        active, slope = gelu_and_slope(dot(low, expand_ref[:, part], NN))
        active = active.astype(BF16)
        active_ref[:, part] = active
        slope_ref[:, part] = slope.astype(BF16)
        total = total + dot(active, reduce_ref[part, :], NN)
    second_ref[...] = total
    rows, _ = normed(total)
    memory = (rows * gain_ref[1:2, :] + shift_ref[1:2, :]).astype(BF16)
    memory_ref[...] = memory
    pair_ref[...] = dot(memory, memory_w_ref[...], NN).astype(BF16)


def encode_rows(x, mixed, combine_w, expand_w, reduce_w, gains, shifts, memory_w):
    rows, width = x.shape
    hidden = expand_w.shape[1]
    block = 256
    line = lambda size: pl.BlockSpec((block, size), lambda i: (i, 0))
    sizes = [(width, F32), (width, BF16), (hidden, BF16), (hidden, BF16), (width, F32), (width, BF16), (2 * width, BF16)]
    return call(
        encode_rows_kernel,
        2 * rows * width * (2 * hidden + 3 * width),
        rows * (hidden * 4 + width * 18) + 8 * width * hidden,
        grid=(rows // block,),
        in_specs=[line(width), pl.BlockSpec((width, block), lambda i: (0, i))]
        + [whole(item) for item in (combine_w, expand_w, reduce_w, gains, shifts, memory_w)],
        out_specs=[line(size) for size, _ in sizes],
        out_shape=[shape_of((rows, size), kind) for size, kind in sizes],
    )(x, mixed, combine_w, expand_w, reduce_w, gains, shifts, memory_w)


def encode_back_kernel(
    pair_ref, first_ref, second_ref, slope_ref, combine_ref, expand_ref, reduce_ref, gain_ref, memory_w_ref,
    grad_memory_ref, branch_ref, hidden_ref, resid_ref, low_ref, mixed_ref, sums_ref,
):
    grad_memory = dot(pair_ref[...], memory_w_ref[...], NT).astype(BF16)
    grad_memory_ref[...] = grad_memory
    grad_last = grad_memory.astype(F32)
    rows, scale = normed(second_ref[...])
    gain_last = column_sum(grad_last * rows)
    shift_last = column_sum(grad_last)
    grad_second = normed_back(grad_last, gain_ref[1:2, :], rows, scale)
    branch = grad_second.astype(BF16)
    branch_ref[...] = branch
    total = grad_second
    hidden_size = expand_ref.shape[1]
    step = hidden_size // 5
    for start in range(0, hidden_size, step):
        part = pl.ds(start, step)
        grad_active = dot(branch, reduce_ref[part, :], NT)
        grad_hidden = (grad_active * slope_ref[:, part].astype(F32)).astype(BF16)
        hidden_ref[:, part] = grad_hidden
        total = total + dot(grad_hidden, expand_ref[:, part], NT)
    rows, scale = normed(first_ref[...])
    gain_first = column_sum(total * rows)
    shift_first = column_sum(total)
    grad_first = normed_back(total, gain_ref[0:1, :], rows, scale)
    resid_ref[...] = grad_first
    low = grad_first.astype(BF16)
    low_ref[...] = low
    mixed_ref[...] = dot(low, combine_ref[...], NT).astype(BF16)
    fresh = jnp.concatenate(
        [gain_first, gain_last, shift_first, shift_last, jnp.zeros((4, gain_first.shape[1]), F32)], axis=0
    )

    @pl.when(pl.program_id(0) == 0)
    def _():
        sums_ref[...] = fresh

    @pl.when(pl.program_id(0) > 0)
    def _():
        sums_ref[...] += fresh


def encode_back(grad_pair, first, second, slope, combine_w, expand_w, reduce_w, gains, memory_w):
    rows, width = first.shape
    hidden = expand_w.shape[1]
    block = 256
    line = lambda size: pl.BlockSpec((block, size), lambda i: (i, 0))
    sizes = [(width, BF16), (width, BF16), (hidden, BF16), (width, F32), (width, BF16), (width, BF16)]
    return call(
        encode_back_kernel,
        2 * rows * width * (2 * hidden + 3 * width),
        rows * (hidden * 4 + width * 18) + 8 * width * hidden,
        grid=(rows // block,),
        in_specs=[line(2 * width), line(width), line(width), line(hidden)]
        + [whole(item) for item in (combine_w, expand_w, reduce_w, gains, memory_w)],
        out_specs=[line(size) for size, _ in sizes] + [pl.BlockSpec((8, width), lambda i: (0, 0))],
        out_shape=[shape_of((rows, size), kind) for size, kind in sizes] + [shape_of((8, width), F32)],
    )(grad_pair, first, second, slope, combine_w, expand_w, reduce_w, gains, memory_w)


def stacked(rows):
    lane = lax.broadcasted_iota(jnp.int32, (1, rows.shape[1]), 1)
    return jnp.concatenate(
        [jnp.where((lane >= 64 * h) & (lane < 64 * h + 64), rows, jnp.zeros_like(rows)) for h in range(4)],
        axis=0,
    )


def unstacked(rows):
    lane = lax.broadcasted_iota(jnp.int32, (1, rows.shape[1]), 1)
    count = rows.shape[0] // 4
    result = rows[:count]
    for h in range(1, 4):
        result = jnp.where(lane >= 64 * h, rows[h * count : h * count + count], result)
    return result


def few_attend(queries, keys, values, valid):
    mixed = []
    kept = []
    for half in range(2):
        part = slice(256 * half, 256 * half + 256)
        scores = dot(stacked(queries[:, part] * jnp.asarray(0.125, BF16)), keys[:, part], NT)
        if valid < scores.shape[1]:
            column = lax.broadcasted_iota(jnp.int32, (1, scores.shape[1]), 1)
            scores = jnp.where(column < valid, scores, -1e30)
        raised = jnp.exp(scores - jnp.max(scores, axis=1, keepdims=True))
        probs = raised * (1.0 / jnp.sum(raised, axis=1, keepdims=True))
        mixed.append(unstacked(dot(probs.astype(BF16), values[:, part], NN)))
        kept.append(probs)
    return jnp.concatenate(mixed, axis=1).astype(BF16), kept


def few_attend_back(queries, keys, values, kept, grads):
    dq, dk, dv = [], [], []
    for half in range(2):
        part = slice(256 * half, 256 * half + 256)
        probs = kept[half]
        own_queries = stacked(queries[:, part] * jnp.asarray(0.125, BF16))
        own_grads = stacked(grads[:, part])
        grad_probs = dot(own_grads, values[:, part], NT)
        product = probs * grad_probs
        grad_scores = (product - probs * jnp.sum(product, axis=1, keepdims=True)).astype(BF16)
        dv.append(dot(probs.astype(BF16), own_grads, TN))
        dk.append(dot(grad_scores, own_queries, TN))
        dq.append(unstacked(dot(grad_scores, keys[:, part], NN)) * 0.125)
    return jnp.concatenate(dq, axis=1), jnp.concatenate(dk, axis=1), jnp.concatenate(dv, axis=1)


def self_block(starts, project_w, combine_w, gain, shift, valid):
    width = starts.shape[1]
    packed = dot(starts, project_w, NN).astype(BF16)
    queries, keys, values = (packed[:, i * width : (i + 1) * width] for i in range(3))
    mixed, kept = few_attend(queries, keys, values, valid)
    residual = starts.astype(F32) + dot(mixed, combine_w, NN)
    rows, scale = normed(residual)
    return queries, keys, values, mixed, kept, rows, scale, rows * gain + shift


def dealt(rows):
    width = rows.shape[1]
    source = lax.broadcasted_iota(jnp.int32, (width, width), 0)
    target = lax.broadcasted_iota(jnp.int32, (width, width), 1)
    half = width // 2
    wanted = (target % half) // 16 * 32 + target // half * 16 + target % 16
    return dot(rows, jnp.where(source == wanted, 1.0, 0.0).astype(BF16), NN).astype(BF16)


def undealt(columns):
    count, width = columns.shape
    return columns.reshape(count, 2, width // 32, 16).transpose(0, 2, 1, 3).reshape(count, width)


def decode_kernel(
    valid, joints,
    starts_ref, project_ref, combine_ref, query_ref, cross_ref, expand_ref, reduce_ref, gain_ref, shift_ref,
    head_ref, pair_ref, target_ref, arm_ref,
    grad_pair_ref, second_low_ref, hidden_ref, active_ref, branch_ref, cross_grad_ref, small_ref, query_grad_ref,
    head_grad_ref, sums_ref,
):
    width = starts_ref.shape[1]
    first = self_block(
        starts_ref[...], project_ref[...], combine_ref[...], gain_ref[0:1, :], shift_ref[0:1, :], valid
    )[-1]
    queries = dot(first.astype(BF16), query_ref[...], NN).astype(BF16)
    keys = pair_ref[:, :width]
    values = pair_ref[:, width:]
    mixed, kept = few_attend(queries, keys, values, keys.shape[0])
    second_rows, second_scale = normed(first + dot(mixed, cross_ref[...], NN))
    second = second_rows * gain_ref[1:2, :] + shift_ref[1:2, :]
    second_low = second.astype(BF16)
    second_low_ref[...] = dealt(second_low)
    hidden_size = expand_ref.shape[1]
    step = hidden_size // 5
    total = second
    slopes = []
    for start in range(0, hidden_size, step):
        part = pl.ds(start, step)
        active, slope = gelu_and_slope(dot(second_low, expand_ref[:, part], NN))
        slopes.append(slope)
        active = active.astype(BF16)
        active_ref[:, part] = active
        total = total + dot(active, reduce_ref[part, :], NN)
    third_rows, third_scale = normed(total)
    third_low = (third_rows * gain_ref[2:3, :] + shift_ref[2:3, :]).astype(BF16)
    misfit = dot(third_low, head_ref[...], NN) - target_ref[...]
    arms = arm_ref[0]
    row = lax.broadcasted_iota(jnp.int32, misfit.shape, 0)
    joint = lax.broadcasted_iota(jnp.int32, misfit.shape, 1)
    factor = 2.0 / jnp.full((1, 1), arms, jnp.int32).astype(F32)
    used = (row < valid) & (joint < joints // 2 * arms)
    grad_pred = jnp.where(used, factor * misfit * lax.rsqrt(misfit * misfit + 1.0), 0.0).astype(BF16)
    head_grad_ref[...] = dot(third_low, grad_pred, TN)
    grad_third = dot(grad_pred, head_ref[...], NT)
    gain_third = column_sum(grad_third * third_rows)
    shift_third = column_sum(grad_third)
    total = normed_back(grad_third, gain_ref[2:3, :], third_rows, third_scale)
    branch = total.astype(BF16)
    branch_ref[...] = branch
    for index, start in enumerate(range(0, hidden_size, step)):
        part = pl.ds(start, step)
        grad_hidden = (dot(branch, reduce_ref[part, :], NT) * slopes[index]).astype(BF16)
        hidden_ref[:, part] = grad_hidden
        total = total + dot(grad_hidden, expand_ref[:, part], NT)
    gain_second = column_sum(total * second_rows)
    shift_second = column_sum(total)
    grad_second = normed_back(total, gain_ref[1:2, :], second_rows, second_scale)
    small_ref[...] = grad_second
    branch = grad_second.astype(BF16)
    cross_grad_ref[...] = dot(mixed, branch, TN).astype(BF16)
    grad_mixed = dot(branch, cross_ref[...], NT).astype(BF16)
    dq, dk, dv = few_attend_back(queries, keys, values, kept, grad_mixed)
    query_grad_ref[...] = dq.astype(BF16).astype(F32)
    grad_pair_ref[:, :width] = dk.astype(BF16)
    grad_pair_ref[:, width:] = dv.astype(BF16)
    sums_ref[...] = jnp.concatenate(
        [gain_second, gain_third, shift_second, shift_third, jnp.zeros((4, width), F32)], axis=0
    )


def decode(valid, joints, starts, weights, pair, target, arm):
    project_w, combine_w, query_w, cross_w, expand_w, reduce_w, gains, shifts, head_w = weights
    count, width = starts.shape
    hidden = expand_w.shape[1]
    shapes = [
        (pair.shape, BF16),
        ((count, width), BF16),
        ((count, hidden), BF16),
        ((count, hidden), BF16),
        ((count, width), BF16),
        ((width, width), BF16),
        ((count, width), F32),
        ((count, width), F32),
        (head_w.shape, F32),
        ((8, width), F32),
    ]
    arrays = (starts, project_w, combine_w, query_w, cross_w, expand_w, reduce_w, gains, shifts, head_w, pair, target)
    return call(
        functools.partial(decode_kernel, valid, joints),
        8 * count * width * hidden * 4,
        16 * 1024 * 1024,
        in_specs=[pl.BlockSpec(memory_space=pltpu.VMEM)] * len(arrays) + [pl.BlockSpec(memory_space=pltpu.SMEM)],
        out_specs=[pl.BlockSpec(memory_space=pltpu.VMEM)] * len(shapes),
        out_shape=[shape_of(dims, kind) for dims, kind in shapes],
    )(*arrays, arm)


def decode_start_back_kernel(
    valid,
    starts_ref, project_ref, combine_ref, query_ref, gain_ref, shift_ref, resid_ref, query_grad_ref,
    start_grad_ref, project_grad_ref, combine_grad_ref, query_w_grad_ref, sums_ref,
):
    starts = starts_ref[...]
    project_w = project_ref[...]
    queries, keys, values, mixed, kept, rows, scale, first = self_block(
        starts, project_w, combine_ref[...], gain_ref[0:1, :], shift_ref[0:1, :], valid
    )
    low = query_grad_ref[...].astype(BF16)
    query_w_grad_ref[...] = dot(first.astype(BF16), low, TN)
    grad_first = resid_ref[...] + dot(low, query_ref[...], NT)
    gain_sum = column_sum(grad_first * rows)
    shift_sum = column_sum(grad_first)
    grad_resid = normed_back(grad_first, gain_ref[0:1, :], rows, scale)
    branch = grad_resid.astype(BF16)
    combine_grad_ref[...] = dot(mixed, branch, TN)
    grad_mixed = dot(branch, combine_ref[...], NT).astype(BF16)
    dq, dk, dv = few_attend_back(queries, keys, values, kept, grad_mixed)
    grad_packed = jnp.concatenate([dq, dk, dv], axis=1).astype(BF16)
    project_grad_ref[...] = dot(starts, grad_packed, TN)
    start_grad_ref[...] = grad_resid + dot(grad_packed, project_w, NT)
    sums_ref[...] = jnp.concatenate([gain_sum, shift_sum, jnp.zeros((6, gain_sum.shape[1]), F32)], axis=0)


def decode_start_back(valid, starts, project_w, combine_w, query_w, gains, shifts, resid, query_grad):
    count, width = starts.shape
    arrays = (starts, project_w, combine_w, query_w, gains, shifts, resid, query_grad)
    shapes = [(count, width), (width, 3 * width), (width, width), (width, width), (8, width)]
    return call(
        functools.partial(decode_start_back_kernel, valid),
        2 * count * width * width * 20,
        8 * 1024 * 1024,
        in_specs=[pl.BlockSpec(memory_space=pltpu.VMEM)] * len(arrays),
        out_specs=[pl.BlockSpec(memory_space=pltpu.VMEM)] * len(shapes),
        out_shape=[shape_of(dims, F32) for dims in shapes],
    )(*arrays)


def forward(x, target, arm, weights):
    (
        encoder_project, encoder_combine, encoder_expand, encoder_reduce, encoder_gains, encoder_shifts,
        starts, decoder_project, decoder_combine, cross_query, cross_memory, cross_combine,
        decoder_expand, decoder_reduce, decoder_gains, decoder_shifts, head,
    ) = weights
    valid, joints = starts.shape[0], head.shape[1]
    packed = dot(x, encoder_project, NN).astype(BF16)
    mixed, logs = attend(packed)
    first, first_low, active, slope, second, memory, pair = encode_rows(
        x, mixed, encoder_combine, encoder_expand, encoder_reduce, encoder_gains, encoder_shifts, cross_memory
    )
    padded = jnp.pad(starts, ((0, PAD_ROWS - valid), (0, 0)))
    wide_head = jnp.pad(head, ((0, 0), (0, LANES - joints)))
    wide_target = jnp.pad(target, ((0, PAD_ROWS - valid), (0, LANES - joints)))
    (
        grad_pair, second_low, grad_hidden_d, active_d, branch_d, cross_grad, resid_d, query_grad, head_grad, sums_d,
    ) = decode(
        valid, joints, padded,
        (
            decoder_project, decoder_combine, cross_query, cross_combine, decoder_expand, decoder_reduce,
            decoder_gains, decoder_shifts, wide_head,
        ),
        pair, wide_target, arm,
    )
    return {
        "starts": padded, "x": x, "packed": packed, "mixed": mixed, "logs": logs, "first": first, "low": first_low, "active": active,
        "slope": slope, "second": second, "memory": memory, "grad_pair": grad_pair, "low_d": second_low,
        "hidden_d": grad_hidden_d, "active_d": active_d, "branch_d": branch_d, "cross": cross_grad,
        "resid_d": resid_d, "query_d": query_grad, "head": head_grad[:, :joints], "sums_d": sums_d,
    }


def backward_alone(saved, weights):
    (encoder_project, encoder_combine, encoder_expand, encoder_reduce, encoder_gains) = weights[:5]
    cross_memory = weights[10]
    grad_memory, branch, grad_hidden, resid, low, grad_mixed, sums_e = encode_back(
        saved["grad_pair"], saved["first"], saved["second"], saved["slope"],
        encoder_combine, encoder_expand, encoder_reduce, encoder_gains, cross_memory,
    )
    dq, dk, dv = attend_back(saved["packed"], grad_mixed, saved["mixed"], saved["logs"])
    grad_packed = jnp.concatenate([dq, dk, dv], axis=1)
    grad_x = (resid + dot(grad_packed, encoder_project, NT)).astype(BF16)
    plain = lambda left, right: dot(left, right, TN)
    return grad_x, grad_memory, {
        "decoder_expand": plain(undealt(saved["low_d"]), saved["hidden_d"]),
        "decoder_reduce": plain(saved["active_d"], saved["branch_d"]),
        "encoder_reduce": plain(saved["active"], branch),
        "encoder_expand": plain(saved["low"], grad_hidden),
        "middle": jnp.concatenate(
            [plain(saved["memory"], saved["grad_pair"]), saved["cross"].astype(F32), dot(saved["mixed"], low, NN)], axis=1
        ),
        "last": plain(saved["x"], grad_packed),
        "sums_e": sums_e[:4], "sums_d": saved["sums_d"][:4], "head": saved["head"].T,
        "resid_d": saved["resid_d"], "query_d": saved["query_d"],
    }


SECTION, SIDE, LINE = range(3)
GROUPS = {
    "decoder_expand0": (SIDE, SECTION, LINE),
    "decoder_expand1": (SECTION, SIDE, LINE),
    "decoder_reduce0": (SECTION, SIDE, LINE),
    "decoder_reduce1": (SIDE, LINE, SECTION),
    "encoder_reduce0": (SIDE, LINE, SECTION),
    "encoder_reduce1": (SECTION, SIDE, LINE),
    "encoder_expand0": (SECTION, SIDE, LINE),
    "encoder_expand1": (SIDE, LINE, SECTION),
    "middle0": (LINE, SIDE, SECTION),
    "middle1": (LINE, SECTION, SIDE),
    "last0": (SECTION, SIDE, LINE),
    "last1": (SIDE, LINE, SECTION),
}
NAMES = tuple(GROUPS)
SCHEDULE = {
    "dmem": ("small",),
    "efr1": ("small",),
    "dwm": ("encoder_reduce0",),
    "du0": ("encoder_reduce1",),
    "du1": ("decoder_reduce1", "middle0",),
    "du3": ("small", "decoder_reduce0",),
    "df": ("middle0", "decoder_reduce1",),
    "ln": ("decoder_expand0",),
    "efe0": ("small", "tiny",),
    "efe1": ("middle0",),
    "dwc": ("encoder_expand0", "encoder_reduce0", "decoder_reduce1",),
    "att0": ("encoder_expand1", "middle1",),
    "att1": ("decoder_reduce0", "small",),
    "att2": ("middle0",),
    "att3": ("encoder_reduce0",),
    "last0": ("decoder_reduce1",),
    "att4": ("encoder_expand1", "middle1", "decoder_expand1", "last0", "decoder_reduce0",),
    "att5": ("encoder_reduce0", "small",),
    "att6": ("encoder_expand1", "middle0",),
    "att7": ("middle1", "encoder_reduce1", "decoder_expand1", "decoder_reduce0",),
    "dx0": ("encoder_reduce0",),
    "dx1": ("encoder_expand1",),
    "last1": ("decoder_expand0", "tiny",),
}
TAIL_FIRST = ()
TAIL = (
    "last1",
    "encoder_reduce1",
    "middle1",
    "decoder_expand0",
    "decoder_expand1",
    "encoder_expand1",
    "decoder_reduce0",
    "tiny",
    "encoder_reduce1",
    "encoder_expand0",
    "decoder_reduce0",
    "decoder_reduce1",
    "decoder_expand0",
    "decoder_expand1",
    "last1",
    "decoder_reduce1",
    "tiny",
    "encoder_reduce1",
    "last0",
    "decoder_expand0",
    "middle0",
    "decoder_expand1",
    "encoder_reduce0",
    "encoder_expand0",
    "last1",
    "decoder_expand0",
    "middle0",
    "decoder_expand1",
    "tiny",
    "encoder_reduce0",
    "last0",
    "encoder_reduce1",
    "encoder_expand0",
    "tiny",
    "encoder_reduce1",
    "last1",
    "last0",
    "encoder_expand0",
    "middle1",
    "last1",
    "last0",
    "encoder_expand1",
    "encoder_expand0",
    "middle1",
    "last1",
    "encoder_expand1",
    "last0",
    "encoder_expand0",
    "middle1",
    "last1",
    "last0",
)
STEPS = 7
LINE_ROUNDS = 3
SMALL_ROWS = 224
TINY_ROWS = 24


class Links:
    def __init__(self):
        core = lax.axis_index("rep")
        section = lax.axis_index("section")
        lane = lax.axis_index("dp")
        self.core = core
        self.section = section
        self.lane = lane
        self.level = lane // 2
        self.side = lane % 2
        self.mine = [section, self.side]
        self.other_core = {"rep": 1 - core}
        self.partner = [{"section": 1 - section}, {"dp": lane + 1 - 2 * self.side}]
        self.above = {"dp": lane + 2}
        self.below = {"dp": lane - 2}

    def signal(self, semaphore, device):
        pl.semaphore_signal(semaphore, inc=1, device_id=device, device_id_type=pl.DeviceIdType.MESH)

    def tell(self, semaphores):
        for semaphore, device in zip(semaphores[:3], [self.other_core] + self.partner):
            self.signal(semaphore, device)

        @pl.when(self.level > 0)
        def _():
            self.signal(semaphores[3], self.below)

        @pl.when(self.level < 3)
        def _():
            self.signal(semaphores[4], self.above)

    def greet(self):
        barrier = pltpu.get_barrier_semaphore()
        self.tell([barrier] * 5)
        pl.semaphore_wait(barrier, 3 + (self.level + 3) // 4 + (6 - self.level) // 4)

    def copy(self, source, target, sems, device):
        return pltpu.make_async_remote_copy(
            src_ref=source,
            dst_ref=target,
            send_sem=sems[0],
            recv_sem=sems[1],
            device_id=device,
            device_id_type=pl.DeviceIdType.MESH,
        )


def stage_blocks(order):
    counts, size = [], 16
    for dim in order:
        counts.append(5 * size // 4 if dim == LINE else size // 2)
        size = size // 4 if dim == LINE else size // 2
    return counts


class Scatter:
    def __init__(self, links, order, keep, sent, arrived, stages, send_sems, recv_sems, index, out, credits=None):
        self.links, self.order, self.keep, self.out = links, order, keep, out
        self.sent, self.arrived, self.credits = sent, arrived, credits
        self.sems = lambda step, way=0: (send_sems.at[index, step, way], recv_sems.at[index, step, way])
        self.plan = [] if sent is None else [("core",)]
        base, size = 0, 16
        for dim, buffer in zip(order, stages):
            if dim == LINE:
                size //= 4
                self.plan += [("line", turn, base, size, buffer) for turn in (1, 2, 3)]
                base = base + links.level * size
            else:
                size //= 2
                mine = links.mine[dim]
                self.plan.append(("halve", dim, base + (1 - mine) * size, base + mine * size, size, buffer))
                base = base + mine * size
        self.base = base
        self.plan.append(("both",))
        self.step = 0

    def place(self, shard):
        index, size = 0, 16
        for dim in self.order:
            size //= 4 if dim == LINE else 2
            index += size * {SECTION: shard // 8, LINE: shard // 2 % 4, SIDE: shard % 2}[dim]
        return index

    def single(self, step):
        links, kind = self.links, self.plan[step][0]
        if kind == "core":
            return links.copy(self.sent, self.arrived, self.sems(step), links.other_core)
        if kind == "halve":
            _, dim, away, _, size, buffer = self.plan[step]
            return links.copy(self.keep.at[pl.ds(away, size)], buffer, self.sems(step), links.partner[dim])
        return links.copy(self.out.at[links.core], self.out.at[links.core], self.sems(step), links.other_core)

    def lines(self, step):
        links, level = self.links, self.links.level
        _, turn, base, size, buffer = self.plan[step]
        shards = lambda ref, index: ref.at[pl.ds(index * size, size)]
        keep = lambda shard: self.keep.at[pl.ds(base + shard * size, size)]
        up, down = level + 4 - turn, level - 4 + turn
        return [
            (
                (level < turn) & (level < 3),
                lambda: links.copy(keep(up), shards(buffer, turn - level - 1), self.sems(step, 0), links.above),
                (level > 0) & (level <= turn),
                lambda: links.copy(keep(up - 1), shards(buffer, turn - level), self.sems(step, 0), links.above),
                lambda: (base + (up - 1) * size, (turn - level) * size),
                level == turn - 1,
            ),
            (
                (3 - level < turn) & (level > 0),
                lambda: links.copy(keep(down), shards(buffer, turn + 1), self.sems(step, 1), links.below),
                (level < 3) & (3 - level <= turn),
                lambda: links.copy(keep(down + 1), shards(buffer, turn + 1), self.sems(step, 1), links.below),
                lambda: (base + (down + 1) * size, (turn + 1) * size),
                3 - level == turn - 1,
            ),
        ]

    def start(self):
        step = self.step
        plan = self.plan[step]
        if plan[0] == "line":
            for way, (sends, sent, _, _, _, opens) in enumerate(self.lines(step)):

                @pl.when(sends)
                def _():
                    if self.credits is not None:

                        @pl.when(opens)
                        def _():
                            pl.semaphore_wait(self.credits.at[3 + way], 1)

                    sent().start()

            return
        if self.credits is not None and plan[0] != "both":
            pl.semaphore_wait(self.credits.at[0 if plan[0] == "core" else 1 + plan[1]], 1)
        if plan[0] == "both":
            self.out[pl.ds(self.links.core, 1)] = self.keep[pl.ds(self.base, 1)]
        self.single(step).start()

    def add(self, source, first, base, size):
        keep = self.keep

        def body(i, carry):
            keep[base + i] = keep[base + i] + source[first + i]
            return carry

        lax.fori_loop(0, size, body, 0)

    def finish(self):
        step = self.step
        plan = self.plan[step]
        if plan[0] == "line":
            for _, _, comes, arrived, where, _ in self.lines(step):

                @pl.when(comes)
                def _():
                    arrived().wait_recv()
                    base, first = where()
                    self.add(plan[4], first, base, plan[3])

        else:
            self.single(step).wait_recv()
            if plan[0] == "core":
                self.add(self.arrived, 0, 0, 16)
            elif plan[0] == "halve":
                self.add(plan[5], 0, plan[3], plan[4])
        self.step += 1

    def advance(self):
        self.finish()
        if self.step < len(self.plan):
            self.start()

    def close(self):
        for step, plan in enumerate(self.plan):
            if plan[0] == "line":
                for sends, sent, _, _, _, _ in self.lines(step):

                    @pl.when(sends)
                    def _():
                        sent().wait_send()

            else:
                self.single(step).wait_send()


class Total:
    def __init__(self, links, levels, arrived, send_sems, recv_sems, index):
        self.links, self.levels, self.arrived = links, levels, arrived
        level = links.level
        everyone = level >= 0
        near = {"dp": links.lane + 2 - 4 * (level % 2)}
        middle = {"dp": links.lane + 6 - 4 * level}
        inner = (level == 1) | (level == 2)
        outer = {"dp": links.lane - 6 + 4 * level}
        self.turns = [
            (everyone, everyone, links.other_core), (everyone, everyone, links.partner[SECTION]),
            (everyone, everyone, near), (inner, inner, middle), (inner, jnp.logical_not(inner), outer),
            (everyone, everyone, links.partner[SIDE]),
        ]
        self.sems = lambda step: (send_sems.at[index, step, 0], recv_sems.at[index, step, 0])
        self.step = 0
        self.result = levels.at[0]

    def copy_of(self, step):
        return self.links.copy(
            self.levels.at[step % 2], self.arrived.at[step - step // 4], self.sems(step), self.turns[step][2]
        )

    def start(self):
        step = self.step

        @pl.when(self.turns[step][0])
        def _():
            self.copy_of(step).start()

    def sent(self, step):
        @pl.when(self.turns[step][0])
        def _():
            self.copy_of(step).wait_send()

    def advance(self):
        step = self.step
        if step > 0:
            self.sent(step - 1)
        comes = self.turns[step][1]

        @pl.when(comes)
        def _():
            self.copy_of(step).wait_recv()
            value = self.arrived[step - step // 4].astype(F32)
            if step != 4:
                value = self.levels[step % 2].astype(F32) + value
            self.levels[(step + 1) % 2] = value.astype(self.levels.dtype)

        @pl.when(jnp.logical_not(comes))
        def _():
            self.levels[(step + 1) % 2] = self.levels[step % 2]

        self.step += 1
        if self.step < 6:
            self.start()

    def close(self):
        self.sent(5)


IN_NAMES = (
    "low_d", "hidden_d", "active_d", "branch_d", "grad_pair", "cross_memory", "second", "memory", "active",
    "reduce", "slope", "expand", "first", "low", "mixed", "combine", "cross", "packed", "logs", "x", "project",
    "starts", "self_project", "self_combine", "cross_query",
)
ATTEND_BLOCK = 256


def backward_kernel(valid, *refs):
    refs = list(refs)

    def draw(count):
        taken = refs[:count]
        del refs[:count]
        return taken

    source = dict(zip(IN_NAMES, draw(len(IN_NAMES))))
    gain_ref, small_ref, tiny_ref = draw(3)
    self_gain_ref, self_shift_ref = draw(2)
    outs = dict(zip(NAMES, draw(len(NAMES))))
    slab_out, grad_memory_out, grad_x_out, self_rows_out, stack_out = draw(5)
    acts = dict(zip(IN_NAMES[:4], draw(4)))
    buffers = {}
    for name in NAMES:
        if name.startswith("decoder"):
            buffers[name] = [None, None] + draw(3)
        elif not name.startswith("encoder_expand"):
            buffers[name] = draw(5)
    keeps = {}
    for name in NAMES:
        if not name.startswith("encoder_expand"):
            keeps[name] = draw(1)[0]
    expand_stages = [draw(3), draw(3)]
    hidden, slope, grad_mixed, resid, mixed, branch, small_levels, small_arrived, tiny_levels, tiny_arrived = draw(10)
    send_sems, recv_sems, act_sems, slab_sems, load_sems, store_sems, credits = draw(7)
    width = resid.shape[1]
    count = resid.shape[0]
    hidden_size = hidden.shape[1]
    cut = split_of(hidden_size)
    for index, columns in enumerate((pl.ds(0, cut), pl.ds(cut, hidden_size - cut))):
        name = "encoder_expand%d" % index
        rows = lambda start, size: slope.at[pl.ds(start, size), :, columns]
        keeps[name] = rows(0, 16)
        buffers[name] = [rows(16, 16), rows(32, 16)] + expand_stages[index]

    links = Links()
    core = links.core
    block = 256
    chunks = [(0, 896), (896, cut - 896), (cut, 768), (cut + 768, hidden_size - cut - 768)]
    own_columns = pl.ds(pl.multiple_of(core * 256, 256), 256)
    other_columns = pl.ds(pl.multiple_of((1 - core) * 256, 256), 256)
    work = {}
    for index, name in enumerate(NAMES):
        sent, arrived, *stages = buffers[name]
        work[name] = Scatter(
            links, GROUPS[name], keeps[name], sent, arrived, stages, send_sems, recv_sems, index, outs[name],
            credits.at[int(name[-1])] if name.startswith("encoder_expand") else None,
        )
    work["small"] = Total(links, small_levels, small_arrived, send_sems, recv_sems, len(NAMES))
    work["tiny"] = Total(links, tiny_levels, tiny_arrived, send_sems, recv_sems, len(NAMES) + 1)

    def tick(label):
        for name in SCHEDULE.get(label, ()):
            work[name].advance()

    def load(name, target):
        copy = pltpu.make_async_copy(source[name], target, load_sems.at[IN_NAMES.index(name)])
        copy.start()
        return copy

    def deal(name, rows, first_column):
        item = work[name]
        columns = pl.ds(first_column, rows.shape[1])
        low = rows.astype(BF16)
        for shard in range(16):
            here = low[32 * shard : 32 * shard + 16]
            there = low[32 * shard + 16 : 32 * shard + 32]
            place = item.place(shard)
            item.keep[place, :, columns] = jnp.where(core == 0, here, there)
            item.sent[place, :, columns] = jnp.where(core == 0, there, here)

    def deal_columns(names, targets, rows):
        size = rows.shape[0] // 16
        for index, (name, target) in enumerate(zip(names, targets)):
            for shard in range(16):
                target[work[name].place(shard)] = rows[
                    size * shard : size * shard + size, LANES * index : LANES * index + LANES
                ].astype(BF16)

    own_acts = {name: load(name, acts[name].at[pl.ds(0, PAD_ROWS)]) for name in IN_NAMES[:4]}
    links.greet()
    def slab_copies(out):
        parts = [pl.ds(index * (count // 2), count // 2) for index in range(2)]
        return [
            links.copy(
                out.at[part], slab_out.at[part], (slab_sems.at[0, index], slab_sems.at[1, index]), links.partner[SECTION]
            )
            for index, part in enumerate(parts)
        ]

    back_copies = slab_copies(grad_memory_out)
    front_copies = slab_copies(grad_x_out)

    def act_copy(index, name):
        return links.copy(
            acts[name].at[pl.ds(0, PAD_ROWS)], acts[name].at[pl.ds(PAD_ROWS, PAD_ROWS)],
            (act_sems.at[0, index], act_sems.at[1, index]), links.other_core,
        )

    def rows_phase(grad_pair, memory_w, residual, rows_low, reduce_w, expand_w, combine_w):
        loads = {
            name: load(name, target)
            for name, target in (
                ("grad_pair", grad_pair), ("cross_memory", memory_w), ("second", residual), ("active", hidden),
                ("memory", rows_low), ("reduce", reduce_w), ("slope", slope), ("expand", expand_w),
                ("mixed", mixed), ("combine", combine_w),
            )
        }
        for index, name in enumerate(IN_NAMES[:4]):
            own_acts[name].wait()
            act_copy(index, name).start()
        small_levels[0] = small_ref[...]
        work["small"].start()

        loads["grad_pair"].wait()
        loads["cross_memory"].wait()
        loads["second"].wait()
        sums = None
        for start in range(0, count, block):
            part = pl.ds(start, block)
            low_grad = dot(grad_pair[part, :], memory_w[...], NT).astype(BF16)
            grad_mixed[part, :] = low_grad
            grad = low_grad.astype(F32)
            rows, scale = normed(residual[part, :])
            fresh = [column_sum(grad * rows), column_sum(grad)]
            sums = fresh if sums is None else [old + new for old, new in zip(sums, fresh)]
            total = normed_back(grad, gain_ref[1:2, :], rows, scale)
            resid[part, :] = total
            branch[part, :] = total.astype(BF16)
        memory_store = pltpu.make_async_copy(grad_mixed, grad_memory_out, store_sems.at[0])
        memory_store.start()
        loads["first"] = load("first", residual)
        last_sums = sums
        tick("dmem")

        for index, name in enumerate(IN_NAMES[:4]):
            act_copy(index, name).wait_recv()
        names = ("decoder_reduce0", "decoder_reduce1")
        deal_columns(
            names, [work[name].keep for name in names],
            dot(acts["active_d"][...], acts["branch_d"][:, own_columns], TN),
        )
        for name in names:
            work[name].start()
        memory_store.wait()

        @pl.when(links.section == 0)
        def _():
            for copy in back_copies:
                copy.start()

        tick("dfr")
        for index, (start, size) in enumerate(chunks):
            rows = dot(acts["low_d"][:, own_columns], acts["hidden_d"][:, pl.ds(start, size)], TN).astype(BF16)
            item = work["decoder_expand%d" % (index // 2)]
            columns = pl.ds(start - (index // 2) * cut, size)
            for shard in range(16):
                item.keep[item.place(shard), :, columns] = rows[16 * shard : 16 * shard + 16]
            if index % 2:
                item.start()
                tick("dfe%d" % (index // 2))

        loads["active"].wait()
        names = ("encoder_reduce0", "encoder_reduce1")
        deal_columns(names, [work[name].sent for name in names], dot(hidden[...], branch[:, other_columns], TN))
        for name in names:
            work[name].start()
        tick("efr0")
        deal_columns(names, [work[name].keep for name in names], dot(hidden[...], branch[:, own_columns], TN))
        tick("efr1")
        loads["memory"].wait()
        deal("middle0", dot(rows_low[...], grad_pair[...], TN), 0)
        loads["low"] = load("low", rows_low)
        work["middle0"].start()
        tick("dwm")
        loads["reduce"].wait()
        loads["slope"].wait()
        for index, (start, size) in enumerate(chunks):
            columns = pl.ds(start, size)
            grad_active = dot(branch[...], reduce_w[columns, :], NT)
            inner = slope[:, :, columns].reshape(count, size).astype(F32)
            hidden[:, columns] = (grad_active * inner).astype(BF16)
            tick("du%d" % index)
        for half in range(2):
            links.tell([credits.at[half, index] for index in range(5)])
        loads["expand"].wait()
        resid[...] += dot(hidden[...], expand_w[...], NT)
        tick("df")

        loads["first"].wait()
        loads["combine"].wait()
        sums = None
        for start in range(0, count, block):
            part = pl.ds(start, block)
            grad = resid[part, :]
            rows, scale = normed(residual[part, :])
            fresh = [column_sum(grad * rows), column_sum(grad)]
            sums = fresh if sums is None else [old + new for old, new in zip(sums, fresh)]
            total = normed_back(grad, gain_ref[0:1, :], rows, scale)
            resid[part, :] = total
            low_grad = total.astype(BF16)
            branch[part, :] = low_grad
            grad_mixed[part, :] = dot(low_grad, combine_w[...], NT).astype(BF16)
        loads["cross"] = load("cross", combine_w)
        tiny_levels[0] = tiny_ref[...]
        tiny_levels[0, 4:8, :] = jnp.concatenate([sums[0], last_sums[0], sums[1], last_sums[1]], axis=0)
        work["tiny"].start()
        tick("ln")
        loads["low"].wait()
        for index, (start, size) in enumerate(chunks):
            name = "encoder_expand%d" % (index // 2)
            deal(name, dot(rows_low[...], hidden[:, pl.ds(start, size)], TN), start - (index // 2) * cut)
            if index % 2:
                work[name].start()
                tick("efe%d" % (index // 2))
        loads["mixed"].wait()
        loads["cross"].wait()
        deal("middle1", combine_w[...].astype(F32), 0)
        deal("middle1", dot(mixed[...], branch[...], NN), width)
        work["middle1"].start()
        tick("dwc")

    pl.run_scoped(
        rows_phase,
        pltpu.VMEM((count, 2 * width), BF16),
        pltpu.VMEM((width, 2 * width), BF16),
        pltpu.VMEM((count, width), F32),
        pltpu.VMEM((count, width), BF16),
        pltpu.VMEM((hidden_size, width), BF16),
        pltpu.VMEM((width, hidden_size), BF16),
        pltpu.VMEM((width, width), BF16),
    )

    def attend_phase(packed, logs, x, project_w, grad_packed, starts, self_project, self_combine, cross_query):
        loads = {
            name: load(name, target)
            for name, target in (
                ("packed", packed), ("logs", logs), ("x", x), ("project", project_w), ("starts", starts),
                ("self_project", self_project), ("self_combine", self_combine), ("cross_query", cross_query),
            )
        }
        loads["packed"].wait()
        loads["logs"].wait()
        pairs = width // LANES
        half = width // 2

        def last(index):
            columns = slice(index * half, index * half + half)
            for third in range(3):
                deal("last%d" % index, dot(x[...], grad_packed[third, :, columns], TN), third * half)
            work["last%d" % index].start()

        for pair in range(pairs):
            columns = pl.ds(pair * LANES, LANES)
            attend_back_pair(
                packed[:, columns],
                packed[:, pl.ds(width + pair * LANES, LANES)],
                packed[:, pl.ds(2 * width + pair * LANES, LANES)],
                grad_mixed[:, columns],
                mixed[columns, :],
                logs[pair],
                grad_packed, columns,
                lambda head: tick("att%d" % (2 * pair + head)),
            )
            if pair == pairs // 2 - 1:
                loads["x"].wait()
                last(0)
                tick("last0")
        loads["project"].wait()
        stores = []
        for index in range(2):
            part = pl.ds(index * (count // 2), count // 2)
            total = resid[part, :]
            for third in range(3):
                total = total + dot(
                    grad_packed[third, part, :], project_w[:, third * width : (third + 1) * width], NT
                )
            packed[part, pl.ds(0, width)] = total.astype(BF16)
            store = pltpu.make_async_copy(packed.at[part, pl.ds(0, width)], grad_x_out.at[part], store_sems.at[1 + index])
            store.start()
            tick("dx%d" % index)
            store.wait()

            @pl.when(links.section == 1)
            def _():
                front_copies[index].start()

        last(1)
        tick("last1")
        for name in IN_NAMES[-4:]:
            loads[name].wait()
        for name in TAIL_FIRST:
            work[name].advance()
        rows = SMALL_ROWS // 2
        start_back(
            valid, starts[...], self_project[...], self_combine[...], cross_query[...], self_gain_ref[0:1, :],
            self_shift_ref[0:1, :], work["small"].result[pl.ds(0, rows), :].astype(F32),
            work["small"].result[pl.ds(rows, rows), :], links, self_rows_out, stack_out,
        )

    pl.run_scoped(
        attend_phase,
        pltpu.VMEM((count, 3 * width), BF16),
        pltpu.VMEM(source["logs"].shape, F32),
        pltpu.VMEM((count, width), BF16),
        pltpu.VMEM((width, 3 * width), BF16),
        pltpu.VMEM((3, count, width), BF16),
        pltpu.VMEM((PAD_ROWS, width), BF16),
        pltpu.VMEM((width, 3 * width), BF16),
        pltpu.VMEM((width, width), BF16),
        pltpu.VMEM((width, width), BF16),
    )
    for name in TAIL:
        work[name].advance()
    stack_out[pl.ds(SMALL_ROWS // 2 + 8, TINY_ROWS), :] = work["tiny"].result[...]
    for copy in back_copies:
        copy.wait_recv()
    for index, name in enumerate(IN_NAMES[:4]):
        act_copy(index, name).wait_send()
    for item in work.values():
        item.close()
    for copy in back_copies:
        copy.wait_send()


def start_back(valid, starts, project_w, combine_w, query_w, gain, shift, resid, query_grad, links, rows_out, stack_out):
    width = starts.shape[1]
    own = rows_out.shape[0]
    place = (links.section * 8 + links.lane) * own
    chosen = lax.broadcasted_iota(jnp.int32, (width, own), 0) == place + lax.broadcasted_iota(
        jnp.int32, (width, own), 1
    )
    chosen = jnp.where(chosen, 1.0, 0.0).astype(BF16)
    select = lambda value: dot(value, chosen, NN).astype(BF16)
    queries, keys, values, mixed, kept, rows, scale, first = self_block(
        starts, project_w, combine_w, gain, shift, valid
    )
    rows_out[:, pl.ds(4 * width, width)] = dot(select(first.astype(BF16)), query_grad, TN)
    grad_first = resid + dot(query_grad, query_w, NT)
    gain_sum = column_sum(grad_first * rows)
    shift_sum = column_sum(grad_first)
    grad_resid = normed_back(grad_first, gain, rows, scale)
    branch = grad_resid.astype(BF16)
    rows_out[:, pl.ds(3 * width, width)] = dot(select(mixed), branch, TN)
    grad_mixed = dot(branch, combine_w, NT).astype(BF16)
    dq, dk, dv = few_attend_back(queries, keys, values, kept, grad_mixed)
    grad_packed = jnp.concatenate([dq, dk, dv], axis=1).astype(BF16)
    rows_out[:, pl.ds(0, 3 * width)] = dot(select(starts), grad_packed, TN)
    count = starts.shape[0]
    stack_out[pl.ds(0, count), :] = grad_resid + dot(grad_packed, project_w, NT)
    stack_out[pl.ds(count, 8), :] = jnp.concatenate([gain_sum, shift_sum, jnp.zeros((6, width), F32)], axis=0)


def attend_back_pair(queries, keys, values, grads, mixed, logs, out, columns, between):
    count = queries.shape[0]
    lane = lax.broadcasted_iota(jnp.int32, (1, LANES), 1)
    queries = queries * jnp.asarray(0.125, BF16)
    scaled_keys = keys * jnp.asarray(0.125, BF16)
    queries_t = queries.T
    grads_t = grads.T
    logs = logs.T
    shared = mixed.astype(F32) * grads_t.astype(F32)
    inner = jnp.concatenate([column_sum(shared[:64]), column_sum(shared[64:])], axis=0).T
    dq_parts = [[], []]
    dk_parts = []
    dv_parts = []
    for head in range(2):
        own = (lane < 64) if head == 0 else (lane >= 64)
        head_queries = jnp.where(own, queries, jnp.zeros_like(queries))
        head_grads = jnp.where(own, grads, jnp.zeros_like(grads))
        dk = None
        dv = None
        for start in range(0, count, ATTEND_BLOCK):
            part = slice(start, start + ATTEND_BLOCK)
            scores = dot(head_queries[part], keys, NT)
            probs = jnp.exp(scores - logs[part, head : head + 1])
            grad_probs = dot(head_grads[part], values, NT)
            grad_scores = (probs * (grad_probs - inner[part, head : head + 1])).astype(BF16)
            new_v = dot(grads_t[64 * head : 64 * head + 64, part], probs.astype(BF16), NN)
            new_k = dot(queries_t[64 * head : 64 * head + 64, part], grad_scores, NN)
            dv = new_v if dv is None else dv + new_v
            dk = new_k if dk is None else dk + new_k
            dq_parts[head].append(dot(grad_scores, scaled_keys, NN))
        dk_parts.append(dk)
        dv_parts.append(dv)
        if head == 0:
            between(0)
    out[1, :, columns] = jnp.concatenate(dk_parts, axis=0).T.astype(BF16)
    out[2, :, columns] = jnp.concatenate(dv_parts, axis=0).T.astype(BF16)
    for index in range(count // ATTEND_BLOCK):
        out[0, pl.ds(index * ATTEND_BLOCK, ATTEND_BLOCK), columns] = jnp.where(
            lane < 64, dq_parts[0][index], dq_parts[1][index]
        ).astype(BF16)
    between(1)


def split_of(hidden_size):
    return hidden_size // 256 * 128 + 128


def chain_blocks(width, hidden_size):
    cut = split_of(hidden_size)
    blocks = {}
    for side in ("decoder", "encoder"):
        blocks[side + "_expand0"] = (16, cut)
        blocks[side + "_expand1"] = (16, hidden_size - cut)
        blocks[side + "_reduce0"] = (hidden_size // 16, LANES)
        blocks[side + "_reduce1"] = (hidden_size // 16, LANES)
    for name in ("middle0", "middle1"):
        blocks[name] = (16, 2 * width)
    for name in ("last0", "last1"):
        blocks[name] = (16, 3 * width // 2)
    return blocks


def backward_linked(saved, weights, small, tiny):
    count, width = saved["x"].shape
    hidden_size = saved["active"].shape[1]
    starts = weights[6]
    valid = starts.shape[0]
    arrays = dict(saved)
    arrays.update(
        cross_memory=weights[10], reduce=weights[3], expand=weights[2], combine=weights[1], project=weights[0],
        self_project=weights[7], self_combine=weights[8], cross_query=weights[9],
        slope=saved["slope"].reshape(count // 16, 16, hidden_size),
    )
    inputs = [arrays[name] for name in IN_NAMES]
    vectors = [weights[4], small, tiny, weights[14], weights[15]]
    blocks = chain_blocks(width, hidden_size)
    own = width // 16
    vmem = lambda counts, name: [pltpu.VMEM((n,) + blocks[name], BF16) for n in counts]
    scratch = [pltpu.VMEM((2 * PAD_ROWS, arrays[name].shape[1]), BF16) for name in IN_NAMES[:4]]
    for name in NAMES:
        if name.startswith("decoder"):
            scratch += vmem(stage_blocks(GROUPS[name]), name)
        elif not name.startswith("encoder_expand"):
            scratch += vmem([16, 16] + stage_blocks(GROUPS[name]), name)
    for name in NAMES:
        if not name.startswith("encoder_expand"):
            scratch += vmem((16,), name)
    for name in ("encoder_expand0", "encoder_expand1"):
        scratch += vmem(stage_blocks(GROUPS[name]), name)
    scratch += [
        pltpu.VMEM((count, hidden_size), BF16),
        pltpu.VMEM((count // 16, 16, hidden_size), BF16),
        pltpu.VMEM((count, width), BF16),
        pltpu.VMEM((count, width), F32),
        pltpu.VMEM((width, count), BF16),
        pltpu.VMEM((count, width), BF16),
        pltpu.VMEM((2,) + small.shape, BF16),
        pltpu.VMEM((5,) + small.shape, BF16),
        pltpu.VMEM((2,) + tiny.shape, F32),
        pltpu.VMEM((5,) + tiny.shape, F32),
        pltpu.SemaphoreType.DMA((len(NAMES) + 2, STEPS, 2)),
        pltpu.SemaphoreType.DMA((len(NAMES) + 2, STEPS, 2)),
        pltpu.SemaphoreType.DMA((2, 4)),
        pltpu.SemaphoreType.DMA((2, 2)),
        pltpu.SemaphoreType.DMA((len(IN_NAMES),)),
        pltpu.SemaphoreType.DMA((3,)),
        pltpu.SemaphoreType.REGULAR((2, 5)),
    ]
    in_any = pl.BlockSpec(memory_space=pl.ANY)
    in_vmem = pl.BlockSpec(memory_space=pltpu.VMEM)
    shape = shape_of((count, width), BF16)
    results = pl.pallas_call(
        functools.partial(backward_kernel, valid),
        in_specs=[in_any] * len(IN_NAMES) + [in_vmem] * len(vectors),
        out_specs=[in_vmem] * len(NAMES) + [in_any] * 3 + [in_vmem] * 2,
        out_shape=[shape_of((2,) + blocks[name], BF16) for name in NAMES]
        + [shape] * 3
        + [shape_of((own, 5 * width), F32), shape_of((SMALL_ROWS // 2 + 8 + TINY_ROWS, width), F32)],
        scratch_shapes=scratch,
        compiler_params=pltpu.CompilerParams(
            collective_id=0, has_side_effects=True, vmem_limit_bytes=LINKED_VMEM_BYTES
        ),
        cost_estimate=pl.CostEstimate(flops=10**8, bytes_accessed=10**8, transcendentals=0),
    )(*inputs, *vectors)
    return results[: len(NAMES)], *results[len(NAMES) :]


def finish_kernel(valid, joints, *refs):
    refs = list(refs)

    def draw(count):
        taken = refs[:count]
        del refs[:count]
        return taken

    halves = dict(zip(NAMES, draw(len(NAMES))))
    rows_ref, stack_ref, memory, other, grad_x, grad_memory, other_slab = draw(7)
    memory_out, slab_out = draw(2)
    (
        project_e, combine_e, expand_e, reduce_e, gains_e, shifts_e, starts_d, project_d, combine_d, query_d,
        memory_d, cross_d, expand_d, reduce_d, gains_d, shifts_d, head_d,
    ) = draw(17)
    section = lax.axis_index("section")
    first = section == 0
    memory_out[0] = jnp.where(first, memory[...], other[...])
    memory_out[1] = jnp.where(first, other[...], memory[...])
    slab_out[0, 0] = jnp.where(first, grad_x[...], other_slab[...])
    slab_out[0, 1] = jnp.where(first, other_slab[...], grad_memory[...])

    width = memory.shape[1]
    own = rows_ref.shape[0]
    place = (section * 8 + lax.axis_index("dp")) * own

    def rows_of(name, out, columns, first=0):
        for core in range(2):
            out[pl.ds(16 * core, 16), columns] = halves[name][core, :, first : first + columns.size].astype(F32)

    cut = halves["encoder_expand0"].shape[2]
    for side, out in (("encoder", expand_e), ("decoder", expand_d)):
        rows_of(side + "_expand0", out, pl.ds(0, cut))
        rows_of(side + "_expand1", out, pl.ds(cut, out.shape[1] - cut))
    for side, out in (("encoder", reduce_e), ("decoder", reduce_d)):
        for core in range(2):
            for index in range(2):
                out[:, pl.ds((2 * core + index) * LANES, LANES)] = halves[side + "_reduce%d" % index][core].astype(F32)
    rows_of("middle0", memory_d, pl.ds(0, 2 * width))
    rows_of("middle1", cross_d, pl.ds(0, width))
    rows_of("middle1", combine_e, pl.ds(0, width), width)
    half = width // 2
    for third in range(3):
        for index in range(2):
            rows_of("last%d" % index, project_e, pl.ds(third * width + index * half, half), third * half)
    project_d[...] = rows_ref[:, : 3 * width]
    combine_d[...] = rows_ref[:, 3 * width : 4 * width]
    query_d[...] = rows_ref[:, 4 * width :]
    chosen = lax.broadcasted_iota(jnp.int32, (width, own), 0) == place + lax.broadcasted_iota(
        jnp.int32, (width, own), 1
    )
    picked = lax.dot_general(
        stack_ref[...], jnp.where(chosen, 1.0, 0.0), NN, precision=lax.Precision.HIGHEST, preferred_element_type=F32
    )
    base = SMALL_ROWS // 2
    tiny = base + 8
    starts_d[...] = picked[:valid]
    gains_d[...] = jnp.concatenate([picked[base : base + 1], picked[tiny : tiny + 2]], axis=0)
    shifts_d[...] = jnp.concatenate([picked[base + 1 : base + 2], picked[tiny + 2 : tiny + 4]], axis=0)
    gains_e[...] = picked[tiny + 4 : tiny + 6]
    shifts_e[...] = picked[tiny + 6 : tiny + 8]
    head_d[...] = picked[tiny + 8 : tiny + 24].T[:, :joints]


def finish(valid, joints, halves, rows, stack, memory, other, grad_x, grad_memory, other_slab):
    count, width = memory.shape
    own = rows.shape[0]
    hidden_size = halves[0].shape[2] + halves[1].shape[2]
    in_vmem = pl.BlockSpec(memory_space=pltpu.VMEM)
    shapes = [
        (own, 3 * width), (own, width), (own, hidden_size), (hidden_size // 16, width), (2, own), (2, own),
        (valid, own), (own, 3 * width), (own, width), (own, width), (own, 2 * width), (own, width),
        (own, hidden_size), (hidden_size // 16, width), (3, own), (3, own), (own, joints),
    ]
    return call(
        functools.partial(finish_kernel, valid, joints),
        10**6, 10**7,
        in_specs=[in_vmem] * (len(halves) + 7),
        out_specs=[in_vmem] * (2 + len(shapes)),
        out_shape=[shape_of((2, count, width), BF16), shape_of((1, 2, count, width), BF16)]
        + [shape_of(dims, F32) for dims in shapes],
    )(*halves, rows, stack, memory, other, grad_x, grad_memory, other_slab)


def swap(value, axis, bit):
    pairs = [(i, i ^ (1 << bit)) for i in range(lax.axis_size(axis))]
    return lax.ppermute(value, axis, pairs)


def plain_scatter(full):
    part = lax.psum_scatter(full.astype(F32), ("section", "dp"), scatter_dimension=0, tiled=True)
    return lax.psum(part, "rep")


def pack_small(saved):
    rows = SMALL_ROWS // 2
    small = jnp.concatenate([saved["resid_d"][:rows], saved["query_d"][:rows]])
    tiny = jnp.concatenate([saved["sums_d"][:4], jnp.zeros_like(saved["sums_d"][:4]), saved["head"].T])
    return small, jnp.pad(tiny, ((0, TINY_ROWS - tiny.shape[0]), (0, 0)))


def per_device(x, targets, arms, *weights):
    section = lax.axis_index("section")
    sections = lax.axis_size("section")
    lanes = lax.axis_size("dp")
    count = x.shape[0] // sections
    starts, head = weights[6], weights[16]
    valid, joints = starts.shape[0], head.shape[1]
    width = starts.shape[1]
    first = section == 0
    place = section * lanes + lax.axis_index("dp")
    own = width // (sections * lanes)
    saved = []
    for index in range(count):
        spot = section * count + index
        pick = lambda array: lax.dynamic_index_in_dim(array, spot, 0, keepdims=False)
        saved.append(forward(pick(x), pick(targets), lax.dynamic_slice(arms, (spot,), (1,)), weights))
    if (sections, lanes, lax.axis_size("rep"), count) == (2, 8, 2, 1):
        small, tiny = pack_small(saved[0])
        other = swap(saved[0]["memory"], "section", 0)
        halves, other_slab, grad_memory, grad_x, rows, stack = backward_linked(
            saved[0], weights, small.astype(BF16), tiny
        )
        return finish(
            valid, joints, halves, rows, stack, saved[0]["memory"], other, grad_x, grad_memory, other_slab
        )
    memory = jnp.concatenate([item["memory"][None] for item in saved])
    results = [backward_alone(item, weights) for item in saved]
    grad_x = jnp.concatenate([item[0][None] for item in results])
    grad_memory = jnp.concatenate([item[1][None] for item in results])
    total = lambda name: functools.reduce(jnp.add, [item[2][name] for item in results])
    other = swap(memory, "section", 0)
    other_slab = swap(jnp.where(first, grad_memory, grad_x), "section", 0)
    small, tiny = pack_small({name: total(name) for name in ("resid_d", "query_d", "sums_d")} | {"head": total("head").T})
    tiny = tiny.at[4:8].set(total("sums_e"))
    small = lax.psum(small, ("section", "dp", "rep"))
    tiny = lax.psum(tiny, ("section", "dp", "rep"))
    done = {
        name: plain_scatter(total(name))
        for name in ("decoder_expand", "decoder_reduce", "encoder_expand", "encoder_reduce", "middle", "last")
    }
    memory_out = jnp.concatenate([jnp.where(first, memory, other), jnp.where(first, other, memory)])
    slab = jnp.concatenate(
        [jnp.where(first, grad_x, other_slab), jnp.where(first, other_slab, grad_memory)]
    )[None]

    columns_of = lambda array: lax.dynamic_slice_in_dim(array, place * own, own, 1)
    rows_of = lambda array: lax.dynamic_slice_in_dim(array, place * own, own, 0)
    rest = PAD_ROWS - SMALL_ROWS // 2
    resid_d = jnp.pad(small[: SMALL_ROWS // 2].astype(F32), ((0, rest), (0, 0)))
    query_d = jnp.pad(small[SMALL_ROWS // 2 :].astype(F32), ((0, rest), (0, 0)))
    start_grad, project_d, combine_d, query_w, sums_s = decode_start_back(
        valid, jnp.pad(starts, ((0, PAD_ROWS - valid), (0, 0))), weights[7], weights[8], weights[9],
        weights[14], weights[15], resid_d, query_d,
    )
    gains_d = jnp.concatenate([sums_s[0:1], tiny[0:2]])
    shifts_d = jnp.concatenate([sums_s[1:2], tiny[2:4]])
    return (
        memory_out,
        slab,
        done["last"],
        done["middle"][:, 3 * width :],
        done["encoder_expand"],
        done["encoder_reduce"],
        columns_of(tiny[4:6]),
        columns_of(tiny[6:8]),
        columns_of(start_grad[:valid]),
        rows_of(project_d),
        rows_of(combine_d),
        rows_of(query_w),
        done["middle"][:, : 2 * width],
        done["middle"][:, 2 * width : 3 * width],
        done["decoder_expand"],
        done["decoder_reduce"],
        columns_of(gains_d),
        columns_of(shifts_d),
        rows_of(tiny[8 : 8 + joints].T),
    )


def solution(mesh):
    spread = ("section", "dp")
    rows = P(spread, None)
    columns = P(None, spread)
    return jax.shard_map(
        per_device,
        mesh=mesh,
        in_specs=(P(("dp", "rep"), None, None), P(("dp", "rep"), None, None), P(("dp", "rep"))) + (P(),) * 17,
        out_specs=(
            P(("dp", "rep"), None, None),
            P("section", ("dp", "rep"), None, None),
            rows, rows, rows, rows, columns, columns, columns,
            rows, rows, rows, rows, rows, rows, rows, columns, columns, rows,
        ),
        check_vma=False,
    )
```

```python
import functools

import jax
import jax.numpy as jnp
from jax import lax
from jax.experimental import pallas as pl
from jax.experimental.pallas import tpu as pltpu
from jax.sharding import PartitionSpec as P

HEADS = 8
EPSILON = 1e-05
LANES = 128
PAD_ROWS = 112
SMALL_ROWS = 2 * PAD_ROWS
TINY_ROWS = 24
F32 = jnp.float32
BF16 = jnp.bfloat16
NN = (((1,), (0,)), ((), ()))
NT = (((1,), (1,)), ((), ()))
TN = (((0,), (0,)), ((), ()))
VMEM_BYTES = 56 * 1024 * 1024
LINKED_VMEM_BYTES = 638 * 1024 * 1024 // 10
ROOT_2_PI = 0.7978845608028654
CUBE = 0.044715


def dot(left, right, dims):
    return lax.dot_general(left, right, dims, preferred_element_type=F32)


def call(kernel, flops, moved, **options):
    return pl.pallas_call(
        kernel,
        compiler_params=pltpu.CompilerParams(vmem_limit_bytes=VMEM_BYTES),
        cost_estimate=pl.CostEstimate(flops=flops, bytes_accessed=moved, transcendentals=0),
        **options,
    )


def shape_of(dims, dtype):
    return jax.ShapeDtypeStruct(dims, dtype)


def whole(array):
    rank = len(array.shape)
    return pl.BlockSpec(array.shape, lambda *_: (0,) * rank, pipeline_mode=pl.Buffered(1))


def normed(residual):
    centre = jnp.mean(residual, axis=-1, keepdims=True)
    centred = residual - centre
    spread = jnp.mean(centred * centred, axis=-1, keepdims=True)
    scale = lax.rsqrt(spread + EPSILON)
    return centred * scale, scale


def normed_back(grad, gain, rows, scale):
    weighted = grad * gain
    return scale * (
        weighted
        - jnp.mean(weighted, axis=-1, keepdims=True)
        - rows * jnp.mean(weighted * rows, axis=-1, keepdims=True)
    )


def gelu_and_slope(value):
    square = value * value
    bend = jnp.tanh(value * (ROOT_2_PI + (ROOT_2_PI * CUBE) * square))
    half = 0.5 + 0.5 * bend
    slope = half + value * (0.5 - 0.5 * bend * bend) * (
        ROOT_2_PI + (3.0 * ROOT_2_PI * CUBE) * square
    )
    return value * half, slope


def column_sum(value):
    return jnp.sum(value, axis=0, keepdims=True)


FORWARD_WEIGHTS = ("project", "combine", "expand", "reduce", "memory_w")
FORWARD_OUTS = ("packed", "mixed", "logs", "first", "low", "active", "slope", "second", "memory", "pair")


def split_of(hidden_size):
    return hidden_size // 256 * 128 + 128


def column_chunks(hidden_size):
    cut = split_of(hidden_size)
    return [(0, 896), (896, cut - 896), (cut, 768), (cut + 768, hidden_size - cut - 768)]


def attend_all(packed, mixed_ref, log_ref):
    count, width = packed.shape[0], packed.shape[1] // 3
    lane = lax.broadcasted_iota(jnp.int32, (1, LANES), 1)
    heads = width // 64
    columns = lambda third, head: pl.ds(third * width + head // 2 * LANES, LANES)

    def scores_of(head):
        keys = packed[:, columns(1, head)]
        own = (lane < 64) if head % 2 == 0 else (lane >= 64)
        queries = packed[:, columns(0, head)] * jnp.asarray(0.125, BF16)
        return dot(jnp.where(own, keys, jnp.zeros_like(keys)), queries, NT)

    scores = scores_of(0)
    for head in range(heads):
        following = scores_of(head + 1) if head + 1 < heads else None
        if head % 2 == 0:
            values = packed[:, columns(2, head)].T
        extended = jnp.concatenate(
            [values[64 * (head % 2) : 64 * (head % 2) + 64], jnp.ones((16, count), BF16)], axis=0
        )
        largest = jnp.max(scores, axis=0, keepdims=True)
        raised = jnp.exp(scores - largest).astype(BF16)
        mixed = dot(extended, raised, NN)
        total = mixed[64:65]
        mixed_ref[pl.ds(64 * head, 64), :] = (mixed[:64] * (1.0 / total)).astype(BF16)
        log_ref[head // 2, pl.ds(head % 2, 1), :] = largest + jnp.log(total)
        scores = following


def encode_kernel(pick, x_ref, *refs):
    refs = list(refs)

    def draw(count):
        taken = refs[:count]
        del refs[:count]
        return taken

    weights = dict(zip(FORWARD_WEIGHTS, draw(5)))
    gain_ref, shift_ref = draw(2)
    outs = dict(zip(FORWARD_OUTS, draw(10)))
    held = dict(zip(FORWARD_WEIGHTS, draw(5)))
    kept = dict(zip(FORWARD_OUTS, draw(10)))
    x, load_sems, store_sems = draw(3)
    here = pltpu.make_async_copy(x_ref.at[pick()], x, load_sems.at[5])
    here.start()
    loads = {}
    for index, name in enumerate(FORWARD_WEIGHTS):
        loads[name] = pltpu.make_async_copy(weights[name], held[name], load_sems.at[index])
        loads[name].start()
    stores = []

    def store(name):
        index = FORWARD_OUTS.index(name)
        stores.append(pltpu.make_async_copy(kept[name], outs[name], store_sems.at[index]))
        stores[-1].start()

    count, width = x.shape
    hidden_size = held["expand"].shape[1]
    block = 256
    here.wait()
    loads["project"].wait()
    for third in range(3):
        columns = pl.ds(third * width, width)
        kept["packed"][:, columns] = dot(x[...], held["project"][:, columns], NN).astype(BF16)
    store("packed")
    attend_all(kept["packed"], kept["mixed"], kept["logs"])
    store("mixed")
    store("logs")
    loads["combine"].wait()
    first, low, second = kept["first"], kept["low"], kept["second"]
    first[...] = x[...].astype(F32) + dot(kept["mixed"][...], held["combine"][...], TN)
    for start in range(0, count, block):
        part = pl.ds(start, block)
        rows, _ = normed(first[part, :])
        value = rows * gain_ref[0:1, :] + shift_ref[0:1, :]
        second[part, :] = value
        low[part, :] = value.astype(BF16)
    store("first")
    store("low")
    loads["expand"].wait()
    chunks = column_chunks(hidden_size)
    before = lambda item: dot(low[...], held["expand"][:, pl.ds(*item)], NN)
    ahead = before(chunks[0])
    for index, (start, size) in enumerate(chunks):
        current = ahead
        if index + 1 < len(chunks):
            ahead = before(chunks[index + 1])
        active, slope = gelu_and_slope(current)
        columns = pl.ds(start, size)
        kept["active"][:, columns] = active.astype(BF16)
        kept["slope"][:, columns] = slope.astype(BF16)
    store("active")
    store("slope")
    loads["reduce"].wait()
    second[...] += dot(kept["active"][...], held["reduce"][...], NN)
    memory = kept["memory"]
    for start in range(0, count, block):
        part = pl.ds(start, block)
        rows, _ = normed(second[part, :])
        memory[part, :] = (rows * gain_ref[1:2, :] + shift_ref[1:2, :]).astype(BF16)
    store("second")
    store("memory")
    loads["memory_w"].wait()
    kept["pair"][...] = dot(memory[...], held["memory_w"][...], NN).astype(BF16)
    store("pair")
    for copy in stores:
        copy.wait()


def encode(x, pick, weights, gains, shifts):
    count, width = x.shape[1:]
    hidden_size = weights[2].shape[1]
    shapes = [
        ((count, 3 * width), BF16), ((width, count), BF16), ((width // LANES, 2, count), F32), ((count, width), F32),
        ((count, width), BF16), ((count, hidden_size), BF16), ((count, hidden_size), BF16), ((count, width), F32),
        ((count, width), BF16), ((count, 2 * width), BF16),
    ]
    in_any = pl.BlockSpec(memory_space=pl.ANY)
    in_vmem = pl.BlockSpec(memory_space=pltpu.VMEM)
    results = call(
        functools.partial(encode_kernel, pick),
        2 * count * width * (2 * hidden_size + 6 * width) + 4 * count * count * width,
        count * (hidden_size * 4 + width * 24) + 8 * width * hidden_size,
        in_specs=[in_any] * 6 + [in_vmem] * 2,
        out_specs=[in_any] * 10,
        out_shape=[shape_of(dims, kind) for dims, kind in shapes],
        scratch_shapes=[pltpu.VMEM(item.shape, BF16) for item in weights]
        + [pltpu.VMEM(dims, kind) for dims, kind in shapes]
        + [pltpu.VMEM((count, width), BF16), pltpu.SemaphoreType.DMA((6,)), pltpu.SemaphoreType.DMA((10,))],
    )(x, *weights, gains, shifts)
    return dict(zip(FORWARD_OUTS, results))


def attend_back_kernel(block, q_ref, k_ref, v_ref, do_ref, mixed_ref, log_ref, dq_ref, dk_ref, dv_ref):
    count = q_ref.shape[0]
    lane = lax.broadcasted_iota(jnp.int32, (1, LANES), 1)
    keys = k_ref[...]
    values = v_ref[...]
    queries = q_ref[...] * jnp.asarray(0.125, BF16)
    scaled_keys = keys * jnp.asarray(0.125, BF16)
    grads = do_ref[...]
    queries_t = queries.T
    grads_t = grads.T
    logs = log_ref[0].T
    shared = mixed_ref[...].astype(F32) * grads_t.astype(F32)
    inner = jnp.concatenate([column_sum(shared[:64]), column_sum(shared[64:])], axis=0).T
    dq_parts = [[], []]
    dk_parts = []
    dv_parts = []
    for head in range(2):
        own = (lane < 64) if head == 0 else (lane >= 64)
        head_queries = jnp.where(own, queries, jnp.zeros_like(queries))
        head_grads = jnp.where(own, grads, jnp.zeros_like(grads))
        dk = None
        dv = None
        for start in range(0, count, block):
            part = slice(start, start + block)
            scores = dot(head_queries[part], keys, NT)
            probs = jnp.exp(scores - logs[part, head : head + 1])
            grad_probs = dot(head_grads[part], values, NT)
            grad_scores = (probs * (grad_probs - inner[part, head : head + 1])).astype(BF16)
            new_v = dot(grads_t[64 * head : 64 * head + 64, part], probs.astype(BF16), NN)
            new_k = dot(queries_t[64 * head : 64 * head + 64, part], grad_scores, NN)
            dv = new_v if dv is None else dv + new_v
            dk = new_k if dk is None else dk + new_k
            dq_parts[head].append(dot(grad_scores, scaled_keys, NN))
        dk_parts.append(dk)
        dv_parts.append(dv)
    dk_ref[...] = jnp.concatenate(dk_parts, axis=0).T.astype(BF16)
    dv_ref[...] = jnp.concatenate(dv_parts, axis=0).T.astype(BF16)
    for index in range(count // block):
        dq_ref[pl.ds(index * block, block), :] = jnp.where(
            lane < 64, dq_parts[0][index], dq_parts[1][index]
        ).astype(BF16)


def attend_back(packed, grad_mixed, mixed, logs):
    rows, width = packed.shape[0], packed.shape[1] // 3
    pairs = width // LANES
    column = lambda first: pl.BlockSpec((rows, LANES), lambda j: (0, first + j))
    return call(
        functools.partial(attend_back_kernel, 256),
        10 * rows * rows * width * 3,
        rows * width * 16,
        grid=(pairs,),
        in_specs=[
            column(0),
            column(pairs),
            column(2 * pairs),
            column(0),
            pl.BlockSpec((LANES, rows), lambda j: (j, 0)),
            pl.BlockSpec((1, 2, rows), lambda j: (j, 0, 0)),
        ],
        out_specs=[column(0)] * 3,
        out_shape=[shape_of((rows, width), BF16)] * 3,
    )(packed, packed, packed, grad_mixed, mixed, logs)

def encode_back_kernel(
    pair_ref, first_ref, second_ref, slope_ref, combine_ref, expand_ref, reduce_ref, gain_ref, memory_w_ref,
    grad_memory_ref, branch_ref, hidden_ref, resid_ref, low_ref, mixed_ref, sums_ref,
):
    grad_memory = dot(pair_ref[...], memory_w_ref[...], NT).astype(BF16)
    grad_memory_ref[...] = grad_memory
    grad_last = grad_memory.astype(F32)
    rows, scale = normed(second_ref[...])
    gain_last = column_sum(grad_last * rows)
    shift_last = column_sum(grad_last)
    grad_second = normed_back(grad_last, gain_ref[1:2, :], rows, scale)
    branch = grad_second.astype(BF16)
    branch_ref[...] = branch
    total = grad_second
    hidden_size = expand_ref.shape[1]
    step = hidden_size // 5
    for start in range(0, hidden_size, step):
        part = pl.ds(start, step)
        grad_active = dot(branch, reduce_ref[part, :], NT)
        grad_hidden = (grad_active * slope_ref[:, part].astype(F32)).astype(BF16)
        hidden_ref[:, part] = grad_hidden
        total = total + dot(grad_hidden, expand_ref[:, part], NT)
    rows, scale = normed(first_ref[...])
    gain_first = column_sum(total * rows)
    shift_first = column_sum(total)
    grad_first = normed_back(total, gain_ref[0:1, :], rows, scale)
    resid_ref[...] = grad_first
    low = grad_first.astype(BF16)
    low_ref[...] = low
    mixed_ref[...] = dot(low, combine_ref[...], NT).astype(BF16)
    fresh = jnp.concatenate(
        [gain_first, gain_last, shift_first, shift_last, jnp.zeros((4, gain_first.shape[1]), F32)], axis=0
    )

    @pl.when(pl.program_id(0) == 0)
    def _():
        sums_ref[...] = fresh

    @pl.when(pl.program_id(0) > 0)
    def _():
        sums_ref[...] += fresh


def encode_back(grad_pair, first, second, slope, combine_w, expand_w, reduce_w, gains, memory_w):
    rows, width = first.shape
    hidden = expand_w.shape[1]
    block = 256
    line = lambda size: pl.BlockSpec((block, size), lambda i: (i, 0))
    sizes = [(width, BF16), (width, BF16), (hidden, BF16), (width, F32), (width, BF16), (width, BF16)]
    return call(
        encode_back_kernel,
        2 * rows * width * (2 * hidden + 3 * width),
        rows * (hidden * 4 + width * 18) + 8 * width * hidden,
        grid=(rows // block,),
        in_specs=[line(2 * width), line(width), line(width), line(hidden)]
        + [whole(item) for item in (combine_w, expand_w, reduce_w, gains, memory_w)],
        out_specs=[line(size) for size, _ in sizes] + [pl.BlockSpec((8, width), lambda i: (0, 0))],
        out_shape=[shape_of((rows, size), kind) for size, kind in sizes] + [shape_of((8, width), F32)],
    )(grad_pair, first, second, slope, combine_w, expand_w, reduce_w, gains, memory_w)


def stacked(rows):
    lane = lax.broadcasted_iota(jnp.int32, (1, rows.shape[1]), 1)
    return jnp.concatenate(
        [jnp.where((lane >= 64 * h) & (lane < 64 * h + 64), rows, jnp.zeros_like(rows)) for h in range(4)],
        axis=0,
    )


def unstacked(rows):
    lane = lax.broadcasted_iota(jnp.int32, (1, rows.shape[1]), 1)
    count = rows.shape[0] // 4
    result = rows[:count]
    for h in range(1, 4):
        result = jnp.where(lane >= 64 * h, rows[h * count : h * count + count], result)
    return result


def few_attend(queries, keys, values, valid):
    mixed = []
    kept = []
    for half in range(2):
        part = slice(256 * half, 256 * half + 256)
        scores = dot(stacked(queries[:, part] * jnp.asarray(0.125, BF16)), keys[:, part], NT)
        if valid < scores.shape[1]:
            column = lax.broadcasted_iota(jnp.int32, (1, scores.shape[1]), 1)
            scores = jnp.where(column < valid, scores, -1e30)
        raised = jnp.exp(scores - jnp.max(scores, axis=1, keepdims=True))
        probs = raised * (1.0 / jnp.sum(raised, axis=1, keepdims=True))
        mixed.append(unstacked(dot(probs.astype(BF16), values[:, part], NN)))
        kept.append(probs)
    return jnp.concatenate(mixed, axis=1).astype(BF16), kept


def few_attend_back(queries, keys, values, kept, grads):
    dq, dk, dv = [], [], []
    for half in range(2):
        part = slice(256 * half, 256 * half + 256)
        probs = kept[half]
        own_queries = stacked(queries[:, part] * jnp.asarray(0.125, BF16))
        own_grads = stacked(grads[:, part])
        grad_probs = dot(own_grads, values[:, part], NT)
        product = probs * grad_probs
        grad_scores = (product - probs * jnp.sum(product, axis=1, keepdims=True)).astype(BF16)
        dv.append(dot(probs.astype(BF16), own_grads, TN))
        dk.append(dot(grad_scores, own_queries, TN))
        dq.append(unstacked(dot(grad_scores, keys[:, part], NN)) * 0.125)
    return jnp.concatenate(dq, axis=1), jnp.concatenate(dk, axis=1), jnp.concatenate(dv, axis=1)


def self_block(starts, project_w, combine_w, gain, shift, valid):
    width = starts.shape[1]
    packed = dot(starts, project_w, NN).astype(BF16)
    queries, keys, values = (packed[:, i * width : (i + 1) * width] for i in range(3))
    mixed, kept = few_attend(queries, keys, values, valid)
    residual = starts.astype(F32) + dot(mixed, combine_w, NN)
    rows, scale = normed(residual)
    return queries, keys, values, mixed, kept, rows, scale, rows * gain + shift


def dealt(rows):
    width = rows.shape[1]
    source = lax.broadcasted_iota(jnp.int32, (width, width), 0)
    target = lax.broadcasted_iota(jnp.int32, (width, width), 1)
    half = width // 2
    wanted = (target % half) // 16 * 32 + target // half * 16 + target % 16
    return dot(rows, jnp.where(source == wanted, 1.0, 0.0).astype(BF16), NN).astype(BF16)


def undealt(columns):
    count, width = columns.shape
    return columns.reshape(count, 2, width // 32, 16).transpose(0, 2, 1, 3).reshape(count, width)


DECODE_WEIGHTS = ("self_project", "self_combine", "cross_query", "pair", "cross_combine", "expand", "reduce")


def decode_kernel(pick, joints, linked, starts_ref, *refs):
    refs = list(refs)

    def draw(count):
        taken = refs[:count]
        del refs[:count]
        return taken

    sources = draw(7)
    gain_ref, shift_ref, head_ref, target_ref, arm_ref = draw(5)
    (
        starts_out, grad_pair_ref, second_low_ref, hidden_ref, active_ref, branch_ref, cross_grad_ref, small_ref, tiny_ref,
    ) = draw(9)
    held = dict(zip(DECODE_WEIGHTS, draw(7)))
    grad_pair, hidden, active_rows, low_rows, branch_rows, target, load_sems, store_sems, send_sems, recv_sems = draw(10)
    other_core = {"rep": 1 - lax.axis_index("rep")}
    stores = []
    remote = []

    def hand_out(index, rows, out):
        stores.append(pltpu.make_async_copy(rows, out.at[pl.ds(0, PAD_ROWS)], store_sems.at[index]))
        stores[-1].start()
        if linked:
            copy = pltpu.make_async_remote_copy(
                src_ref=rows,
                dst_ref=out.at[pl.ds(PAD_ROWS, PAD_ROWS)],
                send_sem=send_sems.at[index],
                recv_sem=recv_sems.at[index],
                device_id=other_core,
                device_id_type=pl.DeviceIdType.MESH,
            )
            copy.start()
            remote.append(copy)

    loads = {}
    for index, (name, source) in enumerate(zip(DECODE_WEIGHTS, sources)):
        loads[name] = pltpu.make_async_copy(source, held[name], load_sems.at[index])
        loads[name].start()
    if linked:
        barrier = pltpu.get_barrier_semaphore()
        pl.semaphore_signal(barrier, inc=1, device_id=other_core, device_id_type=pl.DeviceIdType.MESH)
        pl.semaphore_wait(barrier, 1)
    valid, width = starts_ref.shape
    here = pick()
    starts_out[...] = jnp.zeros_like(starts_out)
    starts_out[pl.ds(0, valid), :] = starts_ref[...]
    target[...] = jnp.zeros_like(target)
    target[pl.ds(0, valid), :] = target_ref[here]
    for name in ("self_project", "self_combine"):
        loads[name].wait()
    first = self_block(
        starts_out[...], held["self_project"][...], held["self_combine"][...], gain_ref[0:1, :], shift_ref[0:1, :],
        valid,
    )[-1]
    loads["cross_query"].wait()
    queries = dot(first.astype(BF16), held["cross_query"][...], NN).astype(BF16)
    loads["pair"].wait()
    keys = held["pair"][:, :width]
    values = held["pair"][:, width:]
    mixed, kept = few_attend(queries, keys, values, keys.shape[0])
    loads["cross_combine"].wait()
    second_rows, second_scale = normed(first + dot(mixed, held["cross_combine"][...], NN))
    second = second_rows * gain_ref[1:2, :] + shift_ref[1:2, :]
    second_low = second.astype(BF16)
    low_rows[...] = dealt(second_low)
    hand_out(1, low_rows, second_low_ref)
    loads["expand"].wait()
    loads["reduce"].wait()
    expand_ref, reduce_ref = held["expand"], held["reduce"]
    chunks = column_chunks(expand_ref.shape[1])
    total = second
    slopes = []
    for start, size in chunks:
        part = pl.ds(start, size)
        active, slope = gelu_and_slope(dot(second_low, expand_ref[:, part], NN))
        slopes.append(slope)
        active = active.astype(BF16)
        active_rows[:, part] = active
        total = total + dot(active, reduce_ref[part, :], NN)
    hand_out(2, active_rows, active_ref)
    third_rows, third_scale = normed(total)
    third_low = (third_rows * gain_ref[2:3, :] + shift_ref[2:3, :]).astype(BF16)
    misfit = dot(third_low, head_ref[...], NN) - target[...]
    arms = arm_ref[here]
    row = lax.broadcasted_iota(jnp.int32, misfit.shape, 0)
    joint = lax.broadcasted_iota(jnp.int32, misfit.shape, 1)
    factor = 2.0 / jnp.full((1, 1), arms, jnp.int32).astype(F32)
    used = (row < valid) & (joint < joints // 2 * arms)
    grad_pred = jnp.where(used, factor * misfit * lax.rsqrt(misfit * misfit + 1.0), 0.0).astype(BF16)
    head_grad = dot(grad_pred, third_low, TN)
    grad_third = dot(grad_pred, head_ref[...], NT)
    gain_third = column_sum(grad_third * third_rows)
    shift_third = column_sum(grad_third)
    total = normed_back(grad_third, gain_ref[2:3, :], third_rows, third_scale)
    branch = total.astype(BF16)
    branch_rows[...] = branch
    hand_out(3, branch_rows, branch_ref)
    for index, (start, size) in enumerate(chunks):
        part = pl.ds(start, size)
        grad_hidden = (dot(branch, reduce_ref[part, :], NT) * slopes[index]).astype(BF16)
        hidden[:, part] = grad_hidden
        total = total + dot(grad_hidden, expand_ref[:, part], NT)
    hand_out(4, hidden, hidden_ref)
    gain_second = column_sum(total * second_rows)
    shift_second = column_sum(total)
    grad_second = normed_back(total, gain_ref[1:2, :], second_rows, second_scale)
    branch = grad_second.astype(BF16)
    small_ref[pl.ds(0, PAD_ROWS), :] = branch
    cross_grad_ref[...] = dot(mixed, branch, TN).astype(BF16)
    grad_mixed = dot(branch, held["cross_combine"][...], NT).astype(BF16)
    dq, dk, dv = few_attend_back(queries, keys, values, kept, grad_mixed)
    grad_pair[:, :width] = dk.astype(BF16)
    grad_pair[:, width:] = dv.astype(BF16)
    stores.append(pltpu.make_async_copy(grad_pair, grad_pair_ref, store_sems.at[0]))
    stores[-1].start()
    small_ref[pl.ds(PAD_ROWS, PAD_ROWS), :] = dq.astype(BF16)
    tiny_ref[...] = jnp.zeros_like(tiny_ref)
    tiny_ref[pl.ds(0, 4), :] = jnp.concatenate([gain_second, gain_third, shift_second, shift_third], axis=0)
    tiny_ref[pl.ds(8, joints), :] = head_grad
    for copy in stores + remote:
        copy.wait()


def decode(pick, targets, arms, weights, pair, linked):
    starts, head = weights[6], weights[16]
    valid, width = starts.shape
    joints = head.shape[1]
    hidden = weights[12].shape[1]
    sources = (weights[7], weights[8], weights[9], pair, weights[11], weights[12], weights[13])
    rows = 2 * PAD_ROWS if linked else PAD_ROWS
    shapes = {
        "starts": ((PAD_ROWS, width), BF16),
        "grad_pair": (pair.shape, BF16),
        "low_d": ((rows, width), BF16),
        "hidden_d": ((rows, hidden), BF16),
        "active_d": ((rows, hidden), BF16),
        "branch_d": ((rows, width), BF16),
        "cross": ((width, width), BF16),
        "small": ((SMALL_ROWS, width), BF16),
        "tiny": ((TINY_ROWS, width), F32),
    }
    in_any = pl.BlockSpec(memory_space=pl.ANY)
    in_vmem = pl.BlockSpec(memory_space=pltpu.VMEM)
    results = pl.pallas_call(
        functools.partial(decode_kernel, pick, joints, linked),
        cost_estimate=pl.CostEstimate(
            flops=8 * PAD_ROWS * width * hidden * 2, bytes_accessed=20 * 1024 * 1024, transcendentals=0
        ),
        compiler_params=pltpu.CompilerParams(
            vmem_limit_bytes=VMEM_BYTES, **(dict(collective_id=1, has_side_effects=True) if linked else {})
        ),
        in_specs=[in_vmem] + [in_any] * 7 + [in_vmem] * 4 + [pl.BlockSpec(memory_space=pltpu.SMEM)],
        out_specs=[in_any if name == "grad_pair" or name.endswith("_d") else in_vmem for name in shapes],
        out_shape=[shape_of(dims, kind) for dims, kind in shapes.values()],
        scratch_shapes=[pltpu.VMEM(item.shape, BF16) for item in sources]
        + [
            pltpu.VMEM(pair.shape, BF16), pltpu.VMEM((PAD_ROWS, hidden), BF16), pltpu.VMEM((PAD_ROWS, hidden), BF16),
            pltpu.VMEM((PAD_ROWS, width), BF16), pltpu.VMEM((PAD_ROWS, width), BF16),
            pltpu.VMEM((PAD_ROWS, joints), F32),
            pltpu.SemaphoreType.DMA((7,)), pltpu.SemaphoreType.DMA((5,)),
            pltpu.SemaphoreType.DMA((5,)), pltpu.SemaphoreType.DMA((5,)),
        ],
    )(starts, *sources, weights[14], weights[15], head, targets, arms)
    return dict(zip(shapes, results))


def decode_start_back_kernel(
    valid,
    starts_ref, project_ref, combine_ref, query_ref, gain_ref, shift_ref, resid_ref, query_grad_ref,
    start_grad_ref, project_grad_ref, combine_grad_ref, query_w_grad_ref, sums_ref,
):
    starts = starts_ref[...]
    project_w = project_ref[...]
    queries, keys, values, mixed, kept, rows, scale, first = self_block(
        starts, project_w, combine_ref[...], gain_ref[0:1, :], shift_ref[0:1, :], valid
    )
    low = query_grad_ref[...].astype(BF16)
    query_w_grad_ref[...] = dot(first.astype(BF16), low, TN)
    grad_first = resid_ref[...] + dot(low, query_ref[...], NT)
    gain_sum = column_sum(grad_first * rows)
    shift_sum = column_sum(grad_first)
    grad_resid = normed_back(grad_first, gain_ref[0:1, :], rows, scale)
    branch = grad_resid.astype(BF16)
    combine_grad_ref[...] = dot(mixed, branch, TN)
    grad_mixed = dot(branch, combine_ref[...], NT).astype(BF16)
    dq, dk, dv = few_attend_back(queries, keys, values, kept, grad_mixed)
    grad_packed = jnp.concatenate([dq, dk, dv], axis=1).astype(BF16)
    project_grad_ref[...] = dot(starts, grad_packed, TN)
    start_grad_ref[...] = grad_resid + dot(grad_packed, project_w, NT)
    sums_ref[...] = jnp.concatenate([gain_sum, shift_sum, jnp.zeros((6, gain_sum.shape[1]), F32)], axis=0)


def decode_start_back(valid, starts, project_w, combine_w, query_w, gains, shifts, resid, query_grad):
    count, width = starts.shape
    arrays = (starts, project_w, combine_w, query_w, gains, shifts, resid, query_grad)
    shapes = [(count, width), (width, 3 * width), (width, width), (width, width), (8, width)]
    return call(
        functools.partial(decode_start_back_kernel, valid),
        2 * count * width * width * 20,
        8 * 1024 * 1024,
        in_specs=[pl.BlockSpec(memory_space=pltpu.VMEM)] * len(arrays),
        out_specs=[pl.BlockSpec(memory_space=pltpu.VMEM)] * len(shapes),
        out_shape=[shape_of(dims, F32) for dims in shapes],
    )(*arrays)


def forward(x, targets, arms, pick, weights, linked):
    cross_memory = weights[10]
    saved = encode(x, pick, weights[:4] + (cross_memory,), weights[4], weights[5])
    saved["x"] = x
    saved.update(decode(pick, targets, arms, weights, saved.pop("pair"), linked))
    return saved


def backward_alone(saved, x, weights):
    (encoder_project, encoder_combine, encoder_expand, encoder_reduce, encoder_gains) = weights[:5]
    cross_memory = weights[10]
    grad_memory, branch, grad_hidden, resid, low, grad_mixed, sums_e = encode_back(
        saved["grad_pair"], saved["first"], saved["second"], saved["slope"],
        encoder_combine, encoder_expand, encoder_reduce, encoder_gains, cross_memory,
    )
    dq, dk, dv = attend_back(saved["packed"], grad_mixed, saved["mixed"], saved["logs"])
    grad_packed = jnp.concatenate([dq, dk, dv], axis=1)
    grad_x = (resid + dot(grad_packed, encoder_project, NT)).astype(BF16)
    plain = lambda left, right: dot(left, right, TN)
    return grad_x, grad_memory, {
        "decoder_expand": plain(undealt(saved["low_d"]), saved["hidden_d"]),
        "decoder_reduce": plain(saved["active_d"], saved["branch_d"]),
        "encoder_reduce": plain(saved["active"], branch),
        "encoder_expand": plain(saved["low"], grad_hidden),
        "middle": jnp.concatenate(
            [plain(saved["memory"], saved["grad_pair"]), saved["cross"].astype(F32), dot(saved["mixed"], low, NN)], axis=1
        ),
        "last": plain(x, grad_packed),
        "small": saved["small"].astype(F32),
        "tiny": saved["tiny"].at[4:8].set(sums_e[:4]),
    }


SECTION, SIDE, LINE = range(3)
GROUPS = {
    "decoder_expand0": (SIDE, LINE, SECTION),
    "decoder_expand1": (SIDE, SECTION, LINE),
    "decoder_reduce0": (SIDE, LINE, SECTION),
    "decoder_reduce1": (SECTION, SIDE, LINE),
    "encoder_reduce0": (SIDE, LINE, SECTION),
    "encoder_reduce1": (SIDE, SECTION, LINE),
    "encoder_expand0": (SECTION, SIDE, LINE),
    "encoder_expand1": (SECTION, SIDE, LINE),
    "middle0": (SECTION, LINE, SIDE),
    "middle1": (SIDE, SECTION, LINE),
    "last0": (LINE, SIDE, SECTION),
    "last1": (SIDE, LINE, SECTION),
}
NAMES = tuple(GROUPS)
SCHEDULE = {
    "dfe0": ("small",),
    "efr1": ("decoder_reduce0", "decoder_reduce1",),
    "dwm": ("encoder_reduce0",),
    "du0": ("encoder_reduce1", "decoder_reduce0",),
    "du1": ("small", "middle0",),
    "du3": ("decoder_reduce0",),
    "df": ("decoder_expand0",),
    "ln": ("small",),
    "efe0": ("decoder_reduce0", "decoder_expand1", "decoder_expand0", "tiny",),
    "dwc": ("encoder_expand0", "decoder_reduce1",),
    "att0": ("encoder_expand1", "middle1", "small", "decoder_expand0",),
    "att1": ("decoder_reduce1",),
    "att3": ("encoder_reduce0", "small",),
    "last0": ("middle0", "decoder_expand0", "decoder_reduce0",),
    "att4": ("last0", "decoder_reduce1",),
    "att5": ("encoder_reduce0", "encoder_reduce1", "decoder_expand1", "tiny", "middle0", "decoder_reduce0",),
    "att6": ("last0", "decoder_reduce1",),
    "att7": ("middle1", "encoder_reduce0", "decoder_expand1", "decoder_reduce1",),
    "dx0": ("tiny",),
    "dx1": ("encoder_expand0", "middle0",),
    "last1": ("last0", "small",),
}
TAIL_FIRST = ()
TAIL = (
    "last1",
    "encoder_expand0",
    "encoder_reduce0",
    "encoder_expand1",
    "tiny",
    "decoder_expand1",
    "last0",
    "middle0",
    "decoder_expand0",
    "encoder_expand0",
    "tiny",
    "decoder_expand0",
    "decoder_expand1",
    "last1",
    "encoder_expand0",
    "encoder_reduce1",
    "decoder_expand1",
    "last1",
    "middle1",
    "encoder_expand0",
    "encoder_expand1",
    "encoder_reduce1",
    "last0",
    "last1",
    "middle0",
    "encoder_expand0",
    "middle1",
    "tiny",
    "encoder_expand1",
    "encoder_reduce1",
    "middle0",
    "last1",
    "middle1",
    "encoder_expand1",
    "encoder_reduce1",
    "encoder_reduce0",
    "middle1",
    "last0",
    "last1",
    "encoder_expand1",
    "encoder_reduce1",
    "encoder_reduce0",
    "middle1",
    "last0",
    "last1",
    "encoder_expand1",
)
STEPS = 7
LINE_ROUNDS = 3


class Links:
    def __init__(self):
        core = lax.axis_index("rep")
        section = lax.axis_index("section")
        lane = lax.axis_index("dp")
        self.core = core
        self.section = section
        self.lane = lane
        self.level = lane // 2
        self.side = lane % 2
        self.mine = [section, self.side]
        self.other_core = {"rep": 1 - core}
        self.partner = [{"section": 1 - section}, {"dp": lane + 1 - 2 * self.side}]
        self.above = {"dp": lane + 2}
        self.below = {"dp": lane - 2}

    def signal(self, semaphore, device):
        pl.semaphore_signal(semaphore, inc=1, device_id=device, device_id_type=pl.DeviceIdType.MESH)

    def tell(self, semaphores):
        for semaphore, device in zip(semaphores[:3], [self.other_core] + self.partner):
            self.signal(semaphore, device)

        @pl.when(self.level > 0)
        def _():
            self.signal(semaphores[3], self.below)

        @pl.when(self.level < 3)
        def _():
            self.signal(semaphores[4], self.above)

    def greet(self):
        barrier = pltpu.get_barrier_semaphore()
        self.tell([barrier] * 5)
        pl.semaphore_wait(barrier, 3 + (self.level + 3) // 4 + (6 - self.level) // 4)

    def copy(self, source, target, sems, device):
        return pltpu.make_async_remote_copy(
            src_ref=source,
            dst_ref=target,
            send_sem=sems[0],
            recv_sem=sems[1],
            device_id=device,
            device_id_type=pl.DeviceIdType.MESH,
        )


def stage_blocks(order):
    counts, size = [], 16
    for dim in order:
        counts.append(5 * size // 4 if dim == LINE else size // 2)
        size = size // 4 if dim == LINE else size // 2
    return counts


class Scatter:
    def __init__(self, links, order, keep, sent, arrived, stages, send_sems, recv_sems, index, out, credits=None):
        self.links, self.order, self.keep, self.out = links, order, keep, out
        self.sent, self.arrived, self.credits = sent, arrived, credits
        self.sems = lambda step, way=0: (send_sems.at[index, step, way], recv_sems.at[index, step, way])
        self.plan = [] if sent is None else [("core",)]
        base, size = 0, 16
        for dim, buffer in zip(order, stages):
            if dim == LINE:
                size //= 4
                self.plan += [("line", turn, base, size, buffer) for turn in (1, 2, 3)]
                base = base + links.level * size
            else:
                size //= 2
                mine = links.mine[dim]
                self.plan.append(("halve", dim, base + (1 - mine) * size, base + mine * size, size, buffer))
                base = base + mine * size
        self.base = base
        self.plan.append(("both",))
        self.step = 0

    def place(self, shard):
        index, size = 0, 16
        for dim in self.order:
            size //= 4 if dim == LINE else 2
            index += size * {SECTION: shard // 8, LINE: shard // 2 % 4, SIDE: shard % 2}[dim]
        return index

    def single(self, step):
        links, kind = self.links, self.plan[step][0]
        if kind == "core":
            return links.copy(self.sent, self.arrived, self.sems(step), links.other_core)
        if kind == "halve":
            _, dim, away, _, size, buffer = self.plan[step]
            return links.copy(self.keep.at[pl.ds(away, size)], buffer, self.sems(step), links.partner[dim])
        return links.copy(self.out.at[links.core], self.out.at[links.core], self.sems(step), links.other_core)

    def lines(self, step):
        links, level = self.links, self.links.level
        _, turn, base, size, buffer = self.plan[step]
        shards = lambda ref, index: ref.at[pl.ds(index * size, size)]
        keep = lambda shard: self.keep.at[pl.ds(base + shard * size, size)]
        up, down = level + 4 - turn, level - 4 + turn
        return [
            (
                (level < turn) & (level < 3),
                lambda: links.copy(keep(up), shards(buffer, turn - level - 1), self.sems(step, 0), links.above),
                (level > 0) & (level <= turn),
                lambda: links.copy(keep(up - 1), shards(buffer, turn - level), self.sems(step, 0), links.above),
                lambda: (base + (up - 1) * size, (turn - level) * size),
                level == turn - 1,
            ),
            (
                (3 - level < turn) & (level > 0),
                lambda: links.copy(keep(down), shards(buffer, turn + 1), self.sems(step, 1), links.below),
                (level < 3) & (3 - level <= turn),
                lambda: links.copy(keep(down + 1), shards(buffer, turn + 1), self.sems(step, 1), links.below),
                lambda: (base + (down + 1) * size, (turn + 1) * size),
                3 - level == turn - 1,
            ),
        ]

    def start(self):
        step = self.step
        plan = self.plan[step]
        if plan[0] == "line":
            for way, (sends, sent, _, _, _, opens) in enumerate(self.lines(step)):

                @pl.when(sends)
                def _():
                    if self.credits is not None:

                        @pl.when(opens)
                        def _():
                            pl.semaphore_wait(self.credits.at[3 + way], 1)

                    sent().start()

            return
        if self.credits is not None and plan[0] != "both":
            pl.semaphore_wait(self.credits.at[0 if plan[0] == "core" else 1 + plan[1]], 1)
        if plan[0] == "both":
            self.out[pl.ds(self.links.core, 1)] = self.keep[pl.ds(self.base, 1)]
        self.single(step).start()

    def add(self, source, first, base, size):
        keep = self.keep

        def body(i, carry):
            keep[base + i] = keep[base + i] + source[first + i]
            return carry

        lax.fori_loop(0, size, body, 0)

    def finish(self):
        step = self.step
        plan = self.plan[step]
        if plan[0] == "line":
            for _, _, comes, arrived, where, _ in self.lines(step):

                @pl.when(comes)
                def _():
                    arrived().wait_recv()
                    base, first = where()
                    self.add(plan[4], first, base, plan[3])

        else:
            self.single(step).wait_recv()
            if plan[0] == "core":
                self.add(self.arrived, 0, 0, 16)
            elif plan[0] == "halve":
                self.add(plan[5], 0, plan[3], plan[4])
        self.step += 1

    def advance(self):
        self.finish()
        if self.step < len(self.plan):
            self.start()

    def close(self):
        for step, plan in enumerate(self.plan):
            if plan[0] == "line":
                for sends, sent, _, _, _, _ in self.lines(step):

                    @pl.when(sends)
                    def _():
                        sent().wait_send()

            else:
                self.single(step).wait_send()


class Total:
    def __init__(self, links, levels, arrived, send_sems, recv_sems, index):
        self.links, self.levels, self.arrived = links, levels, arrived
        level = links.level
        everyone = level >= 0
        near = {"dp": links.lane + 2 - 4 * (level % 2)}
        middle = {"dp": links.lane + 6 - 4 * level}
        inner = (level == 1) | (level == 2)
        outer = {"dp": links.lane - 6 + 4 * level}
        self.turns = [
            (everyone, everyone, links.other_core), (everyone, everyone, links.partner[SECTION]),
            (everyone, everyone, near), (inner, inner, middle), (inner, jnp.logical_not(inner), outer),
            (everyone, everyone, links.partner[SIDE]),
        ]
        self.sems = lambda step: (send_sems.at[index, step, 0], recv_sems.at[index, step, 0])
        self.step = 0
        self.result = levels.at[0]

    def copy_of(self, step):
        return self.links.copy(
            self.levels.at[step % 2], self.arrived.at[step - step // 4], self.sems(step), self.turns[step][2]
        )

    def start(self):
        step = self.step

        @pl.when(self.turns[step][0])
        def _():
            self.copy_of(step).start()

    def sent(self, step):
        @pl.when(self.turns[step][0])
        def _():
            self.copy_of(step).wait_send()

    def advance(self):
        step = self.step
        if step > 0:
            self.sent(step - 1)
        comes = self.turns[step][1]

        @pl.when(comes)
        def _():
            self.copy_of(step).wait_recv()
            value = self.arrived[step - step // 4].astype(F32)
            if step != 4:
                value = self.levels[step % 2].astype(F32) + value
            self.levels[(step + 1) % 2] = value.astype(self.levels.dtype)

        @pl.when(jnp.logical_not(comes))
        def _():
            self.levels[(step + 1) % 2] = self.levels[step % 2]

        self.step += 1
        if self.step < 6:
            self.start()

    def close(self):
        self.sent(5)


IN_NAMES = (
    "low_d", "hidden_d", "active_d", "branch_d", "grad_pair", "cross_memory", "second", "memory", "active",
    "reduce", "slope", "expand", "first", "low", "mixed", "combine", "cross", "packed", "logs", "x", "project",
    "starts", "self_project", "self_combine", "cross_query",
)
ATTEND_BLOCK = 256


def backward_kernel(valid, *refs):
    refs = list(refs)

    def draw(count):
        taken = refs[:count]
        del refs[:count]
        return taken

    source = dict(zip(IN_NAMES, draw(len(IN_NAMES))))
    source["x"] = source["x"].at[lax.axis_index("section")]
    gain_ref, small_ref, tiny_ref = draw(3)
    self_gain_ref, self_shift_ref = draw(2)
    outs = dict(zip(NAMES, draw(len(NAMES))))
    slab_out, grad_memory_out, grad_x_out, self_rows_out, stack_out = draw(5)
    acts = dict(zip(IN_NAMES[:4], draw(4)))
    buffers = {}
    for name in NAMES:
        if name.startswith("decoder"):
            buffers[name] = [None, None] + draw(3)
        elif not name.startswith("encoder_expand"):
            buffers[name] = draw(5)
    keeps = {}
    for name in NAMES:
        if not name.startswith("encoder_expand"):
            keeps[name] = draw(1)[0]
    expand_stages = [draw(3), draw(3)]
    hidden, slope, grad_mixed, resid, mixed, branch, small_levels, small_arrived, tiny_levels, tiny_arrived = draw(10)
    send_sems, recv_sems, slab_sems, load_sems, store_sems, credits = draw(6)
    width = resid.shape[1]
    count = resid.shape[0]
    hidden_size = hidden.shape[1]
    cut = split_of(hidden_size)
    for index, columns in enumerate((pl.ds(0, cut), pl.ds(cut, hidden_size - cut))):
        name = "encoder_expand%d" % index
        rows = lambda start, size: slope.at[pl.ds(start, size), :, columns]
        keeps[name] = rows(0, 16)
        buffers[name] = [rows(16, 16), rows(32, 16)] + expand_stages[index]

    links = Links()
    core = links.core
    block = 256
    chunks = column_chunks(hidden_size)
    own_columns = pl.ds(pl.multiple_of(core * 256, 256), 256)
    other_columns = pl.ds(pl.multiple_of((1 - core) * 256, 256), 256)
    work = {}
    for index, name in enumerate(NAMES):
        sent, arrived, *stages = buffers[name]
        work[name] = Scatter(
            links, GROUPS[name], keeps[name], sent, arrived, stages, send_sems, recv_sems, index, outs[name],
            credits.at[int(name[-1])] if name.startswith("encoder_expand") else None,
        )
    work["small"] = Total(links, small_levels, small_arrived, send_sems, recv_sems, len(NAMES))
    work["tiny"] = Total(links, tiny_levels, tiny_arrived, send_sems, recv_sems, len(NAMES) + 1)

    def tick(label):
        for name in SCHEDULE.get(label, ()):
            work[name].advance()

    def load(name, target):
        copy = pltpu.make_async_copy(source[name], target, load_sems.at[IN_NAMES.index(name)])
        copy.start()
        return copy

    def deal(name, rows, first_column):
        item = work[name]
        columns = pl.ds(first_column, rows.shape[1])
        low = rows.astype(BF16)
        for shard in range(16):
            here = low[32 * shard : 32 * shard + 16]
            there = low[32 * shard + 16 : 32 * shard + 32]
            place = item.place(shard)
            item.keep[place, :, columns] = jnp.where(core == 0, here, there)
            item.sent[place, :, columns] = jnp.where(core == 0, there, here)

    def deal_columns(names, targets, rows):
        size = rows.shape[0] // 16
        for index, (name, target) in enumerate(zip(names, targets)):
            for shard in range(16):
                target[work[name].place(shard)] = rows[
                    size * shard : size * shard + size, LANES * index : LANES * index + LANES
                ].astype(BF16)

    act_loads = {name: load(name, acts[name]) for name in IN_NAMES[:4]}
    links.greet()
    def slab_copies(out):
        parts = [pl.ds(index * (count // 2), count // 2) for index in range(2)]
        return [
            links.copy(
                out.at[part], slab_out.at[part], (slab_sems.at[0, index], slab_sems.at[1, index]), links.partner[SECTION]
            )
            for index, part in enumerate(parts)
        ]

    back_copies = slab_copies(grad_memory_out)
    front_copies = slab_copies(grad_x_out)

    def rows_phase(grad_pair, memory_w, residual, rows_low, reduce_w, expand_w, combine_w):
        loads = {
            name: load(name, target)
            for name, target in (
                ("grad_pair", grad_pair), ("cross_memory", memory_w), ("second", residual), ("active", hidden),
                ("memory", rows_low), ("reduce", reduce_w), ("slope", slope), ("expand", expand_w),
                ("mixed", mixed), ("combine", combine_w),
            )
        }
        small_levels[0] = small_ref[...]
        work["small"].start()

        for name in IN_NAMES[:4]:
            act_loads[name].wait()
        names = ("decoder_reduce0", "decoder_reduce1")
        deal_columns(
            names, [work[name].keep for name in names],
            dot(acts["active_d"][...], acts["branch_d"][:, own_columns], TN),
        )
        for name in names:
            work[name].start()
        tick("dfr")
        for index, (start, size) in enumerate(chunks):
            rows = dot(acts["low_d"][:, own_columns], acts["hidden_d"][:, pl.ds(start, size)], TN).astype(BF16)
            item = work["decoder_expand%d" % (index // 2)]
            columns = pl.ds(start - (index // 2) * cut, size)
            for shard in range(16):
                item.keep[item.place(shard), :, columns] = rows[16 * shard : 16 * shard + 16]
            if index % 2:
                item.start()
                tick("dfe%d" % (index // 2))

        loads["grad_pair"].wait()
        loads["cross_memory"].wait()
        loads["second"].wait()
        sums = None
        for start in range(0, count, block):
            part = pl.ds(start, block)
            low_grad = dot(grad_pair[part, :], memory_w[...], NT).astype(BF16)
            grad_mixed[part, :] = low_grad
            grad = low_grad.astype(F32)
            rows, scale = normed(residual[part, :])
            fresh = [column_sum(grad * rows), column_sum(grad)]
            sums = fresh if sums is None else [old + new for old, new in zip(sums, fresh)]
            total = normed_back(grad, gain_ref[1:2, :], rows, scale)
            resid[part, :] = total
            branch[part, :] = total.astype(BF16)
        memory_store = pltpu.make_async_copy(grad_mixed, grad_memory_out, store_sems.at[0])
        memory_store.start()
        loads["first"] = load("first", residual)
        last_sums = sums

        loads["active"].wait()
        names = ("encoder_reduce0", "encoder_reduce1")
        deal_columns(names, [work[name].sent for name in names], dot(hidden[...], branch[:, other_columns], TN))
        for name in names:
            work[name].start()
        memory_store.wait()

        @pl.when(links.section == 0)
        def _():
            for copy in back_copies:
                copy.start()

        tick("efr0")
        deal_columns(names, [work[name].keep for name in names], dot(hidden[...], branch[:, own_columns], TN))
        tick("efr1")
        loads["memory"].wait()
        deal("middle0", dot(rows_low[...], grad_pair[...], TN), 0)
        loads["low"] = load("low", rows_low)
        work["middle0"].start()
        tick("dwm")
        loads["reduce"].wait()
        loads["slope"].wait()
        for index, (start, size) in enumerate(chunks):
            columns = pl.ds(start, size)
            grad_active = dot(branch[...], reduce_w[columns, :], NT)
            inner = slope[:, :, columns].reshape(count, size).astype(F32)
            hidden[:, columns] = (grad_active * inner).astype(BF16)
            tick("du%d" % index)
        for half in range(2):
            links.tell([credits.at[half, index] for index in range(5)])
        loads["expand"].wait()
        resid[...] += dot(hidden[...], expand_w[...], NT)
        tick("df")

        loads["first"].wait()
        loads["combine"].wait()
        sums = None
        for start in range(0, count, block):
            part = pl.ds(start, block)
            grad = resid[part, :]
            rows, scale = normed(residual[part, :])
            fresh = [column_sum(grad * rows), column_sum(grad)]
            sums = fresh if sums is None else [old + new for old, new in zip(sums, fresh)]
            total = normed_back(grad, gain_ref[0:1, :], rows, scale)
            resid[part, :] = total
            low_grad = total.astype(BF16)
            branch[part, :] = low_grad
            grad_mixed[part, :] = dot(low_grad, combine_w[...], NT).astype(BF16)
        loads["cross"] = load("cross", combine_w)
        tiny_levels[0] = tiny_ref[...]
        tiny_levels[0, 4:8, :] = jnp.concatenate([sums[0], last_sums[0], sums[1], last_sums[1]], axis=0)
        work["tiny"].start()
        tick("ln")
        loads["low"].wait()
        for index, (start, size) in enumerate(chunks):
            name = "encoder_expand%d" % (index // 2)
            deal(name, dot(rows_low[...], hidden[:, pl.ds(start, size)], TN), start - (index // 2) * cut)
            if index % 2:
                work[name].start()
                tick("efe%d" % (index // 2))
        loads["mixed"].wait()
        loads["cross"].wait()
        deal("middle1", combine_w[...].astype(F32), 0)
        deal("middle1", dot(mixed[...], branch[...], NN), width)
        work["middle1"].start()
        tick("dwc")

    pl.run_scoped(
        rows_phase,
        pltpu.VMEM((count, 2 * width), BF16),
        pltpu.VMEM((width, 2 * width), BF16),
        pltpu.VMEM((count, width), F32),
        pltpu.VMEM((count, width), BF16),
        pltpu.VMEM((hidden_size, width), BF16),
        pltpu.VMEM((width, hidden_size), BF16),
        pltpu.VMEM((width, width), BF16),
    )

    def attend_phase(packed, logs, x, project_w, grad_packed, starts, self_project, self_combine, cross_query):
        loads = {
            name: load(name, target)
            for name, target in (
                ("packed", packed), ("logs", logs), ("x", x), ("project", project_w), ("starts", starts),
                ("self_project", self_project), ("self_combine", self_combine), ("cross_query", cross_query),
            )
        }
        loads["packed"].wait()
        loads["logs"].wait()
        pairs = width // LANES
        half = width // 2

        def last(index):
            columns = slice(index * half, index * half + half)
            for third in range(3):
                deal("last%d" % index, dot(x[...], grad_packed[third, :, columns], TN), third * half)
            work["last%d" % index].start()

        for pair in range(pairs):
            columns = pl.ds(pair * LANES, LANES)
            attend_back_pair(
                packed[:, columns],
                packed[:, pl.ds(width + pair * LANES, LANES)],
                packed[:, pl.ds(2 * width + pair * LANES, LANES)],
                grad_mixed[:, columns],
                mixed[columns, :],
                logs[pair],
                grad_packed, columns,
                lambda head: tick("att%d" % (2 * pair + head)),
            )
            if pair == pairs // 2 - 1:
                loads["x"].wait()
                last(0)
                tick("last0")
        loads["project"].wait()
        stores = []
        for index in range(2):
            part = pl.ds(index * (count // 2), count // 2)
            total = resid[part, :]
            for third in range(3):
                total = total + dot(
                    grad_packed[third, part, :], project_w[:, third * width : (third + 1) * width], NT
                )
            packed[part, pl.ds(0, width)] = total.astype(BF16)
            store = pltpu.make_async_copy(packed.at[part, pl.ds(0, width)], grad_x_out.at[part], store_sems.at[1 + index])
            store.start()
            tick("dx%d" % index)
            store.wait()

            @pl.when(links.section == 1)
            def _():
                front_copies[index].start()

        last(1)
        tick("last1")
        for name in IN_NAMES[-4:]:
            loads[name].wait()
        for name in TAIL_FIRST:
            work[name].advance()
        rows = SMALL_ROWS // 2
        start_back(
            valid, starts[...], self_project[...], self_combine[...], cross_query[...], self_gain_ref[0:1, :],
            self_shift_ref[0:1, :], work["small"].result[pl.ds(0, rows), :].astype(F32),
            work["small"].result[pl.ds(rows, rows), :], links, self_rows_out, stack_out,
        )

    pl.run_scoped(
        attend_phase,
        pltpu.VMEM((count, 3 * width), BF16),
        pltpu.VMEM(source["logs"].shape, F32),
        pltpu.VMEM((count, width), BF16),
        pltpu.VMEM((width, 3 * width), BF16),
        pltpu.VMEM((3, count, width), BF16),
        pltpu.VMEM((PAD_ROWS, width), BF16),
        pltpu.VMEM((width, 3 * width), BF16),
        pltpu.VMEM((width, width), BF16),
        pltpu.VMEM((width, width), BF16),
    )
    for name in TAIL:
        work[name].advance()
    stack_out[pl.ds(SMALL_ROWS // 2 + 8, TINY_ROWS), :] = work["tiny"].result[...]
    for copy in back_copies:
        copy.wait_recv()
    for item in work.values():
        item.close()
    for copy in back_copies:
        copy.wait_send()


def start_back(valid, starts, project_w, combine_w, query_w, gain, shift, resid, query_grad, links, rows_out, stack_out):
    width = starts.shape[1]
    own = rows_out.shape[0]
    place = (links.section * 8 + links.lane) * own
    chosen = lax.broadcasted_iota(jnp.int32, (width, own), 0) == place + lax.broadcasted_iota(
        jnp.int32, (width, own), 1
    )
    chosen = jnp.where(chosen, 1.0, 0.0).astype(BF16)
    select = lambda value: dot(value, chosen, NN).astype(BF16)
    queries, keys, values, mixed, kept, rows, scale, first = self_block(
        starts, project_w, combine_w, gain, shift, valid
    )
    rows_out[:, pl.ds(4 * width, width)] = dot(select(first.astype(BF16)), query_grad, TN)
    grad_first = resid + dot(query_grad, query_w, NT)
    gain_sum = column_sum(grad_first * rows)
    shift_sum = column_sum(grad_first)
    grad_resid = normed_back(grad_first, gain, rows, scale)
    branch = grad_resid.astype(BF16)
    rows_out[:, pl.ds(3 * width, width)] = dot(select(mixed), branch, TN)
    grad_mixed = dot(branch, combine_w, NT).astype(BF16)
    dq, dk, dv = few_attend_back(queries, keys, values, kept, grad_mixed)
    grad_packed = jnp.concatenate([dq, dk, dv], axis=1).astype(BF16)
    rows_out[:, pl.ds(0, 3 * width)] = dot(select(starts), grad_packed, TN)
    count = starts.shape[0]
    stack_out[pl.ds(0, count), :] = grad_resid + dot(grad_packed, project_w, NT)
    stack_out[pl.ds(count, 8), :] = jnp.concatenate([gain_sum, shift_sum, jnp.zeros((6, width), F32)], axis=0)


def attend_back_pair(queries, keys, values, grads, mixed, logs, out, columns, between):
    count = queries.shape[0]
    lane = lax.broadcasted_iota(jnp.int32, (1, LANES), 1)
    queries = queries * jnp.asarray(0.125, BF16)
    scaled_keys = keys * jnp.asarray(0.125, BF16)
    queries_t = queries.T
    grads_t = grads.T
    logs = logs.T
    shared = mixed.astype(F32) * grads_t.astype(F32)
    inner = jnp.concatenate([column_sum(shared[:64]), column_sum(shared[64:])], axis=0).T
    dq_parts = [[], []]
    dk_parts = []
    dv_parts = []
    for head in range(2):
        own = (lane < 64) if head == 0 else (lane >= 64)
        head_queries = jnp.where(own, queries, jnp.zeros_like(queries))
        head_grads = jnp.where(own, grads, jnp.zeros_like(grads))
        dk = None
        dv = None
        for start in range(0, count, ATTEND_BLOCK):
            part = slice(start, start + ATTEND_BLOCK)
            scores = dot(head_queries[part], keys, NT)
            probs = jnp.exp(scores - logs[part, head : head + 1])
            grad_probs = dot(head_grads[part], values, NT)
            grad_scores = (probs * (grad_probs - inner[part, head : head + 1])).astype(BF16)
            new_v = dot(grads_t[64 * head : 64 * head + 64, part], probs.astype(BF16), NN)
            new_k = dot(queries_t[64 * head : 64 * head + 64, part], grad_scores, NN)
            dv = new_v if dv is None else dv + new_v
            dk = new_k if dk is None else dk + new_k
            dq_parts[head].append(dot(grad_scores, scaled_keys, NN))
        dk_parts.append(dk)
        dv_parts.append(dv)
        if head == 0:
            between(0)
    out[1, :, columns] = jnp.concatenate(dk_parts, axis=0).T.astype(BF16)
    out[2, :, columns] = jnp.concatenate(dv_parts, axis=0).T.astype(BF16)
    for index in range(count // ATTEND_BLOCK):
        out[0, pl.ds(index * ATTEND_BLOCK, ATTEND_BLOCK), columns] = jnp.where(
            lane < 64, dq_parts[0][index], dq_parts[1][index]
        ).astype(BF16)
    between(1)


def chain_blocks(width, hidden_size):
    cut = split_of(hidden_size)
    blocks = {}
    for side in ("decoder", "encoder"):
        blocks[side + "_expand0"] = (16, cut)
        blocks[side + "_expand1"] = (16, hidden_size - cut)
        blocks[side + "_reduce0"] = (hidden_size // 16, LANES)
        blocks[side + "_reduce1"] = (hidden_size // 16, LANES)
    for name in ("middle0", "middle1"):
        blocks[name] = (16, 2 * width)
    for name in ("last0", "last1"):
        blocks[name] = (16, 3 * width // 2)
    return blocks


def backward_linked(saved, weights):
    count, width = saved["x"].shape[1:]
    small, tiny = saved["small"], saved["tiny"]
    hidden_size = saved["active"].shape[1]
    starts = weights[6]
    valid = starts.shape[0]
    arrays = dict(saved)
    arrays.update(
        cross_memory=weights[10], reduce=weights[3], expand=weights[2], combine=weights[1], project=weights[0],
        self_project=weights[7], self_combine=weights[8], cross_query=weights[9],
        slope=saved["slope"].reshape(count // 16, 16, hidden_size),
    )
    inputs = [arrays[name] for name in IN_NAMES]
    vectors = [weights[4], small, tiny, weights[14], weights[15]]
    blocks = chain_blocks(width, hidden_size)
    own = width // 16
    vmem = lambda counts, name: [pltpu.VMEM((n,) + blocks[name], BF16) for n in counts]
    scratch = [pltpu.VMEM(arrays[name].shape, BF16) for name in IN_NAMES[:4]]
    for name in NAMES:
        if name.startswith("decoder"):
            scratch += vmem(stage_blocks(GROUPS[name]), name)
        elif not name.startswith("encoder_expand"):
            scratch += vmem([16, 16] + stage_blocks(GROUPS[name]), name)
    for name in NAMES:
        if not name.startswith("encoder_expand"):
            scratch += vmem((16,), name)
    for name in ("encoder_expand0", "encoder_expand1"):
        scratch += vmem(stage_blocks(GROUPS[name]), name)
    scratch += [
        pltpu.VMEM((count, hidden_size), BF16),
        pltpu.VMEM((count // 16, 16, hidden_size), BF16),
        pltpu.VMEM((count, width), BF16),
        pltpu.VMEM((count, width), F32),
        pltpu.VMEM((width, count), BF16),
        pltpu.VMEM((count, width), BF16),
        pltpu.VMEM((2,) + small.shape, BF16),
        pltpu.VMEM((5,) + small.shape, BF16),
        pltpu.VMEM((2,) + tiny.shape, F32),
        pltpu.VMEM((5,) + tiny.shape, F32),
        pltpu.SemaphoreType.DMA((len(NAMES) + 2, STEPS, 2)),
        pltpu.SemaphoreType.DMA((len(NAMES) + 2, STEPS, 2)),
        pltpu.SemaphoreType.DMA((2, 2)),
        pltpu.SemaphoreType.DMA((len(IN_NAMES),)),
        pltpu.SemaphoreType.DMA((3,)),
        pltpu.SemaphoreType.REGULAR((2, 5)),
    ]
    in_any = pl.BlockSpec(memory_space=pl.ANY)
    in_vmem = pl.BlockSpec(memory_space=pltpu.VMEM)
    shape = shape_of((count, width), BF16)
    results = pl.pallas_call(
        functools.partial(backward_kernel, valid),
        in_specs=[in_any] * len(IN_NAMES) + [in_vmem] * len(vectors),
        out_specs=[in_vmem] * len(NAMES) + [in_any] * 3 + [in_vmem] * 2,
        out_shape=[shape_of((2,) + blocks[name], BF16) for name in NAMES]
        + [shape] * 3
        + [shape_of((own, 5 * width), F32), shape_of((SMALL_ROWS // 2 + 8 + TINY_ROWS, width), F32)],
        scratch_shapes=scratch,
        compiler_params=pltpu.CompilerParams(
            collective_id=0, has_side_effects=True, vmem_limit_bytes=LINKED_VMEM_BYTES
        ),
        cost_estimate=pl.CostEstimate(flops=10**8, bytes_accessed=10**8, transcendentals=0),
    )(*inputs, *vectors)
    return results[: len(NAMES)], *results[len(NAMES) :]


def finish_kernel(valid, joints, *refs):
    refs = list(refs)

    def draw(count):
        taken = refs[:count]
        del refs[:count]
        return taken

    count = len(NAMES)
    sources = draw(count + 7)
    targets = draw(19)
    held = draw(count + 7)
    results = draw(17)
    load_sems, store_sems = draw(2)
    loads = []
    for index in list(range(count, count + 7)) + list(range(count)):
        copy = pltpu.make_async_copy(sources[index], held[index], load_sems.at[index])
        copy.start()
        loads.append((index, copy))
    loads = dict(loads)
    stores = []
    section = lax.axis_index("section")
    memory, other, grad_x, grad_memory, other_slab = held[count + 2 :]
    memory_out, slab_out = targets[:2]

    def store(result):
        index = next(i for i, item in enumerate(results) if item is result)
        stores.append(pltpu.make_async_copy(result, targets[2 + index], store_sems.at[2 + index]))
        stores[-1].start()

    (
        project_e, combine_e, expand_e, reduce_e, gains_e, shifts_e, starts_d, project_d, combine_d, query_d,
        memory_d, cross_d, expand_d, reduce_d, gains_d, shifts_d, head_d,
    ) = results
    halves = dict(zip(NAMES, held[:count]))
    rows_ref, stack_ref = held[count : count + 2]
    width = memory.shape[1]
    own = rows_ref.shape[0]
    place = (section * 8 + lax.axis_index("dp")) * own
    loads[count].wait()
    loads[count + 1].wait()
    project_d[...] = rows_ref[:, : 3 * width]
    store(project_d)
    combine_d[...] = rows_ref[:, 3 * width : 4 * width]
    store(combine_d)
    query_d[...] = rows_ref[:, 4 * width :]
    store(query_d)
    chosen = lax.broadcasted_iota(jnp.int32, (width, own), 0) == place + lax.broadcasted_iota(
        jnp.int32, (width, own), 1
    )
    chosen = jnp.where(chosen, 1.0, 0.0)
    exact = functools.partial(lax.dot_general, precision=lax.Precision.HIGHEST, preferred_element_type=F32)
    picked = exact(stack_ref[pl.ds(PAD_ROWS, 8 + TINY_ROWS), :], chosen, NN)
    starts_d[...] = exact(chosen, stack_ref[pl.ds(0, PAD_ROWS), :], (((0,), (1,)), ((), ())))[:, :valid]
    store(starts_d)
    gains_d[...] = jnp.concatenate([picked[0:1], picked[8:10]], axis=0)
    shifts_d[...] = jnp.concatenate([picked[1:2], picked[10:12]], axis=0)
    gains_e[...] = picked[12:14]
    shifts_e[...] = picked[14:16]
    head_d[...] = picked[16 : 16 + joints]
    for result in (gains_d, shifts_d, gains_e, shifts_e, head_d):
        store(result)
    for index in range(count + 2, count + 7):
        loads[index].wait()
    for index, (out, front, back) in enumerate(
        (
            ((memory_out.at[0], memory_out.at[1]), (memory, other), (other, memory)),
            ((slab_out.at[0, 0], slab_out.at[0, 1]), (grad_x, other_slab), (other_slab, grad_memory)),
        )
    ):
        for way in range(2):
            ahead = pltpu.make_async_copy(front[way], out[way], store_sems.at[19 + 2 * index + way])
            behind = pltpu.make_async_copy(back[way], out[way], store_sems.at[19 + 2 * index + way])

            @pl.when(section == 0)
            def _():
                ahead.start()

            @pl.when(section == 1)
            def _():
                behind.start()

            stores.append(ahead)

    for index in range(count):
        loads[index].wait()

    def rows_of(name, out, columns, first=0):
        for core in range(2):
            out[pl.ds(16 * core, 16), columns] = halves[name][core, :, first : first + columns.size].astype(F32)

    cut = halves["encoder_expand0"].shape[2]
    for side, out in (("encoder", expand_e), ("decoder", expand_d)):
        rows_of(side + "_expand0", out, pl.ds(0, cut))
        rows_of(side + "_expand1", out, pl.ds(cut, out.shape[1] - cut))
        store(out)
    for side, out in (("encoder", reduce_e), ("decoder", reduce_d)):
        for core in range(2):
            for index in range(2):
                out[:, pl.ds((2 * core + index) * LANES, LANES)] = halves[side + "_reduce%d" % index][core].astype(F32)
        store(out)
    rows_of("middle0", memory_d, pl.ds(0, 2 * width))
    store(memory_d)
    rows_of("middle1", cross_d, pl.ds(0, width))
    store(cross_d)
    rows_of("middle1", combine_e, pl.ds(0, width), width)
    store(combine_e)
    half = width // 2
    for third in range(3):
        for index in range(2):
            rows_of("last%d" % index, project_e, pl.ds(third * width + index * half, half), third * half)
    store(project_e)
    for copy in stores:
        copy.wait()


def finish(valid, joints, halves, rows, stack, memory, other, grad_x, grad_memory, other_slab):
    count, width = memory.shape
    own = rows.shape[0]
    hidden_size = halves[0].shape[2] + halves[1].shape[2]
    in_any = pl.BlockSpec(memory_space=pl.ANY)
    shapes = [
        (own, 3 * width), (own, width), (own, hidden_size), (hidden_size // 16, width), (2, own), (2, own),
        (own, valid), (own, 3 * width), (own, width), (own, width), (own, 2 * width), (own, width),
        (own, hidden_size), (hidden_size // 16, width), (3, own), (3, own), (joints, own),
    ]
    inputs = (*halves, rows, stack, memory, other, grad_x, grad_memory, other_slab)
    results = list(
        call(
            functools.partial(finish_kernel, valid, joints),
            10**6, 10**7,
            in_specs=[in_any] * len(inputs),
            out_specs=[in_any] * (2 + len(shapes)),
            out_shape=[shape_of((2, count, width), BF16), shape_of((1, 2, count, width), BF16)]
            + [shape_of(dims, F32) for dims in shapes],
            scratch_shapes=[pltpu.VMEM(item.shape, item.dtype) for item in inputs]
            + [pltpu.VMEM(dims, F32) for dims in shapes]
            + [pltpu.SemaphoreType.DMA((len(inputs),)), pltpu.SemaphoreType.DMA((23,))],
        )(*inputs)
    )
    results[8] = results[8].T
    results[18] = results[18].T
    return tuple(results)


def swap(value, axis, bit):
    pairs = [(i, i ^ (1 << bit)) for i in range(lax.axis_size(axis))]
    return lax.ppermute(value, axis, pairs)


def plain_scatter(full):
    part = lax.psum_scatter(full.astype(F32), ("section", "dp"), scatter_dimension=0, tiled=True)
    return lax.psum(part, "rep")


def per_device(x, targets, arms, *weights):
    section = lax.axis_index("section")
    sections = lax.axis_size("section")
    lanes = lax.axis_size("dp")
    count = x.shape[0] // sections
    starts, head = weights[6], weights[16]
    valid, joints = starts.shape[0], head.shape[1]
    width = starts.shape[1]
    first = section == 0
    place = section * lanes + lax.axis_index("dp")
    own = width // (sections * lanes)
    linked = (sections, lanes, lax.axis_size("rep"), count) == (2, 8, 2, 1)
    saved = []
    for index in range(count):
        pick = functools.partial(lambda i: lax.axis_index("section") * count + i, index)
        saved.append(forward(x, targets, arms, pick, weights, linked))
    if linked:
        other = swap(saved[0]["memory"], "section", 0)
        halves, other_slab, grad_memory, grad_x, rows, stack = backward_linked(saved[0], weights)
        return finish(
            valid, joints, halves, rows, stack, saved[0]["memory"], other, grad_x, grad_memory, other_slab
        )
    memory = jnp.concatenate([item["memory"][None] for item in saved])
    results = []
    for index, item in enumerate(saved):
        results.append(
            backward_alone(item, lax.dynamic_index_in_dim(x, section * count + index, 0, keepdims=False), weights)
        )
    grad_x = jnp.concatenate([item[0][None] for item in results])
    grad_memory = jnp.concatenate([item[1][None] for item in results])
    total = lambda name: functools.reduce(jnp.add, [item[2][name] for item in results])
    other = swap(memory, "section", 0)
    other_slab = swap(jnp.where(first, grad_memory, grad_x), "section", 0)
    small = lax.psum(total("small"), ("section", "dp", "rep"))
    tiny = lax.psum(total("tiny"), ("section", "dp", "rep"))
    done = {
        name: plain_scatter(total(name))
        for name in ("decoder_expand", "decoder_reduce", "encoder_expand", "encoder_reduce", "middle", "last")
    }
    memory_out = jnp.concatenate([jnp.where(first, memory, other), jnp.where(first, other, memory)])
    slab = jnp.concatenate(
        [jnp.where(first, grad_x, other_slab), jnp.where(first, other_slab, grad_memory)]
    )[None]

    columns_of = lambda array: lax.dynamic_slice_in_dim(array, place * own, own, 1)
    rows_of = lambda array: lax.dynamic_slice_in_dim(array, place * own, own, 0)
    resid_d, query_d = small[:PAD_ROWS], small[PAD_ROWS:]
    start_grad, project_d, combine_d, query_w, sums_s = decode_start_back(
        valid, jnp.pad(starts, ((0, PAD_ROWS - valid), (0, 0))), weights[7], weights[8], weights[9],
        weights[14], weights[15], resid_d, query_d,
    )
    gains_d = jnp.concatenate([sums_s[0:1], tiny[0:2]])
    shifts_d = jnp.concatenate([sums_s[1:2], tiny[2:4]])
    return (
        memory_out,
        slab,
        done["last"],
        done["middle"][:, 3 * width :],
        done["encoder_expand"],
        done["encoder_reduce"],
        columns_of(tiny[4:6]),
        columns_of(tiny[6:8]),
        columns_of(start_grad[:valid]),
        rows_of(project_d),
        rows_of(combine_d),
        rows_of(query_w),
        done["middle"][:, : 2 * width],
        done["middle"][:, 2 * width : 3 * width],
        done["decoder_expand"],
        done["decoder_reduce"],
        columns_of(gains_d),
        columns_of(shifts_d),
        rows_of(tiny[8 : 8 + joints].T),
    )


def solution(mesh):
    spread = ("section", "dp")
    rows = P(spread, None)
    columns = P(None, spread)
    return jax.shard_map(
        per_device,
        mesh=mesh,
        in_specs=(P(("dp", "rep"), None, None), P(("dp", "rep"), None, None), P(("dp", "rep"))) + (P(),) * 17,
        out_specs=(
            P(("dp", "rep"), None, None),
            P("section", ("dp", "rep"), None, None),
            rows, rows, rows, rows, columns, columns, columns,
            rows, rows, rows, rows, rows, rows, rows, columns, columns, rows,
        ),
        check_vma=False,
    )
```

```python
import functools

import jax
import jax.numpy as jnp
from jax import lax
from jax.experimental import pallas as pl
from jax.experimental.pallas import tpu as pltpu
from jax.sharding import PartitionSpec as P

HEADS = 8
EPSILON = 1e-05
LANES = 128
PAD_ROWS = 112
SMALL_ROWS = 2 * PAD_ROWS
TINY_ROWS = 24
F32 = jnp.float32
BF16 = jnp.bfloat16
NN = (((1,), (0,)), ((), ()))
NT = (((1,), (1,)), ((), ()))
TN = (((0,), (0,)), ((), ()))
VMEM_BYTES = 56 * 1024 * 1024
LINKED_VMEM_BYTES = 638 * 1024 * 1024 // 10
ROOT_2_PI = 0.7978845608028654
CUBE = 0.044715


def dot(left, right, dims):
    return lax.dot_general(left, right, dims, preferred_element_type=F32)


def call(kernel, flops, moved, **options):
    return pl.pallas_call(
        kernel,
        compiler_params=pltpu.CompilerParams(vmem_limit_bytes=VMEM_BYTES),
        cost_estimate=pl.CostEstimate(flops=flops, bytes_accessed=moved, transcendentals=0),
        **options,
    )


def shape_of(dims, dtype):
    return jax.ShapeDtypeStruct(dims, dtype)


def whole(array):
    rank = len(array.shape)
    return pl.BlockSpec(array.shape, lambda *_: (0,) * rank, pipeline_mode=pl.Buffered(1))


def normed(residual):
    centre = jnp.mean(residual, axis=-1, keepdims=True)
    centred = residual - centre
    spread = jnp.mean(centred * centred, axis=-1, keepdims=True)
    scale = lax.rsqrt(spread + EPSILON)
    return centred * scale, scale


def normed_back(grad, gain, rows, scale):
    weighted = grad * gain
    return scale * (
        weighted
        - jnp.mean(weighted, axis=-1, keepdims=True)
        - rows * jnp.mean(weighted * rows, axis=-1, keepdims=True)
    )


def gelu_and_slope(value):
    square = value * value
    bend = jnp.tanh(value * (ROOT_2_PI + (ROOT_2_PI * CUBE) * square))
    half = 0.5 + 0.5 * bend
    slope = half + value * (0.5 - 0.5 * bend * bend) * (
        ROOT_2_PI + (3.0 * ROOT_2_PI * CUBE) * square
    )
    return value * half, slope


def column_sum(value):
    return jnp.sum(value, axis=0, keepdims=True)


FORWARD_WEIGHTS = ("project", "combine", "expand", "reduce", "memory_w")
FORWARD_OUTS = ("packed", "mixed", "logs", "first", "low", "active", "slope", "second", "memory", "pair")


def split_of(hidden_size):
    return hidden_size // 256 * 128 + 128


def column_chunks(hidden_size):
    cut = split_of(hidden_size)
    return [(0, 896), (896, cut - 896), (cut, 768), (cut + 768, hidden_size - cut - 768)]


def attend_all(packed, mixed_ref, log_ref):
    count, width = packed.shape[0], packed.shape[1] // 3
    lane = lax.broadcasted_iota(jnp.int32, (1, LANES), 1)
    heads = width // 64
    columns = lambda third, head: pl.ds(third * width + head // 2 * LANES, LANES)

    def scores_of(head):
        keys = packed[:, columns(1, head)]
        own = (lane < 64) if head % 2 == 0 else (lane >= 64)
        queries = packed[:, columns(0, head)] * jnp.asarray(0.125, BF16)
        return dot(jnp.where(own, keys, jnp.zeros_like(keys)), queries, NT)

    scores = scores_of(0)
    for head in range(heads):
        following = scores_of(head + 1) if head + 1 < heads else None
        if head % 2 == 0:
            values = packed[:, columns(2, head)].T
        extended = jnp.concatenate(
            [values[64 * (head % 2) : 64 * (head % 2) + 64], jnp.ones((16, count), BF16)], axis=0
        )
        largest = jnp.max(scores, axis=0, keepdims=True)
        raised = jnp.exp(scores - largest).astype(BF16)
        mixed = dot(extended, raised, NN)
        total = mixed[64:65]
        mixed_ref[pl.ds(64 * head, 64), :] = (mixed[:64] * (1.0 / total)).astype(BF16)
        log_ref[head // 2, pl.ds(head % 2, 1), :] = largest + jnp.log(total)
        scores = following


def encode_kernel(pick, x_ref, *refs):
    refs = list(refs)

    def draw(count):
        taken = refs[:count]
        del refs[:count]
        return taken

    weights = dict(zip(FORWARD_WEIGHTS, draw(5)))
    gain_ref, shift_ref = draw(2)
    outs = dict(zip(FORWARD_OUTS, draw(10)))
    held = dict(zip(FORWARD_WEIGHTS, draw(5)))
    kept = dict(zip(FORWARD_OUTS, draw(10)))
    x, load_sems, store_sems = draw(3)
    here = pltpu.make_async_copy(x_ref.at[pick()], x, load_sems.at[5])
    here.start()
    loads = {}
    for index, name in enumerate(FORWARD_WEIGHTS):
        loads[name] = pltpu.make_async_copy(weights[name], held[name], load_sems.at[index])
        loads[name].start()
    stores = []

    def store(name):
        index = FORWARD_OUTS.index(name)
        stores.append(pltpu.make_async_copy(kept[name], outs[name], store_sems.at[index]))
        stores[-1].start()

    count, width = x.shape
    hidden_size = held["expand"].shape[1]
    block = 256
    here.wait()
    loads["project"].wait()
    for third in range(3):
        columns = pl.ds(third * width, width)
        kept["packed"][:, columns] = dot(x[...], held["project"][:, columns], NN).astype(BF16)
    store("packed")
    attend_all(kept["packed"], kept["mixed"], kept["logs"])
    store("mixed")
    store("logs")
    loads["combine"].wait()
    first, low, second = kept["first"], kept["low"], kept["second"]
    first[...] = x[...].astype(F32) + dot(kept["mixed"][...], held["combine"][...], TN)
    for start in range(0, count, block):
        part = pl.ds(start, block)
        rows, _ = normed(first[part, :])
        value = rows * gain_ref[0:1, :] + shift_ref[0:1, :]
        second[part, :] = value
        low[part, :] = value.astype(BF16)
    store("first")
    store("low")
    loads["expand"].wait()
    chunks = column_chunks(hidden_size)
    before = lambda item: dot(low[...], held["expand"][:, pl.ds(*item)], NN)
    ahead = before(chunks[0])
    for index, (start, size) in enumerate(chunks):
        current = ahead
        if index + 1 < len(chunks):
            ahead = before(chunks[index + 1])
        active, slope = gelu_and_slope(current)
        columns = pl.ds(start, size)
        kept["active"][:, columns] = active.astype(BF16)
        kept["slope"][:, columns] = slope.astype(BF16)
    store("active")
    store("slope")
    loads["reduce"].wait()
    second[...] += dot(kept["active"][...], held["reduce"][...], NN)
    memory = kept["memory"]
    for start in range(0, count, block):
        part = pl.ds(start, block)
        rows, _ = normed(second[part, :])
        memory[part, :] = (rows * gain_ref[1:2, :] + shift_ref[1:2, :]).astype(BF16)
    store("second")
    store("memory")
    loads["memory_w"].wait()
    kept["pair"][...] = dot(memory[...], held["memory_w"][...], NN).astype(BF16)
    store("pair")
    for copy in stores:
        copy.wait()


def encode(x, pick, weights, gains, shifts):
    count, width = x.shape[1:]
    hidden_size = weights[2].shape[1]
    shapes = [
        ((count, 3 * width), BF16), ((width, count), BF16), ((width // LANES, 2, count), F32), ((count, width), F32),
        ((count, width), BF16), ((count, hidden_size), BF16), ((count, hidden_size), BF16), ((count, width), F32),
        ((count, width), BF16), ((count, 2 * width), BF16),
    ]
    in_any = pl.BlockSpec(memory_space=pl.ANY)
    in_vmem = pl.BlockSpec(memory_space=pltpu.VMEM)
    results = call(
        functools.partial(encode_kernel, pick),
        2 * count * width * (2 * hidden_size + 6 * width) + 4 * count * count * width,
        count * (hidden_size * 4 + width * 24) + 8 * width * hidden_size,
        in_specs=[in_any] * 6 + [in_vmem] * 2,
        out_specs=[in_any] * 10,
        out_shape=[shape_of(dims, kind) for dims, kind in shapes],
        scratch_shapes=[pltpu.VMEM(item.shape, BF16) for item in weights]
        + [pltpu.VMEM(dims, kind) for dims, kind in shapes]
        + [pltpu.VMEM((count, width), BF16), pltpu.SemaphoreType.DMA((6,)), pltpu.SemaphoreType.DMA((10,))],
    )(x, *weights, gains, shifts)
    return dict(zip(FORWARD_OUTS, results))


def attend_back_kernel(block, q_ref, k_ref, v_ref, do_ref, mixed_ref, log_ref, dq_ref, dk_ref, dv_ref):
    count = q_ref.shape[0]
    lane = lax.broadcasted_iota(jnp.int32, (1, LANES), 1)
    keys = k_ref[...]
    values = v_ref[...]
    queries = q_ref[...] * jnp.asarray(0.125, BF16)
    scaled_keys = keys * jnp.asarray(0.125, BF16)
    grads = do_ref[...]
    queries_t = queries.T
    grads_t = grads.T
    logs = log_ref[0].T
    shared = mixed_ref[...].astype(F32) * grads_t.astype(F32)
    inner = jnp.concatenate([column_sum(shared[:64]), column_sum(shared[64:])], axis=0).T
    dq_parts = [[], []]
    dk_parts = []
    dv_parts = []
    for head in range(2):
        own = (lane < 64) if head == 0 else (lane >= 64)
        head_queries = jnp.where(own, queries, jnp.zeros_like(queries))
        head_grads = jnp.where(own, grads, jnp.zeros_like(grads))
        dk = None
        dv = None
        for start in range(0, count, block):
            part = slice(start, start + block)
            scores = dot(head_queries[part], keys, NT)
            probs = jnp.exp(scores - logs[part, head : head + 1])
            grad_probs = dot(head_grads[part], values, NT)
            grad_scores = (probs * (grad_probs - inner[part, head : head + 1])).astype(BF16)
            new_v = dot(grads_t[64 * head : 64 * head + 64, part], probs.astype(BF16), NN)
            new_k = dot(queries_t[64 * head : 64 * head + 64, part], grad_scores, NN)
            dv = new_v if dv is None else dv + new_v
            dk = new_k if dk is None else dk + new_k
            dq_parts[head].append(dot(grad_scores, scaled_keys, NN))
        dk_parts.append(dk)
        dv_parts.append(dv)
    dk_ref[...] = jnp.concatenate(dk_parts, axis=0).T.astype(BF16)
    dv_ref[...] = jnp.concatenate(dv_parts, axis=0).T.astype(BF16)
    for index in range(count // block):
        dq_ref[pl.ds(index * block, block), :] = jnp.where(
            lane < 64, dq_parts[0][index], dq_parts[1][index]
        ).astype(BF16)


def attend_back(packed, grad_mixed, mixed, logs):
    rows, width = packed.shape[0], packed.shape[1] // 3
    pairs = width // LANES
    column = lambda first: pl.BlockSpec((rows, LANES), lambda j: (0, first + j))
    return call(
        functools.partial(attend_back_kernel, 256),
        10 * rows * rows * width * 3,
        rows * width * 16,
        grid=(pairs,),
        in_specs=[
            column(0),
            column(pairs),
            column(2 * pairs),
            column(0),
            pl.BlockSpec((LANES, rows), lambda j: (j, 0)),
            pl.BlockSpec((1, 2, rows), lambda j: (j, 0, 0)),
        ],
        out_specs=[column(0)] * 3,
        out_shape=[shape_of((rows, width), BF16)] * 3,
    )(packed, packed, packed, grad_mixed, mixed, logs)

def encode_back_kernel(
    pair_ref, first_ref, second_ref, slope_ref, combine_ref, expand_ref, reduce_ref, gain_ref, memory_w_ref,
    grad_memory_ref, branch_ref, hidden_ref, resid_ref, low_ref, mixed_ref, sums_ref,
):
    grad_memory = dot(pair_ref[...], memory_w_ref[...], NT).astype(BF16)
    grad_memory_ref[...] = grad_memory
    grad_last = grad_memory.astype(F32)
    rows, scale = normed(second_ref[...])
    gain_last = column_sum(grad_last * rows)
    shift_last = column_sum(grad_last)
    grad_second = normed_back(grad_last, gain_ref[1:2, :], rows, scale)
    branch = grad_second.astype(BF16)
    branch_ref[...] = branch
    total = grad_second
    hidden_size = expand_ref.shape[1]
    step = hidden_size // 5
    for start in range(0, hidden_size, step):
        part = pl.ds(start, step)
        grad_active = dot(branch, reduce_ref[part, :], NT)
        grad_hidden = (grad_active * slope_ref[:, part].astype(F32)).astype(BF16)
        hidden_ref[:, part] = grad_hidden
        total = total + dot(grad_hidden, expand_ref[:, part], NT)
    rows, scale = normed(first_ref[...])
    gain_first = column_sum(total * rows)
    shift_first = column_sum(total)
    grad_first = normed_back(total, gain_ref[0:1, :], rows, scale)
    resid_ref[...] = grad_first
    low = grad_first.astype(BF16)
    low_ref[...] = low
    mixed_ref[...] = dot(low, combine_ref[...], NT).astype(BF16)
    fresh = jnp.concatenate(
        [gain_first, gain_last, shift_first, shift_last, jnp.zeros((4, gain_first.shape[1]), F32)], axis=0
    )

    @pl.when(pl.program_id(0) == 0)
    def _():
        sums_ref[...] = fresh

    @pl.when(pl.program_id(0) > 0)
    def _():
        sums_ref[...] += fresh


def encode_back(grad_pair, first, second, slope, combine_w, expand_w, reduce_w, gains, memory_w):
    rows, width = first.shape
    hidden = expand_w.shape[1]
    block = 256
    line = lambda size: pl.BlockSpec((block, size), lambda i: (i, 0))
    sizes = [(width, BF16), (width, BF16), (hidden, BF16), (width, F32), (width, BF16), (width, BF16)]
    return call(
        encode_back_kernel,
        2 * rows * width * (2 * hidden + 3 * width),
        rows * (hidden * 4 + width * 18) + 8 * width * hidden,
        grid=(rows // block,),
        in_specs=[line(2 * width), line(width), line(width), line(hidden)]
        + [whole(item) for item in (combine_w, expand_w, reduce_w, gains, memory_w)],
        out_specs=[line(size) for size, _ in sizes] + [pl.BlockSpec((8, width), lambda i: (0, 0))],
        out_shape=[shape_of((rows, size), kind) for size, kind in sizes] + [shape_of((8, width), F32)],
    )(grad_pair, first, second, slope, combine_w, expand_w, reduce_w, gains, memory_w)


def stacked(rows):
    lane = lax.broadcasted_iota(jnp.int32, (1, rows.shape[1]), 1)
    return jnp.concatenate(
        [jnp.where((lane >= 64 * h) & (lane < 64 * h + 64), rows, jnp.zeros_like(rows)) for h in range(4)],
        axis=0,
    )


def unstacked(rows):
    lane = lax.broadcasted_iota(jnp.int32, (1, rows.shape[1]), 1)
    count = rows.shape[0] // 4
    result = rows[:count]
    for h in range(1, 4):
        result = jnp.where(lane >= 64 * h, rows[h * count : h * count + count], result)
    return result


def few_attend(queries, keys, values, valid):
    mixed = []
    kept = []
    for half in range(2):
        part = slice(256 * half, 256 * half + 256)
        scores = dot(stacked(queries[:, part] * jnp.asarray(0.125, BF16)), keys[:, part], NT)
        if valid < scores.shape[1]:
            column = lax.broadcasted_iota(jnp.int32, (1, scores.shape[1]), 1)
            scores = jnp.where(column < valid, scores, -1e30)
        raised = jnp.exp(scores - jnp.max(scores, axis=1, keepdims=True))
        probs = raised * (1.0 / jnp.sum(raised, axis=1, keepdims=True))
        mixed.append(unstacked(dot(probs.astype(BF16), values[:, part], NN)))
        kept.append(probs)
    return jnp.concatenate(mixed, axis=1).astype(BF16), kept


def few_attend_back(queries, keys, values, kept, grads):
    dq, dk, dv = [], [], []
    for half in range(2):
        part = slice(256 * half, 256 * half + 256)
        probs = kept[half]
        own_queries = stacked(queries[:, part] * jnp.asarray(0.125, BF16))
        own_grads = stacked(grads[:, part])
        grad_probs = dot(own_grads, values[:, part], NT)
        product = probs * grad_probs
        grad_scores = (product - probs * jnp.sum(product, axis=1, keepdims=True)).astype(BF16)
        dv.append(dot(probs.astype(BF16), own_grads, TN))
        dk.append(dot(grad_scores, own_queries, TN))
        dq.append(unstacked(dot(grad_scores, keys[:, part], NN)) * 0.125)
    return jnp.concatenate(dq, axis=1), jnp.concatenate(dk, axis=1), jnp.concatenate(dv, axis=1)


def self_block(starts, project_w, combine_w, gain, shift, valid):
    width = starts.shape[1]
    packed = dot(starts, project_w, NN).astype(BF16)
    queries, keys, values = (packed[:, i * width : (i + 1) * width] for i in range(3))
    mixed, kept = few_attend(queries, keys, values, valid)
    residual = starts.astype(F32) + dot(mixed, combine_w, NN)
    rows, scale = normed(residual)
    return queries, keys, values, mixed, kept, rows, scale, rows * gain + shift


def dealt(rows):
    width = rows.shape[1]
    source = lax.broadcasted_iota(jnp.int32, (width, width), 0)
    target = lax.broadcasted_iota(jnp.int32, (width, width), 1)
    half = width // 2
    wanted = (target % half) // 16 * 32 + target // half * 16 + target % 16
    return dot(rows, jnp.where(source == wanted, 1.0, 0.0).astype(BF16), NN).astype(BF16)


def undealt(columns):
    count, width = columns.shape
    return columns.reshape(count, 2, width // 32, 16).transpose(0, 2, 1, 3).reshape(count, width)


DECODE_WEIGHTS = ("self_project", "self_combine", "cross_query", "pair", "cross_combine", "expand", "reduce")


def cross_attend(queries_ref, pair, stash, mixed_ref):
    width = queries_ref.shape[1]
    rows = 4 * queries_ref.shape[0]

    def half_of(half, carry):
        columns = pl.ds(half * 256, 256)
        value_columns = pl.ds(width + half * 256, 256)
        scores = dot(stacked(queries_ref[:, columns] * jnp.asarray(0.125, BF16)), pair[:, columns], NT)
        raised = jnp.exp(scores - jnp.max(scores, axis=1, keepdims=True))
        probs = (raised * (1.0 / jnp.sum(raised, axis=1, keepdims=True))).astype(BF16)
        stash[pl.ds(half * rows, rows), : pair.shape[0]] = probs
        mixed_ref[:, columns] = unstacked(dot(probs, pair[:, value_columns], NN)).astype(BF16)
        return carry

    for half in range(2):
        half_of(half, None)


def cross_attend_back(queries_ref, pair, stash, grads_ref):
    width = queries_ref.shape[1]
    rows = 4 * queries_ref.shape[0]

    def half_of(half, carry):
        columns = pl.ds(half * 256, 256)
        value_columns = pl.ds(width + half * 256, 256)
        low = stash[pl.ds(half * rows, rows), : pair.shape[0]]
        own_queries = stacked(queries_ref[:, columns] * jnp.asarray(0.125, BF16))
        own_grads = stacked(grads_ref[:, columns])
        probs = low.astype(F32)
        grad_probs = dot(own_grads, pair[:, value_columns], NT)
        inner = jnp.sum(probs * grad_probs, axis=1, keepdims=True)
        grad_scores = (probs * (grad_probs - inner)).astype(BF16)
        dq = unstacked(dot(grad_scores, pair[:, columns], NN)) * 0.125
        pair[:, value_columns] = dot(low, own_grads, TN).astype(BF16)
        pair[:, columns] = dot(grad_scores, own_queries, TN).astype(BF16)
        queries_ref[:, columns] = dq.astype(BF16)
        return carry

    for half in range(2):
        half_of(half, None)


def decode_body(
    pick, valid, loads, held, starts, gain_ref, shift_ref, head_ref, target_ref, arm_ref, acts, hand_out, stash, rooms
):
    for name in ("self_project", "self_combine"):
        loads[name].wait()
    width = starts.shape[1]
    first = self_block(
        starts[...], held["self_project"][...], held["self_combine"][...], gain_ref[0:1, :], shift_ref[0:1, :], valid
    )[-1]
    loads["cross_query"].wait()
    queries, mixed_rows, grads = rooms
    queries[...] = dot(first.astype(BF16), held["cross_query"][...], NN).astype(BF16)
    loads["pair"].wait()
    cross_attend(queries, held["pair"], stash, mixed_rows)
    mixed = mixed_rows[...]
    loads["cross_combine"].wait()
    second_rows, second_scale = normed(first + dot(mixed, held["cross_combine"][...], NN))
    second = second_rows * gain_ref[1:2, :] + shift_ref[1:2, :]
    second_low = second.astype(BF16)
    own = pl.ds(0, PAD_ROWS)
    acts["low_d"][own, :] = dealt(second_low)
    hand_out("low_d")
    loads["expand"].wait()
    loads["reduce"].wait()
    expand_ref, reduce_ref = held["expand"], held["reduce"]
    chunks = column_chunks(expand_ref.shape[1])
    total = second
    slope_rows = pl.ds(8 * PAD_ROWS, PAD_ROWS)
    for start, size in chunks:
        part = pl.ds(start, size)
        active, slope = gelu_and_slope(dot(second_low, expand_ref[:, part], NN))
        stash[slope_rows, part] = slope.astype(BF16)
        active = active.astype(BF16)
        acts["active_d"][own, part] = active
        total = total + dot(active, reduce_ref[part, :], NN)
    hand_out("active_d")
    third_rows, third_scale = normed(total)
    third_low = (third_rows * gain_ref[2:3, :] + shift_ref[2:3, :]).astype(BF16)
    here = pick()
    joints, rows = head_ref.shape[0], starts.shape[0]
    target = target_ref[:, 0, :]
    for index in range(1, target_ref.shape[1]):
        target = jnp.where(here == index, target_ref[:, index, :], target)
    target = jnp.concatenate([target, jnp.zeros((joints, rows - valid), F32)], axis=1)
    misfit = dot(head_ref[...], third_low, NT) - target
    arms = arm_ref[here]
    joint = lax.broadcasted_iota(jnp.int32, misfit.shape, 0)
    row = lax.broadcasted_iota(jnp.int32, misfit.shape, 1)
    factor = 2.0 / jnp.full((1, 1), arms, jnp.int32).astype(F32)
    used = (row < valid) & (joint < joints // 2 * arms)
    grad_pred = jnp.where(used, factor * misfit * lax.rsqrt(misfit * misfit + 1.0), 0.0).astype(BF16)
    head_grad = dot(grad_pred, third_low, NN)
    grad_third = dot(grad_pred, head_ref[...], TN)
    gain_third = column_sum(grad_third * third_rows)
    shift_third = column_sum(grad_third)
    total = normed_back(grad_third, gain_ref[2:3, :], third_rows, third_scale)
    branch = total.astype(BF16)
    acts["branch_d"][own, :] = branch
    hand_out("branch_d")
    for start, size in chunks:
        part = pl.ds(start, size)
        grad_hidden = (dot(branch, reduce_ref[part, :], NT) * stash[slope_rows, part].astype(F32)).astype(BF16)
        acts["hidden_d"][own, part] = grad_hidden
        total = total + dot(grad_hidden, expand_ref[:, part], NT)
    hand_out("hidden_d")
    gain_second = column_sum(total * second_rows)
    shift_second = column_sum(total)
    grad_second = normed_back(total, gain_ref[1:2, :], second_rows, second_scale)
    branch = grad_second.astype(BF16)
    grads[...] = dot(branch, held["cross_combine"][...], NT).astype(BF16)
    cross_attend_back(queries, held["pair"], stash, grads)
    sums = jnp.concatenate([gain_second, gain_third, shift_second, shift_third], axis=0)
    return branch, queries[...], mixed, sums, head_grad


DECODE_VECTORS = ("gains", "shifts", "head", "targets")


def decode_kernel(pick, starts_ref, *refs):
    refs = list(refs)

    def draw(count):
        taken = refs[:count]
        del refs[:count]
        return taken

    sources = draw(7)
    gain_ref, shift_ref, head_ref, target_ref, arm_ref = draw(5)
    starts_out, grad_pair_ref, low_ref, hidden_ref, active_ref, branch_ref, cross_grad_ref, small_ref, tiny_ref = draw(9)
    held = dict(zip(DECODE_WEIGHTS, draw(7)))
    stash, *rooms, load_sems = draw(5)
    loads = {}
    for index, (name, source) in enumerate(zip(DECODE_WEIGHTS, sources)):
        loads[name] = pltpu.make_async_copy(source, held[name], load_sems.at[index])
        loads[name].start()
    valid = starts_ref.shape[0]
    starts_out[...] = jnp.zeros_like(starts_out)
    starts_out[pl.ds(0, valid), :] = starts_ref[...]
    acts = {"low_d": low_ref, "hidden_d": hidden_ref, "active_d": active_ref, "branch_d": branch_ref}
    branch, dq, mixed, sums, head_grad = decode_body(
        pick, valid, loads, held, starts_out, gain_ref, shift_ref, head_ref, target_ref, arm_ref, acts, lambda name: None,
        stash, rooms,
    )
    small_ref[pl.ds(0, PAD_ROWS), :] = branch
    small_ref[pl.ds(PAD_ROWS, PAD_ROWS), :] = dq
    cross_grad_ref[...] = dot(mixed, branch, TN).astype(BF16)
    grad_pair_ref[...] = held["pair"][...]
    tiny_ref[...] = jnp.zeros_like(tiny_ref)
    tiny_ref[pl.ds(0, 4), :] = sums
    tiny_ref[pl.ds(8, head_ref.shape[0]), :] = head_grad


def decode_sources(weights, pair):
    return (weights[7], weights[8], weights[9], pair, weights[11], weights[12], weights[13])


def decode(pick, targets, arms, weights, pair):
    starts, head = weights[6], weights[16]
    width = starts.shape[1]
    hidden = weights[12].shape[1]
    sources = decode_sources(weights, pair)
    shapes = {
        "starts": ((PAD_ROWS, width), BF16),
        "grad_pair": (pair.shape, BF16),
        "low_d": ((PAD_ROWS, width), BF16),
        "hidden_d": ((PAD_ROWS, hidden), BF16),
        "active_d": ((PAD_ROWS, hidden), BF16),
        "branch_d": ((PAD_ROWS, width), BF16),
        "cross": ((width, width), BF16),
        "small": ((SMALL_ROWS, width), BF16),
        "tiny": ((TINY_ROWS, width), F32),
    }
    in_vmem = pl.BlockSpec(memory_space=pltpu.VMEM)
    results = call(
        functools.partial(decode_kernel, pick),
        8 * PAD_ROWS * width * hidden * 2,
        20 * 1024 * 1024,
        in_specs=[in_vmem] + [pl.BlockSpec(memory_space=pl.ANY)] * 7 + [in_vmem] * 4
        + [pl.BlockSpec(memory_space=pltpu.SMEM)],
        out_specs=[in_vmem] * len(shapes),
        out_shape=[shape_of(dims, kind) for dims, kind in shapes.values()],
        scratch_shapes=[pltpu.VMEM(item.shape, BF16) for item in sources]
        + [pltpu.VMEM((pair.shape[0], hidden), BF16)] + [pltpu.VMEM((PAD_ROWS, width), BF16)] * 3
        + [pltpu.SemaphoreType.DMA((7,))],
    )(starts, *sources, weights[14], weights[15], head.T, targets.transpose(2, 0, 1), arms)
    return dict(zip(shapes, results))


def decode_start_back_kernel(
    valid,
    starts_ref, project_ref, combine_ref, query_ref, gain_ref, shift_ref, resid_ref, query_grad_ref,
    start_grad_ref, project_grad_ref, combine_grad_ref, query_w_grad_ref, sums_ref,
):
    starts = starts_ref[...]
    project_w = project_ref[...]
    queries, keys, values, mixed, kept, rows, scale, first = self_block(
        starts, project_w, combine_ref[...], gain_ref[0:1, :], shift_ref[0:1, :], valid
    )
    low = query_grad_ref[...].astype(BF16)
    query_w_grad_ref[...] = dot(first.astype(BF16), low, TN)
    grad_first = resid_ref[...] + dot(low, query_ref[...], NT)
    gain_sum = column_sum(grad_first * rows)
    shift_sum = column_sum(grad_first)
    grad_resid = normed_back(grad_first, gain_ref[0:1, :], rows, scale)
    branch = grad_resid.astype(BF16)
    combine_grad_ref[...] = dot(mixed, branch, TN)
    grad_mixed = dot(branch, combine_ref[...], NT).astype(BF16)
    dq, dk, dv = few_attend_back(queries, keys, values, kept, grad_mixed)
    grad_packed = jnp.concatenate([dq, dk, dv], axis=1).astype(BF16)
    project_grad_ref[...] = dot(starts, grad_packed, TN)
    start_grad_ref[...] = grad_resid + dot(grad_packed, project_w, NT)
    sums_ref[...] = jnp.concatenate([gain_sum, shift_sum, jnp.zeros((6, gain_sum.shape[1]), F32)], axis=0)


def decode_start_back(valid, starts, project_w, combine_w, query_w, gains, shifts, resid, query_grad):
    count, width = starts.shape
    arrays = (starts, project_w, combine_w, query_w, gains, shifts, resid, query_grad)
    shapes = [(count, width), (width, 3 * width), (width, width), (width, width), (8, width)]
    return call(
        functools.partial(decode_start_back_kernel, valid),
        2 * count * width * width * 20,
        8 * 1024 * 1024,
        in_specs=[pl.BlockSpec(memory_space=pltpu.VMEM)] * len(arrays),
        out_specs=[pl.BlockSpec(memory_space=pltpu.VMEM)] * len(shapes),
        out_shape=[shape_of(dims, F32) for dims in shapes],
    )(*arrays)


def forward(x, pick, weights):
    saved = encode(x, pick, weights[:4] + (weights[10],), weights[4], weights[5])
    saved["x"] = x
    return saved


def backward_alone(saved, x, weights):
    (encoder_project, encoder_combine, encoder_expand, encoder_reduce, encoder_gains) = weights[:5]
    cross_memory = weights[10]
    grad_memory, branch, grad_hidden, resid, low, grad_mixed, sums_e = encode_back(
        saved["grad_pair"], saved["first"], saved["second"], saved["slope"],
        encoder_combine, encoder_expand, encoder_reduce, encoder_gains, cross_memory,
    )
    dq, dk, dv = attend_back(saved["packed"], grad_mixed, saved["mixed"], saved["logs"])
    grad_packed = jnp.concatenate([dq, dk, dv], axis=1)
    grad_x = (resid + dot(grad_packed, encoder_project, NT)).astype(BF16)
    plain = lambda left, right: dot(left, right, TN)
    return grad_x, grad_memory, {
        "decoder_expand": plain(undealt(saved["low_d"]), saved["hidden_d"]),
        "decoder_reduce": plain(saved["active_d"], saved["branch_d"]),
        "encoder_reduce": plain(saved["active"], branch),
        "encoder_expand": plain(saved["low"], grad_hidden),
        "middle": jnp.concatenate(
            [plain(saved["memory"], saved["grad_pair"]), saved["cross"].astype(F32), dot(saved["mixed"], low, NN)], axis=1
        ),
        "last": plain(x, grad_packed),
        "small": saved["small"].astype(F32),
        "tiny": saved["tiny"].at[4:8].set(sums_e[:4]),
    }


SECTION, SIDE, LINE = range(3)
GROUPS = {
    "decoder_expand0": (SIDE, SECTION, LINE),
    "decoder_expand1": (LINE, SIDE, SECTION),
    "decoder_reduce0": (SIDE, LINE, SECTION),
    "decoder_reduce1": (LINE, SIDE, SECTION),
    "encoder_reduce0": (SECTION, SIDE, LINE),
    "encoder_reduce1": (SIDE, SECTION, LINE),
    "encoder_expand0": (SECTION, SIDE, LINE),
    "encoder_expand1": (SIDE, LINE, SECTION),
    "middle0": (SIDE, LINE, SECTION),
    "middle1": (SIDE, SECTION, LINE),
    "last0": (SECTION, SIDE, LINE),
    "last1": (SIDE, LINE, SECTION),
}
NAMES = tuple(GROUPS)
SCHEDULE = {
    "dfe0": ("small",),
    "dmem": ("decoder_reduce1",),
    "efr1": ("decoder_reduce0", "small", "decoder_expand1",),
    "dwm": ("encoder_reduce0",),
    "du0": ("encoder_reduce1", "decoder_reduce1",),
    "du1": ("middle0", "decoder_reduce0",),
    "df": ("decoder_expand0", "small",),
    "ln": ("decoder_expand1",),
    "efe0": ("encoder_reduce1", "tiny",),
    "efe1": ("decoder_reduce1",),
    "dwc": ("encoder_expand0", "decoder_reduce0",),
    "att0": ("encoder_expand1", "middle0", "middle1",),
    "att1": ("small", "decoder_reduce1",),
    "att3": ("decoder_expand1",),
    "last0": ("encoder_reduce0", "decoder_reduce0",),
    "att4": ("encoder_expand1", "middle0",),
    "att5": ("last0", "decoder_expand0",),
    "att6": ("small", "middle1",),
    "att7": ("encoder_reduce1", "encoder_expand1", "tiny", "middle0", "decoder_expand1",),
    "dx0": ("decoder_expand0",),
    "dx1": ("encoder_reduce1",),
    "last1": ("encoder_reduce0", "encoder_expand1",),
}
TAIL_FIRST = ("tiny", "middle0", "last1", "decoder_expand0", "encoder_expand0", "small", )
TAIL = (
    "last1",
    "encoder_reduce0",
    "encoder_expand1",
    "tiny",
    "encoder_reduce1",
    "decoder_reduce0",
    "decoder_reduce1",
    "decoder_expand0",
    "last0",
    "last1",
    "decoder_reduce0",
    "decoder_reduce1",
    "encoder_reduce0",
    "decoder_expand0",
    "encoder_expand0",
    "tiny",
    "middle1",
    "decoder_expand1",
    "encoder_reduce1",
    "last0",
    "last1",
    "tiny",
    "encoder_reduce0",
    "decoder_expand1",
    "encoder_reduce1",
    "encoder_expand0",
    "middle1",
    "last0",
    "encoder_reduce0",
    "last1",
    "encoder_expand0",
    "middle1",
    "last0",
    "middle0",
    "encoder_expand0",
    "middle1",
    "encoder_expand1",
    "last0",
    "last1",
    "middle0",
    "encoder_expand0",
    "middle1",
    "encoder_expand1",
    "last0",
    "last1",
)
STEPS = 7
LINE_ROUNDS = 3


class Links:
    def __init__(self):
        core = lax.axis_index("rep")
        section = lax.axis_index("section")
        lane = lax.axis_index("dp")
        self.core = core
        self.section = section
        self.lane = lane
        self.level = lane // 2
        self.side = lane % 2
        self.mine = [section, self.side]
        self.other_core = {"rep": 1 - core}
        self.partner = [{"section": 1 - section}, {"dp": lane + 1 - 2 * self.side}]
        self.above = {"dp": lane + 2}
        self.below = {"dp": lane - 2}

    def signal(self, semaphore, device):
        pl.semaphore_signal(semaphore, inc=1, device_id=device, device_id_type=pl.DeviceIdType.MESH)

    def tell(self, semaphores):
        for semaphore, device in zip(semaphores[:3], [self.other_core] + self.partner):
            self.signal(semaphore, device)

        @pl.when(self.level > 0)
        def _():
            self.signal(semaphores[3], self.below)

        @pl.when(self.level < 3)
        def _():
            self.signal(semaphores[4], self.above)

    def greet(self):
        barrier = pltpu.get_barrier_semaphore()
        self.tell([barrier] * 5)
        pl.semaphore_wait(barrier, 3 + (self.level + 3) // 4 + (6 - self.level) // 4)

    def copy(self, source, target, sems, device):
        return pltpu.make_async_remote_copy(
            src_ref=source,
            dst_ref=target,
            send_sem=sems[0],
            recv_sem=sems[1],
            device_id=device,
            device_id_type=pl.DeviceIdType.MESH,
        )


def stage_blocks(order):
    counts, size = [], 16
    for dim in order:
        counts.append(5 * size // 4 if dim == LINE else size // 2)
        size = size // 4 if dim == LINE else size // 2
    return counts


class Scatter:
    def __init__(self, links, order, keep, sent, arrived, stages, send_sems, recv_sems, index, out, credits=None):
        self.links, self.order, self.keep, self.out = links, order, keep, out
        self.sent, self.arrived, self.credits = sent, arrived, credits
        self.sems = lambda step, way=0: (send_sems.at[index, step, way], recv_sems.at[index, step, way])
        self.plan = [] if sent is None else [("core",)]
        base, size = 0, 16
        for dim, buffer in zip(order, stages):
            if dim == LINE:
                size //= 4
                self.plan += [("line", turn, base, size, buffer) for turn in (1, 2, 3)]
                base = base + links.level * size
            else:
                size //= 2
                mine = links.mine[dim]
                self.plan.append(("halve", dim, base + (1 - mine) * size, base + mine * size, size, buffer))
                base = base + mine * size
        self.base = base
        self.plan.append(("both",))
        self.step = 0

    def place(self, shard):
        index, size = 0, 16
        for dim in self.order:
            size //= 4 if dim == LINE else 2
            index += size * {SECTION: shard // 8, LINE: shard // 2 % 4, SIDE: shard % 2}[dim]
        return index

    def single(self, step):
        links, kind = self.links, self.plan[step][0]
        if kind == "core":
            return links.copy(self.sent, self.arrived, self.sems(step), links.other_core)
        if kind == "halve":
            _, dim, away, _, size, buffer = self.plan[step]
            return links.copy(self.keep.at[pl.ds(away, size)], buffer, self.sems(step), links.partner[dim])
        return links.copy(self.out.at[links.core], self.out.at[links.core], self.sems(step), links.other_core)

    def lines(self, step):
        links, level = self.links, self.links.level
        _, turn, base, size, buffer = self.plan[step]
        shards = lambda ref, index: ref.at[pl.ds(index * size, size)]
        keep = lambda shard: self.keep.at[pl.ds(base + shard * size, size)]
        up, down = level + 4 - turn, level - 4 + turn
        return [
            (
                (level < turn) & (level < 3),
                lambda: links.copy(keep(up), shards(buffer, turn - level - 1), self.sems(step, 0), links.above),
                (level > 0) & (level <= turn),
                lambda: links.copy(keep(up - 1), shards(buffer, turn - level), self.sems(step, 0), links.above),
                lambda: (base + (up - 1) * size, (turn - level) * size),
                level == turn - 1,
            ),
            (
                (3 - level < turn) & (level > 0),
                lambda: links.copy(keep(down), shards(buffer, turn + 1), self.sems(step, 1), links.below),
                (level < 3) & (3 - level <= turn),
                lambda: links.copy(keep(down + 1), shards(buffer, turn + 1), self.sems(step, 1), links.below),
                lambda: (base + (down + 1) * size, (turn + 1) * size),
                3 - level == turn - 1,
            ),
        ]

    def start(self):
        step = self.step
        plan = self.plan[step]
        if plan[0] == "line":
            for way, (sends, sent, _, _, _, opens) in enumerate(self.lines(step)):

                @pl.when(sends)
                def _():
                    if self.credits is not None:

                        @pl.when(opens)
                        def _():
                            pl.semaphore_wait(self.credits.at[3 + way], 1)

                    sent().start()

            return
        if self.credits is not None and plan[0] != "both":
            pl.semaphore_wait(self.credits.at[0 if plan[0] == "core" else 1 + plan[1]], 1)
        if plan[0] == "both":
            self.out[pl.ds(self.links.core, 1)] = self.keep[pl.ds(self.base, 1)]
        self.single(step).start()

    def add(self, source, first, base, size):
        keep = self.keep

        def body(i, carry):
            keep[base + i] = keep[base + i] + source[first + i]
            return carry

        lax.fori_loop(0, size, body, 0)

    def finish(self):
        step = self.step
        plan = self.plan[step]
        if plan[0] == "line":
            for _, _, comes, arrived, where, _ in self.lines(step):

                @pl.when(comes)
                def _():
                    arrived().wait_recv()
                    base, first = where()
                    self.add(plan[4], first, base, plan[3])

        else:
            self.single(step).wait_recv()
            if plan[0] == "core":
                self.add(self.arrived, 0, 0, 16)
            elif plan[0] == "halve":
                self.add(plan[5], 0, plan[3], plan[4])
        self.step += 1

    def advance(self):
        self.finish()
        if self.step < len(self.plan):
            self.start()

    def close(self):
        assert self.step == len(self.plan)
        for step, plan in enumerate(self.plan):
            if plan[0] == "line":
                for sends, sent, _, _, _, _ in self.lines(step):

                    @pl.when(sends)
                    def _():
                        sent().wait_send()

            else:
                self.single(step).wait_send()


class Total:
    def __init__(self, links, levels, arrived, send_sems, recv_sems, index):
        self.links, self.levels, self.arrived = links, levels, arrived
        level = links.level
        everyone = level >= 0
        near = {"dp": links.lane + 2 - 4 * (level % 2)}
        middle = {"dp": links.lane + 6 - 4 * level}
        inner = (level == 1) | (level == 2)
        outer = {"dp": links.lane - 6 + 4 * level}
        self.turns = [
            (everyone, everyone, links.other_core), (everyone, everyone, links.partner[SECTION]),
            (everyone, everyone, near), (inner, inner, middle), (inner, jnp.logical_not(inner), outer),
            (everyone, everyone, links.partner[SIDE]),
        ]
        self.sems = lambda step: (send_sems.at[index, step, 0], recv_sems.at[index, step, 0])
        self.step = 0
        self.result = levels.at[0]

    def copy_of(self, step):
        return self.links.copy(
            self.levels.at[step % 2], self.arrived.at[step - step // 4], self.sems(step), self.turns[step][2]
        )

    def start(self):
        step = self.step

        @pl.when(self.turns[step][0])
        def _():
            self.copy_of(step).start()

    def sent(self, step):
        @pl.when(self.turns[step][0])
        def _():
            self.copy_of(step).wait_send()

    def advance(self):
        step = self.step
        if step > 0:
            self.sent(step - 1)
        comes = self.turns[step][1]

        @pl.when(comes)
        def _():
            self.copy_of(step).wait_recv()
            value = self.arrived[step - step // 4].astype(F32)
            if step != 4:
                value = self.levels[step % 2].astype(F32) + value
            self.levels[(step + 1) % 2] = value.astype(self.levels.dtype)

        @pl.when(jnp.logical_not(comes))
        def _():
            self.levels[(step + 1) % 2] = self.levels[step % 2]

        self.step += 1
        if self.step < 6:
            self.start()

    def close(self):
        assert self.step == 6
        self.sent(5)


ACT_NAMES = ("low_d", "hidden_d", "active_d", "branch_d")
IN_NAMES = (
    "memory", "cross_memory", "second", "active", "reduce", "slope", "expand", "first", "low", "mixed", "combine",
    "packed", "logs", "x", "project", "self_project", "self_combine", "cross_query",
)
ATTEND_BLOCK = 256


def backward_kernel(*refs):
    refs = list(refs)

    def draw(count):
        taken = refs[:count]
        del refs[:count]
        return taken

    source = dict(zip(IN_NAMES, draw(len(IN_NAMES))))
    source["x"] = source["x"].at[lax.axis_index("section")]
    decode_refs = dict(zip(DECODE_WEIGHTS, draw(7)))
    gain_ref, starts_ref, self_gain_ref, self_shift_ref, head_ref, target_ref, arm_ref = draw(7)
    outs = dict(zip(NAMES, draw(len(NAMES))))
    memory_out, slab_out, grad_memory_out, grad_x_out, self_rows_out, stack_out = draw(6)
    acts = dict(zip(ACT_NAMES, draw(4)))
    buffers = {}
    for name in NAMES:
        if name.startswith("decoder"):
            buffers[name] = [None, None] + draw(3)
        elif not name.startswith("encoder_expand"):
            buffers[name] = draw(5)
    keeps = {}
    for name in NAMES:
        if not name.startswith("encoder_expand"):
            keeps[name] = draw(1)[0]
    expand_stages = [draw(3), draw(3)]
    hidden, slope, grad_mixed, resid, mixed, branch, small_levels, small_arrived, tiny_levels, tiny_arrived = draw(10)
    send_sems, recv_sems, act_sems, slab_sems, load_sems, decode_sems, store_sems, credits = draw(8)
    valid = starts_ref.shape[0]
    width = resid.shape[1]
    count = resid.shape[0]
    hidden_size = hidden.shape[1]
    cut = split_of(hidden_size)
    for index, columns in enumerate((pl.ds(0, cut), pl.ds(cut, hidden_size - cut))):
        name = "encoder_expand%d" % index
        rows = lambda start, size: slope.at[pl.ds(start, size), :, columns]
        keeps[name] = rows(0, 16)
        buffers[name] = [rows(16, 16), rows(32, 16)] + expand_stages[index]

    links = Links()
    core = links.core
    block = 256
    chunks = column_chunks(hidden_size)
    own_columns = pl.ds(pl.multiple_of(core * 256, 256), 256)
    other_columns = pl.ds(pl.multiple_of((1 - core) * 256, 256), 256)
    work = {}
    for index, name in enumerate(NAMES):
        sent, arrived, *stages = buffers[name]
        work[name] = Scatter(
            links, GROUPS[name], keeps[name], sent, arrived, stages, send_sems, recv_sems, index, outs[name],
            credits.at[int(name[-1])] if name.startswith("encoder_expand") else None,
        )
    work["small"] = Total(links, small_levels, small_arrived, send_sems, recv_sems, len(NAMES))
    work["tiny"] = Total(links, tiny_levels, tiny_arrived, send_sems, recv_sems, len(NAMES) + 1)

    def tick(label):
        for name in SCHEDULE.get(label, ()):
            work[name].advance()

    def loading(name, target):
        return pltpu.make_async_copy(source[name], target, load_sems.at[IN_NAMES.index(name)])

    def load(name, target):
        copy = loading(name, target)
        copy.start()
        return copy

    def deal(name, rows, first_column):
        item = work[name]
        columns = pl.ds(first_column, rows.shape[1])
        low = rows.astype(BF16)
        for shard in range(16):
            here = low[32 * shard : 32 * shard + 16]
            there = low[32 * shard + 16 : 32 * shard + 32]
            place = item.place(shard)
            item.keep[place, :, columns] = jnp.where(core == 0, here, there)
            item.sent[place, :, columns] = jnp.where(core == 0, there, here)

    def deal_columns(names, targets, rows):
        size = rows.shape[0] // 16
        for index, (name, target) in enumerate(zip(names, targets)):
            for shard in range(16):
                target[work[name].place(shard)] = rows[
                    size * shard : size * shard + size, LANES * index : LANES * index + LANES
                ].astype(BF16)

    links.greet()
    def slab_copies(out):
        parts = [pl.ds(index * (count // 2), count // 2) for index in range(2)]
        return [
            links.copy(
                out.at[part], slab_out.at[part], (slab_sems.at[0, index], slab_sems.at[1, index]), links.partner[SECTION]
            )
            for index, part in enumerate(parts)
        ]

    memory_copy = links.copy(source["memory"], memory_out, (act_sems.at[0, 4], act_sems.at[1, 4]), links.partner[SECTION])
    memory_copy.start()

    def act_copy(name):
        index = ACT_NAMES.index(name)
        return links.copy(
            acts[name].at[pl.ds(0, PAD_ROWS)], acts[name].at[pl.ds(PAD_ROWS, PAD_ROWS)],
            (act_sems.at[0, index], act_sems.at[1, index]), links.other_core,
        )

    def pad_starts(starts):
        starts[...] = jnp.zeros_like(starts)
        starts[pl.ds(0, valid), :] = starts_ref[...]

    def decode_phase(pair, starts, room0, room1, room2, *weights):
        held = dict(zip([name for name in DECODE_WEIGHTS if name != "pair"], weights), pair=pair)
        loads = {}
        for index, name in enumerate(DECODE_WEIGHTS):
            loads[name] = pltpu.make_async_copy(decode_refs[name], held[name], decode_sems.at[index])
            loads[name].start()
        pad_starts(starts)
        branch, dq, mixed, sums, head_grad = decode_body(
            lambda: links.section, valid, loads, held, starts, self_gain_ref, self_shift_ref, head_ref, target_ref,
            arm_ref, acts, lambda name: act_copy(name).start(), hidden, (room0, room1, room2),
        )
        load("active", hidden)
        load("slope", slope)
        small_levels[0, pl.ds(0, PAD_ROWS), :] = branch
        small_levels[0, pl.ds(PAD_ROWS, PAD_ROWS), :] = dq
        work["small"].start()
        tiny_levels[0] = jnp.zeros(tiny_levels.shape[1:], F32)
        tiny_levels[0, pl.ds(0, 4), :] = sums
        tiny_levels[0, pl.ds(8, head_ref.shape[0]), :] = head_grad
        deal("middle1", dot(mixed, branch, TN), 0)

    back_copies = slab_copies(grad_memory_out)
    front_copies = slab_copies(grad_x_out)

    def rows_phase(grad_pair, memory_w, residual, rows_low, reduce_w, expand_w, combine_w):
        loads = {
            name: load(name, target)
            for name, target in (
                ("cross_memory", memory_w), ("second", residual), ("memory", rows_low), ("reduce", reduce_w),
                ("expand", expand_w), ("mixed", mixed), ("combine", combine_w),
            )
        }
        loads.update(active=loading("active", hidden), slope=loading("slope", slope))

        for name in ACT_NAMES:
            act_copy(name).wait_recv()
        names = ("decoder_reduce0", "decoder_reduce1")
        deal_columns(
            names, [work[name].keep for name in names],
            dot(acts["active_d"][...], acts["branch_d"][:, own_columns], TN),
        )
        for name in names:
            work[name].start()
        tick("dfr")
        for index, (start, size) in enumerate(chunks):
            rows = dot(acts["low_d"][:, own_columns], acts["hidden_d"][:, pl.ds(start, size)], TN).astype(BF16)
            item = work["decoder_expand%d" % (index // 2)]
            columns = pl.ds(start - (index // 2) * cut, size)
            for shard in range(16):
                item.keep[item.place(shard), :, columns] = rows[16 * shard : 16 * shard + 16]
            if index % 2:
                item.start()
                tick("dfe%d" % (index // 2))

        loads["cross_memory"].wait()
        loads["second"].wait()
        sums = None
        for start in range(0, count, block):
            part = pl.ds(start, block)
            low_grad = dot(grad_pair[part, :], memory_w[...], NT).astype(BF16)
            grad_mixed[part, :] = low_grad
            grad = low_grad.astype(F32)
            rows, scale = normed(residual[part, :])
            fresh = [column_sum(grad * rows), column_sum(grad)]
            sums = fresh if sums is None else [old + new for old, new in zip(sums, fresh)]
            total = normed_back(grad, gain_ref[1:2, :], rows, scale)
            resid[part, :] = total
            branch[part, :] = total.astype(BF16)
        memory_store = pltpu.make_async_copy(grad_mixed, grad_memory_out, store_sems.at[0])
        memory_store.start()
        loads["first"] = load("first", residual)
        last_sums = sums
        tick("dmem")

        loads["active"].wait()
        names = ("encoder_reduce0", "encoder_reduce1")
        deal_columns(names, [work[name].sent for name in names], dot(hidden[...], branch[:, other_columns], TN))
        for name in names:
            work[name].start()
        memory_store.wait()

        @pl.when(links.section == 0)
        def _():
            for copy in back_copies:
                copy.start()

        tick("efr0")
        deal_columns(names, [work[name].keep for name in names], dot(hidden[...], branch[:, own_columns], TN))
        tick("efr1")
        loads["memory"].wait()
        deal("middle0", dot(rows_low[...], grad_pair[...], TN), 0)
        loads["low"] = load("low", rows_low)
        work["middle0"].start()
        tick("dwm")
        loads["reduce"].wait()
        loads["slope"].wait()
        for index, (start, size) in enumerate(chunks):
            columns = pl.ds(start, size)
            grad_active = dot(branch[...], reduce_w[columns, :], NT)
            inner = slope[:, :, columns].reshape(count, size).astype(F32)
            hidden[:, columns] = (grad_active * inner).astype(BF16)
            tick("du%d" % index)
        for half in range(2):
            links.tell([credits.at[half, index] for index in range(5)])
        loads["expand"].wait()
        resid[...] += dot(hidden[...], expand_w[...], NT)
        tick("df")

        loads["first"].wait()
        loads["combine"].wait()
        sums = None
        for start in range(0, count, block):
            part = pl.ds(start, block)
            grad = resid[part, :]
            rows, scale = normed(residual[part, :])
            fresh = [column_sum(grad * rows), column_sum(grad)]
            sums = fresh if sums is None else [old + new for old, new in zip(sums, fresh)]
            total = normed_back(grad, gain_ref[0:1, :], rows, scale)
            resid[part, :] = total
            low_grad = total.astype(BF16)
            branch[part, :] = low_grad
            grad_mixed[part, :] = dot(low_grad, combine_w[...], NT).astype(BF16)
        tiny_levels[0, 4:8, :] = jnp.concatenate([sums[0], last_sums[0], sums[1], last_sums[1]], axis=0)
        work["tiny"].start()
        tick("ln")
        loads["low"].wait()
        for index, (start, size) in enumerate(chunks):
            name = "encoder_expand%d" % (index // 2)
            deal(name, dot(rows_low[...], hidden[:, pl.ds(start, size)], TN), start - (index // 2) * cut)
            if index % 2:
                work[name].start()
                tick("efe%d" % (index // 2))
        loads["mixed"].wait()
        deal("middle1", dot(mixed[...], branch[...], NN), width)
        work["middle1"].start()
        tick("dwc")

    def first_phases(pair):
        pl.run_scoped(
            functools.partial(decode_phase, pair),
            *[pltpu.VMEM((PAD_ROWS, width), BF16)] * 4,
            *[pltpu.VMEM(decode_refs[name].shape, BF16) for name in DECODE_WEIGHTS if name != "pair"],
        )
        pl.run_scoped(
            functools.partial(rows_phase, pair),
            pltpu.VMEM((width, 2 * width), BF16),
            pltpu.VMEM((count, width), F32),
            pltpu.VMEM((count, width), BF16),
            pltpu.VMEM((hidden_size, width), BF16),
            pltpu.VMEM((width, hidden_size), BF16),
            pltpu.VMEM((width, width), BF16),
        )

    pl.run_scoped(first_phases, pltpu.VMEM((count, 2 * width), BF16))

    def attend_phase(packed, logs, x, project_w, grad_packed, starts, self_project, self_combine, cross_query):
        loads = {
            name: load(name, target)
            for name, target in (
                ("packed", packed), ("logs", logs), ("x", x), ("project", project_w),
                ("self_project", self_project), ("self_combine", self_combine), ("cross_query", cross_query),
            )
        }
        loads["packed"].wait()
        loads["logs"].wait()
        pairs = width // LANES
        half = width // 2

        def last(index):
            columns = slice(index * half, index * half + half)
            for third in range(3):
                deal("last%d" % index, dot(x[...], grad_packed[third, :, columns], TN), third * half)
            work["last%d" % index].start()

        for pair in range(pairs):
            columns = pl.ds(pair * LANES, LANES)
            attend_back_pair(
                packed[:, columns],
                packed[:, pl.ds(width + pair * LANES, LANES)],
                packed[:, pl.ds(2 * width + pair * LANES, LANES)],
                grad_mixed[:, columns],
                mixed[columns, :],
                logs[pair],
                grad_packed, columns,
                lambda head: tick("att%d" % (2 * pair + head)),
            )
            if pair == pairs // 2 - 1:
                loads["x"].wait()
                last(0)
                tick("last0")
        loads["project"].wait()
        stores = []
        for index in range(2):
            part = pl.ds(index * (count // 2), count // 2)
            total = resid[part, :]
            for third in range(3):
                total = total + dot(
                    grad_packed[third, part, :], project_w[:, third * width : (third + 1) * width], NT
                )
            packed[part, pl.ds(0, width)] = total.astype(BF16)
            store = pltpu.make_async_copy(packed.at[part, pl.ds(0, width)], grad_x_out.at[part], store_sems.at[1 + index])
            store.start()
            tick("dx%d" % index)
            store.wait()

            @pl.when(links.section == 1)
            def _():
                front_copies[index].start()

        last(1)
        tick("last1")
        pad_starts(starts)
        for name in IN_NAMES[-3:]:
            loads[name].wait()
        for name in TAIL_FIRST:
            work[name].advance()
        rows = SMALL_ROWS // 2
        start_back(
            valid, starts[...], self_project[...], self_combine[...], cross_query[...], self_gain_ref[0:1, :],
            self_shift_ref[0:1, :], work["small"].result[pl.ds(0, rows), :].astype(F32),
            work["small"].result[pl.ds(rows, rows), :], links, self_rows_out, stack_out,
        )

    pl.run_scoped(
        attend_phase,
        pltpu.VMEM((count, 3 * width), BF16),
        pltpu.VMEM(source["logs"].shape, F32),
        pltpu.VMEM((count, width), BF16),
        pltpu.VMEM((width, 3 * width), BF16),
        pltpu.VMEM((3, count, width), BF16),
        pltpu.VMEM((PAD_ROWS, width), BF16),
        pltpu.VMEM((width, 3 * width), BF16),
        pltpu.VMEM((width, width), BF16),
        pltpu.VMEM((width, width), BF16),
    )
    for name in TAIL:
        work[name].advance()
    stack_out[pl.ds(SMALL_ROWS // 2 + 8, TINY_ROWS), :] = work["tiny"].result[...]
    memory_copy.wait()
    for copy in back_copies:
        copy.wait_recv()
    for name in ACT_NAMES:
        act_copy(name).wait_send()
    for item in work.values():
        item.close()
    for copy in back_copies:
        copy.wait_send()


def start_back(valid, starts, project_w, combine_w, query_w, gain, shift, resid, query_grad, links, rows_out, stack_out):
    width = starts.shape[1]
    own = rows_out.shape[0]
    place = (links.section * 8 + links.lane) * own
    chosen = lax.broadcasted_iota(jnp.int32, (width, own), 0) == place + lax.broadcasted_iota(
        jnp.int32, (width, own), 1
    )
    chosen = jnp.where(chosen, 1.0, 0.0).astype(BF16)
    select = lambda value: dot(value, chosen, NN).astype(BF16)
    queries, keys, values, mixed, kept, rows, scale, first = self_block(
        starts, project_w, combine_w, gain, shift, valid
    )
    rows_out[:, pl.ds(4 * width, width)] = dot(select(first.astype(BF16)), query_grad, TN)
    grad_first = resid + dot(query_grad, query_w, NT)
    gain_sum = column_sum(grad_first * rows)
    shift_sum = column_sum(grad_first)
    grad_resid = normed_back(grad_first, gain, rows, scale)
    branch = grad_resid.astype(BF16)
    rows_out[:, pl.ds(3 * width, width)] = dot(select(mixed), branch, TN)
    grad_mixed = dot(branch, combine_w, NT).astype(BF16)
    dq, dk, dv = few_attend_back(queries, keys, values, kept, grad_mixed)
    grad_packed = jnp.concatenate([dq, dk, dv], axis=1).astype(BF16)
    rows_out[:, pl.ds(0, 3 * width)] = dot(select(starts), grad_packed, TN)
    count = starts.shape[0]
    stack_out[pl.ds(0, count), :] = grad_resid + dot(grad_packed, project_w, NT)
    stack_out[pl.ds(count, 8), :] = jnp.concatenate([gain_sum, shift_sum, jnp.zeros((6, width), F32)], axis=0)


def attend_back_pair(queries, keys, values, grads, mixed, logs, out, columns, between):
    count = queries.shape[0]
    lane = lax.broadcasted_iota(jnp.int32, (1, LANES), 1)
    queries = queries * jnp.asarray(0.125, BF16)
    scaled_keys = keys * jnp.asarray(0.125, BF16)
    queries_t = queries.T
    grads_t = grads.T
    logs = logs.T
    shared = mixed.astype(F32) * grads_t.astype(F32)
    inner = jnp.concatenate([column_sum(shared[:64]), column_sum(shared[64:])], axis=0).T
    dq_parts = [[], []]
    dk_parts = []
    dv_parts = []
    for head in range(2):
        own = (lane < 64) if head == 0 else (lane >= 64)
        head_queries = jnp.where(own, queries, jnp.zeros_like(queries))
        head_grads = jnp.where(own, grads, jnp.zeros_like(grads))
        dk = None
        dv = None
        for start in range(0, count, ATTEND_BLOCK):
            part = slice(start, start + ATTEND_BLOCK)
            scores = dot(head_queries[part], keys, NT)
            probs = jnp.exp(scores - logs[part, head : head + 1])
            grad_probs = dot(head_grads[part], values, NT)
            grad_scores = (probs * (grad_probs - inner[part, head : head + 1])).astype(BF16)
            new_v = dot(grads_t[64 * head : 64 * head + 64, part], probs.astype(BF16), NN)
            new_k = dot(queries_t[64 * head : 64 * head + 64, part], grad_scores, NN)
            dv = new_v if dv is None else dv + new_v
            dk = new_k if dk is None else dk + new_k
            dq_parts[head].append(dot(grad_scores, scaled_keys, NN))
        dk_parts.append(dk)
        dv_parts.append(dv)
        if head == 0:
            between(0)
    out[1, :, columns] = jnp.concatenate(dk_parts, axis=0).T.astype(BF16)
    out[2, :, columns] = jnp.concatenate(dv_parts, axis=0).T.astype(BF16)
    for index in range(count // ATTEND_BLOCK):
        out[0, pl.ds(index * ATTEND_BLOCK, ATTEND_BLOCK), columns] = jnp.where(
            lane < 64, dq_parts[0][index], dq_parts[1][index]
        ).astype(BF16)
    between(1)


def chain_blocks(width, hidden_size):
    cut = split_of(hidden_size)
    blocks = {}
    for side in ("decoder", "encoder"):
        blocks[side + "_expand0"] = (16, cut)
        blocks[side + "_expand1"] = (16, hidden_size - cut)
        blocks[side + "_reduce0"] = (hidden_size // 16, LANES)
        blocks[side + "_reduce1"] = (hidden_size // 16, LANES)
    for name in ("middle0", "middle1"):
        blocks[name] = (16, 2 * width)
    for name in ("last0", "last1"):
        blocks[name] = (16, 3 * width // 2)
    return blocks


def backward_linked(saved, targets, arms, weights):
    count, width = saved["x"].shape[1:]
    hidden_size = saved["active"].shape[1]
    starts, head = weights[6], weights[16]
    arrays = dict(saved)
    arrays.update(
        cross_memory=weights[10], reduce=weights[3], expand=weights[2], combine=weights[1], project=weights[0],
        self_project=weights[7], self_combine=weights[8], cross_query=weights[9],
        slope=saved["slope"].reshape(count // 16, 16, hidden_size),
    )
    inputs = [arrays[name] for name in IN_NAMES]
    inputs += decode_sources(weights, saved["pair"])
    vectors = [weights[4], starts, weights[14], weights[15], head.T, targets.transpose(2, 0, 1)]
    blocks = chain_blocks(width, hidden_size)
    own = width // 16
    vmem = lambda counts, name: [pltpu.VMEM((n,) + blocks[name], BF16) for n in counts]
    scratch = [pltpu.VMEM((2 * PAD_ROWS, columns), BF16) for columns in (width, hidden_size, hidden_size, width)]
    for name in NAMES:
        if name.startswith("decoder"):
            scratch += vmem(stage_blocks(GROUPS[name]), name)
        elif not name.startswith("encoder_expand"):
            scratch += vmem([16, 16] + stage_blocks(GROUPS[name]), name)
    for name in NAMES:
        if not name.startswith("encoder_expand"):
            scratch += vmem((16,), name)
    for name in ("encoder_expand0", "encoder_expand1"):
        scratch += vmem(stage_blocks(GROUPS[name]), name)
    scratch += [
        pltpu.VMEM((count, hidden_size), BF16),
        pltpu.VMEM((count // 16, 16, hidden_size), BF16),
        pltpu.VMEM((count, width), BF16),
        pltpu.VMEM((count, width), F32),
        pltpu.VMEM((width, count), BF16),
        pltpu.VMEM((count, width), BF16),
        pltpu.VMEM((2, SMALL_ROWS, width), BF16),
        pltpu.VMEM((5, SMALL_ROWS, width), BF16),
        pltpu.VMEM((2, TINY_ROWS, width), F32),
        pltpu.VMEM((5, TINY_ROWS, width), F32),
        pltpu.SemaphoreType.DMA((len(NAMES) + 2, STEPS, 2)),
        pltpu.SemaphoreType.DMA((len(NAMES) + 2, STEPS, 2)),
        pltpu.SemaphoreType.DMA((2, 5)),
        pltpu.SemaphoreType.DMA((2, 2)),
        pltpu.SemaphoreType.DMA((len(IN_NAMES),)),
        pltpu.SemaphoreType.DMA((len(DECODE_WEIGHTS),)),
        pltpu.SemaphoreType.DMA((3,)),
        pltpu.SemaphoreType.REGULAR((2, 5)),
    ]
    in_any = pl.BlockSpec(memory_space=pl.ANY)
    in_vmem = pl.BlockSpec(memory_space=pltpu.VMEM)
    shape = shape_of((count, width), BF16)
    results = pl.pallas_call(
        backward_kernel,
        in_specs=[in_any] * len(inputs) + [in_vmem] * len(vectors) + [pl.BlockSpec(memory_space=pltpu.SMEM)],
        out_specs=[in_vmem] * len(NAMES) + [in_any] * 4 + [in_vmem] * 2,
        out_shape=[shape_of((2,) + blocks[name], BF16) for name in NAMES]
        + [shape] * 4
        + [shape_of((own, 5 * width), F32), shape_of((SMALL_ROWS // 2 + 8 + TINY_ROWS, width), F32)],
        scratch_shapes=scratch,
        compiler_params=pltpu.CompilerParams(
            collective_id=0, has_side_effects=True, vmem_limit_bytes=LINKED_VMEM_BYTES
        ),
        cost_estimate=pl.CostEstimate(flops=10**8, bytes_accessed=10**8, transcendentals=0),
    )(*inputs, *vectors, arms)
    memory, slab, grad_memory, grad_x, rows, stack = results[len(NAMES) :]
    return results[: len(NAMES)], memory, slab, grad_memory, grad_x, rows, stack


def finish_kernel(valid, joints, *refs):
    refs = list(refs)

    def draw(count):
        taken = refs[:count]
        del refs[:count]
        return taken

    count = len(NAMES)
    sources = draw(count + 7)
    targets = draw(19)
    held = draw(count + 7)
    results = draw(17)
    load_sems, store_sems = draw(2)
    loads = []
    for index in list(range(count, count + 7)) + list(range(count)):
        copy = pltpu.make_async_copy(sources[index], held[index], load_sems.at[index])
        copy.start()
        loads.append((index, copy))
    loads = dict(loads)
    stores = []
    section = lax.axis_index("section")
    memory, other, grad_x, grad_memory, other_slab = held[count + 2 :]
    memory_out, slab_out = targets[:2]

    def store(result):
        index = next(i for i, item in enumerate(results) if item is result)
        stores.append(pltpu.make_async_copy(result, targets[2 + index], store_sems.at[2 + index]))
        stores[-1].start()

    (
        project_e, combine_e, expand_e, reduce_e, gains_e, shifts_e, starts_d, project_d, combine_d, query_d,
        memory_d, cross_d, expand_d, reduce_d, gains_d, shifts_d, head_d,
    ) = results
    halves = dict(zip(NAMES, held[:count]))
    rows_ref, stack_ref = held[count : count + 2]
    width = memory.shape[1]
    own = rows_ref.shape[0]
    place = (section * 8 + lax.axis_index("dp")) * own
    loads[count].wait()
    loads[count + 1].wait()
    project_d[...] = rows_ref[:, : 3 * width]
    store(project_d)
    combine_d[...] = rows_ref[:, 3 * width : 4 * width]
    store(combine_d)
    query_d[...] = rows_ref[:, 4 * width :]
    store(query_d)
    chosen = lax.broadcasted_iota(jnp.int32, (width, own), 0) == place + lax.broadcasted_iota(
        jnp.int32, (width, own), 1
    )
    chosen = jnp.where(chosen, 1.0, 0.0)
    exact = functools.partial(lax.dot_general, precision=lax.Precision.HIGHEST, preferred_element_type=F32)
    picked = exact(stack_ref[pl.ds(PAD_ROWS, 8 + TINY_ROWS), :], chosen, NN)
    starts_d[...] = exact(chosen, stack_ref[pl.ds(0, PAD_ROWS), :], (((0,), (1,)), ((), ())))[:, :valid]
    store(starts_d)
    gains_d[...] = jnp.concatenate([picked[0:1], picked[8:10]], axis=0)
    shifts_d[...] = jnp.concatenate([picked[1:2], picked[10:12]], axis=0)
    gains_e[...] = picked[12:14]
    shifts_e[...] = picked[14:16]
    head_d[...] = picked[16 : 16 + joints]
    for result in (gains_d, shifts_d, gains_e, shifts_e, head_d):
        store(result)
    for index in range(count + 2, count + 7):
        loads[index].wait()
    for index, (out, front, back) in enumerate(
        (
            ((memory_out.at[0], memory_out.at[1]), (memory, other), (other, memory)),
            ((slab_out.at[0, 0], slab_out.at[0, 1]), (grad_x, other_slab), (other_slab, grad_memory)),
        )
    ):
        for way in range(2):
            ahead = pltpu.make_async_copy(front[way], out[way], store_sems.at[19 + 2 * index + way])
            behind = pltpu.make_async_copy(back[way], out[way], store_sems.at[19 + 2 * index + way])

            @pl.when(section == 0)
            def _():
                ahead.start()

            @pl.when(section == 1)
            def _():
                behind.start()

            stores.append(ahead)

    for index in range(count):
        loads[index].wait()

    def rows_of(name, out, columns, first=0):
        for core in range(2):
            out[pl.ds(16 * core, 16), columns] = halves[name][core, :, first : first + columns.size].astype(F32)

    cut = halves["encoder_expand0"].shape[2]
    for side, out in (("encoder", expand_e), ("decoder", expand_d)):
        rows_of(side + "_expand0", out, pl.ds(0, cut))
        rows_of(side + "_expand1", out, pl.ds(cut, out.shape[1] - cut))
        store(out)
    for side, out in (("encoder", reduce_e), ("decoder", reduce_d)):
        for core in range(2):
            for index in range(2):
                out[:, pl.ds((2 * core + index) * LANES, LANES)] = halves[side + "_reduce%d" % index][core].astype(F32)
        store(out)
    rows_of("middle0", memory_d, pl.ds(0, 2 * width))
    store(memory_d)
    rows_of("middle1", cross_d, pl.ds(0, width))
    store(cross_d)
    rows_of("middle1", combine_e, pl.ds(0, width), width)
    store(combine_e)
    half = width // 2
    for third in range(3):
        for index in range(2):
            rows_of("last%d" % index, project_e, pl.ds(third * width + index * half, half), third * half)
    store(project_e)
    for copy in stores:
        copy.wait()


def finish(valid, joints, halves, rows, stack, memory, other, grad_x, grad_memory, other_slab):
    count, width = memory.shape
    own = rows.shape[0]
    hidden_size = halves[0].shape[2] + halves[1].shape[2]
    in_any = pl.BlockSpec(memory_space=pl.ANY)
    shapes = [
        (own, 3 * width), (own, width), (own, hidden_size), (hidden_size // 16, width), (2, own), (2, own),
        (own, valid), (own, 3 * width), (own, width), (own, width), (own, 2 * width), (own, width),
        (own, hidden_size), (hidden_size // 16, width), (3, own), (3, own), (joints, own),
    ]
    inputs = (*halves, rows, stack, memory, other, grad_x, grad_memory, other_slab)
    results = list(
        call(
            functools.partial(finish_kernel, valid, joints),
            10**6, 10**7,
            in_specs=[in_any] * len(inputs),
            out_specs=[in_any] * (2 + len(shapes)),
            out_shape=[shape_of((2, count, width), BF16), shape_of((1, 2, count, width), BF16)]
            + [shape_of(dims, F32) for dims in shapes],
            scratch_shapes=[pltpu.VMEM(item.shape, item.dtype) for item in inputs]
            + [pltpu.VMEM(dims, F32) for dims in shapes]
            + [pltpu.SemaphoreType.DMA((len(inputs),)), pltpu.SemaphoreType.DMA((23,))],
        )(*inputs)
    )
    results[8] = results[8].T
    results[18] = results[18].T
    return tuple(results)


def swap(value, axis, bit):
    pairs = [(i, i ^ (1 << bit)) for i in range(lax.axis_size(axis))]
    return lax.ppermute(value, axis, pairs)


def plain_scatter(full):
    part = lax.psum_scatter(full.astype(F32), ("section", "dp"), scatter_dimension=0, tiled=True)
    return lax.psum(part, "rep")


def per_device(x, targets, arms, *weights):
    section = lax.axis_index("section")
    sections = lax.axis_size("section")
    lanes = lax.axis_size("dp")
    count = x.shape[0] // sections
    starts, head = weights[6], weights[16]
    valid, joints = starts.shape[0], head.shape[1]
    width = starts.shape[1]
    first = section == 0
    place = section * lanes + lax.axis_index("dp")
    own = width // (sections * lanes)
    linked = (sections, lanes, lax.axis_size("rep"), count) == (2, 8, 2, 1)
    saved = []
    for index in range(count):
        pick = functools.partial(lambda i: lax.axis_index("section") * count + i, index)
        saved.append(forward(x, pick, weights))
        if not linked:
            saved[-1].update(decode(pick, targets, arms, weights, saved[-1].pop("pair")))
    if linked:
        halves, other, other_slab, grad_memory, grad_x, rows, stack = backward_linked(saved[0], targets, arms, weights)
        return finish(
            valid, joints, halves, rows, stack, saved[0]["memory"], other, grad_x, grad_memory, other_slab
        )
    memory = jnp.concatenate([item["memory"][None] for item in saved])
    results = []
    for index, item in enumerate(saved):
        results.append(
            backward_alone(item, lax.dynamic_index_in_dim(x, section * count + index, 0, keepdims=False), weights)
        )
    grad_x = jnp.concatenate([item[0][None] for item in results])
    grad_memory = jnp.concatenate([item[1][None] for item in results])
    total = lambda name: functools.reduce(jnp.add, [item[2][name] for item in results])
    other = swap(memory, "section", 0)
    other_slab = swap(jnp.where(first, grad_memory, grad_x), "section", 0)
    small = lax.psum(total("small"), ("section", "dp", "rep"))
    tiny = lax.psum(total("tiny"), ("section", "dp", "rep"))
    done = {
        name: plain_scatter(total(name))
        for name in ("decoder_expand", "decoder_reduce", "encoder_expand", "encoder_reduce", "middle", "last")
    }
    memory_out = jnp.concatenate([jnp.where(first, memory, other), jnp.where(first, other, memory)])
    slab = jnp.concatenate(
        [jnp.where(first, grad_x, other_slab), jnp.where(first, other_slab, grad_memory)]
    )[None]

    columns_of = lambda array: lax.dynamic_slice_in_dim(array, place * own, own, 1)
    rows_of = lambda array: lax.dynamic_slice_in_dim(array, place * own, own, 0)
    resid_d, query_d = small[:PAD_ROWS], small[PAD_ROWS:]
    start_grad, project_d, combine_d, query_w, sums_s = decode_start_back(
        valid, jnp.pad(starts, ((0, PAD_ROWS - valid), (0, 0))), weights[7], weights[8], weights[9],
        weights[14], weights[15], resid_d, query_d,
    )
    gains_d = jnp.concatenate([sums_s[0:1], tiny[0:2]])
    shifts_d = jnp.concatenate([sums_s[1:2], tiny[2:4]])
    return (
        memory_out,
        slab,
        done["last"],
        done["middle"][:, 3 * width :],
        done["encoder_expand"],
        done["encoder_reduce"],
        columns_of(tiny[4:6]),
        columns_of(tiny[6:8]),
        columns_of(start_grad[:valid]),
        rows_of(project_d),
        rows_of(combine_d),
        rows_of(query_w),
        done["middle"][:, : 2 * width],
        done["middle"][:, 2 * width : 3 * width],
        done["decoder_expand"],
        done["decoder_reduce"],
        columns_of(gains_d),
        columns_of(shifts_d),
        rows_of(tiny[8 : 8 + joints].T),
    )


def solution(mesh):
    spread = ("section", "dp")
    rows = P(spread, None)
    columns = P(None, spread)
    return jax.shard_map(
        per_device,
        mesh=mesh,
        in_specs=(P(("dp", "rep"), None, None), P(("dp", "rep"), None, None), P(("dp", "rep"))) + (P(),) * 17,
        out_specs=(
            P(("dp", "rep"), None, None),
            P("section", ("dp", "rep"), None, None),
            rows, rows, rows, rows, columns, columns, columns,
            rows, rows, rows, rows, rows, rows, rows, columns, columns, rows,
        ),
        check_vma=False,
    )
```

```python
import functools

import jax
import jax.numpy as jnp
from jax import lax
from jax.experimental import pallas as pl
from jax.experimental.pallas import tpu as pltpu
from jax.sharding import PartitionSpec as P

HEADS = 8
EPSILON = 1e-05
LANES = 128
PAD_ROWS = 112
SMALL_ROWS = 2 * PAD_ROWS
TINY_ROWS = 24
F32 = jnp.float32
BF16 = jnp.bfloat16
NN = (((1,), (0,)), ((), ()))
NT = (((1,), (1,)), ((), ()))
TN = (((0,), (0,)), ((), ()))
VMEM_BYTES = 56 * 1024 * 1024
LINKED_VMEM_BYTES = 638 * 1024 * 1024 // 10
ROOT_2_PI = 0.7978845608028654
CUBE = 0.044715


def dot(left, right, dims):
    return lax.dot_general(left, right, dims, preferred_element_type=F32)


def call(kernel, flops, moved, **options):
    return pl.pallas_call(
        kernel,
        compiler_params=pltpu.CompilerParams(vmem_limit_bytes=VMEM_BYTES),
        cost_estimate=pl.CostEstimate(flops=flops, bytes_accessed=moved, transcendentals=0),
        **options,
    )


def shape_of(dims, dtype):
    return jax.ShapeDtypeStruct(dims, dtype)


def whole(array):
    rank = len(array.shape)
    return pl.BlockSpec(array.shape, lambda *_: (0,) * rank, pipeline_mode=pl.Buffered(1))


def normed(residual):
    centre = jnp.mean(residual, axis=-1, keepdims=True)
    centred = residual - centre
    spread = jnp.mean(centred * centred, axis=-1, keepdims=True)
    scale = lax.rsqrt(spread + EPSILON)
    return centred * scale, scale


def normed_back(grad, gain, rows, scale):
    weighted = grad * gain
    return scale * (
        weighted
        - jnp.mean(weighted, axis=-1, keepdims=True)
        - rows * jnp.mean(weighted * rows, axis=-1, keepdims=True)
    )


def gelu_and_slope(value):
    square = value * value
    bend = jnp.tanh(value * (ROOT_2_PI + (ROOT_2_PI * CUBE) * square))
    half = 0.5 + 0.5 * bend
    slope = half + value * (0.5 - 0.5 * bend * bend) * (
        ROOT_2_PI + (3.0 * ROOT_2_PI * CUBE) * square
    )
    return value * half, slope


def column_sum(value):
    return jnp.sum(value, axis=0, keepdims=True)


FORWARD_WEIGHTS = ("project", "combine", "expand", "reduce", "memory_w")
FORWARD_OUTS = ("packed", "mixed", "logs", "first", "low", "active", "slope", "second", "memory", "pair")


def split_of(hidden_size):
    return hidden_size // 256 * 128 + 128


def column_chunks(hidden_size):
    cut = split_of(hidden_size)
    return [(0, 896), (896, cut - 896), (cut, 768), (cut + 768, hidden_size - cut - 768)]


def attend_all(packed, mixed_ref, log_ref):
    count, width = packed.shape[0], packed.shape[1] // 3
    lane = lax.broadcasted_iota(jnp.int32, (1, LANES), 1)
    heads = width // 64
    columns = lambda third, head: pl.ds(third * width + head // 2 * LANES, LANES)

    def scores_of(head):
        keys = packed[:, columns(1, head)]
        own = (lane < 64) if head % 2 == 0 else (lane >= 64)
        queries = packed[:, columns(0, head)] * jnp.asarray(0.125, BF16)
        return dot(jnp.where(own, keys, jnp.zeros_like(keys)), queries, NT)

    scores = scores_of(0)
    for head in range(heads):
        following = scores_of(head + 1) if head + 1 < heads else None
        if head % 2 == 0:
            values = packed[:, columns(2, head)].T
        extended = jnp.concatenate(
            [values[64 * (head % 2) : 64 * (head % 2) + 64], jnp.ones((16, count), BF16)], axis=0
        )
        largest = jnp.max(scores, axis=0, keepdims=True)
        raised = jnp.exp(scores - largest).astype(BF16)
        mixed = dot(extended, raised, NN)
        total = mixed[64:65]
        mixed_ref[pl.ds(64 * head, 64), :] = (mixed[:64] * (1.0 / total)).astype(BF16)
        log_ref[head // 2, pl.ds(head % 2, 1), :] = largest + jnp.log(total)
        scores = following


def encode_kernel(pick, x_ref, *refs):
    refs = list(refs)

    def draw(count):
        taken = refs[:count]
        del refs[:count]
        return taken

    weights = dict(zip(FORWARD_WEIGHTS, draw(5)))
    gain_ref, shift_ref = draw(2)
    outs = dict(zip(FORWARD_OUTS, draw(10)))
    held = dict(zip(FORWARD_WEIGHTS, draw(5)))
    kept = dict(zip(FORWARD_OUTS, draw(10)))
    x, load_sems, store_sems = draw(3)
    here = pltpu.make_async_copy(x_ref.at[pick()], x, load_sems.at[5])
    here.start()
    loads = {}
    for index, name in enumerate(FORWARD_WEIGHTS):
        loads[name] = pltpu.make_async_copy(weights[name], held[name], load_sems.at[index])
        loads[name].start()
    stores = []

    def store(name):
        index = FORWARD_OUTS.index(name)
        stores.append(pltpu.make_async_copy(kept[name], outs[name], store_sems.at[index]))
        stores[-1].start()

    count, width = x.shape
    hidden_size = held["expand"].shape[1]
    block = 256
    here.wait()
    loads["project"].wait()
    for third in range(3):
        columns = pl.ds(third * width, width)
        kept["packed"][:, columns] = dot(x[...], held["project"][:, columns], NN).astype(BF16)
    store("packed")
    attend_all(kept["packed"], kept["mixed"], kept["logs"])
    store("mixed")
    store("logs")
    loads["combine"].wait()
    first, low, second = kept["first"], kept["low"], kept["second"]
    first[...] = x[...].astype(F32) + dot(kept["mixed"][...], held["combine"][...], TN)
    for start in range(0, count, block):
        part = pl.ds(start, block)
        rows, _ = normed(first[part, :])
        value = rows * gain_ref[0:1, :] + shift_ref[0:1, :]
        second[part, :] = value
        low[part, :] = value.astype(BF16)
    store("first")
    store("low")
    loads["expand"].wait()
    chunks = column_chunks(hidden_size)
    before = lambda item: dot(low[...], held["expand"][:, pl.ds(*item)], NN)
    ahead = before(chunks[0])
    for index, (start, size) in enumerate(chunks):
        current = ahead
        if index + 1 < len(chunks):
            ahead = before(chunks[index + 1])
        active, slope = gelu_and_slope(current)
        columns = pl.ds(start, size)
        kept["active"][:, columns] = active.astype(BF16)
        kept["slope"][:, columns] = slope.astype(BF16)
    store("active")
    store("slope")
    loads["reduce"].wait()
    second[...] += dot(kept["active"][...], held["reduce"][...], NN)
    memory = kept["memory"]
    for start in range(0, count, block):
        part = pl.ds(start, block)
        rows, _ = normed(second[part, :])
        memory[part, :] = (rows * gain_ref[1:2, :] + shift_ref[1:2, :]).astype(BF16)
    store("second")
    store("memory")
    loads["memory_w"].wait()
    for half in range(2):
        columns = pl.ds(half * width, width)
        kept["pair"][:, columns] = dot(memory[...], held["memory_w"][:, columns], NN).astype(BF16)
        stores.append(
            pltpu.make_async_copy(
                kept["pair"].at[:, columns], outs["pair"].at[:, columns], store_sems.at[len(FORWARD_OUTS) - 1 + half]
            )
        )
        stores[-1].start()
    for copy in stores:
        copy.wait()


def encode(x, pick, weights, gains, shifts):
    count, width = x.shape[1:]
    hidden_size = weights[2].shape[1]
    shapes = [
        ((count, 3 * width), BF16), ((width, count), BF16), ((width // LANES, 2, count), F32), ((count, width), F32),
        ((count, width), BF16), ((count, hidden_size), BF16), ((count, hidden_size), BF16), ((count, width), F32),
        ((count, width), BF16), ((count, 2 * width), BF16),
    ]
    in_any = pl.BlockSpec(memory_space=pl.ANY)
    in_vmem = pl.BlockSpec(memory_space=pltpu.VMEM)
    results = call(
        functools.partial(encode_kernel, pick),
        2 * count * width * (2 * hidden_size + 6 * width) + 4 * count * count * width,
        count * (hidden_size * 4 + width * 24) + 8 * width * hidden_size,
        in_specs=[in_any] * 6 + [in_vmem] * 2,
        out_specs=[in_any] * 10,
        out_shape=[shape_of(dims, kind) for dims, kind in shapes],
        scratch_shapes=[pltpu.VMEM(item.shape, BF16) for item in weights]
        + [pltpu.VMEM(dims, kind) for dims, kind in shapes]
        + [pltpu.VMEM((count, width), BF16), pltpu.SemaphoreType.DMA((6,)), pltpu.SemaphoreType.DMA((11,))],
    )(x, *weights, gains, shifts)
    return dict(zip(FORWARD_OUTS, results))


def attend_back_kernel(block, q_ref, k_ref, v_ref, do_ref, mixed_ref, log_ref, dq_ref, dk_ref, dv_ref):
    count = q_ref.shape[0]
    lane = lax.broadcasted_iota(jnp.int32, (1, LANES), 1)
    keys = k_ref[...]
    values = v_ref[...]
    queries = q_ref[...] * jnp.asarray(0.125, BF16)
    scaled_keys = keys * jnp.asarray(0.125, BF16)
    grads = do_ref[...]
    queries_t = queries.T
    grads_t = grads.T
    logs = log_ref[0].T
    shared = mixed_ref[...].astype(F32) * grads_t.astype(F32)
    inner = jnp.concatenate([column_sum(shared[:64]), column_sum(shared[64:])], axis=0).T
    dq_parts = [[], []]
    dk_parts = []
    dv_parts = []
    for head in range(2):
        own = (lane < 64) if head == 0 else (lane >= 64)
        head_queries = jnp.where(own, queries, jnp.zeros_like(queries))
        head_grads = jnp.where(own, grads, jnp.zeros_like(grads))
        dk = None
        dv = None
        for start in range(0, count, block):
            part = slice(start, start + block)
            scores = dot(head_queries[part], keys, NT)
            probs = jnp.exp(scores - logs[part, head : head + 1])
            grad_probs = dot(head_grads[part], values, NT)
            grad_scores = (probs * (grad_probs - inner[part, head : head + 1])).astype(BF16)
            new_v = dot(grads_t[64 * head : 64 * head + 64, part], probs.astype(BF16), NN)
            new_k = dot(queries_t[64 * head : 64 * head + 64, part], grad_scores, NN)
            dv = new_v if dv is None else dv + new_v
            dk = new_k if dk is None else dk + new_k
            dq_parts[head].append(dot(grad_scores, scaled_keys, NN))
        dk_parts.append(dk)
        dv_parts.append(dv)
    dk_ref[...] = jnp.concatenate(dk_parts, axis=0).T.astype(BF16)
    dv_ref[...] = jnp.concatenate(dv_parts, axis=0).T.astype(BF16)
    for index in range(count // block):
        dq_ref[pl.ds(index * block, block), :] = jnp.where(
            lane < 64, dq_parts[0][index], dq_parts[1][index]
        ).astype(BF16)


def attend_back(packed, grad_mixed, mixed, logs):
    rows, width = packed.shape[0], packed.shape[1] // 3
    pairs = width // LANES
    column = lambda first: pl.BlockSpec((rows, LANES), lambda j: (0, first + j))
    return call(
        functools.partial(attend_back_kernel, 256),
        10 * rows * rows * width * 3,
        rows * width * 16,
        grid=(pairs,),
        in_specs=[
            column(0),
            column(pairs),
            column(2 * pairs),
            column(0),
            pl.BlockSpec((LANES, rows), lambda j: (j, 0)),
            pl.BlockSpec((1, 2, rows), lambda j: (j, 0, 0)),
        ],
        out_specs=[column(0)] * 3,
        out_shape=[shape_of((rows, width), BF16)] * 3,
    )(packed, packed, packed, grad_mixed, mixed, logs)

def encode_back_kernel(
    pair_ref, first_ref, second_ref, slope_ref, combine_ref, expand_ref, reduce_ref, gain_ref, memory_w_ref,
    grad_memory_ref, branch_ref, hidden_ref, resid_ref, low_ref, mixed_ref, sums_ref,
):
    grad_memory = dot(pair_ref[...], memory_w_ref[...], NT).astype(BF16)
    grad_memory_ref[...] = grad_memory
    grad_last = grad_memory.astype(F32)
    rows, scale = normed(second_ref[...])
    gain_last = column_sum(grad_last * rows)
    shift_last = column_sum(grad_last)
    grad_second = normed_back(grad_last, gain_ref[1:2, :], rows, scale)
    branch = grad_second.astype(BF16)
    branch_ref[...] = branch
    total = grad_second
    hidden_size = expand_ref.shape[1]
    step = hidden_size // 5
    for start in range(0, hidden_size, step):
        part = pl.ds(start, step)
        grad_active = dot(branch, reduce_ref[part, :], NT)
        grad_hidden = (grad_active * slope_ref[:, part].astype(F32)).astype(BF16)
        hidden_ref[:, part] = grad_hidden
        total = total + dot(grad_hidden, expand_ref[:, part], NT)
    rows, scale = normed(first_ref[...])
    gain_first = column_sum(total * rows)
    shift_first = column_sum(total)
    grad_first = normed_back(total, gain_ref[0:1, :], rows, scale)
    resid_ref[...] = grad_first
    low = grad_first.astype(BF16)
    low_ref[...] = low
    mixed_ref[...] = dot(low, combine_ref[...], NT).astype(BF16)
    fresh = jnp.concatenate(
        [gain_first, gain_last, shift_first, shift_last, jnp.zeros((4, gain_first.shape[1]), F32)], axis=0
    )

    @pl.when(pl.program_id(0) == 0)
    def _():
        sums_ref[...] = fresh

    @pl.when(pl.program_id(0) > 0)
    def _():
        sums_ref[...] += fresh


def encode_back(grad_pair, first, second, slope, combine_w, expand_w, reduce_w, gains, memory_w):
    rows, width = first.shape
    hidden = expand_w.shape[1]
    block = 256
    line = lambda size: pl.BlockSpec((block, size), lambda i: (i, 0))
    sizes = [(width, BF16), (width, BF16), (hidden, BF16), (width, F32), (width, BF16), (width, BF16)]
    return call(
        encode_back_kernel,
        2 * rows * width * (2 * hidden + 3 * width),
        rows * (hidden * 4 + width * 18) + 8 * width * hidden,
        grid=(rows // block,),
        in_specs=[line(2 * width), line(width), line(width), line(hidden)]
        + [whole(item) for item in (combine_w, expand_w, reduce_w, gains, memory_w)],
        out_specs=[line(size) for size, _ in sizes] + [pl.BlockSpec((8, width), lambda i: (0, 0))],
        out_shape=[shape_of((rows, size), kind) for size, kind in sizes] + [shape_of((8, width), F32)],
    )(grad_pair, first, second, slope, combine_w, expand_w, reduce_w, gains, memory_w)


def stacked(rows):
    lane = lax.broadcasted_iota(jnp.int32, (1, rows.shape[1]), 1)
    return jnp.concatenate(
        [jnp.where((lane >= 64 * h) & (lane < 64 * h + 64), rows, jnp.zeros_like(rows)) for h in range(4)],
        axis=0,
    )


def unstacked(rows):
    lane = lax.broadcasted_iota(jnp.int32, (1, rows.shape[1]), 1)
    count = rows.shape[0] // 4
    result = rows[:count]
    for h in range(1, 4):
        result = jnp.where(lane >= 64 * h, rows[h * count : h * count + count], result)
    return result


def few_attend(queries, keys, values, valid):
    mixed = []
    kept = []
    for half in range(2):
        part = slice(256 * half, 256 * half + 256)
        scores = dot(stacked(queries[:, part] * jnp.asarray(0.125, BF16)), keys[:, part], NT)
        if valid < scores.shape[1]:
            column = lax.broadcasted_iota(jnp.int32, (1, scores.shape[1]), 1)
            scores = jnp.where(column < valid, scores, -1e30)
        raised = jnp.exp(scores - jnp.max(scores, axis=1, keepdims=True))
        probs = raised * (1.0 / jnp.sum(raised, axis=1, keepdims=True))
        mixed.append(unstacked(dot(probs.astype(BF16), values[:, part], NN)))
        kept.append(probs)
    return jnp.concatenate(mixed, axis=1).astype(BF16), kept


def few_attend_back(queries, keys, values, kept, grads):
    dq, dk, dv = [], [], []
    for half in range(2):
        part = slice(256 * half, 256 * half + 256)
        probs = kept[half]
        own_queries = stacked(queries[:, part] * jnp.asarray(0.125, BF16))
        own_grads = stacked(grads[:, part])
        grad_probs = dot(own_grads, values[:, part], NT)
        product = probs * grad_probs
        grad_scores = (product - probs * jnp.sum(product, axis=1, keepdims=True)).astype(BF16)
        dv.append(dot(probs.astype(BF16), own_grads, TN))
        dk.append(dot(grad_scores, own_queries, TN))
        dq.append(unstacked(dot(grad_scores, keys[:, part], NN)) * 0.125)
    return jnp.concatenate(dq, axis=1), jnp.concatenate(dk, axis=1), jnp.concatenate(dv, axis=1)


def self_block(starts, project_w, combine_w, gain, shift, valid):
    width = starts.shape[1]
    packed = dot(starts, project_w, NN).astype(BF16)
    queries, keys, values = (packed[:, i * width : (i + 1) * width] for i in range(3))
    mixed, kept = few_attend(queries, keys, values, valid)
    residual = starts.astype(F32) + dot(mixed, combine_w, NN)
    rows, scale = normed(residual)
    return queries, keys, values, mixed, kept, rows, scale, rows * gain + shift


def dealt(rows):
    width = rows.shape[1]
    source = lax.broadcasted_iota(jnp.int32, (width, width), 0)
    target = lax.broadcasted_iota(jnp.int32, (width, width), 1)
    half = width // 2
    wanted = (target % half) // 16 * 32 + target // half * 16 + target % 16
    return dot(rows, jnp.where(source == wanted, 1.0, 0.0).astype(BF16), NN).astype(BF16)


def undealt(columns):
    count, width = columns.shape
    return columns.reshape(count, 2, width // 32, 16).transpose(0, 2, 1, 3).reshape(count, width)


DECODE_WEIGHTS = ("self_project", "self_combine", "cross_query", "pair", "cross_combine", "expand", "reduce")


def cross_attend(queries_ref, pair, stash, mixed_ref):
    width = queries_ref.shape[1]
    rows = 4 * queries_ref.shape[0]

    def half_of(half, carry):
        columns = pl.ds(half * 256, 256)
        value_columns = pl.ds(width + half * 256, 256)
        scores = dot(stacked(queries_ref[:, columns] * jnp.asarray(0.125, BF16)), pair[:, columns], NT)
        raised = jnp.exp(scores - jnp.max(scores, axis=1, keepdims=True))
        probs = (raised * (1.0 / jnp.sum(raised, axis=1, keepdims=True))).astype(BF16)
        stash[pl.ds(half * rows, rows), : pair.shape[0]] = probs
        mixed_ref[:, columns] = unstacked(dot(probs, pair[:, value_columns], NN)).astype(BF16)
        return carry

    for half in range(2):
        half_of(half, None)


def cross_attend_back(queries_ref, pair, stash, grads_ref):
    width = queries_ref.shape[1]
    rows = 4 * queries_ref.shape[0]

    def half_of(half, carry):
        columns = pl.ds(half * 256, 256)
        value_columns = pl.ds(width + half * 256, 256)
        low = stash[pl.ds(half * rows, rows), : pair.shape[0]]
        own_queries = stacked(queries_ref[:, columns] * jnp.asarray(0.125, BF16))
        own_grads = stacked(grads_ref[:, columns])
        probs = low.astype(F32)
        grad_probs = dot(own_grads, pair[:, value_columns], NT)
        inner = jnp.sum(probs * grad_probs, axis=1, keepdims=True)
        grad_scores = (probs * (grad_probs - inner)).astype(BF16)
        dq = unstacked(dot(grad_scores, pair[:, columns], NN)) * 0.125
        pair[:, value_columns] = dot(low, own_grads, TN).astype(BF16)
        pair[:, columns] = dot(grad_scores, own_queries, TN).astype(BF16)
        queries_ref[:, columns] = dq.astype(BF16)
        return carry

    for half in range(2):
        half_of(half, None)


def decode_body(
    pick, valid, loads, held, starts, gain_ref, shift_ref, head_ref, target_ref, arm_ref, acts, hand_out, stash, rooms
):
    for name in ("self_project", "self_combine"):
        loads[name].wait()
    width = starts.shape[1]
    first = self_block(
        starts[...], held["self_project"][...], held["self_combine"][...], gain_ref[0:1, :], shift_ref[0:1, :], valid
    )[-1]
    loads["cross_query"].wait()
    queries, mixed_rows, grads = rooms
    queries[...] = dot(first.astype(BF16), held["cross_query"][...], NN).astype(BF16)
    loads["pair"].wait()
    cross_attend(queries, held["pair"], stash, mixed_rows)
    mixed = mixed_rows[...]
    loads["cross_combine"].wait()
    second_rows, second_scale = normed(first + dot(mixed, held["cross_combine"][...], NN))
    second = second_rows * gain_ref[1:2, :] + shift_ref[1:2, :]
    second_low = second.astype(BF16)
    own = pl.ds(0, PAD_ROWS)
    acts["low_d"][own, :] = dealt(second_low)
    hand_out("low_d")
    loads["expand"].wait()
    loads["reduce"].wait()
    expand_ref, reduce_ref = held["expand"], held["reduce"]
    chunks = column_chunks(expand_ref.shape[1])
    total = second
    slope_rows = pl.ds(8 * PAD_ROWS, PAD_ROWS)
    for start, size in chunks:
        part = pl.ds(start, size)
        active, slope = gelu_and_slope(dot(second_low, expand_ref[:, part], NN))
        stash[slope_rows, part] = slope.astype(BF16)
        active = active.astype(BF16)
        acts["active_d"][own, part] = active
        total = total + dot(active, reduce_ref[part, :], NN)
    hand_out("active_d")
    third_rows, third_scale = normed(total)
    third_low = (third_rows * gain_ref[2:3, :] + shift_ref[2:3, :]).astype(BF16)
    here = pick()
    joints, rows = head_ref.shape[0], starts.shape[0]
    target = target_ref[:, 0, :]
    for index in range(1, target_ref.shape[1]):
        target = jnp.where(here == index, target_ref[:, index, :], target)
    target = jnp.concatenate([target, jnp.zeros((joints, rows - valid), F32)], axis=1)
    misfit = dot(head_ref[...], third_low, NT) - target
    arms = arm_ref[here]
    joint = lax.broadcasted_iota(jnp.int32, misfit.shape, 0)
    row = lax.broadcasted_iota(jnp.int32, misfit.shape, 1)
    factor = 2.0 / jnp.full((1, 1), arms, jnp.int32).astype(F32)
    used = (row < valid) & (joint < joints // 2 * arms)
    grad_pred = jnp.where(used, factor * misfit * lax.rsqrt(misfit * misfit + 1.0), 0.0).astype(BF16)
    head_grad = dot(grad_pred, third_low, NN)
    grad_third = dot(grad_pred, head_ref[...], TN)
    gain_third = column_sum(grad_third * third_rows)
    shift_third = column_sum(grad_third)
    total = normed_back(grad_third, gain_ref[2:3, :], third_rows, third_scale)
    branch = total.astype(BF16)
    acts["branch_d"][own, :] = branch
    hand_out("branch_d")
    for start, size in chunks:
        part = pl.ds(start, size)
        grad_hidden = (dot(branch, reduce_ref[part, :], NT) * stash[slope_rows, part].astype(F32)).astype(BF16)
        acts["hidden_d"][own, part] = grad_hidden
        total = total + dot(grad_hidden, expand_ref[:, part], NT)
    hand_out("hidden_d")
    gain_second = column_sum(total * second_rows)
    shift_second = column_sum(total)
    grad_second = normed_back(total, gain_ref[1:2, :], second_rows, second_scale)
    branch = grad_second.astype(BF16)
    grads[...] = dot(branch, held["cross_combine"][...], NT).astype(BF16)
    cross_attend_back(queries, held["pair"], stash, grads)
    sums = jnp.concatenate([gain_second, gain_third, shift_second, shift_third], axis=0)
    return branch, queries[...], mixed, sums, head_grad


DECODE_VECTORS = ("gains", "shifts", "head", "targets")


def decode_kernel(pick, starts_ref, *refs):
    refs = list(refs)

    def draw(count):
        taken = refs[:count]
        del refs[:count]
        return taken

    sources = draw(7)
    gain_ref, shift_ref, head_ref, target_ref, arm_ref = draw(5)
    starts_out, grad_pair_ref, low_ref, hidden_ref, active_ref, branch_ref, cross_grad_ref, small_ref, tiny_ref = draw(9)
    held = dict(zip(DECODE_WEIGHTS, draw(7)))
    stash, *rooms, load_sems = draw(5)
    loads = {}
    for index, (name, source) in enumerate(zip(DECODE_WEIGHTS, sources)):
        loads[name] = pltpu.make_async_copy(source, held[name], load_sems.at[index])
        loads[name].start()
    valid = starts_ref.shape[0]
    starts_out[...] = jnp.zeros_like(starts_out)
    starts_out[pl.ds(0, valid), :] = starts_ref[...]
    acts = {"low_d": low_ref, "hidden_d": hidden_ref, "active_d": active_ref, "branch_d": branch_ref}
    branch, dq, mixed, sums, head_grad = decode_body(
        pick, valid, loads, held, starts_out, gain_ref, shift_ref, head_ref, target_ref, arm_ref, acts, lambda name: None,
        stash, rooms,
    )
    small_ref[pl.ds(0, PAD_ROWS), :] = branch
    small_ref[pl.ds(PAD_ROWS, PAD_ROWS), :] = dq
    cross_grad_ref[...] = dot(mixed, branch, TN).astype(BF16)
    grad_pair_ref[...] = held["pair"][...]
    tiny_ref[...] = jnp.zeros_like(tiny_ref)
    tiny_ref[pl.ds(0, 4), :] = sums
    tiny_ref[pl.ds(8, head_ref.shape[0]), :] = head_grad


def decode_sources(weights, pair):
    return (weights[7], weights[8], weights[9], pair, weights[11], weights[12], weights[13])


def decode(pick, targets, arms, weights, pair):
    starts, head = weights[6], weights[16]
    width = starts.shape[1]
    hidden = weights[12].shape[1]
    sources = decode_sources(weights, pair)
    shapes = {
        "starts": ((PAD_ROWS, width), BF16),
        "grad_pair": (pair.shape, BF16),
        "low_d": ((PAD_ROWS, width), BF16),
        "hidden_d": ((PAD_ROWS, hidden), BF16),
        "active_d": ((PAD_ROWS, hidden), BF16),
        "branch_d": ((PAD_ROWS, width), BF16),
        "cross": ((width, width), BF16),
        "small": ((SMALL_ROWS, width), BF16),
        "tiny": ((TINY_ROWS, width), F32),
    }
    in_vmem = pl.BlockSpec(memory_space=pltpu.VMEM)
    results = call(
        functools.partial(decode_kernel, pick),
        8 * PAD_ROWS * width * hidden * 2,
        20 * 1024 * 1024,
        in_specs=[in_vmem] + [pl.BlockSpec(memory_space=pl.ANY)] * 7 + [in_vmem] * 4
        + [pl.BlockSpec(memory_space=pltpu.SMEM)],
        out_specs=[in_vmem] * len(shapes),
        out_shape=[shape_of(dims, kind) for dims, kind in shapes.values()],
        scratch_shapes=[pltpu.VMEM(item.shape, BF16) for item in sources]
        + [pltpu.VMEM((pair.shape[0], hidden), BF16)] + [pltpu.VMEM((PAD_ROWS, width), BF16)] * 3
        + [pltpu.SemaphoreType.DMA((7,))],
    )(starts, *sources, weights[14], weights[15], head.T, targets.transpose(2, 0, 1), arms)
    return dict(zip(shapes, results))


def decode_start_back_kernel(
    valid,
    starts_ref, project_ref, combine_ref, query_ref, gain_ref, shift_ref, resid_ref, query_grad_ref,
    start_grad_ref, project_grad_ref, combine_grad_ref, query_w_grad_ref, sums_ref,
):
    starts = starts_ref[...]
    project_w = project_ref[...]
    queries, keys, values, mixed, kept, rows, scale, first = self_block(
        starts, project_w, combine_ref[...], gain_ref[0:1, :], shift_ref[0:1, :], valid
    )
    low = query_grad_ref[...].astype(BF16)
    query_w_grad_ref[...] = dot(first.astype(BF16), low, TN)
    grad_first = resid_ref[...] + dot(low, query_ref[...], NT)
    gain_sum = column_sum(grad_first * rows)
    shift_sum = column_sum(grad_first)
    grad_resid = normed_back(grad_first, gain_ref[0:1, :], rows, scale)
    branch = grad_resid.astype(BF16)
    combine_grad_ref[...] = dot(mixed, branch, TN)
    grad_mixed = dot(branch, combine_ref[...], NT).astype(BF16)
    dq, dk, dv = few_attend_back(queries, keys, values, kept, grad_mixed)
    grad_packed = jnp.concatenate([dq, dk, dv], axis=1).astype(BF16)
    project_grad_ref[...] = dot(starts, grad_packed, TN)
    start_grad_ref[...] = grad_resid + dot(grad_packed, project_w, NT)
    sums_ref[...] = jnp.concatenate([gain_sum, shift_sum, jnp.zeros((6, gain_sum.shape[1]), F32)], axis=0)


def decode_start_back(valid, starts, project_w, combine_w, query_w, gains, shifts, resid, query_grad):
    count, width = starts.shape
    arrays = (starts, project_w, combine_w, query_w, gains, shifts, resid, query_grad)
    shapes = [(count, width), (width, 3 * width), (width, width), (width, width), (8, width)]
    return call(
        functools.partial(decode_start_back_kernel, valid),
        2 * count * width * width * 20,
        8 * 1024 * 1024,
        in_specs=[pl.BlockSpec(memory_space=pltpu.VMEM)] * len(arrays),
        out_specs=[pl.BlockSpec(memory_space=pltpu.VMEM)] * len(shapes),
        out_shape=[shape_of(dims, F32) for dims in shapes],
    )(*arrays)


def forward(x, pick, weights):
    saved = encode(x, pick, weights[:4] + (weights[10],), weights[4], weights[5])
    saved["x"] = x
    return saved


def backward_alone(saved, x, weights):
    (encoder_project, encoder_combine, encoder_expand, encoder_reduce, encoder_gains) = weights[:5]
    cross_memory = weights[10]
    grad_memory, branch, grad_hidden, resid, low, grad_mixed, sums_e = encode_back(
        saved["grad_pair"], saved["first"], saved["second"], saved["slope"],
        encoder_combine, encoder_expand, encoder_reduce, encoder_gains, cross_memory,
    )
    dq, dk, dv = attend_back(saved["packed"], grad_mixed, saved["mixed"], saved["logs"])
    grad_packed = jnp.concatenate([dq, dk, dv], axis=1)
    grad_x = (resid + dot(grad_packed, encoder_project, NT)).astype(BF16)
    plain = lambda left, right: dot(left, right, TN)
    return grad_x, grad_memory, {
        "decoder_expand": plain(undealt(saved["low_d"]), saved["hidden_d"]),
        "decoder_reduce": plain(saved["active_d"], saved["branch_d"]),
        "encoder_reduce": plain(saved["active"], branch),
        "encoder_expand": plain(saved["low"], grad_hidden),
        "middle": jnp.concatenate(
            [plain(saved["memory"], saved["grad_pair"]), saved["cross"].astype(F32), dot(saved["mixed"], low, NN)], axis=1
        ),
        "last": plain(x, grad_packed),
        "small": saved["small"].astype(F32),
        "tiny": saved["tiny"].at[4:8].set(sums_e[:4]),
    }


SECTION, SIDE, LINE = range(3)
GROUPS = {
    "decoder_expand0": (SIDE, SECTION, LINE),
    "decoder_expand1": (LINE, SIDE, SECTION),
    "decoder_reduce0": (SIDE, LINE, SECTION),
    "decoder_reduce1": (LINE, SIDE, SECTION),
    "encoder_reduce0": (SECTION, SIDE, LINE),
    "encoder_reduce1": (SIDE, SECTION, LINE),
    "encoder_expand0": (SECTION, SIDE, LINE),
    "encoder_expand1": (SIDE, LINE, SECTION),
    "middle0": (SIDE, LINE, SECTION),
    "middle1": (SIDE, SECTION, LINE),
    "last0": (SECTION, SIDE, LINE),
    "last1": (SIDE, LINE, SECTION),
}
NAMES = tuple(GROUPS)
SCHEDULE = {
    "dfe0": ("small",),
    "dmem": ("decoder_reduce1",),
    "efr1": ("decoder_reduce0", "small", "decoder_expand1",),
    "dwm": ("encoder_reduce0",),
    "du0": ("encoder_reduce1", "decoder_reduce1",),
    "du1": ("middle0", "decoder_reduce0",),
    "df": ("decoder_expand0", "small",),
    "ln": ("decoder_expand1",),
    "efe0": ("encoder_reduce1", "tiny",),
    "efe1": ("decoder_reduce1",),
    "dwc": ("encoder_expand0", "decoder_reduce0",),
    "att0": ("encoder_expand1", "middle0", "middle1",),
    "att1": ("small", "decoder_reduce1",),
    "att3": ("decoder_expand1",),
    "last0": ("encoder_reduce0", "decoder_reduce0",),
    "att4": ("encoder_expand1", "middle0",),
    "att5": ("last0", "decoder_expand0",),
    "att6": ("small", "middle1",),
    "att7": ("encoder_reduce1", "encoder_expand1", "tiny", "middle0", "decoder_expand1",),
    "dx0": ("decoder_expand0",),
    "dx1": ("encoder_reduce1",),
    "last1": ("encoder_reduce0", "encoder_expand1",),
}
TAIL_FIRST = ("tiny", "middle0", "last1", "decoder_expand0", "encoder_expand0", "small", )
TAIL = (
    "last1",
    "encoder_reduce0",
    "encoder_expand1",
    "tiny",
    "encoder_reduce1",
    "decoder_reduce0",
    "decoder_reduce1",
    "decoder_expand0",
    "last0",
    "last1",
    "decoder_reduce0",
    "decoder_reduce1",
    "encoder_reduce0",
    "decoder_expand0",
    "encoder_expand0",
    "tiny",
    "middle1",
    "decoder_expand1",
    "encoder_reduce1",
    "last0",
    "last1",
    "tiny",
    "encoder_reduce0",
    "decoder_expand1",
    "encoder_reduce1",
    "encoder_expand0",
    "middle1",
    "last0",
    "encoder_reduce0",
    "last1",
    "encoder_expand0",
    "middle1",
    "last0",
    "middle0",
    "encoder_expand0",
    "middle1",
    "encoder_expand1",
    "last0",
    "last1",
    "middle0",
    "encoder_expand0",
    "middle1",
    "encoder_expand1",
    "last0",
    "last1",
)
STEPS = 7
LINE_ROUNDS = 3


class Links:
    def __init__(self):
        core = lax.axis_index("rep")
        section = lax.axis_index("section")
        lane = lax.axis_index("dp")
        self.core = core
        self.section = section
        self.lane = lane
        self.level = lane // 2
        self.side = lane % 2
        self.mine = [section, self.side]
        self.other_core = {"rep": 1 - core}
        self.partner = [{"section": 1 - section}, {"dp": lane + 1 - 2 * self.side}]
        self.above = {"dp": lane + 2}
        self.below = {"dp": lane - 2}

    def signal(self, semaphore, device):
        pl.semaphore_signal(semaphore, inc=1, device_id=device, device_id_type=pl.DeviceIdType.MESH)

    def tell(self, semaphores):
        for semaphore, device in zip(semaphores[:3], [self.other_core] + self.partner):
            self.signal(semaphore, device)

        @pl.when(self.level > 0)
        def _():
            self.signal(semaphores[3], self.below)

        @pl.when(self.level < 3)
        def _():
            self.signal(semaphores[4], self.above)

    def greet(self):
        self.tell([pltpu.get_barrier_semaphore()] * 5)

    def meet(self):
        barrier = pltpu.get_barrier_semaphore()
        pl.semaphore_wait(barrier, 3 + (self.level + 3) // 4 + (6 - self.level) // 4)

    def copy(self, source, target, sems, device):
        return pltpu.make_async_remote_copy(
            src_ref=source,
            dst_ref=target,
            send_sem=sems[0],
            recv_sem=sems[1],
            device_id=device,
            device_id_type=pl.DeviceIdType.MESH,
        )


def stage_blocks(order):
    counts, size = [], 16
    for dim in order:
        counts.append(5 * size // 4 if dim == LINE else size // 2)
        size = size // 4 if dim == LINE else size // 2
    return counts


class Scatter:
    def __init__(self, links, order, keep, sent, arrived, stages, send_sems, recv_sems, index, out, credits=None):
        self.links, self.order, self.keep, self.out = links, order, keep, out
        self.sent, self.arrived, self.credits = sent, arrived, credits
        self.sems = lambda step, way=0: (send_sems.at[index, step, way], recv_sems.at[index, step, way])
        self.plan = [] if sent is None else [("core",)]
        base, size = 0, 16
        for dim, buffer in zip(order, stages):
            if dim == LINE:
                size //= 4
                self.plan += [("line", turn, base, size, buffer) for turn in (1, 2, 3)]
                base = base + links.level * size
            else:
                size //= 2
                mine = links.mine[dim]
                self.plan.append(("halve", dim, base + (1 - mine) * size, base + mine * size, size, buffer))
                base = base + mine * size
        self.base = base
        self.plan.append(("both",))
        self.step = 0

    def place(self, shard):
        index, size = 0, 16
        for dim in self.order:
            size //= 4 if dim == LINE else 2
            index += size * {SECTION: shard // 8, LINE: shard // 2 % 4, SIDE: shard % 2}[dim]
        return index

    def single(self, step):
        links, kind = self.links, self.plan[step][0]
        if kind == "core":
            return links.copy(self.sent, self.arrived, self.sems(step), links.other_core)
        if kind == "halve":
            _, dim, away, _, size, buffer = self.plan[step]
            return links.copy(self.keep.at[pl.ds(away, size)], buffer, self.sems(step), links.partner[dim])
        return links.copy(self.out.at[links.core], self.out.at[links.core], self.sems(step), links.other_core)

    def lines(self, step):
        links, level = self.links, self.links.level
        _, turn, base, size, buffer = self.plan[step]
        shards = lambda ref, index: ref.at[pl.ds(index * size, size)]
        keep = lambda shard: self.keep.at[pl.ds(base + shard * size, size)]
        up, down = level + 4 - turn, level - 4 + turn
        return [
            (
                (level < turn) & (level < 3),
                lambda: links.copy(keep(up), shards(buffer, turn - level - 1), self.sems(step, 0), links.above),
                (level > 0) & (level <= turn),
                lambda: links.copy(keep(up - 1), shards(buffer, turn - level), self.sems(step, 0), links.above),
                lambda: (base + (up - 1) * size, (turn - level) * size),
                level == turn - 1,
            ),
            (
                (3 - level < turn) & (level > 0),
                lambda: links.copy(keep(down), shards(buffer, turn + 1), self.sems(step, 1), links.below),
                (level < 3) & (3 - level <= turn),
                lambda: links.copy(keep(down + 1), shards(buffer, turn + 1), self.sems(step, 1), links.below),
                lambda: (base + (down + 1) * size, (turn + 1) * size),
                3 - level == turn - 1,
            ),
        ]

    def start(self):
        step = self.step
        plan = self.plan[step]
        if plan[0] == "line":
            for way, (sends, sent, _, _, _, opens) in enumerate(self.lines(step)):

                @pl.when(sends)
                def _():
                    if self.credits is not None:

                        @pl.when(opens)
                        def _():
                            pl.semaphore_wait(self.credits.at[3 + way], 1)

                    sent().start()

            return
        if self.credits is not None and plan[0] != "both":
            pl.semaphore_wait(self.credits.at[0 if plan[0] == "core" else 1 + plan[1]], 1)
        if plan[0] == "both":
            self.out[pl.ds(self.links.core, 1)] = self.keep[pl.ds(self.base, 1)]
        self.single(step).start()

    def add(self, source, first, base, size):
        keep = self.keep

        def body(i, carry):
            keep[base + i] = keep[base + i] + source[first + i]
            return carry

        lax.fori_loop(0, size, body, 0)

    def finish(self):
        step = self.step
        plan = self.plan[step]
        if plan[0] == "line":
            for _, _, comes, arrived, where, _ in self.lines(step):

                @pl.when(comes)
                def _():
                    arrived().wait_recv()
                    base, first = where()
                    self.add(plan[4], first, base, plan[3])

        else:
            self.single(step).wait_recv()
            if plan[0] == "core":
                self.add(self.arrived, 0, 0, 16)
            elif plan[0] == "halve":
                self.add(plan[5], 0, plan[3], plan[4])
        self.step += 1

    def advance(self):
        self.finish()
        if self.step < len(self.plan):
            self.start()

    def close(self):
        assert self.step == len(self.plan)
        for step, plan in enumerate(self.plan):
            if plan[0] == "line":
                for sends, sent, _, _, _, _ in self.lines(step):

                    @pl.when(sends)
                    def _():
                        sent().wait_send()

            else:
                self.single(step).wait_send()


class Total:
    def __init__(self, links, levels, arrived, send_sems, recv_sems, index):
        self.links, self.levels, self.arrived = links, levels, arrived
        level = links.level
        everyone = level >= 0
        near = {"dp": links.lane + 2 - 4 * (level % 2)}
        middle = {"dp": links.lane + 6 - 4 * level}
        inner = (level == 1) | (level == 2)
        outer = {"dp": links.lane - 6 + 4 * level}
        self.turns = [
            (everyone, everyone, links.other_core), (everyone, everyone, links.partner[SECTION]),
            (everyone, everyone, near), (inner, inner, middle), (inner, jnp.logical_not(inner), outer),
            (everyone, everyone, links.partner[SIDE]),
        ]
        self.sems = lambda step: (send_sems.at[index, step, 0], recv_sems.at[index, step, 0])
        self.step = 0
        self.result = levels.at[0]

    def copy_of(self, step):
        return self.links.copy(
            self.levels.at[step % 2], self.arrived.at[step - step // 4], self.sems(step), self.turns[step][2]
        )

    def start(self):
        step = self.step

        @pl.when(self.turns[step][0])
        def _():
            self.copy_of(step).start()

    def sent(self, step):
        @pl.when(self.turns[step][0])
        def _():
            self.copy_of(step).wait_send()

    def advance(self):
        step = self.step
        if step > 0:
            self.sent(step - 1)
        comes = self.turns[step][1]

        @pl.when(comes)
        def _():
            self.copy_of(step).wait_recv()
            value = self.arrived[step - step // 4].astype(F32)
            if step != 4:
                value = self.levels[step % 2].astype(F32) + value
            self.levels[(step + 1) % 2] = value.astype(self.levels.dtype)

        @pl.when(jnp.logical_not(comes))
        def _():
            self.levels[(step + 1) % 2] = self.levels[step % 2]

        self.step += 1
        if self.step < 6:
            self.start()

    def close(self):
        assert self.step == 6
        self.sent(5)


ACT_NAMES = ("low_d", "hidden_d", "active_d", "branch_d")
IN_NAMES = (
    "memory", "cross_memory", "second", "active", "reduce", "slope", "expand", "first", "low", "mixed", "combine",
    "packed", "logs", "x", "project", "self_project", "self_combine", "cross_query",
)
ATTEND_BLOCK = 256


def backward_kernel(*refs):
    refs = list(refs)

    def draw(count):
        taken = refs[:count]
        del refs[:count]
        return taken

    source = dict(zip(IN_NAMES, draw(len(IN_NAMES))))
    source["x"] = source["x"].at[lax.axis_index("section")]
    decode_refs = dict(zip(DECODE_WEIGHTS, draw(7)))
    gain_ref, starts_ref, self_gain_ref, self_shift_ref, head_ref, target_ref, arm_ref = draw(7)
    outs = dict(zip(NAMES, draw(len(NAMES))))
    memory_out, slab_out, grad_memory_out, grad_x_out, self_rows_out, stack_out = draw(6)
    acts = dict(zip(ACT_NAMES, draw(4)))
    buffers = {}
    for name in NAMES:
        if name.startswith("decoder"):
            buffers[name] = [None, None] + draw(3)
        elif not name.startswith("encoder_expand"):
            buffers[name] = draw(5)
    keeps = {}
    for name in NAMES:
        if not name.startswith("encoder_expand"):
            keeps[name] = draw(1)[0]
    expand_stages = [draw(3), draw(3)]
    hidden, slope, grad_mixed, resid, mixed, branch, small_levels, small_arrived, tiny_levels, tiny_arrived = draw(10)
    send_sems, recv_sems, act_sems, slab_sems, load_sems, decode_sems, store_sems, credits = draw(8)
    valid = starts_ref.shape[0]
    width = resid.shape[1]
    count = resid.shape[0]
    hidden_size = hidden.shape[1]
    cut = split_of(hidden_size)
    for index, columns in enumerate((pl.ds(0, cut), pl.ds(cut, hidden_size - cut))):
        name = "encoder_expand%d" % index
        rows = lambda start, size: slope.at[pl.ds(start, size), :, columns]
        keeps[name] = rows(0, 16)
        buffers[name] = [rows(16, 16), rows(32, 16)] + expand_stages[index]

    links = Links()
    core = links.core
    block = 256
    chunks = column_chunks(hidden_size)
    own_columns = pl.ds(pl.multiple_of(core * 256, 256), 256)
    other_columns = pl.ds(pl.multiple_of((1 - core) * 256, 256), 256)
    work = {}
    for index, name in enumerate(NAMES):
        sent, arrived, *stages = buffers[name]
        work[name] = Scatter(
            links, GROUPS[name], keeps[name], sent, arrived, stages, send_sems, recv_sems, index, outs[name],
            credits.at[int(name[-1])] if name.startswith("encoder_expand") else None,
        )
    work["small"] = Total(links, small_levels, small_arrived, send_sems, recv_sems, len(NAMES))
    work["tiny"] = Total(links, tiny_levels, tiny_arrived, send_sems, recv_sems, len(NAMES) + 1)

    def tick(label):
        for name in SCHEDULE.get(label, ()):
            work[name].advance()

    def loading(name, target):
        return pltpu.make_async_copy(source[name], target, load_sems.at[IN_NAMES.index(name)])

    def load(name, target):
        copy = loading(name, target)
        copy.start()
        return copy

    def deal(name, rows, first_column):
        item = work[name]
        columns = pl.ds(first_column, rows.shape[1])
        low = rows.astype(BF16)
        for shard in range(16):
            here = low[32 * shard : 32 * shard + 16]
            there = low[32 * shard + 16 : 32 * shard + 32]
            place = item.place(shard)
            item.keep[place, :, columns] = jnp.where(core == 0, here, there)
            item.sent[place, :, columns] = jnp.where(core == 0, there, here)

    def deal_columns(names, targets, rows):
        size = rows.shape[0] // 16
        for index, (name, target) in enumerate(zip(names, targets)):
            for shard in range(16):
                target[work[name].place(shard)] = rows[
                    size * shard : size * shard + size, LANES * index : LANES * index + LANES
                ].astype(BF16)

    links.greet()
    def slab_copies(out):
        parts = [pl.ds(index * (count // 2), count // 2) for index in range(2)]
        return [
            links.copy(
                out.at[part], slab_out.at[part], (slab_sems.at[0, index], slab_sems.at[1, index]), links.partner[SECTION]
            )
            for index, part in enumerate(parts)
        ]

    memory_copy = links.copy(source["memory"], memory_out, (act_sems.at[0, 4], act_sems.at[1, 4]), links.partner[SECTION])

    def act_copy(name):
        index = ACT_NAMES.index(name)
        return links.copy(
            acts[name].at[pl.ds(0, PAD_ROWS)], acts[name].at[pl.ds(PAD_ROWS, PAD_ROWS)],
            (act_sems.at[0, index], act_sems.at[1, index]), links.other_core,
        )

    def pad_starts(starts):
        starts[...] = jnp.zeros_like(starts)
        starts[pl.ds(0, valid), :] = starts_ref[...]

    def decode_phase(pair, starts, room0, room1, room2, *weights):
        held = dict(zip([name for name in DECODE_WEIGHTS if name != "pair"], weights), pair=pair)
        loads = {}
        for index, name in enumerate(DECODE_WEIGHTS):
            loads[name] = pltpu.make_async_copy(decode_refs[name], held[name], decode_sems.at[index])
            loads[name].start()
        links.meet()
        memory_copy.start()
        pad_starts(starts)

        def hand_out(name):
            act_copy(name).start()
            if name == "low_d":
                load("slope", slope)

        branch, dq, mixed, sums, head_grad = decode_body(
            lambda: links.section, valid, loads, held, starts, self_gain_ref, self_shift_ref, head_ref, target_ref,
            arm_ref, acts, hand_out, hidden, (room0, room1, room2),
        )
        load("active", hidden)
        small_levels[0, pl.ds(0, PAD_ROWS), :] = branch
        small_levels[0, pl.ds(PAD_ROWS, PAD_ROWS), :] = dq
        work["small"].start()
        tiny_levels[0] = jnp.zeros(tiny_levels.shape[1:], F32)
        tiny_levels[0, pl.ds(0, 4), :] = sums
        tiny_levels[0, pl.ds(8, head_ref.shape[0]), :] = head_grad
        deal("middle1", dot(mixed, branch, TN), 0)

    back_copies = slab_copies(grad_memory_out)
    front_copies = slab_copies(grad_x_out)

    def rows_phase(grad_pair, memory_w, residual, rows_low, reduce_w, expand_w, combine_w):
        loads = {
            name: load(name, target)
            for name, target in (
                ("cross_memory", memory_w), ("second", residual), ("memory", rows_low), ("reduce", reduce_w),
                ("expand", expand_w), ("mixed", mixed), ("combine", combine_w),
            )
        }
        loads.update(active=loading("active", hidden), slope=loading("slope", slope))

        for name in ACT_NAMES:
            act_copy(name).wait_recv()
        names = ("decoder_reduce0", "decoder_reduce1")
        deal_columns(
            names, [work[name].keep for name in names],
            dot(acts["active_d"][...], acts["branch_d"][:, own_columns], TN),
        )
        for name in names:
            work[name].start()
        tick("dfr")
        for index, (start, size) in enumerate(chunks):
            rows = dot(acts["low_d"][:, own_columns], acts["hidden_d"][:, pl.ds(start, size)], TN).astype(BF16)
            item = work["decoder_expand%d" % (index // 2)]
            columns = pl.ds(start - (index // 2) * cut, size)
            for shard in range(16):
                item.keep[item.place(shard), :, columns] = rows[16 * shard : 16 * shard + 16]
            if index % 2:
                item.start()
                tick("dfe%d" % (index // 2))

        loads["cross_memory"].wait()
        loads["second"].wait()
        sums = None
        for start in range(0, count, block):
            part = pl.ds(start, block)
            low_grad = dot(grad_pair[part, :], memory_w[...], NT).astype(BF16)
            grad_mixed[part, :] = low_grad
            grad = low_grad.astype(F32)
            rows, scale = normed(residual[part, :])
            fresh = [column_sum(grad * rows), column_sum(grad)]
            sums = fresh if sums is None else [old + new for old, new in zip(sums, fresh)]
            total = normed_back(grad, gain_ref[1:2, :], rows, scale)
            resid[part, :] = total
            branch[part, :] = total.astype(BF16)
        memory_store = pltpu.make_async_copy(grad_mixed, grad_memory_out, store_sems.at[0])
        memory_store.start()
        loads["first"] = load("first", residual)
        last_sums = sums
        tick("dmem")

        loads["active"].wait()
        names = ("encoder_reduce0", "encoder_reduce1")
        deal_columns(names, [work[name].sent for name in names], dot(hidden[...], branch[:, other_columns], TN))
        for name in names:
            work[name].start()
        memory_store.wait()

        @pl.when(links.section == 0)
        def _():
            for copy in back_copies:
                copy.start()

        tick("efr0")
        deal_columns(names, [work[name].keep for name in names], dot(hidden[...], branch[:, own_columns], TN))
        tick("efr1")
        loads["memory"].wait()
        deal("middle0", dot(rows_low[...], grad_pair[...], TN), 0)
        loads["low"] = load("low", rows_low)
        work["middle0"].start()
        tick("dwm")
        loads["reduce"].wait()
        loads["slope"].wait()
        for index, (start, size) in enumerate(chunks):
            columns = pl.ds(start, size)
            grad_active = dot(branch[...], reduce_w[columns, :], NT)
            inner = slope[:, :, columns].reshape(count, size).astype(F32)
            hidden[:, columns] = (grad_active * inner).astype(BF16)
            tick("du%d" % index)
        for half in range(2):
            links.tell([credits.at[half, index] for index in range(5)])
        loads["expand"].wait()
        resid[...] += dot(hidden[...], expand_w[...], NT)
        tick("df")

        loads["first"].wait()
        loads["combine"].wait()
        sums = None
        for start in range(0, count, block):
            part = pl.ds(start, block)
            grad = resid[part, :]
            rows, scale = normed(residual[part, :])
            fresh = [column_sum(grad * rows), column_sum(grad)]
            sums = fresh if sums is None else [old + new for old, new in zip(sums, fresh)]
            total = normed_back(grad, gain_ref[0:1, :], rows, scale)
            resid[part, :] = total
            low_grad = total.astype(BF16)
            branch[part, :] = low_grad
            grad_mixed[part, :] = dot(low_grad, combine_w[...], NT).astype(BF16)
        tiny_levels[0, 4:8, :] = jnp.concatenate([sums[0], last_sums[0], sums[1], last_sums[1]], axis=0)
        work["tiny"].start()
        tick("ln")
        loads["low"].wait()
        for index, (start, size) in enumerate(chunks):
            name = "encoder_expand%d" % (index // 2)
            deal(name, dot(rows_low[...], hidden[:, pl.ds(start, size)], TN), start - (index // 2) * cut)
            if index % 2:
                work[name].start()
                tick("efe%d" % (index // 2))

    def first_phases(pair):
        pl.run_scoped(
            functools.partial(decode_phase, pair),
            *[pltpu.VMEM((PAD_ROWS, width), BF16)] * 4,
            *[pltpu.VMEM(decode_refs[name].shape, BF16) for name in DECODE_WEIGHTS if name != "pair"],
        )
        pl.run_scoped(
            functools.partial(rows_phase, pair),
            pltpu.VMEM((width, 2 * width), BF16),
            pltpu.VMEM((count, width), F32),
            pltpu.VMEM((count, width), BF16),
            pltpu.VMEM((hidden_size, width), BF16),
            pltpu.VMEM((width, hidden_size), BF16),
            pltpu.VMEM((width, width), BF16),
        )

    pl.run_scoped(first_phases, pltpu.VMEM((count, 2 * width), BF16))

    def attend_phase(packed, logs, x, project_w, grad_packed, starts, self_project, self_combine, cross_query):
        loads = {
            name: load(name, target)
            for name, target in (
                ("packed", packed), ("logs", logs), ("x", x), ("project", project_w),
                ("self_project", self_project), ("self_combine", self_combine), ("cross_query", cross_query),
            )
        }
        loading("mixed", mixed).wait()
        deal("middle1", dot(mixed[...], branch[...], NN), width)
        work["middle1"].start()
        tick("dwc")
        loads["packed"].wait()
        loads["logs"].wait()
        pairs = width // LANES
        half = width // 2

        def last(index):
            columns = slice(index * half, index * half + half)
            for third in range(3):
                deal("last%d" % index, dot(x[...], grad_packed[third, :, columns], TN), third * half)
            work["last%d" % index].start()

        for pair in range(pairs):
            columns = pl.ds(pair * LANES, LANES)
            attend_back_pair(
                packed[:, columns],
                packed[:, pl.ds(width + pair * LANES, LANES)],
                packed[:, pl.ds(2 * width + pair * LANES, LANES)],
                grad_mixed[:, columns],
                mixed[columns, :],
                logs[pair],
                grad_packed, columns,
                lambda head: tick("att%d" % (2 * pair + head)),
            )
            if pair == pairs // 2 - 1:
                loads["x"].wait()
                last(0)
                tick("last0")
        loads["project"].wait()
        stores = []
        for index in range(2):
            part = pl.ds(index * (count // 2), count // 2)
            total = resid[part, :]
            for third in range(3):
                total = total + dot(
                    grad_packed[third, part, :], project_w[:, third * width : (third + 1) * width], NT
                )
            packed[part, pl.ds(0, width)] = total.astype(BF16)
            store = pltpu.make_async_copy(packed.at[part, pl.ds(0, width)], grad_x_out.at[part], store_sems.at[1 + index])
            store.start()
            tick("dx%d" % index)
            store.wait()

            @pl.when(links.section == 1)
            def _():
                front_copies[index].start()

        last(1)
        tick("last1")
        pad_starts(starts)
        for name in IN_NAMES[-3:]:
            loads[name].wait()
        for name in TAIL_FIRST:
            work[name].advance()
        rows = SMALL_ROWS // 2
        start_back(
            valid, starts[...], self_project[...], self_combine[...], cross_query[...], self_gain_ref[0:1, :],
            self_shift_ref[0:1, :], work["small"].result[pl.ds(0, rows), :].astype(F32),
            work["small"].result[pl.ds(rows, rows), :], links, self_rows_out, stack_out,
        )

    pl.run_scoped(
        attend_phase,
        pltpu.VMEM((count, 3 * width), BF16),
        pltpu.VMEM(source["logs"].shape, F32),
        pltpu.VMEM((count, width), BF16),
        pltpu.VMEM((width, 3 * width), BF16),
        pltpu.VMEM((3, count, width), BF16),
        pltpu.VMEM((PAD_ROWS, width), BF16),
        pltpu.VMEM((width, 3 * width), BF16),
        pltpu.VMEM((width, width), BF16),
        pltpu.VMEM((width, width), BF16),
    )
    for name in TAIL:
        work[name].advance()
    stack_out[pl.ds(SMALL_ROWS // 2 + 8, TINY_ROWS), :] = work["tiny"].result[...]
    memory_copy.wait()
    for copy in back_copies:
        copy.wait_recv()
    for name in ACT_NAMES:
        act_copy(name).wait_send()
    for item in work.values():
        item.close()
    for copy in back_copies:
        copy.wait_send()


def start_back(valid, starts, project_w, combine_w, query_w, gain, shift, resid, query_grad, links, rows_out, stack_out):
    width = starts.shape[1]
    own = rows_out.shape[0]
    place = (links.section * 8 + links.lane) * own
    chosen = lax.broadcasted_iota(jnp.int32, (width, own), 0) == place + lax.broadcasted_iota(
        jnp.int32, (width, own), 1
    )
    chosen = jnp.where(chosen, 1.0, 0.0).astype(BF16)
    select = lambda value: dot(value, chosen, NN).astype(BF16)
    queries, keys, values, mixed, kept, rows, scale, first = self_block(
        starts, project_w, combine_w, gain, shift, valid
    )
    rows_out[:, pl.ds(4 * width, width)] = dot(select(first.astype(BF16)), query_grad, TN)
    grad_first = resid + dot(query_grad, query_w, NT)
    gain_sum = column_sum(grad_first * rows)
    shift_sum = column_sum(grad_first)
    grad_resid = normed_back(grad_first, gain, rows, scale)
    branch = grad_resid.astype(BF16)
    rows_out[:, pl.ds(3 * width, width)] = dot(select(mixed), branch, TN)
    grad_mixed = dot(branch, combine_w, NT).astype(BF16)
    dq, dk, dv = few_attend_back(queries, keys, values, kept, grad_mixed)
    grad_packed = jnp.concatenate([dq, dk, dv], axis=1).astype(BF16)
    rows_out[:, pl.ds(0, 3 * width)] = dot(select(starts), grad_packed, TN)
    count = starts.shape[0]
    stack_out[pl.ds(0, count), :] = grad_resid + dot(grad_packed, project_w, NT)
    stack_out[pl.ds(count, 8), :] = jnp.concatenate([gain_sum, shift_sum, jnp.zeros((6, width), F32)], axis=0)


def attend_back_pair(queries, keys, values, grads, mixed, logs, out, columns, between):
    count = queries.shape[0]
    lane = lax.broadcasted_iota(jnp.int32, (1, LANES), 1)
    queries = queries * jnp.asarray(0.125, BF16)
    scaled_keys = keys * jnp.asarray(0.125, BF16)
    queries_t = queries.T
    grads_t = grads.T
    logs = logs.T
    shared = mixed.astype(F32) * grads_t.astype(F32)
    inner = jnp.concatenate([column_sum(shared[:64]), column_sum(shared[64:])], axis=0).T
    dq_parts = [[], []]
    dk_parts = []
    dv_parts = []
    for head in range(2):
        own = (lane < 64) if head == 0 else (lane >= 64)
        head_queries = jnp.where(own, queries, jnp.zeros_like(queries))
        head_grads = jnp.where(own, grads, jnp.zeros_like(grads))
        dk = None
        dv = None
        for start in range(0, count, ATTEND_BLOCK):
            part = slice(start, start + ATTEND_BLOCK)
            scores = dot(head_queries[part], keys, NT)
            probs = jnp.exp(scores - logs[part, head : head + 1])
            grad_probs = dot(head_grads[part], values, NT)
            grad_scores = (probs * (grad_probs - inner[part, head : head + 1])).astype(BF16)
            new_v = dot(grads_t[64 * head : 64 * head + 64, part], probs.astype(BF16), NN)
            new_k = dot(queries_t[64 * head : 64 * head + 64, part], grad_scores, NN)
            dv = new_v if dv is None else dv + new_v
            dk = new_k if dk is None else dk + new_k
            dq_parts[head].append(dot(grad_scores, scaled_keys, NN))
        dk_parts.append(dk)
        dv_parts.append(dv)
        if head == 0:
            between(0)
    out[1, :, columns] = jnp.concatenate(dk_parts, axis=0).T.astype(BF16)
    out[2, :, columns] = jnp.concatenate(dv_parts, axis=0).T.astype(BF16)
    for index in range(count // ATTEND_BLOCK):
        out[0, pl.ds(index * ATTEND_BLOCK, ATTEND_BLOCK), columns] = jnp.where(
            lane < 64, dq_parts[0][index], dq_parts[1][index]
        ).astype(BF16)
    between(1)


def chain_blocks(width, hidden_size):
    cut = split_of(hidden_size)
    blocks = {}
    for side in ("decoder", "encoder"):
        blocks[side + "_expand0"] = (16, cut)
        blocks[side + "_expand1"] = (16, hidden_size - cut)
        blocks[side + "_reduce0"] = (hidden_size // 16, LANES)
        blocks[side + "_reduce1"] = (hidden_size // 16, LANES)
    for name in ("middle0", "middle1"):
        blocks[name] = (16, 2 * width)
    for name in ("last0", "last1"):
        blocks[name] = (16, 3 * width // 2)
    return blocks


def backward_linked(saved, targets, arms, weights):
    count, width = saved["x"].shape[1:]
    hidden_size = saved["active"].shape[1]
    starts, head = weights[6], weights[16]
    arrays = dict(saved)
    arrays.update(
        cross_memory=weights[10], reduce=weights[3], expand=weights[2], combine=weights[1], project=weights[0],
        self_project=weights[7], self_combine=weights[8], cross_query=weights[9],
        slope=saved["slope"].reshape(count // 16, 16, hidden_size),
    )
    inputs = [arrays[name] for name in IN_NAMES]
    inputs += decode_sources(weights, saved["pair"])
    vectors = [weights[4], starts, weights[14], weights[15], head.T, targets.transpose(2, 0, 1)]
    blocks = chain_blocks(width, hidden_size)
    own = width // 16
    vmem = lambda counts, name: [pltpu.VMEM((n,) + blocks[name], BF16) for n in counts]
    scratch = [pltpu.VMEM((2 * PAD_ROWS, columns), BF16) for columns in (width, hidden_size, hidden_size, width)]
    for name in NAMES:
        if name.startswith("decoder"):
            scratch += vmem(stage_blocks(GROUPS[name]), name)
        elif not name.startswith("encoder_expand"):
            scratch += vmem([16, 16] + stage_blocks(GROUPS[name]), name)
    for name in NAMES:
        if not name.startswith("encoder_expand"):
            scratch += vmem((16,), name)
    for name in ("encoder_expand0", "encoder_expand1"):
        scratch += vmem(stage_blocks(GROUPS[name]), name)
    scratch += [
        pltpu.VMEM((count, hidden_size), BF16),
        pltpu.VMEM((count // 16, 16, hidden_size), BF16),
        pltpu.VMEM((count, width), BF16),
        pltpu.VMEM((count, width), F32),
        pltpu.VMEM((width, count), BF16),
        pltpu.VMEM((count, width), BF16),
        pltpu.VMEM((2, SMALL_ROWS, width), BF16),
        pltpu.VMEM((5, SMALL_ROWS, width), BF16),
        pltpu.VMEM((2, TINY_ROWS, width), F32),
        pltpu.VMEM((5, TINY_ROWS, width), F32),
        pltpu.SemaphoreType.DMA((len(NAMES) + 2, STEPS, 2)),
        pltpu.SemaphoreType.DMA((len(NAMES) + 2, STEPS, 2)),
        pltpu.SemaphoreType.DMA((2, 5)),
        pltpu.SemaphoreType.DMA((2, 2)),
        pltpu.SemaphoreType.DMA((len(IN_NAMES),)),
        pltpu.SemaphoreType.DMA((len(DECODE_WEIGHTS),)),
        pltpu.SemaphoreType.DMA((3,)),
        pltpu.SemaphoreType.REGULAR((2, 5)),
    ]
    in_any = pl.BlockSpec(memory_space=pl.ANY)
    in_vmem = pl.BlockSpec(memory_space=pltpu.VMEM)
    shape = shape_of((count, width), BF16)
    results = pl.pallas_call(
        backward_kernel,
        in_specs=[in_any] * len(inputs) + [in_vmem] * len(vectors) + [pl.BlockSpec(memory_space=pltpu.SMEM)],
        out_specs=[in_vmem] * len(NAMES) + [in_any] * 4 + [in_vmem] * 2,
        out_shape=[shape_of((2,) + blocks[name], BF16) for name in NAMES]
        + [shape] * 4
        + [shape_of((own, 5 * width), F32), shape_of((SMALL_ROWS // 2 + 8 + TINY_ROWS, width), F32)],
        scratch_shapes=scratch,
        compiler_params=pltpu.CompilerParams(
            collective_id=0, has_side_effects=True, vmem_limit_bytes=LINKED_VMEM_BYTES
        ),
        cost_estimate=pl.CostEstimate(flops=10**8, bytes_accessed=10**8, transcendentals=0),
    )(*inputs, *vectors, arms)
    memory, slab, grad_memory, grad_x, rows, stack = results[len(NAMES) :]
    return results[: len(NAMES)], memory, slab, grad_memory, grad_x, rows, stack


def finish_kernel(valid, joints, *refs):
    refs = list(refs)

    def draw(count):
        taken = refs[:count]
        del refs[:count]
        return taken

    count = len(NAMES)
    sources = draw(count + 7)
    targets = draw(19)
    held = draw(count + 7)
    results = draw(17)
    load_sems, store_sems = draw(2)
    loads = []
    for index in list(range(count, count + 7)) + list(range(count)):
        copy = pltpu.make_async_copy(sources[index], held[index], load_sems.at[index])
        copy.start()
        loads.append((index, copy))
    loads = dict(loads)
    stores = []
    section = lax.axis_index("section")
    memory, other, grad_x, grad_memory, other_slab = held[count + 2 :]
    memory_out, slab_out = targets[:2]

    def store(result):
        index = next(i for i, item in enumerate(results) if item is result)
        stores.append(pltpu.make_async_copy(result, targets[2 + index], store_sems.at[2 + index]))
        stores[-1].start()

    (
        project_e, combine_e, expand_e, reduce_e, gains_e, shifts_e, starts_d, project_d, combine_d, query_d,
        memory_d, cross_d, expand_d, reduce_d, gains_d, shifts_d, head_d,
    ) = results
    halves = dict(zip(NAMES, held[:count]))
    rows_ref, stack_ref = held[count : count + 2]
    width = memory.shape[1]
    own = rows_ref.shape[0]
    place = (section * 8 + lax.axis_index("dp")) * own
    loads[count].wait()
    loads[count + 1].wait()
    project_d[...] = rows_ref[:, : 3 * width]
    store(project_d)
    combine_d[...] = rows_ref[:, 3 * width : 4 * width]
    store(combine_d)
    query_d[...] = rows_ref[:, 4 * width :]
    store(query_d)
    chosen = lax.broadcasted_iota(jnp.int32, (width, own), 0) == place + lax.broadcasted_iota(
        jnp.int32, (width, own), 1
    )
    chosen = jnp.where(chosen, 1.0, 0.0)
    exact = functools.partial(lax.dot_general, precision=lax.Precision.HIGHEST, preferred_element_type=F32)
    picked = exact(stack_ref[pl.ds(PAD_ROWS, 8 + TINY_ROWS), :], chosen, NN)
    starts_d[...] = exact(chosen, stack_ref[pl.ds(0, PAD_ROWS), :], (((0,), (1,)), ((), ())))[:, :valid]
    store(starts_d)
    gains_d[...] = jnp.concatenate([picked[0:1], picked[8:10]], axis=0)
    shifts_d[...] = jnp.concatenate([picked[1:2], picked[10:12]], axis=0)
    gains_e[...] = picked[12:14]
    shifts_e[...] = picked[14:16]
    head_d[...] = picked[16 : 16 + joints]
    for result in (gains_d, shifts_d, gains_e, shifts_e, head_d):
        store(result)
    for index in range(count + 2, count + 7):
        loads[index].wait()
    for index, (out, front, back) in enumerate(
        (
            ((memory_out.at[0], memory_out.at[1]), (memory, other), (other, memory)),
            ((slab_out.at[0, 0], slab_out.at[0, 1]), (grad_x, other_slab), (other_slab, grad_memory)),
        )
    ):
        for way in range(2):
            ahead = pltpu.make_async_copy(front[way], out[way], store_sems.at[19 + 2 * index + way])
            behind = pltpu.make_async_copy(back[way], out[way], store_sems.at[19 + 2 * index + way])

            @pl.when(section == 0)
            def _():
                ahead.start()

            @pl.when(section == 1)
            def _():
                behind.start()

            stores.append(ahead)

    for index in range(count):
        loads[index].wait()

    def rows_of(name, out, columns, first=0):
        for core in range(2):
            out[pl.ds(16 * core, 16), columns] = halves[name][core, :, first : first + columns.size].astype(F32)

    cut = halves["encoder_expand0"].shape[2]
    for side, out in (("encoder", expand_e), ("decoder", expand_d)):
        rows_of(side + "_expand0", out, pl.ds(0, cut))
        rows_of(side + "_expand1", out, pl.ds(cut, out.shape[1] - cut))
        store(out)
    for side, out in (("encoder", reduce_e), ("decoder", reduce_d)):
        for core in range(2):
            for index in range(2):
                out[:, pl.ds((2 * core + index) * LANES, LANES)] = halves[side + "_reduce%d" % index][core].astype(F32)
        store(out)
    rows_of("middle0", memory_d, pl.ds(0, 2 * width))
    store(memory_d)
    rows_of("middle1", cross_d, pl.ds(0, width))
    store(cross_d)
    rows_of("middle1", combine_e, pl.ds(0, width), width)
    store(combine_e)
    half = width // 2
    for third in range(3):
        for index in range(2):
            rows_of("last%d" % index, project_e, pl.ds(third * width + index * half, half), third * half)
    store(project_e)
    for copy in stores:
        copy.wait()


def finish(valid, joints, halves, rows, stack, memory, other, grad_x, grad_memory, other_slab):
    count, width = memory.shape
    own = rows.shape[0]
    hidden_size = halves[0].shape[2] + halves[1].shape[2]
    in_any = pl.BlockSpec(memory_space=pl.ANY)
    shapes = [
        (own, 3 * width), (own, width), (own, hidden_size), (hidden_size // 16, width), (2, own), (2, own),
        (own, valid), (own, 3 * width), (own, width), (own, width), (own, 2 * width), (own, width),
        (own, hidden_size), (hidden_size // 16, width), (3, own), (3, own), (joints, own),
    ]
    inputs = (*halves, rows, stack, memory, other, grad_x, grad_memory, other_slab)
    results = list(
        call(
            functools.partial(finish_kernel, valid, joints),
            10**6, 10**7,
            in_specs=[in_any] * len(inputs),
            out_specs=[in_any] * (2 + len(shapes)),
            out_shape=[shape_of((2, count, width), BF16), shape_of((1, 2, count, width), BF16)]
            + [shape_of(dims, F32) for dims in shapes],
            scratch_shapes=[pltpu.VMEM(item.shape, item.dtype) for item in inputs]
            + [pltpu.VMEM(dims, F32) for dims in shapes]
            + [pltpu.SemaphoreType.DMA((len(inputs),)), pltpu.SemaphoreType.DMA((23,))],
        )(*inputs)
    )
    results[8] = results[8].T
    results[18] = results[18].T
    return tuple(results)


def swap(value, axis, bit):
    pairs = [(i, i ^ (1 << bit)) for i in range(lax.axis_size(axis))]
    return lax.ppermute(value, axis, pairs)


def plain_scatter(full):
    part = lax.psum_scatter(full.astype(F32), ("section", "dp"), scatter_dimension=0, tiled=True)
    return lax.psum(part, "rep")


def per_device(x, targets, arms, *weights):
    section = lax.axis_index("section")
    sections = lax.axis_size("section")
    lanes = lax.axis_size("dp")
    count = x.shape[0] // sections
    starts, head = weights[6], weights[16]
    valid, joints = starts.shape[0], head.shape[1]
    width = starts.shape[1]
    first = section == 0
    place = section * lanes + lax.axis_index("dp")
    own = width // (sections * lanes)
    linked = (sections, lanes, lax.axis_size("rep"), count) == (2, 8, 2, 1)
    saved = []
    for index in range(count):
        pick = functools.partial(lambda i: lax.axis_index("section") * count + i, index)
        saved.append(forward(x, pick, weights))
        if not linked:
            saved[-1].update(decode(pick, targets, arms, weights, saved[-1].pop("pair")))
    if linked:
        halves, other, other_slab, grad_memory, grad_x, rows, stack = backward_linked(saved[0], targets, arms, weights)
        return finish(
            valid, joints, halves, rows, stack, saved[0]["memory"], other, grad_x, grad_memory, other_slab
        )
    memory = jnp.concatenate([item["memory"][None] for item in saved])
    results = []
    for index, item in enumerate(saved):
        results.append(
            backward_alone(item, lax.dynamic_index_in_dim(x, section * count + index, 0, keepdims=False), weights)
        )
    grad_x = jnp.concatenate([item[0][None] for item in results])
    grad_memory = jnp.concatenate([item[1][None] for item in results])
    total = lambda name: functools.reduce(jnp.add, [item[2][name] for item in results])
    other = swap(memory, "section", 0)
    other_slab = swap(jnp.where(first, grad_memory, grad_x), "section", 0)
    small = lax.psum(total("small"), ("section", "dp", "rep"))
    tiny = lax.psum(total("tiny"), ("section", "dp", "rep"))
    done = {
        name: plain_scatter(total(name))
        for name in ("decoder_expand", "decoder_reduce", "encoder_expand", "encoder_reduce", "middle", "last")
    }
    memory_out = jnp.concatenate([jnp.where(first, memory, other), jnp.where(first, other, memory)])
    slab = jnp.concatenate(
        [jnp.where(first, grad_x, other_slab), jnp.where(first, other_slab, grad_memory)]
    )[None]

    columns_of = lambda array: lax.dynamic_slice_in_dim(array, place * own, own, 1)
    rows_of = lambda array: lax.dynamic_slice_in_dim(array, place * own, own, 0)
    resid_d, query_d = small[:PAD_ROWS], small[PAD_ROWS:]
    start_grad, project_d, combine_d, query_w, sums_s = decode_start_back(
        valid, jnp.pad(starts, ((0, PAD_ROWS - valid), (0, 0))), weights[7], weights[8], weights[9],
        weights[14], weights[15], resid_d, query_d,
    )
    gains_d = jnp.concatenate([sums_s[0:1], tiny[0:2]])
    shifts_d = jnp.concatenate([sums_s[1:2], tiny[2:4]])
    return (
        memory_out,
        slab,
        done["last"],
        done["middle"][:, 3 * width :],
        done["encoder_expand"],
        done["encoder_reduce"],
        columns_of(tiny[4:6]),
        columns_of(tiny[6:8]),
        columns_of(start_grad[:valid]),
        rows_of(project_d),
        rows_of(combine_d),
        rows_of(query_w),
        done["middle"][:, : 2 * width],
        done["middle"][:, 2 * width : 3 * width],
        done["decoder_expand"],
        done["decoder_reduce"],
        columns_of(gains_d),
        columns_of(shifts_d),
        rows_of(tiny[8 : 8 + joints].T),
    )


def solution(mesh):
    spread = ("section", "dp")
    rows = P(spread, None)
    columns = P(None, spread)
    return jax.shard_map(
        per_device,
        mesh=mesh,
        in_specs=(P(("dp", "rep"), None, None), P(("dp", "rep"), None, None), P(("dp", "rep"))) + (P(),) * 17,
        out_specs=(
            P(("dp", "rep"), None, None),
            P("section", ("dp", "rep"), None, None),
            rows, rows, rows, rows, columns, columns, columns,
            rows, rows, rows, rows, rows, rows, rows, columns, columns, rows,
        ),
        check_vma=False,
    )
```

```python
import functools

import jax
import jax.numpy as jnp
from jax import lax
from jax.experimental import pallas as pl
from jax.experimental.pallas import tpu as pltpu
from jax.sharding import PartitionSpec as P

HEADS = 8
EPSILON = 1e-05
LANES = 128
PAD_ROWS = 112
SMALL_ROWS = 2 * PAD_ROWS
TINY_ROWS = 24
F32 = jnp.float32
BF16 = jnp.bfloat16
NN = (((1,), (0,)), ((), ()))
NT = (((1,), (1,)), ((), ()))
TN = (((0,), (0,)), ((), ()))
VMEM_BYTES = 56 * 1024 * 1024
LINKED_VMEM_BYTES = 638 * 1024 * 1024 // 10
ROOT_2_PI = 0.7978845608028654
CUBE = 0.044715


def dot(left, right, dims):
    return lax.dot_general(left, right, dims, preferred_element_type=F32)


def call(kernel, flops, moved, **options):
    return pl.pallas_call(
        kernel,
        compiler_params=pltpu.CompilerParams(vmem_limit_bytes=VMEM_BYTES),
        cost_estimate=pl.CostEstimate(flops=flops, bytes_accessed=moved, transcendentals=0),
        **options,
    )


def shape_of(dims, dtype):
    return jax.ShapeDtypeStruct(dims, dtype)


def whole(array):
    rank = len(array.shape)
    return pl.BlockSpec(array.shape, lambda *_: (0,) * rank, pipeline_mode=pl.Buffered(1))


def normed(residual):
    centre = jnp.mean(residual, axis=-1, keepdims=True)
    centred = residual - centre
    spread = jnp.mean(centred * centred, axis=-1, keepdims=True)
    scale = lax.rsqrt(spread + EPSILON)
    return centred * scale, scale


def normed_back(grad, gain, rows, scale):
    weighted = grad * gain
    return scale * (
        weighted
        - jnp.mean(weighted, axis=-1, keepdims=True)
        - rows * jnp.mean(weighted * rows, axis=-1, keepdims=True)
    )


def gelu_and_slope(value):
    square = value * value
    bend = jnp.tanh(value * (ROOT_2_PI + (ROOT_2_PI * CUBE) * square))
    half = 0.5 + 0.5 * bend
    slope = half + value * (0.5 - 0.5 * bend * bend) * (
        ROOT_2_PI + (3.0 * ROOT_2_PI * CUBE) * square
    )
    return value * half, slope


def column_sum(value):
    return jnp.sum(value, axis=0, keepdims=True)


FORWARD_WEIGHTS = ("project", "combine", "expand", "reduce", "memory_w")
FORWARD_OUTS = ("packed", "mixed", "logs", "first", "low", "active", "slope", "second", "memory", "pair")


def split_of(hidden_size):
    return hidden_size // 256 * 128 + 128


def column_chunks(hidden_size):
    cut = split_of(hidden_size)
    return [(0, 896), (896, cut - 896), (cut, 768), (cut + 768, hidden_size - cut - 768)]


def attend_all(packed, mixed_ref, log_ref):
    count, width = packed.shape[0], packed.shape[1] // 3
    lane = lax.broadcasted_iota(jnp.int32, (1, LANES), 1)
    heads = width // 64
    columns = lambda third, head: pl.ds(third * width + head // 2 * LANES, LANES)

    def scores_of(head):
        keys = packed[:, columns(1, head)]
        own = (lane < 64) if head % 2 == 0 else (lane >= 64)
        queries = packed[:, columns(0, head)] * jnp.asarray(0.125, BF16)
        return dot(jnp.where(own, keys, jnp.zeros_like(keys)), queries, NT)

    scores = scores_of(0)
    for head in range(heads):
        following = scores_of(head + 1) if head + 1 < heads else None
        if head % 2 == 0:
            values = packed[:, columns(2, head)].T
        extended = jnp.concatenate(
            [values[64 * (head % 2) : 64 * (head % 2) + 64], jnp.ones((16, count), BF16)], axis=0
        )
        largest = jnp.max(scores, axis=0, keepdims=True)
        raised = jnp.exp(scores - largest).astype(BF16)
        mixed = dot(extended, raised, NN)
        total = mixed[64:65]
        mixed_ref[pl.ds(64 * head, 64), :] = (mixed[:64] * (1.0 / total)).astype(BF16)
        log_ref[head // 2, pl.ds(head % 2, 1), :] = largest + jnp.log(total)
        scores = following


def encode_kernel(pick, x_ref, *refs):
    refs = list(refs)

    def draw(count):
        taken = refs[:count]
        del refs[:count]
        return taken

    weights = dict(zip(FORWARD_WEIGHTS, draw(5)))
    gain_ref, shift_ref = draw(2)
    outs = dict(zip(FORWARD_OUTS, draw(10)))
    held = dict(zip(FORWARD_WEIGHTS, draw(5)))
    kept = dict(zip(FORWARD_OUTS, draw(10)))
    x, load_sems, store_sems = draw(3)
    here = pltpu.make_async_copy(x_ref.at[pick()], x, load_sems.at[5])
    here.start()
    loads = {}
    for index, name in enumerate(FORWARD_WEIGHTS):
        loads[name] = pltpu.make_async_copy(weights[name], held[name], load_sems.at[index])
        loads[name].start()
    stores = []

    def store(name):
        index = FORWARD_OUTS.index(name)
        stores.append(pltpu.make_async_copy(kept[name], outs[name], store_sems.at[index]))
        stores[-1].start()

    count, width = x.shape
    hidden_size = held["expand"].shape[1]
    block = 256
    here.wait()
    loads["project"].wait()
    for third in range(3):
        columns = pl.ds(third * width, width)
        kept["packed"][:, columns] = dot(x[...], held["project"][:, columns], NN).astype(BF16)
    store("packed")
    attend_all(kept["packed"], kept["mixed"], kept["logs"])
    store("mixed")
    store("logs")
    loads["combine"].wait()
    first, low, second = kept["first"], kept["low"], kept["second"]
    first[...] = x[...].astype(F32) + dot(kept["mixed"][...], held["combine"][...], TN)
    for start in range(0, count, block):
        part = pl.ds(start, block)
        rows, _ = normed(first[part, :])
        value = rows * gain_ref[0:1, :] + shift_ref[0:1, :]
        second[part, :] = value
        low[part, :] = value.astype(BF16)
    store("first")
    store("low")
    loads["expand"].wait()
    chunks = column_chunks(hidden_size)
    before = lambda item: dot(low[...], held["expand"][:, pl.ds(*item)], NN)
    ahead = before(chunks[0])
    for index, (start, size) in enumerate(chunks):
        current = ahead
        if index + 1 < len(chunks):
            ahead = before(chunks[index + 1])
        active, slope = gelu_and_slope(current)
        columns = pl.ds(start, size)
        kept["active"][:, columns] = active.astype(BF16)
        kept["slope"][:, columns] = slope.astype(BF16)
    store("active")
    store("slope")
    loads["reduce"].wait()
    second[...] += dot(kept["active"][...], held["reduce"][...], NN)
    memory = kept["memory"]
    for start in range(0, count, block):
        part = pl.ds(start, block)
        rows, _ = normed(second[part, :])
        memory[part, :] = (rows * gain_ref[1:2, :] + shift_ref[1:2, :]).astype(BF16)
    store("second")
    store("memory")
    loads["memory_w"].wait()
    for half in range(2):
        columns = pl.ds(half * width, width)
        kept["pair"][:, columns] = dot(memory[...], held["memory_w"][:, columns], NN).astype(BF16)
        stores.append(
            pltpu.make_async_copy(
                kept["pair"].at[:, columns], outs["pair"].at[:, columns], store_sems.at[len(FORWARD_OUTS) - 1 + half]
            )
        )
        stores[-1].start()
    for copy in stores:
        copy.wait()


def encode(x, pick, weights, gains, shifts):
    count, width = x.shape[1:]
    hidden_size = weights[2].shape[1]
    shapes = [
        ((count, 3 * width), BF16), ((width, count), BF16), ((width // LANES, 2, count), F32), ((count, width), F32),
        ((count, width), BF16), ((count, hidden_size), BF16), ((count, hidden_size), BF16), ((count, width), F32),
        ((count, width), BF16), ((count, 2 * width), BF16),
    ]
    in_any = pl.BlockSpec(memory_space=pl.ANY)
    in_vmem = pl.BlockSpec(memory_space=pltpu.VMEM)
    results = call(
        functools.partial(encode_kernel, pick),
        2 * count * width * (2 * hidden_size + 6 * width) + 4 * count * count * width,
        count * (hidden_size * 4 + width * 24) + 8 * width * hidden_size,
        in_specs=[in_any] * 6 + [in_vmem] * 2,
        out_specs=[in_any] * 10,
        out_shape=[shape_of(dims, kind) for dims, kind in shapes],
        scratch_shapes=[pltpu.VMEM(item.shape, BF16) for item in weights]
        + [pltpu.VMEM(dims, kind) for dims, kind in shapes]
        + [pltpu.VMEM((count, width), BF16), pltpu.SemaphoreType.DMA((6,)), pltpu.SemaphoreType.DMA((11,))],
    )(x, *weights, gains, shifts)
    return dict(zip(FORWARD_OUTS, results))


def attend_back_kernel(block, q_ref, k_ref, v_ref, do_ref, mixed_ref, log_ref, dq_ref, dk_ref, dv_ref):
    count = q_ref.shape[0]
    lane = lax.broadcasted_iota(jnp.int32, (1, LANES), 1)
    keys = k_ref[...]
    values = v_ref[...]
    queries = q_ref[...] * jnp.asarray(0.125, BF16)
    scaled_keys = keys * jnp.asarray(0.125, BF16)
    grads = do_ref[...]
    queries_t = queries.T
    grads_t = grads.T
    logs = log_ref[0].T
    shared = mixed_ref[...].astype(F32) * grads_t.astype(F32)
    inner = jnp.concatenate([column_sum(shared[:64]), column_sum(shared[64:])], axis=0).T
    dq_parts = [[], []]
    dk_parts = []
    dv_parts = []
    for head in range(2):
        own = (lane < 64) if head == 0 else (lane >= 64)
        head_queries = jnp.where(own, queries, jnp.zeros_like(queries))
        head_grads = jnp.where(own, grads, jnp.zeros_like(grads))
        dk = None
        dv = None
        for start in range(0, count, block):
            part = slice(start, start + block)
            scores = dot(head_queries[part], keys, NT)
            probs = jnp.exp(scores - logs[part, head : head + 1])
            grad_probs = dot(head_grads[part], values, NT)
            grad_scores = (probs * (grad_probs - inner[part, head : head + 1])).astype(BF16)
            new_v = dot(grads_t[64 * head : 64 * head + 64, part], probs.astype(BF16), NN)
            new_k = dot(queries_t[64 * head : 64 * head + 64, part], grad_scores, NN)
            dv = new_v if dv is None else dv + new_v
            dk = new_k if dk is None else dk + new_k
            dq_parts[head].append(dot(grad_scores, scaled_keys, NN))
        dk_parts.append(dk)
        dv_parts.append(dv)
    dk_ref[...] = jnp.concatenate(dk_parts, axis=0).T.astype(BF16)
    dv_ref[...] = jnp.concatenate(dv_parts, axis=0).T.astype(BF16)
    for index in range(count // block):
        dq_ref[pl.ds(index * block, block), :] = jnp.where(
            lane < 64, dq_parts[0][index], dq_parts[1][index]
        ).astype(BF16)


def attend_back(packed, grad_mixed, mixed, logs):
    rows, width = packed.shape[0], packed.shape[1] // 3
    pairs = width // LANES
    column = lambda first: pl.BlockSpec((rows, LANES), lambda j: (0, first + j))
    return call(
        functools.partial(attend_back_kernel, 256),
        10 * rows * rows * width * 3,
        rows * width * 16,
        grid=(pairs,),
        in_specs=[
            column(0),
            column(pairs),
            column(2 * pairs),
            column(0),
            pl.BlockSpec((LANES, rows), lambda j: (j, 0)),
            pl.BlockSpec((1, 2, rows), lambda j: (j, 0, 0)),
        ],
        out_specs=[column(0)] * 3,
        out_shape=[shape_of((rows, width), BF16)] * 3,
    )(packed, packed, packed, grad_mixed, mixed, logs)

def encode_back_kernel(
    pair_ref, first_ref, second_ref, slope_ref, combine_ref, expand_ref, reduce_ref, gain_ref, memory_w_ref,
    grad_memory_ref, branch_ref, hidden_ref, resid_ref, low_ref, mixed_ref, sums_ref,
):
    grad_memory = dot(pair_ref[...], memory_w_ref[...], NT).astype(BF16)
    grad_memory_ref[...] = grad_memory
    grad_last = grad_memory.astype(F32)
    rows, scale = normed(second_ref[...])
    gain_last = column_sum(grad_last * rows)
    shift_last = column_sum(grad_last)
    grad_second = normed_back(grad_last, gain_ref[1:2, :], rows, scale)
    branch = grad_second.astype(BF16)
    branch_ref[...] = branch
    total = grad_second
    hidden_size = expand_ref.shape[1]
    step = hidden_size // 5
    for start in range(0, hidden_size, step):
        part = pl.ds(start, step)
        grad_active = dot(branch, reduce_ref[part, :], NT)
        grad_hidden = (grad_active * slope_ref[:, part].astype(F32)).astype(BF16)
        hidden_ref[:, part] = grad_hidden
        total = total + dot(grad_hidden, expand_ref[:, part], NT)
    rows, scale = normed(first_ref[...])
    gain_first = column_sum(total * rows)
    shift_first = column_sum(total)
    grad_first = normed_back(total, gain_ref[0:1, :], rows, scale)
    resid_ref[...] = grad_first
    low = grad_first.astype(BF16)
    low_ref[...] = low
    mixed_ref[...] = dot(low, combine_ref[...], NT).astype(BF16)
    fresh = jnp.concatenate(
        [gain_first, gain_last, shift_first, shift_last, jnp.zeros((4, gain_first.shape[1]), F32)], axis=0
    )

    @pl.when(pl.program_id(0) == 0)
    def _():
        sums_ref[...] = fresh

    @pl.when(pl.program_id(0) > 0)
    def _():
        sums_ref[...] += fresh


def encode_back(grad_pair, first, second, slope, combine_w, expand_w, reduce_w, gains, memory_w):
    rows, width = first.shape
    hidden = expand_w.shape[1]
    block = 256
    line = lambda size: pl.BlockSpec((block, size), lambda i: (i, 0))
    sizes = [(width, BF16), (width, BF16), (hidden, BF16), (width, F32), (width, BF16), (width, BF16)]
    return call(
        encode_back_kernel,
        2 * rows * width * (2 * hidden + 3 * width),
        rows * (hidden * 4 + width * 18) + 8 * width * hidden,
        grid=(rows // block,),
        in_specs=[line(2 * width), line(width), line(width), line(hidden)]
        + [whole(item) for item in (combine_w, expand_w, reduce_w, gains, memory_w)],
        out_specs=[line(size) for size, _ in sizes] + [pl.BlockSpec((8, width), lambda i: (0, 0))],
        out_shape=[shape_of((rows, size), kind) for size, kind in sizes] + [shape_of((8, width), F32)],
    )(grad_pair, first, second, slope, combine_w, expand_w, reduce_w, gains, memory_w)


def stacked(rows):
    lane = lax.broadcasted_iota(jnp.int32, (1, rows.shape[1]), 1)
    return jnp.concatenate(
        [jnp.where((lane >= 64 * h) & (lane < 64 * h + 64), rows, jnp.zeros_like(rows)) for h in range(4)],
        axis=0,
    )


def unstacked(rows):
    lane = lax.broadcasted_iota(jnp.int32, (1, rows.shape[1]), 1)
    count = rows.shape[0] // 4
    result = rows[:count]
    for h in range(1, 4):
        result = jnp.where(lane >= 64 * h, rows[h * count : h * count + count], result)
    return result


def few_attend(queries, keys, values, valid):
    mixed = []
    kept = []
    for half in range(2):
        part = slice(256 * half, 256 * half + 256)
        scores = dot(stacked(queries[:, part] * jnp.asarray(0.125, BF16)), keys[:, part], NT)
        if valid < scores.shape[1]:
            column = lax.broadcasted_iota(jnp.int32, (1, scores.shape[1]), 1)
            scores = jnp.where(column < valid, scores, -1e30)
        raised = jnp.exp(scores - jnp.max(scores, axis=1, keepdims=True))
        probs = raised * (1.0 / jnp.sum(raised, axis=1, keepdims=True))
        mixed.append(unstacked(dot(probs.astype(BF16), values[:, part], NN)))
        kept.append(probs)
    return jnp.concatenate(mixed, axis=1).astype(BF16), kept


def few_attend_back(queries, keys, values, kept, grads):
    dq, dk, dv = [], [], []
    for half in range(2):
        part = slice(256 * half, 256 * half + 256)
        probs = kept[half]
        own_queries = stacked(queries[:, part] * jnp.asarray(0.125, BF16))
        own_grads = stacked(grads[:, part])
        grad_probs = dot(own_grads, values[:, part], NT)
        product = probs * grad_probs
        grad_scores = (product - probs * jnp.sum(product, axis=1, keepdims=True)).astype(BF16)
        dv.append(dot(probs.astype(BF16), own_grads, TN))
        dk.append(dot(grad_scores, own_queries, TN))
        dq.append(unstacked(dot(grad_scores, keys[:, part], NN)) * 0.125)
    return jnp.concatenate(dq, axis=1), jnp.concatenate(dk, axis=1), jnp.concatenate(dv, axis=1)


def self_block(starts, project_w, combine_w, gain, shift, valid):
    width = starts.shape[1]
    packed = dot(starts, project_w, NN).astype(BF16)
    queries, keys, values = (packed[:, i * width : (i + 1) * width] for i in range(3))
    mixed, kept = few_attend(queries, keys, values, valid)
    residual = starts.astype(F32) + dot(mixed, combine_w, NN)
    rows, scale = normed(residual)
    return queries, keys, values, mixed, kept, rows, scale, rows * gain + shift


def dealt(rows):
    width = rows.shape[1]
    source = lax.broadcasted_iota(jnp.int32, (width, width), 0)
    target = lax.broadcasted_iota(jnp.int32, (width, width), 1)
    half = width // 2
    wanted = (target % half) // 16 * 32 + target // half * 16 + target % 16
    return dot(rows, jnp.where(source == wanted, 1.0, 0.0).astype(BF16), NN).astype(BF16)


def undealt(columns):
    count, width = columns.shape
    return columns.reshape(count, 2, width // 32, 16).transpose(0, 2, 1, 3).reshape(count, width)


DECODE_WEIGHTS = ("self_project", "self_combine", "cross_query", "pair", "cross_combine", "expand", "reduce")


def cross_attend(queries_ref, pair, stash, mixed_ref):
    width = queries_ref.shape[1]
    rows = 4 * queries_ref.shape[0]

    def half_of(half, carry):
        columns = pl.ds(half * 256, 256)
        value_columns = pl.ds(width + half * 256, 256)
        scores = dot(stacked(queries_ref[:, columns] * jnp.asarray(0.125, BF16)), pair[:, columns], NT)
        raised = jnp.exp(scores - jnp.max(scores, axis=1, keepdims=True))
        probs = (raised * (1.0 / jnp.sum(raised, axis=1, keepdims=True))).astype(BF16)
        stash[pl.ds(half * rows, rows), : pair.shape[0]] = probs
        mixed_ref[:, columns] = unstacked(dot(probs, pair[:, value_columns], NN)).astype(BF16)
        return carry

    for half in range(2):
        half_of(half, None)


def cross_attend_back(queries_ref, pair, stash, grads_ref):
    width = queries_ref.shape[1]
    rows = 4 * queries_ref.shape[0]

    def half_of(half, carry):
        columns = pl.ds(half * 256, 256)
        value_columns = pl.ds(width + half * 256, 256)
        low = stash[pl.ds(half * rows, rows), : pair.shape[0]]
        own_queries = stacked(queries_ref[:, columns] * jnp.asarray(0.125, BF16))
        own_grads = stacked(grads_ref[:, columns])
        probs = low.astype(F32)
        grad_probs = dot(own_grads, pair[:, value_columns], NT)
        inner = jnp.sum(probs * grad_probs, axis=1, keepdims=True)
        grad_scores = (probs * (grad_probs - inner)).astype(BF16)
        dq = unstacked(dot(grad_scores, pair[:, columns], NN)) * 0.125
        pair[:, value_columns] = dot(low, own_grads, TN).astype(BF16)
        pair[:, columns] = dot(grad_scores, own_queries, TN).astype(BF16)
        queries_ref[:, columns] = dq.astype(BF16)
        return carry

    for half in range(2):
        half_of(half, None)


def decode_body(
    pick, valid, loads, held, starts, gain_ref, shift_ref, head_ref, target_ref, arm_ref, acts, hand_out, stash, rooms
):
    for name in ("self_project", "self_combine"):
        loads[name].wait()
    width = starts.shape[1]
    first = self_block(
        starts[...], held["self_project"][...], held["self_combine"][...], gain_ref[0:1, :], shift_ref[0:1, :], valid
    )[-1]
    loads["cross_query"].wait()
    queries, mixed_rows, grads = rooms
    queries[...] = dot(first.astype(BF16), held["cross_query"][...], NN).astype(BF16)
    loads["pair"].wait()
    cross_attend(queries, held["pair"], stash, mixed_rows)
    mixed = mixed_rows[...]
    loads["cross_combine"].wait()
    second_rows, second_scale = normed(first + dot(mixed, held["cross_combine"][...], NN))
    second = second_rows * gain_ref[1:2, :] + shift_ref[1:2, :]
    second_low = second.astype(BF16)
    own = pl.ds(0, PAD_ROWS)
    acts["low_d"][own, :] = dealt(second_low)
    hand_out("low_d")
    loads["expand"].wait()
    loads["reduce"].wait()
    expand_ref, reduce_ref = held["expand"], held["reduce"]
    chunks = column_chunks(expand_ref.shape[1])
    total = second
    slope_rows = pl.ds(8 * PAD_ROWS, PAD_ROWS)
    for start, size in chunks:
        part = pl.ds(start, size)
        active, slope = gelu_and_slope(dot(second_low, expand_ref[:, part], NN))
        stash[slope_rows, part] = slope.astype(BF16)
        active = active.astype(BF16)
        acts["active_d"][own, part] = active
        total = total + dot(active, reduce_ref[part, :], NN)
    hand_out("active_d")
    third_rows, third_scale = normed(total)
    third_low = (third_rows * gain_ref[2:3, :] + shift_ref[2:3, :]).astype(BF16)
    here = pick()
    joints, rows = head_ref.shape[0], starts.shape[0]
    target = target_ref[:, 0, :]
    for index in range(1, target_ref.shape[1]):
        target = jnp.where(here == index, target_ref[:, index, :], target)
    target = jnp.concatenate([target, jnp.zeros((joints, rows - valid), F32)], axis=1)
    misfit = dot(head_ref[...], third_low, NT) - target
    arms = arm_ref[here]
    joint = lax.broadcasted_iota(jnp.int32, misfit.shape, 0)
    row = lax.broadcasted_iota(jnp.int32, misfit.shape, 1)
    factor = 2.0 / jnp.full((1, 1), arms, jnp.int32).astype(F32)
    used = (row < valid) & (joint < joints // 2 * arms)
    grad_pred = jnp.where(used, factor * misfit * lax.rsqrt(misfit * misfit + 1.0), 0.0).astype(BF16)
    head_grad = dot(grad_pred, third_low, NN)
    grad_third = dot(grad_pred, head_ref[...], TN)
    gain_third = column_sum(grad_third * third_rows)
    shift_third = column_sum(grad_third)
    total = normed_back(grad_third, gain_ref[2:3, :], third_rows, third_scale)
    branch = total.astype(BF16)
    acts["branch_d"][own, :] = branch
    hand_out("branch_d")
    for start, size in chunks:
        part = pl.ds(start, size)
        grad_hidden = (dot(branch, reduce_ref[part, :], NT) * stash[slope_rows, part].astype(F32)).astype(BF16)
        acts["hidden_d"][own, part] = grad_hidden
        total = total + dot(grad_hidden, expand_ref[:, part], NT)
    hand_out("hidden_d")
    gain_second = column_sum(total * second_rows)
    shift_second = column_sum(total)
    grad_second = normed_back(total, gain_ref[1:2, :], second_rows, second_scale)
    branch = grad_second.astype(BF16)
    grads[...] = dot(branch, held["cross_combine"][...], NT).astype(BF16)
    cross_attend_back(queries, held["pair"], stash, grads)
    sums = jnp.concatenate([gain_second, gain_third, shift_second, shift_third], axis=0)
    return branch, queries[...], mixed, sums, head_grad


DECODE_VECTORS = ("gains", "shifts", "head", "targets")


def decode_kernel(pick, starts_ref, *refs):
    refs = list(refs)

    def draw(count):
        taken = refs[:count]
        del refs[:count]
        return taken

    sources = draw(7)
    gain_ref, shift_ref, head_ref, target_ref, arm_ref = draw(5)
    starts_out, grad_pair_ref, low_ref, hidden_ref, active_ref, branch_ref, cross_grad_ref, small_ref, tiny_ref = draw(9)
    held = dict(zip(DECODE_WEIGHTS, draw(7)))
    stash, *rooms, load_sems = draw(5)
    loads = {}
    for index, (name, source) in enumerate(zip(DECODE_WEIGHTS, sources)):
        loads[name] = pltpu.make_async_copy(source, held[name], load_sems.at[index])
        loads[name].start()
    valid = starts_ref.shape[0]
    starts_out[...] = jnp.zeros_like(starts_out)
    starts_out[pl.ds(0, valid), :] = starts_ref[...]
    acts = {"low_d": low_ref, "hidden_d": hidden_ref, "active_d": active_ref, "branch_d": branch_ref}
    branch, dq, mixed, sums, head_grad = decode_body(
        pick, valid, loads, held, starts_out, gain_ref, shift_ref, head_ref, target_ref, arm_ref, acts, lambda name: None,
        stash, rooms,
    )
    small_ref[pl.ds(0, PAD_ROWS), :] = branch
    small_ref[pl.ds(PAD_ROWS, PAD_ROWS), :] = dq
    cross_grad_ref[...] = dot(mixed, branch, TN).astype(BF16)
    grad_pair_ref[...] = held["pair"][...]
    tiny_ref[...] = jnp.zeros_like(tiny_ref)
    tiny_ref[pl.ds(0, 4), :] = sums
    tiny_ref[pl.ds(8, head_ref.shape[0]), :] = head_grad


def decode_sources(weights, pair):
    return (weights[7], weights[8], weights[9], pair, weights[11], weights[12], weights[13])


def decode(pick, targets, arms, weights, pair):
    starts, head = weights[6], weights[16]
    width = starts.shape[1]
    hidden = weights[12].shape[1]
    sources = decode_sources(weights, pair)
    shapes = {
        "starts": ((PAD_ROWS, width), BF16),
        "grad_pair": (pair.shape, BF16),
        "low_d": ((PAD_ROWS, width), BF16),
        "hidden_d": ((PAD_ROWS, hidden), BF16),
        "active_d": ((PAD_ROWS, hidden), BF16),
        "branch_d": ((PAD_ROWS, width), BF16),
        "cross": ((width, width), BF16),
        "small": ((SMALL_ROWS, width), BF16),
        "tiny": ((TINY_ROWS, width), F32),
    }
    in_vmem = pl.BlockSpec(memory_space=pltpu.VMEM)
    results = call(
        functools.partial(decode_kernel, pick),
        8 * PAD_ROWS * width * hidden * 2,
        20 * 1024 * 1024,
        in_specs=[in_vmem] + [pl.BlockSpec(memory_space=pl.ANY)] * 7 + [in_vmem] * 4
        + [pl.BlockSpec(memory_space=pltpu.SMEM)],
        out_specs=[in_vmem] * len(shapes),
        out_shape=[shape_of(dims, kind) for dims, kind in shapes.values()],
        scratch_shapes=[pltpu.VMEM(item.shape, BF16) for item in sources]
        + [pltpu.VMEM((pair.shape[0], hidden), BF16)] + [pltpu.VMEM((PAD_ROWS, width), BF16)] * 3
        + [pltpu.SemaphoreType.DMA((7,))],
    )(starts, *sources, weights[14], weights[15], head.T, targets.transpose(2, 0, 1), arms)
    return dict(zip(shapes, results))


def decode_start_back_kernel(
    valid,
    starts_ref, project_ref, combine_ref, query_ref, gain_ref, shift_ref, resid_ref, query_grad_ref,
    start_grad_ref, project_grad_ref, combine_grad_ref, query_w_grad_ref, sums_ref,
):
    starts = starts_ref[...]
    project_w = project_ref[...]
    queries, keys, values, mixed, kept, rows, scale, first = self_block(
        starts, project_w, combine_ref[...], gain_ref[0:1, :], shift_ref[0:1, :], valid
    )
    low = query_grad_ref[...].astype(BF16)
    query_w_grad_ref[...] = dot(first.astype(BF16), low, TN)
    grad_first = resid_ref[...] + dot(low, query_ref[...], NT)
    gain_sum = column_sum(grad_first * rows)
    shift_sum = column_sum(grad_first)
    grad_resid = normed_back(grad_first, gain_ref[0:1, :], rows, scale)
    branch = grad_resid.astype(BF16)
    combine_grad_ref[...] = dot(mixed, branch, TN)
    grad_mixed = dot(branch, combine_ref[...], NT).astype(BF16)
    dq, dk, dv = few_attend_back(queries, keys, values, kept, grad_mixed)
    grad_packed = jnp.concatenate([dq, dk, dv], axis=1).astype(BF16)
    project_grad_ref[...] = dot(starts, grad_packed, TN)
    start_grad_ref[...] = grad_resid + dot(grad_packed, project_w, NT)
    sums_ref[...] = jnp.concatenate([gain_sum, shift_sum, jnp.zeros((6, gain_sum.shape[1]), F32)], axis=0)


def decode_start_back(valid, starts, project_w, combine_w, query_w, gains, shifts, resid, query_grad):
    count, width = starts.shape
    arrays = (starts, project_w, combine_w, query_w, gains, shifts, resid, query_grad)
    shapes = [(count, width), (width, 3 * width), (width, width), (width, width), (8, width)]
    return call(
        functools.partial(decode_start_back_kernel, valid),
        2 * count * width * width * 20,
        8 * 1024 * 1024,
        in_specs=[pl.BlockSpec(memory_space=pltpu.VMEM)] * len(arrays),
        out_specs=[pl.BlockSpec(memory_space=pltpu.VMEM)] * len(shapes),
        out_shape=[shape_of(dims, F32) for dims in shapes],
    )(*arrays)


def forward(x, pick, weights):
    saved = encode(x, pick, weights[:4] + (weights[10],), weights[4], weights[5])
    saved["x"] = x
    return saved


def backward_alone(saved, x, weights):
    (encoder_project, encoder_combine, encoder_expand, encoder_reduce, encoder_gains) = weights[:5]
    cross_memory = weights[10]
    grad_memory, branch, grad_hidden, resid, low, grad_mixed, sums_e = encode_back(
        saved["grad_pair"], saved["first"], saved["second"], saved["slope"],
        encoder_combine, encoder_expand, encoder_reduce, encoder_gains, cross_memory,
    )
    dq, dk, dv = attend_back(saved["packed"], grad_mixed, saved["mixed"], saved["logs"])
    grad_packed = jnp.concatenate([dq, dk, dv], axis=1)
    grad_x = (resid + dot(grad_packed, encoder_project, NT)).astype(BF16)
    plain = lambda left, right: dot(left, right, TN)
    return grad_x, grad_memory, {
        "decoder_expand": plain(undealt(saved["low_d"]), saved["hidden_d"]),
        "decoder_reduce": plain(saved["active_d"], saved["branch_d"]),
        "encoder_reduce": plain(saved["active"], branch),
        "encoder_expand": plain(saved["low"], grad_hidden),
        "middle": jnp.concatenate(
            [plain(saved["memory"], saved["grad_pair"]), saved["cross"].astype(F32), dot(saved["mixed"], low, NN)], axis=1
        ),
        "last": plain(x, grad_packed),
        "small": saved["small"].astype(F32),
        "tiny": saved["tiny"].at[4:8].set(sums_e[:4]),
    }


SECTION, SIDE, LINE = range(3)
GROUPS = {
    "decoder_expand0": (SIDE, SECTION, LINE),
    "decoder_expand1": (LINE, SIDE, SECTION),
    "decoder_reduce0": (SIDE, LINE, SECTION),
    "decoder_reduce1": (LINE, SIDE, SECTION),
    "encoder_reduce0": (SECTION, SIDE, LINE),
    "encoder_reduce1": (SIDE, SECTION, LINE),
    "encoder_expand0": (SECTION, SIDE, LINE),
    "encoder_expand1": (SIDE, LINE, SECTION),
    "middle0": (SIDE, LINE, SECTION),
    "middle1": (SIDE, SECTION, LINE),
    "last0": (SECTION, SIDE, LINE),
    "last1": (SIDE, LINE, SECTION),
}
NAMES = tuple(GROUPS)
SCHEDULE = {
    "dfe0": ("small",),
    "dmem": ("decoder_reduce1",),
    "efr1": ("decoder_reduce0", "small", "decoder_expand1",),
    "dwm": ("encoder_reduce0",),
    "du0": ("encoder_reduce1", "decoder_reduce1",),
    "du1": ("middle0", "decoder_reduce0",),
    "df": ("decoder_expand0", "small",),
    "ln": ("decoder_expand1",),
    "efe0": ("encoder_reduce1", "tiny",),
    "efe1": ("decoder_reduce1",),
    "dwc": ("encoder_expand0", "decoder_reduce0",),
    "att0": ("encoder_expand1", "middle0", "middle1",),
    "att1": ("small", "decoder_reduce1",),
    "att3": ("decoder_expand1",),
    "last0": ("encoder_reduce0", "decoder_reduce0",),
    "att4": ("encoder_expand1", "middle0",),
    "att5": ("last0", "decoder_expand0",),
    "att6": ("small", "middle1",),
    "att7": ("encoder_reduce1", "encoder_expand1", "tiny", "middle0", "decoder_expand1",),
    "dx0": ("decoder_expand0",),
    "dx1": ("encoder_reduce1",),
    "last1": ("encoder_reduce0", "encoder_expand1",),
}
TAIL_FIRST = ("tiny", "middle0", "last1", "decoder_expand0", "encoder_expand0", "small", )
TAIL = (
    "last1",
    "encoder_reduce0",
    "encoder_expand1",
    "tiny",
    "encoder_reduce1",
    "decoder_reduce0",
    "decoder_reduce1",
    "decoder_expand0",
    "last0",
    "last1",
    "decoder_reduce0",
    "decoder_reduce1",
    "encoder_reduce0",
    "decoder_expand0",
    "encoder_expand0",
    "tiny",
    "middle1",
    "decoder_expand1",
    "encoder_reduce1",
    "last0",
    "last1",
    "tiny",
    "encoder_reduce0",
    "decoder_expand1",
    "encoder_reduce1",
    "encoder_expand0",
    "middle1",
    "last0",
    "encoder_reduce0",
    "last1",
    "encoder_expand0",
    "middle1",
    "last0",
    "middle0",
    "encoder_expand0",
    "middle1",
    "encoder_expand1",
    "last0",
    "last1",
    "middle0",
    "encoder_expand0",
    "middle1",
    "encoder_expand1",
    "last0",
    "last1",
)
STEPS = 7
LINE_ROUNDS = 3


class Links:
    def __init__(self):
        core = lax.axis_index("rep")
        section = lax.axis_index("section")
        lane = lax.axis_index("dp")
        self.core = core
        self.section = section
        self.lane = lane
        self.level = lane // 2
        self.side = lane % 2
        self.mine = [section, self.side]
        self.other_core = {"rep": 1 - core}
        self.partner = [{"section": 1 - section}, {"dp": lane + 1 - 2 * self.side}]
        self.above = {"dp": lane + 2}
        self.below = {"dp": lane - 2}

    def signal(self, semaphore, device):
        pl.semaphore_signal(semaphore, inc=1, device_id=device, device_id_type=pl.DeviceIdType.MESH)

    def tell(self, semaphores):
        for semaphore, device in zip(semaphores[:3], [self.other_core] + self.partner):
            self.signal(semaphore, device)

        @pl.when(self.level > 0)
        def _():
            self.signal(semaphores[3], self.below)

        @pl.when(self.level < 3)
        def _():
            self.signal(semaphores[4], self.above)

    def greet(self):
        self.tell([pltpu.get_barrier_semaphore()] * 5)

    def meet(self):
        barrier = pltpu.get_barrier_semaphore()
        pl.semaphore_wait(barrier, 3 + (self.level + 3) // 4 + (6 - self.level) // 4)

    def copy(self, source, target, sems, device):
        return pltpu.make_async_remote_copy(
            src_ref=source,
            dst_ref=target,
            send_sem=sems[0],
            recv_sem=sems[1],
            device_id=device,
            device_id_type=pl.DeviceIdType.MESH,
        )


def stage_blocks(order):
    counts, size = [], 16
    for dim in order:
        counts.append(5 * size // 4 if dim == LINE else size // 2)
        size = size // 4 if dim == LINE else size // 2
    return counts


class Scatter:
    def __init__(self, links, order, keep, sent, arrived, stages, send_sems, recv_sems, index, out, credits=None):
        self.links, self.order, self.keep, self.out = links, order, keep, out
        self.sent, self.arrived, self.credits = sent, arrived, credits
        self.sems = lambda step, way=0: (send_sems.at[index, step, way], recv_sems.at[index, step, way])
        self.plan = [] if sent is None else [("core",)]
        base, size = 0, 16
        for dim, buffer in zip(order, stages):
            if dim == LINE:
                size //= 4
                self.plan += [("line", turn, base, size, buffer) for turn in (1, 2, 3)]
                base = base + links.level * size
            else:
                size //= 2
                mine = links.mine[dim]
                self.plan.append(("halve", dim, base + (1 - mine) * size, base + mine * size, size, buffer))
                base = base + mine * size
        self.base = base
        self.plan.append(("both",))
        self.step = 0

    def place(self, shard):
        index, size = 0, 16
        for dim in self.order:
            size //= 4 if dim == LINE else 2
            index += size * {SECTION: shard // 8, LINE: shard // 2 % 4, SIDE: shard % 2}[dim]
        return index

    def single(self, step):
        links, kind = self.links, self.plan[step][0]
        if kind == "core":
            return links.copy(self.sent, self.arrived, self.sems(step), links.other_core)
        if kind == "halve":
            _, dim, away, _, size, buffer = self.plan[step]
            return links.copy(self.keep.at[pl.ds(away, size)], buffer, self.sems(step), links.partner[dim])
        return links.copy(self.out.at[links.core], self.out.at[links.core], self.sems(step), links.other_core)

    def lines(self, step):
        links, level = self.links, self.links.level
        _, turn, base, size, buffer = self.plan[step]
        shards = lambda ref, index: ref.at[pl.ds(index * size, size)]
        keep = lambda shard: self.keep.at[pl.ds(base + shard * size, size)]
        up, down = level + 4 - turn, level - 4 + turn
        return [
            (
                (level < turn) & (level < 3),
                lambda: links.copy(keep(up), shards(buffer, turn - level - 1), self.sems(step, 0), links.above),
                (level > 0) & (level <= turn),
                lambda: links.copy(keep(up - 1), shards(buffer, turn - level), self.sems(step, 0), links.above),
                lambda: (base + (up - 1) * size, (turn - level) * size),
                level == turn - 1,
            ),
            (
                (3 - level < turn) & (level > 0),
                lambda: links.copy(keep(down), shards(buffer, turn + 1), self.sems(step, 1), links.below),
                (level < 3) & (3 - level <= turn),
                lambda: links.copy(keep(down + 1), shards(buffer, turn + 1), self.sems(step, 1), links.below),
                lambda: (base + (down + 1) * size, (turn + 1) * size),
                3 - level == turn - 1,
            ),
        ]

    def start(self):
        step = self.step
        plan = self.plan[step]
        if plan[0] == "line":
            for way, (sends, sent, _, _, _, opens) in enumerate(self.lines(step)):

                @pl.when(sends)
                def _():
                    if self.credits is not None:

                        @pl.when(opens)
                        def _():
                            pl.semaphore_wait(self.credits.at[3 + way], 1)

                    sent().start()

            return
        if self.credits is not None and plan[0] != "both":
            pl.semaphore_wait(self.credits.at[0 if plan[0] == "core" else 1 + plan[1]], 1)
        if plan[0] == "both":
            self.out[pl.ds(self.links.core, 1)] = self.keep[pl.ds(self.base, 1)]
        self.single(step).start()

    def add(self, source, first, base, size):
        keep = self.keep

        def body(i, carry):
            keep[base + i] = keep[base + i] + source[first + i]
            return carry

        lax.fori_loop(0, size, body, 0)

    def finish(self):
        step = self.step
        plan = self.plan[step]
        if plan[0] == "line":
            for _, _, comes, arrived, where, _ in self.lines(step):

                @pl.when(comes)
                def _():
                    arrived().wait_recv()
                    base, first = where()
                    self.add(plan[4], first, base, plan[3])

        else:
            self.single(step).wait_recv()
            if plan[0] == "core":
                self.add(self.arrived, 0, 0, 16)
            elif plan[0] == "halve":
                self.add(plan[5], 0, plan[3], plan[4])
        self.step += 1

    def advance(self):
        self.finish()
        if self.step < len(self.plan):
            self.start()

    def close(self):
        assert self.step == len(self.plan)
        for step, plan in enumerate(self.plan):
            if plan[0] == "line":
                for sends, sent, _, _, _, _ in self.lines(step):

                    @pl.when(sends)
                    def _():
                        sent().wait_send()

            else:
                self.single(step).wait_send()


class Total:
    def __init__(self, links, levels, arrived, send_sems, recv_sems, index):
        self.links, self.levels, self.arrived = links, levels, arrived
        level = links.level
        everyone = level >= 0
        near = {"dp": links.lane + 2 - 4 * (level % 2)}
        middle = {"dp": links.lane + 6 - 4 * level}
        inner = (level == 1) | (level == 2)
        outer = {"dp": links.lane - 6 + 4 * level}
        self.turns = [
            (everyone, everyone, links.other_core), (everyone, everyone, links.partner[SECTION]),
            (everyone, everyone, near), (inner, inner, middle), (inner, jnp.logical_not(inner), outer),
            (everyone, everyone, links.partner[SIDE]),
        ]
        self.sems = lambda step: (send_sems.at[index, step, 0], recv_sems.at[index, step, 0])
        self.step = 0
        self.result = levels.at[0]

    def copy_of(self, step):
        return self.links.copy(
            self.levels.at[step % 2], self.arrived.at[step - step // 4], self.sems(step), self.turns[step][2]
        )

    def start(self):
        step = self.step

        @pl.when(self.turns[step][0])
        def _():
            self.copy_of(step).start()

    def sent(self, step):
        @pl.when(self.turns[step][0])
        def _():
            self.copy_of(step).wait_send()

    def advance(self):
        step = self.step
        if step > 0:
            self.sent(step - 1)
        comes = self.turns[step][1]

        @pl.when(comes)
        def _():
            self.copy_of(step).wait_recv()
            value = self.arrived[step - step // 4].astype(F32)
            if step != 4:
                value = self.levels[step % 2].astype(F32) + value
            self.levels[(step + 1) % 2] = value.astype(self.levels.dtype)

        @pl.when(jnp.logical_not(comes))
        def _():
            self.levels[(step + 1) % 2] = self.levels[step % 2]

        self.step += 1
        if self.step < 6:
            self.start()

    def close(self):
        assert self.step == 6
        self.sent(5)


ACT_NAMES = ("low_d", "hidden_d", "active_d", "branch_d")
IN_NAMES = (
    "memory", "cross_memory", "second", "active", "reduce", "slope", "expand", "first", "low", "mixed", "combine",
    "packed", "logs", "x", "project", "self_project", "self_combine", "cross_query",
)
ATTEND_BLOCK = 256


def backward_kernel(*refs):
    refs = list(refs)

    def draw(count):
        taken = refs[:count]
        del refs[:count]
        return taken

    source = dict(zip(IN_NAMES, draw(len(IN_NAMES))))
    source["x"] = source["x"].at[lax.axis_index("section")]
    decode_refs = dict(zip(DECODE_WEIGHTS, draw(7)))
    gain_ref, starts_ref, self_gain_ref, self_shift_ref, head_ref, target_ref, arm_ref = draw(7)
    outs = dict(zip(NAMES, draw(len(NAMES))))
    memory_out, slab_out, grad_memory_out, grad_x_out, self_rows_out, stack_out = draw(6)
    acts = dict(zip(ACT_NAMES, draw(4)))
    buffers = {}
    for name in NAMES:
        if name.startswith("decoder"):
            buffers[name] = [None, None] + draw(3)
        elif not name.startswith("encoder_expand"):
            buffers[name] = draw(5)
    keeps = {}
    for name in NAMES:
        if not name.startswith("encoder_expand"):
            keeps[name] = draw(1)[0]
    expand_stages = [draw(3), draw(3)]
    hidden, slope, grad_mixed, resid, mixed, branch, small_levels, small_arrived, tiny_levels, tiny_arrived = draw(10)
    send_sems, recv_sems, act_sems, slab_sems, load_sems, decode_sems, store_sems, credits = draw(8)
    valid = starts_ref.shape[0]
    width = resid.shape[1]
    count = resid.shape[0]
    hidden_size = hidden.shape[1]
    cut = split_of(hidden_size)
    for index, columns in enumerate((pl.ds(0, cut), pl.ds(cut, hidden_size - cut))):
        name = "encoder_expand%d" % index
        rows = lambda start, size: slope.at[pl.ds(start, size), :, columns]
        keeps[name] = rows(0, 16)
        buffers[name] = [rows(16, 16), rows(32, 16)] + expand_stages[index]

    links = Links()
    core = links.core
    block = 256
    chunks = column_chunks(hidden_size)
    own_columns = pl.ds(pl.multiple_of(core * 256, 256), 256)
    other_columns = pl.ds(pl.multiple_of((1 - core) * 256, 256), 256)
    work = {}
    for index, name in enumerate(NAMES):
        sent, arrived, *stages = buffers[name]
        work[name] = Scatter(
            links, GROUPS[name], keeps[name], sent, arrived, stages, send_sems, recv_sems, index, outs[name],
            credits.at[int(name[-1])] if name.startswith("encoder_expand") else None,
        )
    work["small"] = Total(links, small_levels, small_arrived, send_sems, recv_sems, len(NAMES))
    work["tiny"] = Total(links, tiny_levels, tiny_arrived, send_sems, recv_sems, len(NAMES) + 1)

    def tick(label):
        for name in SCHEDULE.get(label, ()):
            work[name].advance()

    def loading(name, target):
        return pltpu.make_async_copy(source[name], target, load_sems.at[IN_NAMES.index(name)])

    def load(name, target):
        copy = loading(name, target)
        copy.start()
        return copy

    def deal(name, rows, first_column):
        item = work[name]
        columns = pl.ds(first_column, rows.shape[1])
        low = rows.astype(BF16)
        for shard in range(16):
            here = low[32 * shard : 32 * shard + 16]
            there = low[32 * shard + 16 : 32 * shard + 32]
            place = item.place(shard)
            item.keep[place, :, columns] = jnp.where(core == 0, here, there)
            item.sent[place, :, columns] = jnp.where(core == 0, there, here)

    def deal_columns(names, targets, rows):
        size = rows.shape[0] // 16
        for index, (name, target) in enumerate(zip(names, targets)):
            for shard in range(16):
                target[work[name].place(shard)] = rows[
                    size * shard : size * shard + size, LANES * index : LANES * index + LANES
                ].astype(BF16)

    links.greet()
    def slab_copies(out):
        parts = [pl.ds(index * (count // 2), count // 2) for index in range(2)]
        return [
            links.copy(
                out.at[part], slab_out.at[part], (slab_sems.at[0, index], slab_sems.at[1, index]), links.partner[SECTION]
            )
            for index, part in enumerate(parts)
        ]

    memory_copy = links.copy(source["memory"], memory_out, (act_sems.at[0, 4], act_sems.at[1, 4]), links.partner[SECTION])

    def act_copy(name):
        index = ACT_NAMES.index(name)
        return links.copy(
            acts[name].at[pl.ds(0, PAD_ROWS)], acts[name].at[pl.ds(PAD_ROWS, PAD_ROWS)],
            (act_sems.at[0, index], act_sems.at[1, index]), links.other_core,
        )

    def pad_starts(starts):
        starts[...] = jnp.zeros_like(starts)
        starts[pl.ds(0, valid), :] = starts_ref[...]

    def decode_phase(pair, starts, room0, room1, room2, *weights):
        held = dict(zip([name for name in DECODE_WEIGHTS if name != "pair"], weights), pair=pair)
        loads = {}
        for index, name in enumerate(DECODE_WEIGHTS):
            loads[name] = pltpu.make_async_copy(decode_refs[name], held[name], decode_sems.at[index])
            loads[name].start()
        links.meet()
        memory_copy.start()
        pad_starts(starts)

        def hand_out(name):
            act_copy(name).start()
            if name == "low_d":
                load("slope", slope)

        branch, dq, mixed, sums, head_grad = decode_body(
            lambda: links.section, valid, loads, held, starts, self_gain_ref, self_shift_ref, head_ref, target_ref,
            arm_ref, acts, hand_out, hidden, (room0, room1, room2),
        )
        load("active", hidden)
        small_levels[0, pl.ds(0, PAD_ROWS), :] = branch
        small_levels[0, pl.ds(PAD_ROWS, PAD_ROWS), :] = dq
        work["small"].start()
        tiny_levels[0] = jnp.zeros(tiny_levels.shape[1:], F32)
        tiny_levels[0, pl.ds(0, 4), :] = sums
        tiny_levels[0, pl.ds(8, head_ref.shape[0]), :] = head_grad
        deal("middle1", dot(mixed, branch, TN), 0)

    back_copies = slab_copies(grad_memory_out)
    front_copies = slab_copies(grad_x_out)

    def rows_phase(grad_pair, memory_w, residual, rows_low, reduce_w, expand_w, combine_w):
        loads = {
            name: load(name, target)
            for name, target in (
                ("cross_memory", memory_w), ("second", residual), ("memory", rows_low), ("reduce", reduce_w),
                ("expand", expand_w), ("mixed", mixed), ("combine", combine_w),
            )
        }
        loads.update(active=loading("active", hidden), slope=loading("slope", slope))

        for name in ACT_NAMES:
            act_copy(name).wait_recv()
        names = ("decoder_reduce0", "decoder_reduce1")
        deal_columns(
            names, [work[name].keep for name in names],
            dot(acts["active_d"][...], acts["branch_d"][:, own_columns], TN),
        )
        for name in names:
            work[name].start()
        tick("dfr")
        for index, (start, size) in enumerate(chunks):
            rows = dot(acts["low_d"][:, own_columns], acts["hidden_d"][:, pl.ds(start, size)], TN).astype(BF16)
            item = work["decoder_expand%d" % (index // 2)]
            columns = pl.ds(start - (index // 2) * cut, size)
            for shard in range(16):
                item.keep[item.place(shard), :, columns] = rows[16 * shard : 16 * shard + 16]
            if index % 2:
                item.start()
                tick("dfe%d" % (index // 2))

        loads["cross_memory"].wait()
        loads["second"].wait()
        sums = None
        for start in range(0, count, block):
            part = pl.ds(start, block)
            low_grad = dot(grad_pair[part, :], memory_w[...], NT).astype(BF16)
            grad_mixed[part, :] = low_grad
            grad = low_grad.astype(F32)
            rows, scale = normed(residual[part, :])
            fresh = [column_sum(grad * rows), column_sum(grad)]
            sums = fresh if sums is None else [old + new for old, new in zip(sums, fresh)]
            total = normed_back(grad, gain_ref[1:2, :], rows, scale)
            resid[part, :] = total
            branch[part, :] = total.astype(BF16)
        memory_store = pltpu.make_async_copy(grad_mixed, grad_memory_out, store_sems.at[0])
        memory_store.start()
        loads["first"] = load("first", residual)
        last_sums = sums
        tick("dmem")

        loads["active"].wait()
        names = ("encoder_reduce0", "encoder_reduce1")
        deal_columns(names, [work[name].sent for name in names], dot(hidden[...], branch[:, other_columns], TN))
        for name in names:
            work[name].start()
        memory_store.wait()

        @pl.when(links.section == 0)
        def _():
            for copy in back_copies:
                copy.start()

        tick("efr0")
        deal_columns(names, [work[name].keep for name in names], dot(hidden[...], branch[:, own_columns], TN))
        tick("efr1")
        loads["memory"].wait()
        deal("middle0", dot(rows_low[...], grad_pair[...], TN), 0)
        loads["low"] = load("low", rows_low)
        work["middle0"].start()
        tick("dwm")
        loads["reduce"].wait()
        loads["slope"].wait()
        for index, (start, size) in enumerate(chunks):
            columns = pl.ds(start, size)
            grad_active = dot(branch[...], reduce_w[columns, :], NT)
            inner = slope[:, :, columns].reshape(count, size).astype(F32)
            hidden[:, columns] = (grad_active * inner).astype(BF16)
            tick("du%d" % index)
        for half in range(2):
            links.tell([credits.at[half, index] for index in range(5)])
        loads["expand"].wait()
        resid[...] += dot(hidden[...], expand_w[...], NT)
        tick("df")

        loads["first"].wait()
        loads["combine"].wait()
        sums = None
        for start in range(0, count, block):
            part = pl.ds(start, block)
            grad = resid[part, :]
            rows, scale = normed(residual[part, :])
            fresh = [column_sum(grad * rows), column_sum(grad)]
            sums = fresh if sums is None else [old + new for old, new in zip(sums, fresh)]
            total = normed_back(grad, gain_ref[0:1, :], rows, scale)
            resid[part, :] = total
            low_grad = total.astype(BF16)
            branch[part, :] = low_grad
            grad_mixed[part, :] = dot(low_grad, combine_w[...], NT).astype(BF16)
        tiny_levels[0, 4:8, :] = jnp.concatenate([sums[0], last_sums[0], sums[1], last_sums[1]], axis=0)
        work["tiny"].start()
        tick("ln")
        loads["low"].wait()
        for index, (start, size) in enumerate(chunks):
            name = "encoder_expand%d" % (index // 2)
            deal(name, dot(rows_low[...], hidden[:, pl.ds(start, size)], TN), start - (index // 2) * cut)
            if index % 2:
                work[name].start()
                tick("efe%d" % (index // 2))

    def first_phases(pair):
        pl.run_scoped(
            functools.partial(decode_phase, pair),
            *[pltpu.VMEM((PAD_ROWS, width), BF16)] * 4,
            *[pltpu.VMEM(decode_refs[name].shape, BF16) for name in DECODE_WEIGHTS if name != "pair"],
        )
        pl.run_scoped(
            functools.partial(rows_phase, pair),
            pltpu.VMEM((width, 2 * width), BF16),
            pltpu.VMEM((count, width), F32),
            pltpu.VMEM((count, width), BF16),
            pltpu.VMEM((hidden_size, width), BF16),
            pltpu.VMEM((width, hidden_size), BF16),
            pltpu.VMEM((width, width), BF16),
        )

    pl.run_scoped(first_phases, pltpu.VMEM((count, 2 * width), BF16))

    def attend_phase(packed, logs, x, project_w, grad_packed, starts, self_project, self_combine, cross_query):
        loads = {
            name: load(name, target)
            for name, target in (
                ("packed", packed), ("logs", logs), ("x", x), ("project", project_w),
                ("self_project", self_project), ("self_combine", self_combine), ("cross_query", cross_query),
            )
        }
        loading("mixed", mixed).wait()
        deal("middle1", dot(mixed[...], branch[...], NN), width)
        work["middle1"].start()
        tick("dwc")
        loads["packed"].wait()
        loads["logs"].wait()
        pairs = width // LANES
        half = width // 2

        def last(index):
            columns = slice(index * half, index * half + half)
            for third in range(3):
                deal("last%d" % index, dot(x[...], grad_packed[third, :, columns], TN), third * half)
            work["last%d" % index].start()

        for pair in range(pairs):
            columns = pl.ds(pair * LANES, LANES)
            attend_back_pair(
                packed[:, columns],
                packed[:, pl.ds(width + pair * LANES, LANES)],
                packed[:, pl.ds(2 * width + pair * LANES, LANES)],
                grad_mixed[:, columns],
                mixed[columns, :],
                logs[pair],
                grad_packed, columns,
                lambda head: tick("att%d" % (2 * pair + head)),
            )
            if pair == pairs // 2 - 1:
                loads["x"].wait()
                last(0)
                tick("last0")
        loads["project"].wait()
        stores = []
        for index in range(2):
            part = pl.ds(index * (count // 2), count // 2)
            total = resid[part, :]
            for third in range(3):
                total = total + dot(
                    grad_packed[third, part, :], project_w[:, third * width : (third + 1) * width], NT
                )
            packed[part, pl.ds(0, width)] = total.astype(BF16)
            store = pltpu.make_async_copy(packed.at[part, pl.ds(0, width)], grad_x_out.at[part], store_sems.at[1 + index])
            store.start()
            tick("dx%d" % index)
            store.wait()

            @pl.when(links.section == 1)
            def _():
                front_copies[index].start()

        last(1)
        tick("last1")
        pad_starts(starts)
        for name in IN_NAMES[-3:]:
            loads[name].wait()
        for name in TAIL_FIRST:
            work[name].advance()
        rows = SMALL_ROWS // 2
        start_back(
            valid, starts[...], self_project[...], self_combine[...], cross_query[...], self_gain_ref[0:1, :],
            self_shift_ref[0:1, :], work["small"].result[pl.ds(0, rows), :].astype(F32),
            work["small"].result[pl.ds(rows, rows), :], links, self_rows_out, stack_out,
        )

    pl.run_scoped(
        attend_phase,
        pltpu.VMEM((count, 3 * width), BF16),
        pltpu.VMEM(source["logs"].shape, F32),
        pltpu.VMEM((count, width), BF16),
        pltpu.VMEM((width, 3 * width), BF16),
        pltpu.VMEM((3, count, width), BF16),
        pltpu.VMEM((PAD_ROWS, width), BF16),
        pltpu.VMEM((width, 3 * width), BF16),
        pltpu.VMEM((width, width), BF16),
        pltpu.VMEM((width, width), BF16),
    )
    for name in TAIL:
        work[name].advance()
    stack_out[pl.ds(SMALL_ROWS // 2 + 8, TINY_ROWS), :] = work["tiny"].result[...]
    memory_copy.wait()
    for copy in back_copies:
        copy.wait_recv()
    for name in ACT_NAMES:
        act_copy(name).wait_send()
    for item in work.values():
        item.close()
    for copy in back_copies:
        copy.wait_send()


def start_back(valid, starts, project_w, combine_w, query_w, gain, shift, resid, query_grad, links, rows_out, stack_out):
    width = starts.shape[1]
    own = rows_out.shape[0]
    place = (links.section * 8 + links.lane) * own
    chosen = lax.broadcasted_iota(jnp.int32, (width, own), 0) == place + lax.broadcasted_iota(
        jnp.int32, (width, own), 1
    )
    chosen = jnp.where(chosen, 1.0, 0.0).astype(BF16)
    select = lambda value: dot(value, chosen, NN).astype(BF16)
    queries, keys, values, mixed, kept, rows, scale, first = self_block(
        starts, project_w, combine_w, gain, shift, valid
    )
    rows_out[:, pl.ds(4 * width, width)] = dot(select(first.astype(BF16)), query_grad, TN)
    grad_first = resid + dot(query_grad, query_w, NT)
    gain_sum = column_sum(grad_first * rows)
    shift_sum = column_sum(grad_first)
    grad_resid = normed_back(grad_first, gain, rows, scale)
    branch = grad_resid.astype(BF16)
    rows_out[:, pl.ds(3 * width, width)] = dot(select(mixed), branch, TN)
    grad_mixed = dot(branch, combine_w, NT).astype(BF16)
    dq, dk, dv = few_attend_back(queries, keys, values, kept, grad_mixed)
    grad_packed = jnp.concatenate([dq, dk, dv], axis=1).astype(BF16)
    rows_out[:, pl.ds(0, 3 * width)] = dot(select(starts), grad_packed, TN)
    count = starts.shape[0]
    stack_out[pl.ds(0, count), :] = grad_resid + dot(grad_packed, project_w, NT)
    stack_out[pl.ds(count, 8), :] = jnp.concatenate([gain_sum, shift_sum, jnp.zeros((6, width), F32)], axis=0)


def attend_back_pair(queries, keys, values, grads, mixed, logs, out, columns, between):
    count = queries.shape[0]
    lane = lax.broadcasted_iota(jnp.int32, (1, LANES), 1)
    queries = queries * jnp.asarray(0.125, BF16)
    scaled_keys = keys * jnp.asarray(0.125, BF16)
    queries_t = queries.T
    grads_t = grads.T
    logs = logs.T
    shared = mixed.astype(F32) * grads_t.astype(F32)
    inner = jnp.concatenate([column_sum(shared[:64]), column_sum(shared[64:])], axis=0).T
    dq_parts = [[], []]
    dk_parts = []
    dv_parts = []
    for head in range(2):
        own = (lane < 64) if head == 0 else (lane >= 64)
        head_queries = jnp.where(own, queries, jnp.zeros_like(queries))
        head_grads = jnp.where(own, grads, jnp.zeros_like(grads))
        dk = None
        dv = None
        for start in range(0, count, ATTEND_BLOCK):
            part = slice(start, start + ATTEND_BLOCK)
            scores = dot(head_queries[part], keys, NT)
            probs = jnp.exp(scores - logs[part, head : head + 1])
            grad_probs = dot(head_grads[part], values, NT)
            grad_scores = (probs * (grad_probs - inner[part, head : head + 1])).astype(BF16)
            new_v = dot(grads_t[64 * head : 64 * head + 64, part], probs.astype(BF16), NN)
            new_k = dot(queries_t[64 * head : 64 * head + 64, part], grad_scores, NN)
            dv = new_v if dv is None else dv + new_v
            dk = new_k if dk is None else dk + new_k
            dq_parts[head].append(dot(grad_scores, scaled_keys, NN))
        dk_parts.append(dk)
        dv_parts.append(dv)
        if head == 0:
            between(0)
    out[1, :, columns] = jnp.concatenate(dk_parts, axis=0).T.astype(BF16)
    out[2, :, columns] = jnp.concatenate(dv_parts, axis=0).T.astype(BF16)
    for index in range(count // ATTEND_BLOCK):
        out[0, pl.ds(index * ATTEND_BLOCK, ATTEND_BLOCK), columns] = jnp.where(
            lane < 64, dq_parts[0][index], dq_parts[1][index]
        ).astype(BF16)
    between(1)


def chain_blocks(width, hidden_size):
    cut = split_of(hidden_size)
    blocks = {}
    for side in ("decoder", "encoder"):
        blocks[side + "_expand0"] = (16, cut)
        blocks[side + "_expand1"] = (16, hidden_size - cut)
        blocks[side + "_reduce0"] = (hidden_size // 16, LANES)
        blocks[side + "_reduce1"] = (hidden_size // 16, LANES)
    for name in ("middle0", "middle1"):
        blocks[name] = (16, 2 * width)
    for name in ("last0", "last1"):
        blocks[name] = (16, 3 * width // 2)
    return blocks


def backward_linked(saved, targets, arms, weights):
    count, width = saved["x"].shape[1:]
    hidden_size = saved["active"].shape[1]
    starts, head = weights[6], weights[16]
    arrays = dict(saved)
    arrays.update(
        cross_memory=weights[10], reduce=weights[3], expand=weights[2], combine=weights[1], project=weights[0],
        self_project=weights[7], self_combine=weights[8], cross_query=weights[9],
        slope=saved["slope"].reshape(count // 16, 16, hidden_size),
    )
    inputs = [arrays[name] for name in IN_NAMES]
    inputs += decode_sources(weights, saved["pair"])
    vectors = [weights[4], starts, weights[14], weights[15], head.T, targets.transpose(2, 0, 1)]
    blocks = chain_blocks(width, hidden_size)
    own = width // 16
    vmem = lambda counts, name: [pltpu.VMEM((n,) + blocks[name], BF16) for n in counts]
    scratch = [pltpu.VMEM((2 * PAD_ROWS, columns), BF16) for columns in (width, hidden_size, hidden_size, width)]
    for name in NAMES:
        if name.startswith("decoder"):
            scratch += vmem(stage_blocks(GROUPS[name]), name)
        elif not name.startswith("encoder_expand"):
            scratch += vmem([16, 16] + stage_blocks(GROUPS[name]), name)
    for name in NAMES:
        if not name.startswith("encoder_expand"):
            scratch += vmem((16,), name)
    for name in ("encoder_expand0", "encoder_expand1"):
        scratch += vmem(stage_blocks(GROUPS[name]), name)
    scratch += [
        pltpu.VMEM((count, hidden_size), BF16),
        pltpu.VMEM((count // 16, 16, hidden_size), BF16),
        pltpu.VMEM((count, width), BF16),
        pltpu.VMEM((count, width), F32),
        pltpu.VMEM((width, count), BF16),
        pltpu.VMEM((count, width), BF16),
        pltpu.VMEM((2, SMALL_ROWS, width), BF16),
        pltpu.VMEM((5, SMALL_ROWS, width), BF16),
        pltpu.VMEM((2, TINY_ROWS, width), F32),
        pltpu.VMEM((5, TINY_ROWS, width), F32),
        pltpu.SemaphoreType.DMA((len(NAMES) + 2, STEPS, 2)),
        pltpu.SemaphoreType.DMA((len(NAMES) + 2, STEPS, 2)),
        pltpu.SemaphoreType.DMA((2, 5)),
        pltpu.SemaphoreType.DMA((2, 2)),
        pltpu.SemaphoreType.DMA((len(IN_NAMES),)),
        pltpu.SemaphoreType.DMA((len(DECODE_WEIGHTS),)),
        pltpu.SemaphoreType.DMA((3,)),
        pltpu.SemaphoreType.REGULAR((2, 5)),
    ]
    in_any = pl.BlockSpec(memory_space=pl.ANY)
    in_vmem = pl.BlockSpec(memory_space=pltpu.VMEM)
    shape = shape_of((count, width), BF16)
    results = pl.pallas_call(
        backward_kernel,
        in_specs=[in_any] * len(inputs) + [in_vmem] * len(vectors) + [pl.BlockSpec(memory_space=pltpu.SMEM)],
        out_specs=[in_vmem] * len(NAMES) + [in_any] * 4 + [in_vmem] * 2,
        out_shape=[shape_of((2,) + blocks[name], BF16) for name in NAMES]
        + [shape] * 4
        + [shape_of((own, 5 * width), F32), shape_of((SMALL_ROWS // 2 + 8 + TINY_ROWS, width), F32)],
        scratch_shapes=scratch,
        compiler_params=pltpu.CompilerParams(
            collective_id=0, has_side_effects=True, vmem_limit_bytes=LINKED_VMEM_BYTES
        ),
        cost_estimate=pl.CostEstimate(flops=10**8, bytes_accessed=10**8, transcendentals=0),
    )(*inputs, *vectors, arms)
    memory, slab, grad_memory, grad_x, rows, stack = results[len(NAMES) :]
    return results[: len(NAMES)], memory, slab, grad_memory, grad_x, rows, stack


def finish_kernel(valid, joints, *refs):
    refs = list(refs)

    def draw(count):
        taken = refs[:count]
        del refs[:count]
        return taken

    count = len(NAMES)
    sources = draw(count + 7)
    targets = draw(19)
    held = draw(count + 7)
    results = draw(17)
    load_sems, store_sems = draw(2)
    loads = []
    for index in list(range(count, count + 7)) + list(range(count)):
        copy = pltpu.make_async_copy(sources[index], held[index], load_sems.at[index])
        copy.start()
        loads.append((index, copy))
    loads = dict(loads)
    stores = []
    section = lax.axis_index("section")
    memory, other, grad_x, grad_memory, other_slab = held[count + 2 :]
    memory_out, slab_out = targets[:2]

    def store(result):
        index = next(i for i, item in enumerate(results) if item is result)
        stores.append(pltpu.make_async_copy(result, targets[2 + index], store_sems.at[2 + index]))
        stores[-1].start()

    (
        project_e, combine_e, expand_e, reduce_e, gains_e, shifts_e, starts_d, project_d, combine_d, query_d,
        memory_d, cross_d, expand_d, reduce_d, gains_d, shifts_d, head_d,
    ) = results
    halves = dict(zip(NAMES, held[:count]))
    rows_ref, stack_ref = held[count : count + 2]
    width = memory.shape[1]
    own = rows_ref.shape[0]
    place = (section * 8 + lax.axis_index("dp")) * own
    loads[count].wait()
    loads[count + 1].wait()
    project_d[...] = rows_ref[:, : 3 * width]
    store(project_d)
    combine_d[...] = rows_ref[:, 3 * width : 4 * width]
    store(combine_d)
    query_d[...] = rows_ref[:, 4 * width :]
    store(query_d)
    chosen = lax.broadcasted_iota(jnp.int32, (width, own), 0) == place + lax.broadcasted_iota(
        jnp.int32, (width, own), 1
    )
    chosen = jnp.where(chosen, 1.0, 0.0)
    exact = functools.partial(lax.dot_general, precision=lax.Precision.HIGHEST, preferred_element_type=F32)
    picked = exact(stack_ref[pl.ds(PAD_ROWS, 8 + TINY_ROWS), :], chosen, NN)
    starts_d[...] = exact(chosen, stack_ref[pl.ds(0, PAD_ROWS), :], (((0,), (1,)), ((), ())))[:, :valid]
    store(starts_d)
    gains_d[...] = jnp.concatenate([picked[0:1], picked[8:10]], axis=0)
    shifts_d[...] = jnp.concatenate([picked[1:2], picked[10:12]], axis=0)
    gains_e[...] = picked[12:14]
    shifts_e[...] = picked[14:16]
    head_d[...] = picked[16 : 16 + joints]
    for result in (gains_d, shifts_d, gains_e, shifts_e, head_d):
        store(result)
    for index, (out, front, back) in enumerate(
        (
            ((memory_out.at[0], memory_out.at[1]), (memory, other), (other, memory)),
            ((slab_out.at[0, 0], slab_out.at[0, 1]), (grad_x, other_slab), (other_slab, grad_memory)),
        )
    ):
        for number in (2, 3) if index == 0 else (4, 5, 6):
            loads[count + number].wait()
        for way in range(2):
            ahead = pltpu.make_async_copy(front[way], out[way], store_sems.at[19 + 2 * index + way])
            behind = pltpu.make_async_copy(back[way], out[way], store_sems.at[19 + 2 * index + way])

            @pl.when(section == 0)
            def _():
                ahead.start()

            @pl.when(section == 1)
            def _():
                behind.start()

            stores.append(ahead)

    waiting = set(NAMES)

    def arrive(name):
        if name in waiting:
            waiting.remove(name)
            loads[NAMES.index(name)].wait()

    def rows_of(name, out, columns, first=0):
        arrive(name)
        for core in range(2):
            out[pl.ds(16 * core, 16), columns] = halves[name][core, :, first : first + columns.size].astype(F32)

    cut = halves["encoder_expand0"].shape[2]
    for side, out in (("encoder", expand_e), ("decoder", expand_d)):
        rows_of(side + "_expand0", out, pl.ds(0, cut))
        rows_of(side + "_expand1", out, pl.ds(cut, out.shape[1] - cut))
        store(out)
    for side, out in (("encoder", reduce_e), ("decoder", reduce_d)):
        for core in range(2):
            for index in range(2):
                arrive(side + "_reduce%d" % index)
                out[:, pl.ds((2 * core + index) * LANES, LANES)] = halves[side + "_reduce%d" % index][core].astype(F32)
        store(out)
    rows_of("middle0", memory_d, pl.ds(0, 2 * width))
    store(memory_d)
    rows_of("middle1", cross_d, pl.ds(0, width))
    store(cross_d)
    rows_of("middle1", combine_e, pl.ds(0, width), width)
    store(combine_e)
    half = width // 2
    for third in range(3):
        for index in range(2):
            rows_of("last%d" % index, project_e, pl.ds(third * width + index * half, half), third * half)
    store(project_e)
    for copy in stores:
        copy.wait()


def finish(valid, joints, halves, rows, stack, memory, other, grad_x, grad_memory, other_slab):
    count, width = memory.shape
    own = rows.shape[0]
    hidden_size = halves[0].shape[2] + halves[1].shape[2]
    in_any = pl.BlockSpec(memory_space=pl.ANY)
    shapes = [
        (own, 3 * width), (own, width), (own, hidden_size), (hidden_size // 16, width), (2, own), (2, own),
        (own, valid), (own, 3 * width), (own, width), (own, width), (own, 2 * width), (own, width),
        (own, hidden_size), (hidden_size // 16, width), (3, own), (3, own), (joints, own),
    ]
    inputs = (*halves, rows, stack, memory, other, grad_x, grad_memory, other_slab)
    results = list(
        call(
            functools.partial(finish_kernel, valid, joints),
            10**6, 10**7,
            in_specs=[in_any] * len(inputs),
            out_specs=[in_any] * (2 + len(shapes)),
            out_shape=[shape_of((2, count, width), BF16), shape_of((1, 2, count, width), BF16)]
            + [shape_of(dims, F32) for dims in shapes],
            scratch_shapes=[pltpu.VMEM(item.shape, item.dtype) for item in inputs]
            + [pltpu.VMEM(dims, F32) for dims in shapes]
            + [pltpu.SemaphoreType.DMA((len(inputs),)), pltpu.SemaphoreType.DMA((23,))],
        )(*inputs)
    )
    results[8] = results[8].T
    results[18] = results[18].T
    return tuple(results)


def swap(value, axis, bit):
    pairs = [(i, i ^ (1 << bit)) for i in range(lax.axis_size(axis))]
    return lax.ppermute(value, axis, pairs)


def plain_scatter(full):
    part = lax.psum_scatter(full.astype(F32), ("section", "dp"), scatter_dimension=0, tiled=True)
    return lax.psum(part, "rep")


def per_device(x, targets, arms, *weights):
    section = lax.axis_index("section")
    sections = lax.axis_size("section")
    lanes = lax.axis_size("dp")
    count = x.shape[0] // sections
    starts, head = weights[6], weights[16]
    valid, joints = starts.shape[0], head.shape[1]
    width = starts.shape[1]
    first = section == 0
    place = section * lanes + lax.axis_index("dp")
    own = width // (sections * lanes)
    linked = (sections, lanes, lax.axis_size("rep"), count) == (2, 8, 2, 1)
    saved = []
    for index in range(count):
        pick = functools.partial(lambda i: lax.axis_index("section") * count + i, index)
        saved.append(forward(x, pick, weights))
        if not linked:
            saved[-1].update(decode(pick, targets, arms, weights, saved[-1].pop("pair")))
    if linked:
        halves, other, other_slab, grad_memory, grad_x, rows, stack = backward_linked(saved[0], targets, arms, weights)
        return finish(
            valid, joints, halves, rows, stack, saved[0]["memory"], other, grad_x, grad_memory, other_slab
        )
    memory = jnp.concatenate([item["memory"][None] for item in saved])
    results = []
    for index, item in enumerate(saved):
        results.append(
            backward_alone(item, lax.dynamic_index_in_dim(x, section * count + index, 0, keepdims=False), weights)
        )
    grad_x = jnp.concatenate([item[0][None] for item in results])
    grad_memory = jnp.concatenate([item[1][None] for item in results])
    total = lambda name: functools.reduce(jnp.add, [item[2][name] for item in results])
    other = swap(memory, "section", 0)
    other_slab = swap(jnp.where(first, grad_memory, grad_x), "section", 0)
    small = lax.psum(total("small"), ("section", "dp", "rep"))
    tiny = lax.psum(total("tiny"), ("section", "dp", "rep"))
    done = {
        name: plain_scatter(total(name))
        for name in ("decoder_expand", "decoder_reduce", "encoder_expand", "encoder_reduce", "middle", "last")
    }
    memory_out = jnp.concatenate([jnp.where(first, memory, other), jnp.where(first, other, memory)])
    slab = jnp.concatenate(
        [jnp.where(first, grad_x, other_slab), jnp.where(first, other_slab, grad_memory)]
    )[None]

    columns_of = lambda array: lax.dynamic_slice_in_dim(array, place * own, own, 1)
    rows_of = lambda array: lax.dynamic_slice_in_dim(array, place * own, own, 0)
    resid_d, query_d = small[:PAD_ROWS], small[PAD_ROWS:]
    start_grad, project_d, combine_d, query_w, sums_s = decode_start_back(
        valid, jnp.pad(starts, ((0, PAD_ROWS - valid), (0, 0))), weights[7], weights[8], weights[9],
        weights[14], weights[15], resid_d, query_d,
    )
    gains_d = jnp.concatenate([sums_s[0:1], tiny[0:2]])
    shifts_d = jnp.concatenate([sums_s[1:2], tiny[2:4]])
    return (
        memory_out,
        slab,
        done["last"],
        done["middle"][:, 3 * width :],
        done["encoder_expand"],
        done["encoder_reduce"],
        columns_of(tiny[4:6]),
        columns_of(tiny[6:8]),
        columns_of(start_grad[:valid]),
        rows_of(project_d),
        rows_of(combine_d),
        rows_of(query_w),
        done["middle"][:, : 2 * width],
        done["middle"][:, 2 * width : 3 * width],
        done["decoder_expand"],
        done["decoder_reduce"],
        columns_of(gains_d),
        columns_of(shifts_d),
        rows_of(tiny[8 : 8 + joints].T),
    )


def solution(mesh):
    spread = ("section", "dp")
    rows = P(spread, None)
    columns = P(None, spread)
    return jax.shard_map(
        per_device,
        mesh=mesh,
        in_specs=(P(("dp", "rep"), None, None), P(("dp", "rep"), None, None), P(("dp", "rep"))) + (P(),) * 17,
        out_specs=(
            P(("dp", "rep"), None, None),
            P("section", ("dp", "rep"), None, None),
            rows, rows, rows, rows, columns, columns, columns,
            rows, rows, rows, rows, rows, rows, rows, columns, columns, rows,
        ),
        check_vma=False,
    )
```
